32 devices in a mesh: dp: 4 (over y, x), fsdp: 8 (over z, core).
Axes of the slice: x: 2, y: 2, z: 4, core: 2. Of those that a mesh axis runs over, the one named last changes fastest.
Arguments:
- tokens: bfloat16 [2, 5120, 960], P(None, ('dp', 'fsdp')), may hold values from -6 to 6
- cotangent: bfloat16 [2, 5120, 960], P(None, ('dp', 'fsdp')), may hold values from -6 to 6
- counts: int32 [2, 32], P(None, ('dp', 'fsdp')), may hold values from 128 to 160, as said below
- w_query: bfloat16 [960, 960], P('dp', 'fsdp'), may hold values from -0.25 to 0.25
- key_weight: bfloat16 [960, 320], P('dp', 'fsdp'), may hold values from -0.25 to 0.25
- value_weight: bfloat16 [960, 320], P('dp', 'fsdp'), may hold values from -0.1875 to 0.1875
- w_out: bfloat16 [960, 960], P('dp', 'fsdp'), may hold values from -0.75 to 0.75
- w_gate: bfloat16 [960, 2560], P('dp', 'fsdp'), may hold values from -0.1875 to 0.1875
- w_up: bfloat16 [960, 2560], P('dp', 'fsdp'), may hold values from -0.1875 to 0.1875
- w_down: bfloat16 [2560, 960], P('dp', 'fsdp'), may hold values from -0.125 to 0.125
- gains: bfloat16 [2, 960], P(None, 'fsdp'), may hold values from 0.5 to 1.5
Outputs:
- output: bfloat16 [2, 5120, 960], P(None, ('dp', 'fsdp'))
- grad_tokens: float32 [2, 5120, 960], P(None, ('dp', 'fsdp'))
- grad_query: float32 [960, 960], P('dp', 'fsdp')
- grad_key: float32 [960, 320], P('dp', 'fsdp')
- grad_value: float32 [960, 320], P('dp', 'fsdp')
- grad_out: float32 [960, 960], P('dp', 'fsdp')
- grad_gate: float32 [960, 2560], P('dp', 'fsdp')
- grad_up: float32 [960, 2560], P('dp', 'fsdp')
- grad_down: float32 [2560, 960], P('dp', 'fsdp')
- grad_gains: float32 [2, 960], P(None, 'fsdp')
The draws below stay inside these ranges and needn't reach their ends.
Inputs may be any that keep to these rules, and one draw needn't show every extreme that they name: `counts`: the used slots of the 8 devices that share a dp index form one sequence per micro-batch, in device order; in every such group and micro-batch some device uses all 160 slots.
All inputs are finite; a program needn't handle non-finite values.
Results may differ from the reference program's by a relative error of at most 0.02.
Values may be sent and summed in bfloat16 or wider, within the bound.
No kernel may reach another device: no remote copies, remote signals or barrier semaphores. Data moves between devices by JAX's collectives and lax.ppermute only.
A program may use at most 192 MiB of HBM per device.

```python
import jax
import jax.numpy as jnp
from jax import lax

MODEL_WIDTH = 960
QUERY_HEADS = 15
KEY_HEADS = 5
HEAD_WIDTH = 64
FF = 2560
MB = 2
CAP = 160
TOKENS = 5120
N_DP = 4
N_FSDP = 8


def draw_counts(key, part):
    key = jax.random.fold_in(key, 7)
    key_fill, key_full = jax.random.split(key)
    load_base = jax.random.randint(key_fill, (MB, N_DP, N_FSDP), CAP - CAP // 5, CAP + 1)
    chosen = jax.random.randint(key_full, (MB, N_DP, 1), 0, N_FSDP)
    device_slot = jnp.arange(N_FSDP, dtype=jnp.int32)[None, None, :]
    filled = jnp.where(device_slot == chosen, CAP, load_base)
    return filled.reshape(MB, N_DP * N_FSDP).astype(jnp.int32)


def steps_of(own_key, extent, pieces, low, high):
    def one(dim, shards_of):
        steps = jax.random.uniform(jax.random.fold_in(jax.random.fold_in(own_key, 6), dim), (shards_of,), jnp.float32, low / len(pieces), high / len(pieces))
        return jnp.repeat(jnp.exp(steps), extent[dim] // shards_of).reshape((-1,) + (1,) * (len(extent) - dim - 1))

    level = one(*pieces[0])
    for cut in pieces[1:]:
        level = level * one(*cut)
    return level


def noise(rng, dims, scale, reach, pieces=(), kind=jnp.bfloat16):
    drawn = jax.random.normal(rng, dims, jnp.float32) * scale
    if len(pieces) > 0:
        drawn = steps_of(rng, dims, pieces, -0.22, 0.18) * drawn
    return jnp.clip(drawn, min=-reach, max=reach).astype(kind)


def setup_inputs(seed: int = 0) -> dict:
    arg_keys = jax.random.split(jax.random.key(seed), 12)
    tokens = noise(arg_keys[0], (MB, TOKENS, MODEL_WIDTH), 1.0, 6.0, ((1, 32),))
    cotangent = noise(arg_keys[1], (MB, TOKENS, MODEL_WIDTH), 1.0, 6.0, ((1, 32),))
    counts = draw_counts(jax.random.fold_in(arg_keys[11], 71), 0)
    w_query = noise(arg_keys[3], (MODEL_WIDTH, MODEL_WIDTH), (MODEL_WIDTH // 2) ** -0.5, 0.25, ((0, 4), (1, 8)))
    key_weight = noise(arg_keys[4], (MODEL_WIDTH, KEY_HEADS * HEAD_WIDTH), (MODEL_WIDTH // 2) ** -0.5, 0.25, ((0, 4), (1, 8)))
    value_weight = noise(arg_keys[5], (MODEL_WIDTH, KEY_HEADS * HEAD_WIDTH), MODEL_WIDTH ** -0.5, 0.1875, ((0, 4), (1, 8)))
    w_out = noise(arg_keys[6], (MODEL_WIDTH, MODEL_WIDTH), (MODEL_WIDTH // 16) ** -0.5, 0.75, ((0, 4), (1, 8)))
    w_gate = noise(arg_keys[7], (MODEL_WIDTH, FF), MODEL_WIDTH ** -0.5, 0.1875, ((0, 4), (1, 8)))
    w_up = noise(arg_keys[8], (MODEL_WIDTH, FF), MODEL_WIDTH ** -0.5, 0.1875, ((0, 4), (1, 8)))
    w_down = noise(arg_keys[9], (FF, MODEL_WIDTH), FF ** -0.5, 0.125, ((0, 4), (1, 8)))
    gains = jnp.clip(1.0 + 0.1 * jax.random.normal(arg_keys[10], (2, MODEL_WIDTH), jnp.float32), 0.5, 1.5).astype(jnp.bfloat16)
    return {"tokens": tokens, "cotangent": cotangent, "counts": counts, "w_query": w_query, "key_weight": key_weight, "value_weight": value_weight, "w_out": w_out, "w_gate": w_gate, "w_up": w_up, "w_down": w_down, "gains": gains}


EPSILON = 1e-05
ROPE_BASE = 100000.0
SCORE_SCALE = 0.125
PRECISE = lax.Precision.HIGHEST

@jax.custom_vjp
def low(v):
    return lax.optimization_barrier(v.astype(jnp.bfloat16)).astype(jnp.float32)

@jax.custom_vjp
def low_back(v):
    return v

def low_keep(v):
    return (low(v), None)

def low_pass(kept, grad):
    return (grad,)

def back_keep(v):
    return (v, None)

def back_low(kept, grad):
    return (low(grad),)
low.defvjp(low_keep, low_pass)
low_back.defvjp(back_keep, back_low)

def exact_product(left, right):
    return jnp.dot(left, right, precision=PRECISE)

def rms_norm(values, gain_row):
    inv_rms = lax.rsqrt(lax.optimization_barrier(jnp.mean(values * values, -1, keepdims=True)) + EPSILON)
    return values * inv_rms * gain_row

def rope_tables(position, head_size):
    half_size = head_size // 2
    frequency = ROPE_BASE ** (-(jnp.arange(half_size, dtype=jnp.float32) * 2.0) / head_size)
    angles = position.astype(jnp.float32)[:, None] * frequency[None, :]
    return (jnp.cos(angles)[:, None, :], jnp.sin(angles)[:, None, :])

def apply_rotation(values, cosine_table, sine_values):
    half_size = values.shape[-1] // 2
    front_half = values[..., :half_size]
    back_half = values[..., half_size:]
    return jnp.concatenate([front_half * cosine_table - back_half * sine_values, back_half * cosine_table + front_half * sine_values], -1)

def group_forward(group_tokens, group_counts, weights):
    w_query, key_weight, value_weight, w_out, w_gate, w_up, w_down, gains = weights
    sequence_length = group_tokens.shape[0]
    local_slot = jnp.arange(CAP, dtype=jnp.int32)
    offsets = (jnp.cumsum(group_counts) - group_counts).astype(jnp.int32)
    position = (offsets[:, None] + local_slot[None, :]).reshape(-1).astype(jnp.int32)
    is_valid = (local_slot[None, :] < group_counts[:, None]).reshape(-1)
    slot_ids = jnp.arange(sequence_length, dtype=jnp.int32)
    allowed = is_valid[:, None] & is_valid[None, :] & (position[None, :] <= position[:, None]) | (slot_ids[:, None] == slot_ids[None, :])
    cosine_table, sine_values = rope_tables(position, HEAD_WIDTH)
    first_normed = low(rms_norm(group_tokens, gains[0]))
    query_rows = low(apply_rotation(low_back(exact_product(first_normed, w_query)).reshape(sequence_length, QUERY_HEADS, HEAD_WIDTH), cosine_table, sine_values))
    rows_of_key = low(apply_rotation(low_back(exact_product(first_normed, key_weight)).reshape(sequence_length, KEY_HEADS, HEAD_WIDTH), cosine_table, sine_values))
    rows_of_value = low(low_back(exact_product(first_normed, value_weight))).reshape(sequence_length, KEY_HEADS, HEAD_WIDTH)
    heads_of_query = query_rows.reshape(sequence_length, KEY_HEADS, QUERY_HEADS // KEY_HEADS, HEAD_WIDTH)
    scores = low_back(jnp.einsum('qngd,knd->ngqk', heads_of_query, rows_of_key, precision=PRECISE) * SCORE_SCALE)
    masked = jnp.where(allowed, scores, -1e+30)
    row_top = lax.optimization_barrier(jnp.max(masked, -1, keepdims=True))
    exponent = jnp.where(allowed, jnp.exp(masked - row_top), 0.0)
    probability = low(exponent / lax.optimization_barrier(jnp.sum(exponent, -1, keepdims=True)))
    mixed_heads = jnp.einsum('ngqk,knd->qngd', probability, rows_of_value, precision=PRECISE).reshape(sequence_length, MODEL_WIDTH)
    attended = low(low_back(mixed_heads))
    hidden_state = group_tokens + low_back(exact_product(attended, w_out))
    normed_two = low(rms_norm(hidden_state, gains[1]))
    gate_act = low_back(exact_product(normed_two, w_gate))
    upward = low_back(exact_product(normed_two, w_up))
    product = low(jax.nn.silu(gate_act) * upward)
    return hidden_state + exact_product(product, w_down)

def reference(tokens, cotangent, counts, w_query, key_weight, value_weight, w_out, w_gate, w_up, w_down, gains):
    primals = tuple((member.astype(jnp.float32) for member in (tokens, w_query, key_weight, value_weight, w_out, w_gate, w_up, w_down, gains)))
    group_counts = counts.reshape(MB * N_DP, N_FSDP).astype(jnp.int32)

    def forward(inputs, q_weight, k_weight, v_weight, o_weight, g_weight, u_weight, d_weight, gain_rows):
        weights = (q_weight, k_weight, v_weight, o_weight, g_weight, u_weight, d_weight, gain_rows)
        grouped = inputs.reshape(MB * N_DP, N_FSDP * CAP, MODEL_WIDTH)

        def group_step(member):
            return group_forward(member[0], member[1], weights)
        results = lax.map(jax.checkpoint(group_step), (grouped, group_counts))
        return results.reshape(MB, TOKENS, MODEL_WIDTH)
    output, pullback = jax.vjp(forward, *primals)
    gradients = pullback(cotangent.astype(jnp.float32))
    return (output.astype(jnp.bfloat16), gradients[0], gradients[1], gradients[2], gradients[3], gradients[4], gradients[5], gradients[6], gradients[7], gradients[8])
```

```python
import jax
import jax.numpy as jnp
from jax import lax
from jax.experimental import pallas as pl
from jax.experimental.pallas import tpu as pltpu
from jax.sharding import PartitionSpec as P

MODEL_WIDTH = 960
QUERY_HEADS = 15
KEY_HEADS = 5
HEAD_WIDTH = 64


EPSILON = 1e-05
ROPE_BASE = 100000.0
SCORE_SCALE = 0.125


def rope_tables(position, head_size):
    half_size = head_size // 2
    frequency = ROPE_BASE ** (-(jnp.arange(half_size, dtype=jnp.float32) * 2.0) / head_size)
    angles = position.astype(jnp.float32)[:, None] * frequency[None, :]
    return (jnp.cos(angles)[:, None, :], jnp.sin(angles)[:, None, :])


def apply_rotation(values, cosine_table, sine_values):
    half_size = values.shape[-1] // 2
    front_half = values[..., :half_size]
    back_half = values[..., half_size:]
    return jnp.concatenate(
        [
            front_half * cosine_table - back_half * sine_values,
            back_half * cosine_table + front_half * sine_values,
        ],
        -1,
    )


def normalize(values, gain_row):
    inv_rms = lax.rsqrt(jnp.mean(values * values, -1, keepdims=True) + EPSILON)
    return (values * inv_rms * gain_row, inv_rms)


def norm_back(values, inv_rms, gain_row, incoming):
    weighted = incoming * gain_row
    return inv_rms * weighted - values * inv_rms * inv_rms * inv_rms * jnp.mean(
        weighted * values, -1, keepdims=True
    )


def build_mask(count_row, device, slot_capacity):
    group_width = count_row.shape[0]
    local_slot = jnp.arange(slot_capacity, dtype=jnp.int32)
    offsets = jnp.cumsum(count_row) - count_row
    is_mine = jnp.arange(group_width, dtype=jnp.int32) == device
    own_offset = jnp.sum(jnp.where(is_mine, offsets, 0))
    own_count = jnp.sum(jnp.where(is_mine, count_row, 0))
    query_pos = own_offset + local_slot
    query_valid = local_slot < own_count
    key_pos = (offsets[:, None] + local_slot[None, :]).reshape(-1)
    key_valid = (local_slot[None, :] < count_row[:, None]).reshape(-1)
    slot_ids = jnp.arange(group_width * slot_capacity, dtype=jnp.int32)
    own_slots = device * slot_capacity + local_slot
    allowed = query_valid[:, None] & key_valid[None, :] & (
        key_pos[None, :] <= query_pos[:, None]
    ) | (slot_ids[None, :] == own_slots[:, None])
    return (allowed, query_pos)


def kept_fetch(w_query, key_weight, value_weight, w_out, w_gate, w_up, w_down, gains):
    columns = (
        lax.all_gather(w_query, "fsdp", axis=1, tiled=True),
        lax.all_gather(key_weight, "fsdp", axis=1, tiled=True),
        lax.all_gather(value_weight, "fsdp", axis=1, tiled=True),
        lax.all_gather(w_out, "fsdp", axis=1, tiled=True),
        lax.all_gather(w_gate, "fsdp", axis=1, tiled=True),
        lax.all_gather(w_up, "fsdp", axis=1, tiled=True),
        lax.all_gather(w_down, "fsdp", axis=1, tiled=True),
        lax.all_gather(gains, "fsdp", axis=1, tiled=True),
    )
    matrices = (
        lax.all_gather(columns[0], "dp", axis=0, tiled=True),
        lax.all_gather(columns[1], "dp", axis=0, tiled=True),
        lax.all_gather(columns[2], "dp", axis=0, tiled=True),
        lax.all_gather(columns[3], "dp", axis=0, tiled=True),
        lax.all_gather(columns[4], "dp", axis=0, tiled=True),
        lax.all_gather(columns[5], "dp", axis=0, tiled=True),
        lax.all_gather(columns[6], "dp", axis=0, tiled=True),
    )
    return (matrices, columns[7].astype(jnp.float32))


def times_transpose(left, right):
    return jnp.einsum("rk,jk->rj", left, right, preferred_element_type=jnp.float32)


def rows_product(left, right):
    return jnp.einsum("rd,rk->dk", left, right, preferred_element_type=jnp.float32)


def local(
    tokens, cotangent, counts, w_query, key_weight, value_weight, w_out, w_gate, w_up, w_down, gains
):
    group_counts = lax.all_gather(counts, "fsdp", axis=1, tiled=True)
    device = lax.axis_index("fsdp")
    slot_capacity = tokens.shape[1]
    key_value_width = KEY_HEADS * HEAD_WIDTH
    device_share = QUERY_HEADS // KEY_HEADS
    kept_weights, kept_gain = kept_fetch(
        w_query, key_weight, value_weight, w_out, w_gate, w_up, w_down, gains
    )
    outputs = []
    grad_inputs = []
    saved = [[] for index_unused in range(11)]
    gain_one_total = jnp.zeros((MODEL_WIDTH,), jnp.float32)
    gain_two_total = jnp.zeros((MODEL_WIDTH,), jnp.float32)
    for micro_idx in range(tokens.shape[0]):
        matrices, gain_pair = (kept_weights, kept_gain)
        full_query, full_key, full_value, full_out, full_gate, full_up, full_down = matrices
        inputs = tokens[micro_idx].astype(jnp.float32)
        allowed, query_pos = build_mask(group_counts[micro_idx], device, slot_capacity)
        cosine_table, sine_values = rope_tables(query_pos, HEAD_WIDTH)
        first_normed, scale_one = normalize(inputs, gain_pair[0])
        normed_low = first_normed.astype(jnp.bfloat16)
        reduced_query = apply_rotation(
            jnp.dot(normed_low, full_query, preferred_element_type=jnp.float32).reshape(
                slot_capacity, QUERY_HEADS, HEAD_WIDTH
            ),
            cosine_table,
            sine_values,
        ).astype(jnp.bfloat16)
        key_low = (
            apply_rotation(
                jnp.dot(normed_low, full_key, preferred_element_type=jnp.float32).reshape(
                    slot_capacity, KEY_HEADS, HEAD_WIDTH
                ),
                cosine_table,
                sine_values,
            )
            .astype(jnp.bfloat16)
            .reshape(slot_capacity, key_value_width)
        )
        value_low = jnp.dot(normed_low, full_value, preferred_element_type=jnp.float32).astype(
            jnp.bfloat16
        )
        grouped_keys, grouped_values = (
            lax.all_gather(key_low, "fsdp", axis=0, tiled=True),
            lax.all_gather(value_low, "fsdp", axis=0, tiled=True),
        )
        heads_of_key = grouped_keys.reshape(-1, KEY_HEADS, HEAD_WIDTH)
        heads_of_value = grouped_values.reshape(-1, KEY_HEADS, HEAD_WIDTH)
        heads_of_query = reduced_query.reshape(slot_capacity, KEY_HEADS, device_share, HEAD_WIDTH)
        scores = (
            jnp.einsum(
                "qngd,knd->ngqk", heads_of_query, heads_of_key, preferred_element_type=jnp.float32
            )
            * SCORE_SCALE
        )
        masked = jnp.where(allowed, scores, -1e30)
        row_top = jnp.max(masked, -1, keepdims=True)
        exponent = jnp.where(allowed, jnp.exp(masked - row_top), 0.0)
        row_total = jnp.sum(exponent, -1, keepdims=True)
        prob_low = (exponent / row_total).astype(jnp.bfloat16)
        log_total = row_top + jnp.log(row_total)
        mixed_heads = jnp.einsum(
            "ngqk,knd->qngd", prob_low, heads_of_value, preferred_element_type=jnp.float32
        ).reshape(slot_capacity, MODEL_WIDTH)
        attended = mixed_heads.astype(jnp.bfloat16)
        hidden_state = inputs + jnp.dot(attended, full_out, preferred_element_type=jnp.float32)
        normed_two, scale_two = normalize(hidden_state, gain_pair[1])
        normed_two_low = normed_two.astype(jnp.bfloat16)
        gate_act = jnp.dot(normed_two_low, full_gate, preferred_element_type=jnp.float32)
        upward = jnp.dot(normed_two_low, full_up, preferred_element_type=jnp.float32)
        sigmoid_gate = jax.nn.sigmoid(gate_act)
        product = (gate_act * sigmoid_gate * upward).astype(jnp.bfloat16)
        outputs.append(
            (hidden_state + jnp.dot(product, full_down, preferred_element_type=jnp.float32)).astype(
                jnp.bfloat16
            )
        )
        matrices, gain_pair = (kept_weights, kept_gain)
        full_query, full_key, full_value, full_out, full_gate, full_up, full_down = matrices
        grad_low = cotangent[micro_idx]
        grad_product = times_transpose(grad_low, full_down)
        grad_gate = (
            grad_product * upward * sigmoid_gate * (1.0 + gate_act * (1.0 - sigmoid_gate))
        ).astype(jnp.bfloat16)
        grad_upward = (grad_product * gate_act * sigmoid_gate).astype(jnp.bfloat16)
        grad_normed_two = times_transpose(grad_gate, full_gate) + times_transpose(
            grad_upward, full_up
        )
        gain_two_total = gain_two_total + jnp.sum(grad_normed_two * hidden_state * scale_two, 0)
        grad_hidden = grad_low.astype(jnp.float32) + norm_back(
            hidden_state, scale_two, gain_pair[1], grad_normed_two
        )
        grad_branch = grad_hidden.astype(jnp.bfloat16)
        mixed_gradient = times_transpose(grad_branch, full_out).astype(jnp.bfloat16)
        head_gradient = mixed_gradient.reshape(slot_capacity, KEY_HEADS, device_share, HEAD_WIDTH)
        again_scores = (
            jnp.einsum(
                "qngd,knd->ngqk", heads_of_query, heads_of_key, preferred_element_type=jnp.float32
            )
            * SCORE_SCALE
        )
        probability = jnp.where(allowed, jnp.exp(again_scores - log_total), 0.0)
        grad_prob = jnp.einsum(
            "qngd,knd->ngqk", head_gradient, heads_of_value, preferred_element_type=jnp.float32
        )
        row_delta = jnp.sum(probability * grad_prob, -1, keepdims=True)
        grad_scores = (probability * (grad_prob - row_delta)).astype(jnp.bfloat16)
        grad_query_rot = (
            jnp.einsum(
                "ngqk,knd->qngd", grad_scores, heads_of_key, preferred_element_type=jnp.float32
            ).reshape(slot_capacity, QUERY_HEADS, HEAD_WIDTH)
            * SCORE_SCALE
        )
        key_part = (
            jnp.einsum(
                "ngqk,qngd->knd", grad_scores, heads_of_query, preferred_element_type=jnp.float32
            ).reshape(-1, key_value_width)
            * SCORE_SCALE
        )
        value_part = jnp.einsum(
            "ngqk,qngd->knd",
            probability.astype(jnp.bfloat16),
            head_gradient,
            preferred_element_type=jnp.float32,
        ).reshape(-1, key_value_width)
        key_gradient, value_grad = (
            lax.psum_scatter(
                key_part.astype(jnp.bfloat16), "fsdp", scatter_dimension=0, tiled=True
            ).astype(jnp.float32),
            lax.psum_scatter(
                value_part.astype(jnp.bfloat16), "fsdp", scatter_dimension=0, tiled=True
            ).astype(jnp.float32),
        )
        grad_query = (
            apply_rotation(grad_query_rot, cosine_table, -sine_values)
            .astype(jnp.bfloat16)
            .reshape(slot_capacity, MODEL_WIDTH)
        )
        grad_key = (
            apply_rotation(
                key_gradient.reshape(slot_capacity, KEY_HEADS, HEAD_WIDTH),
                cosine_table,
                -sine_values,
            )
            .astype(jnp.bfloat16)
            .reshape(slot_capacity, key_value_width)
        )
        grad_value = value_grad.astype(jnp.bfloat16)
        grad_normed_one = (
            times_transpose(grad_query, full_query)
            + times_transpose(grad_key, full_key)
            + times_transpose(grad_value, full_value)
        )
        gain_one_total = gain_one_total + jnp.sum(grad_normed_one * inputs * scale_one, 0)
        grad_inputs.append(
            grad_hidden + norm_back(inputs, scale_one, gain_pair[0], grad_normed_one)
        )
        kept_rows = (
            normed_low,
            grad_query,
            grad_key,
            grad_value,
            attended,
            grad_branch,
            normed_two_low,
            grad_gate,
            grad_upward,
            product,
            grad_low,
        )
        for slot_index in range(11):
            saved[slot_index].append(kept_rows[slot_index])
    joined = [jnp.concatenate(column_list, 0) for column_list in saved]
    gain_terms = jnp.stack([gain_one_total, gain_two_total], 0)
    slices = (
        lax.all_to_all(joined[1], "fsdp", split_axis=1, concat_axis=0, tiled=True),
        lax.all_to_all(joined[2], "fsdp", split_axis=1, concat_axis=0, tiled=True),
        lax.all_to_all(joined[3], "fsdp", split_axis=1, concat_axis=0, tiled=True),
        lax.all_to_all(joined[5], "fsdp", split_axis=1, concat_axis=0, tiled=True),
        lax.all_to_all(joined[7], "fsdp", split_axis=1, concat_axis=0, tiled=True),
        lax.all_to_all(joined[8], "fsdp", split_axis=1, concat_axis=0, tiled=True),
        lax.all_to_all(joined[10], "fsdp", split_axis=1, concat_axis=0, tiled=True),
    )
    pieces = (
        lax.all_gather(joined[0], "fsdp", axis=0, tiled=True),
        lax.all_gather(joined[4], "fsdp", axis=0, tiled=True),
        lax.all_gather(joined[6], "fsdp", axis=0, tiled=True),
        lax.all_gather(joined[9], "fsdp", axis=0, tiled=True),
    )
    picked = [member for member in slices]
    gain_part = lax.psum_scatter(gain_terms, "fsdp", scatter_dimension=1, tiled=True)
    summed_rows = (
        lax.psum_scatter(
            rows_product(pieces[0], picked[0]).astype(jnp.bfloat16),
            "dp",
            scatter_dimension=0,
            tiled=True,
        ).astype(jnp.float32),
        lax.psum_scatter(
            rows_product(pieces[0], picked[1]).astype(jnp.bfloat16),
            "dp",
            scatter_dimension=0,
            tiled=True,
        ).astype(jnp.float32),
        lax.psum_scatter(
            rows_product(pieces[0], picked[2]).astype(jnp.bfloat16),
            "dp",
            scatter_dimension=0,
            tiled=True,
        ).astype(jnp.float32),
        lax.psum_scatter(
            rows_product(pieces[1], picked[3]).astype(jnp.bfloat16),
            "dp",
            scatter_dimension=0,
            tiled=True,
        ).astype(jnp.float32),
        lax.psum_scatter(
            rows_product(pieces[2], picked[4]).astype(jnp.bfloat16),
            "dp",
            scatter_dimension=0,
            tiled=True,
        ).astype(jnp.float32),
        lax.psum_scatter(
            rows_product(pieces[2], picked[5]).astype(jnp.bfloat16),
            "dp",
            scatter_dimension=0,
            tiled=True,
        ).astype(jnp.float32),
        lax.psum_scatter(
            rows_product(pieces[3], picked[6]).astype(jnp.bfloat16),
            "dp",
            scatter_dimension=0,
            tiled=True,
        ).astype(jnp.float32),
    )
    gain_grad = lax.psum(gain_part, "dp")
    return (
        jnp.stack(outputs, 0),
        jnp.stack(grad_inputs, 0),
        summed_rows[0],
        summed_rows[1],
        summed_rows[2],
        summed_rows[3],
        summed_rows[4],
        summed_rows[5],
        summed_rows[6],
        gain_grad,
    )


def swap_core(value):
    return lax.ppermute(value, "fsdp", [(j, j ^ 1) for j in range(8)])


def swap_dp(value, mask):
    return lax.ppermute(value, "dp", [(j, j ^ mask) for j in range(4)])


def shift_z(value, step):
    return lax.ppermute(value, "fsdp", [(j, (j + 2 * step) % 8) for j in range(8)])


def shift_z_up(value, step):
    return lax.ppermute(value, "fsdp", [(j, j + 2 * step) for j in range(8) if j + 2 * step < 8])


def shift_z_down(value, step):
    return lax.ppermute(value, "fsdp", [(j, j - 2 * step) for j in range(8) if j - 2 * step >= 0])


def place(pieces):
    total = len(pieces)
    buffer = jnp.zeros((total,) + pieces[0][1].shape, pieces[0][1].dtype)
    for index, piece in pieces:
        buffer = lax.dynamic_update_slice_in_dim(buffer, piece[None], index, 0)
    return buffer


def pick(stacked, index):
    return lax.dynamic_index_in_dim(stacked, index, 0, keepdims=False)


def gather_all(piece, dp_id, z_id, core_id):
    along = place([(z_id, piece)] + [((z_id - s) % 4, shift_z(piece, s)) for s in (1, 2, 3)])
    from_x = swap_dp(along, 1)
    from_y = swap_dp(along, 2)
    diagonal = jnp.concatenate([swap_dp(from_x[:2], 2), swap_dp(from_y[2:], 1)], 0)
    square = place(
        [(dp_id, along), (dp_id ^ 1, from_x), (dp_id ^ 2, from_y), (dp_id ^ 3, diagonal)]
    )
    other = swap_core(square)
    return place([(core_id, square), (1 - core_id, other)])


def add_low(*terms):
    total = terms[0].astype(jnp.float32)
    for term in terms[1:]:
        total = total + term.astype(jnp.float32)
    return total.astype(jnp.bfloat16)


def reduce_all(parts, dp_id, z_id, core_id):
    mine = add_low(pick(parts, core_id), swap_core(pick(parts, 1 - core_id)))
    home, to_x, to_y, far = [pick(mine, dp_id ^ k) for k in range(4)]
    half = far.shape[0] // 2
    via_y = swap_dp(far[:half], 2)
    via_x = swap_dp(far[half:], 1)
    to_x = jnp.concatenate([add_low(to_x[:half], via_y), to_x[half:]], 0)
    to_y = jnp.concatenate([to_y[:half], add_low(to_y[half:], via_x)], 0)
    summed = add_low(home, swap_dp(to_x, 1), swap_dp(to_y, 2))
    total = pick(summed, z_id).astype(jnp.float32)
    for s in (1, 2, 3):
        total = total + shift_z(pick(summed, (z_id - s) % 4), -s).astype(jnp.float32)
    return total


def product_nn(left, right):
    return lax.dot_general(
        left, right, (((1,), (0,)), ((), ())), preferred_element_type=jnp.float32
    )


def product_nt(left, right):
    return lax.dot_general(
        left, right, (((1,), (1,)), ((), ())), preferred_element_type=jnp.float32
    )


def product_tn(left, right):
    return lax.dot_general(
        left, right, (((0,), (0,)), ((), ())), preferred_element_type=jnp.float32
    )


def mlp_kernel(
    place_ref, w_ref, normed_ref, dy_ref, out_ref, dn_ref, grad_ref, gu_ref, prod_ref, dgu_ref
):
    dp_id = place_ref[0]
    z_id = place_ref[1]
    half = prod_ref.shape[1]

    def forward(s, carry):
        m = lax.rem(z_id - s + 4, 4)
        total = product_nn(w_ref[s * 4, : 2 * half, :], normed_ref[dp_id])
        for k in range(1, 4):
            total += product_nn(w_ref[s * 4 + k, : 2 * half, :], normed_ref[dp_id ^ k])
        gu_ref[m] = total
        gate = total[:half]
        prod_ref[m] = (gate * jax.nn.sigmoid(gate) * total[half:]).astype(jnp.bfloat16)
        return carry

    lax.fori_loop(0, 4, forward, 0)
    out_ref[...] = jnp.zeros_like(out_ref)
    dn_ref[...] = jnp.zeros_like(dn_ref)

    def middle(k, carry):
        m = dp_id ^ k
        product = prod_ref[m]
        dprod = jnp.zeros(product.shape, jnp.float32)
        for s in range(4):
            zz = lax.rem(z_id - s + 4, 4)
            weight = w_ref[s * 4 + k, 2 * half :, :]
            dy = dy_ref[zz]
            dprod += product_nn(weight, dy)
            out_ref[zz] += product_tn(weight, product)
            grad_ref[s * 4 + k, 2 * half :, :] = product_nt(product, dy).astype(jnp.bfloat16)
        gate = gu_ref[m, :half, :]
        up = gu_ref[m, half:, :]
        sig = jax.nn.sigmoid(gate)
        dgu_ref[m, :half, :] = (dprod * up * sig * (1.0 + gate * (1.0 - sig))).astype(jnp.bfloat16)
        dgu_ref[m, half:, :] = (dprod * gate * sig).astype(jnp.bfloat16)
        return carry

    lax.fori_loop(0, 4, middle, 0)

    def backward(s, carry):
        m = lax.rem(z_id - s + 4, 4)
        dgu = dgu_ref[m]
        for k in range(4):
            i = dp_id ^ k
            dn_ref[i] += product_tn(w_ref[s * 4 + k, : 2 * half, :], dgu)
            grad_ref[s * 4 + k, : 2 * half, :] = product_nt(dgu, normed_ref[i]).astype(
                jnp.bfloat16
            )
        return carry

    lax.fori_loop(0, 4, backward, 0)


def mlp(where, weights, normed, dy):
    count, depth, block = weights.shape
    half = depth // 3
    pair = normed.shape[2]
    vmem = pl.BlockSpec(memory_space=pltpu.VMEM)
    return pl.pallas_call(
        mlp_kernel,
        out_shape=(
            jax.ShapeDtypeStruct((4, block, pair), jnp.float32),
            jax.ShapeDtypeStruct((4, block, pair), jnp.float32),
            jax.ShapeDtypeStruct((count, depth, block), jnp.bfloat16),
        ),
        in_specs=[pl.BlockSpec(memory_space=pltpu.SMEM), vmem, vmem, vmem],
        out_specs=(vmem, vmem, vmem),
        scratch_shapes=[
            pltpu.VMEM((4, 2 * half, pair), jnp.float32),
            pltpu.VMEM((4, half, pair), jnp.bfloat16),
            pltpu.VMEM((4, 2 * half, pair), jnp.bfloat16),
        ],
        compiler_params=pltpu.CompilerParams(vmem_limit_bytes=56 * 1024 * 1024),
        cost_estimate=pl.CostEstimate(
            flops=18 * count * (depth // 3) * block * pair,
            bytes_accessed=4 * count * depth * block,
            transcendentals=0,
        ),
        name="mlp",
    )(where, weights, normed, dy)


def mean_square(values):
    return lax.rsqrt(jnp.mean(values * values, 0, keepdims=True) + EPSILON)


def turn(values, cosine, sine):
    heads = values.reshape(-1, 2, HEAD_WIDTH // 2, values.shape[-1])
    front, back = heads[:, 0], heads[:, 1]
    return jnp.stack([front * cosine - back * sine, back * cosine + front * sine], 1).reshape(
        values.shape
    )


def fast(
    tokens, cotangent, counts, w_query, key_weight, value_weight, w_out, w_gate, w_up, w_down, gains
):
    dp_id = lax.axis_index("dp")
    slot = lax.axis_index("fsdp")
    z_id = slot // 2
    core_id = slot % 2
    batches, cap, width = tokens.shape
    rows = batches * cap
    block = w_query.shape[0]
    q_cols, k_cols = w_query.shape[1], key_weight.shape[1]
    half = w_gate.shape[1]
    kv_width = KEY_HEADS * HEAD_WIDTH
    share = QUERY_HEADS // KEY_HEADS

    extra = jnp.zeros((16, block), jnp.bfloat16)
    extra = extra.at[:2, :q_cols].set(gains)
    extra = extra.at[2:4, :1].set(counts.astype(jnp.bfloat16))
    first_piece = jnp.concatenate([w_query.T, key_weight.T, value_weight.T, extra], 0)
    first = gather_all(first_piece, dp_id, z_id, core_id)
    first = first.transpose(1, 2, 0, 3, 4).reshape(4, 8, -1, block)
    o1, o2, o3 = q_cols, q_cols + k_cols, q_cols + 2 * k_cols
    qkv = jnp.concatenate(
        [
            first[:, :, :o1].reshape(4, width, block),
            first[:, :, o1:o2].reshape(4, kv_width, block),
            first[:, :, o2:o3].reshape(4, kv_width, block),
        ],
        1,
    )
    own_first = pick(first, dp_id)
    gain = (
        own_first[:, o3 : o3 + 2, :q_cols].transpose(1, 0, 2).reshape(2, width).astype(jnp.float32)
    )
    group_counts = own_first[:, o3 + 2 : o3 + 4, 0].T.astype(jnp.int32)

    second = gather_all(w_out.T, dp_id, z_id, core_id)
    out_weight = second.transpose(1, 2, 0, 3, 4).reshape(4, width, block)

    down_halves = w_down.reshape(2, half, -1)
    own_down = pick(down_halves, core_id)
    other_down = swap_core(pick(down_halves, 1 - core_id))
    down = jnp.where(
        core_id == 0,
        jnp.concatenate([own_down, other_down], 1),
        jnp.concatenate([other_down, own_down], 1),
    )
    mlp_piece = jnp.concatenate([w_gate.T, w_up.T, down], 0)
    middle = mlp_piece.shape[0] // 2
    pieces = []
    for s in range(4):
        own = mlp_piece if s == 0 else shift_z(mlp_piece, s)
        from_x = swap_dp(own, 1)
        from_y = swap_dp(own, 2)
        far = jnp.concatenate([swap_dp(from_x[:middle], 2), swap_dp(from_y[middle:], 1)], 0)
        pieces += [own, from_x, from_y, far]
    mlp_weights = jnp.stack(pieces, 0)

    dy = cotangent.reshape(rows, width).T
    dy_pair = jnp.concatenate([dy, swap_core(dy)], 1).reshape(4, block, 2 * rows)
    dy_wide = dy.astype(jnp.float32)

    x = tokens.reshape(rows, width).T.astype(jnp.float32)
    rms1 = mean_square(x)
    n1 = (x * rms1 * gain[0][:, None]).astype(jnp.bfloat16)
    n1_blocks = n1.reshape(4, block, rows)
    projected = sum(product_nn(qkv[i], n1_blocks[i]) for i in range(4))

    masks, cosines, sines = [], [], []
    for mb in range(batches):
        allowed, position = build_mask(group_counts[mb], slot, cap)
        cosine, sine = rope_tables(position, HEAD_WIDTH)
        masks.append(allowed)
        cosines.append(cosine[:, 0, :].T)
        sines.append(sine[:, 0, :].T)
    cosine = jnp.concatenate(cosines, 1)
    sine = jnp.concatenate(sines, 1)
    query = turn(projected[:width], cosine, sine).astype(jnp.bfloat16)
    key = turn(projected[width : width + kv_width], cosine, sine).astype(jnp.bfloat16)
    value = projected[width + kv_width :].astype(jnp.bfloat16)
    kv = jnp.concatenate([key, value], 0).T.reshape(batches, cap, 2 * kv_width)

    attended_parts, saved = [], []
    for mb in range(batches):
        along = place(
            [(z_id, kv[mb])] + [((z_id - s) % 4, shift_z_up(kv[mb], s)) for s in (1, 2, 3)]
        )
        grouped = place([(core_id, along), (1 - core_id, swap_core(along))])
        grouped = grouped.transpose(1, 0, 2, 3).reshape(-1, 2, KEY_HEADS, HEAD_WIDTH)
        keys, values = grouped[:, 0], grouped[:, 1]
        queries = query[:, mb * cap : (mb + 1) * cap].T.reshape(cap, KEY_HEADS, share, HEAD_WIDTH)
        allowed = masks[mb]
        scores = (
            jnp.einsum("qngd,knd->ngqk", queries, keys, preferred_element_type=jnp.float32)
            * SCORE_SCALE
        )
        masked = jnp.where(allowed, scores, -1e30)
        top = jnp.max(masked, -1, keepdims=True)
        exponent = jnp.where(allowed, jnp.exp(masked - top), 0.0)
        row_total = jnp.sum(exponent, -1, keepdims=True)
        prob = (exponent / row_total).astype(jnp.bfloat16)
        log_total = top + jnp.log(row_total)
        mixed = jnp.einsum("ngqk,knd->qngd", prob, values, preferred_element_type=jnp.float32)
        attended_parts.append(mixed.reshape(cap, width).astype(jnp.bfloat16).T)
        saved.append((keys, values, queries, log_total))
    attended = jnp.concatenate(attended_parts, 1)
    attended_blocks = attended.reshape(4, block, rows)
    h = x + sum(product_nn(out_weight[i], attended_blocks[i]) for i in range(4))
    rms2 = mean_square(h)
    n2 = (h * rms2 * gain[1][:, None]).astype(jnp.bfloat16)
    n2_pair = jnp.concatenate([n2, swap_core(n2)], 1).reshape(4, block, 2 * rows)
    where = jnp.stack([dp_id, z_id]).astype(jnp.int32)
    out_part, dn_part, mlp_grad = mlp(where, mlp_weights, n2_pair, dy_pair)
    parts = jnp.stack([out_part, dn_part], 0).reshape(2, width, 2 * rows)
    arrived = swap_core(parts[:, :, rows:].astype(jnp.bfloat16)).astype(jnp.float32)
    both = parts[:, :, :rows] + arrived
    output = (h + both[0]).astype(jnp.bfloat16).T.reshape(batches, cap, width)
    dn2 = both[1]
    gain_two = jnp.sum(dn2 * h * rms2, 1)
    weighted = dn2 * gain[1][:, None]
    dh = (
        dy_wide
        + rms2 * weighted
        - h * rms2 * rms2 * rms2 * jnp.mean(weighted * h, 0, keepdims=True)
    )
    da = dh.astype(jnp.bfloat16)

    mlp_total = jnp.zeros(mlp_piece.shape, jnp.float32)
    for s in range(4):
        home, to_x, to_y, far = [mlp_grad[s * 4 + k] for k in range(4)]
        via_y = swap_dp(far[:middle], 2)
        via_x = swap_dp(far[middle:], 1)
        to_x = jnp.concatenate([add_low(to_x[:middle], via_y), to_x[middle:]], 0)
        to_y = jnp.concatenate([to_y[:middle], add_low(to_y[middle:], via_x)], 0)
        summed = add_low(home, swap_dp(to_x, 1), swap_dp(to_y, 2))
        if s:
            summed = shift_z(summed, -s)
        mlp_total = mlp_total + summed.astype(jnp.float32)
    grad_gate = mlp_total[:half].T
    grad_up = mlp_total[half : 2 * half].T
    down_total = mlp_total[2 * half :]
    col = w_down.shape[1]
    left, right = down_total[:, :col], down_total[:, col:]
    keep = jnp.where(core_id == 0, left, right)
    give = jnp.where(core_id == 0, right, left).astype(jnp.bfloat16)
    taken = swap_core(give).astype(jnp.float32)
    grad_down = jnp.where(
        core_id == 0, jnp.concatenate([keep, taken], 0), jnp.concatenate([taken, keep], 0)
    )

    out_parts = jnp.stack([product_nt(da, attended_blocks[i]) for i in range(4)], 0)
    out_parts = out_parts.astype(jnp.bfloat16).reshape(4, 4, 2, q_cols, block)
    grad_out = reduce_all(out_parts.transpose(2, 0, 1, 3, 4), dp_id, z_id, core_id).T

    mixed_gradient = jnp.concatenate([product_tn(out_weight[i], da) for i in range(4)], 0).astype(
        jnp.bfloat16
    )
    dq_parts, dkv_parts = [], []
    for mb in range(batches):
        keys, values, queries, log_total = saved[mb]
        allowed = masks[mb]
        head_gradient = (
            mixed_gradient[:, mb * cap : (mb + 1) * cap]
            .T.reshape(cap, KEY_HEADS, share, HEAD_WIDTH)
        )
        again = (
            jnp.einsum("qngd,knd->ngqk", queries, keys, preferred_element_type=jnp.float32)
            * SCORE_SCALE
        )
        probability = jnp.where(allowed, jnp.exp(again - log_total), 0.0)
        dprob = jnp.einsum(
            "qngd,knd->ngqk", head_gradient, values, preferred_element_type=jnp.float32
        )
        delta = jnp.sum(probability * dprob, -1, keepdims=True)
        dscore = (probability * (dprob - delta)).astype(jnp.bfloat16)
        dq = jnp.einsum("ngqk,knd->qngd", dscore, keys, preferred_element_type=jnp.float32)
        dq_parts.append(dq.reshape(cap, width).T * SCORE_SCALE)
        dk = (
            jnp.einsum("ngqk,qngd->knd", dscore, queries, preferred_element_type=jnp.float32)
            * SCORE_SCALE
        )
        dv = jnp.einsum(
            "ngqk,qngd->knd",
            probability.astype(jnp.bfloat16),
            head_gradient,
            preferred_element_type=jnp.float32,
        )
        dkv = jnp.concatenate([dk.reshape(-1, kv_width), dv.reshape(-1, kv_width)], 1)
        dkv = dkv.astype(jnp.bfloat16).reshape(4, 2, cap, 2 * kv_width).transpose(1, 0, 2, 3)
        mine = add_low(pick(dkv, core_id), swap_core(pick(dkv, 1 - core_id)))
        total = pick(mine, z_id).astype(jnp.float32)
        for s in (1, 2, 3):
            total = total + shift_z_down(pick(mine, (z_id - s) % 4), s).astype(jnp.float32)
        dkv_parts.append(total.T)
    dq = turn(jnp.concatenate(dq_parts, 1), cosine, -sine).astype(jnp.bfloat16)
    dkv = jnp.concatenate(dkv_parts, 1)
    dk = turn(dkv[:kv_width], cosine, -sine).astype(jnp.bfloat16)
    dv = dkv[kv_width:].astype(jnp.bfloat16)
    dqkv = jnp.concatenate([dq, dk, dv], 0)
    dn1 = jnp.concatenate([product_tn(qkv[i], dqkv) for i in range(4)], 0)
    gain_one = jnp.sum(dn1 * x * rms1, 1)
    weighted = dn1 * gain[0][:, None]
    grad_tokens = (
        dh + rms1 * weighted - x * rms1 * rms1 * rms1 * jnp.mean(weighted * x, 0, keepdims=True)
    )
    grad_tokens = grad_tokens.T.reshape(batches, cap, width)
    first_grad = jnp.stack([product_nt(dqkv, n1_blocks[i]) for i in range(4)], 0)
    first_grad = first_grad.astype(jnp.bfloat16)
    first_grad = jnp.concatenate(
        [
            first_grad[:, :width].reshape(4, 8, q_cols, block),
            first_grad[:, width : width + kv_width].reshape(4, 8, k_cols, block),
            first_grad[:, width + kv_width :].reshape(4, 8, k_cols, block),
        ],
        2,
    ).reshape(4, 4, 2, o3, block)
    first_total = reduce_all(first_grad.transpose(2, 0, 1, 3, 4), dp_id, z_id, core_id)
    gain_total = lax.psum(jnp.stack([gain_one, gain_two], 0), ("dp", "fsdp"))
    gain_grad = lax.dynamic_slice_in_dim(gain_total, slot * q_cols, q_cols, 1)
    return (
        output,
        grad_tokens,
        first_total[:o1].T,
        first_total[o1:o2].T,
        first_total[o2:].T,
        grad_out,
        grad_gate,
        grad_up,
        grad_down,
        gain_grad,
    )


def solution(mesh):
    in_specs = (
        P(None, ("dp", "fsdp"), None),
        P(None, ("dp", "fsdp"), None),
        P(None, ("dp", "fsdp")),
        P("dp", "fsdp"),
        P("dp", "fsdp"),
        P("dp", "fsdp"),
        P("dp", "fsdp"),
        P("dp", "fsdp"),
        P("dp", "fsdp"),
        P("dp", "fsdp"),
        P(None, "fsdp"),
    )
    out_specs = (
        P(None, ("dp", "fsdp"), None),
        P(None, ("dp", "fsdp"), None),
        P("dp", "fsdp"),
        P("dp", "fsdp"),
        P("dp", "fsdp"),
        P("dp", "fsdp"),
        P("dp", "fsdp"),
        P("dp", "fsdp"),
        P("dp", "fsdp"),
        P(None, "fsdp"),
    )
    square = mesh.shape["dp"] == 4 and mesh.shape["fsdp"] == 8
    return jax.shard_map(
        fast if square else local, mesh=mesh, in_specs=in_specs, out_specs=out_specs, check_vma=False)
```

```python
import jax
import jax.numpy as jnp
from jax import lax
from jax.experimental import pallas as pl
from jax.experimental.pallas import tpu as pltpu
from jax.sharding import PartitionSpec as P

MODEL_WIDTH = 960
QUERY_HEADS = 15
KEY_HEADS = 5
HEAD_WIDTH = 64


EPSILON = 1e-05
ROPE_BASE = 100000.0
SCORE_SCALE = 0.125


def rope_tables(position, head_size):
    half_size = head_size // 2
    frequency = ROPE_BASE ** (-(jnp.arange(half_size, dtype=jnp.float32) * 2.0) / head_size)
    angles = position.astype(jnp.float32)[:, None] * frequency[None, :]
    return (jnp.cos(angles)[:, None, :], jnp.sin(angles)[:, None, :])


def apply_rotation(values, cosine_table, sine_values):
    half_size = values.shape[-1] // 2
    front_half = values[..., :half_size]
    back_half = values[..., half_size:]
    return jnp.concatenate(
        [
            front_half * cosine_table - back_half * sine_values,
            back_half * cosine_table + front_half * sine_values,
        ],
        -1,
    )


def normalize(values, gain_row):
    inv_rms = lax.rsqrt(jnp.mean(values * values, -1, keepdims=True) + EPSILON)
    return (values * inv_rms * gain_row, inv_rms)


def norm_back(values, inv_rms, gain_row, incoming):
    weighted = incoming * gain_row
    return inv_rms * weighted - values * inv_rms * inv_rms * inv_rms * jnp.mean(
        weighted * values, -1, keepdims=True
    )


def build_mask(count_row, device, slot_capacity):
    group_width = count_row.shape[0]
    local_slot = jnp.arange(slot_capacity, dtype=jnp.int32)
    offsets = jnp.cumsum(count_row) - count_row
    is_mine = jnp.arange(group_width, dtype=jnp.int32) == device
    own_offset = jnp.sum(jnp.where(is_mine, offsets, 0))
    own_count = jnp.sum(jnp.where(is_mine, count_row, 0))
    query_pos = own_offset + local_slot
    query_valid = local_slot < own_count
    key_pos = (offsets[:, None] + local_slot[None, :]).reshape(-1)
    key_valid = (local_slot[None, :] < count_row[:, None]).reshape(-1)
    slot_ids = jnp.arange(group_width * slot_capacity, dtype=jnp.int32)
    own_slots = device * slot_capacity + local_slot
    allowed = query_valid[:, None] & key_valid[None, :] & (
        key_pos[None, :] <= query_pos[:, None]
    ) | (slot_ids[None, :] == own_slots[:, None])
    return (allowed, query_pos)


def kept_fetch(w_query, key_weight, value_weight, w_out, w_gate, w_up, w_down, gains):
    columns = (
        lax.all_gather(w_query, "fsdp", axis=1, tiled=True),
        lax.all_gather(key_weight, "fsdp", axis=1, tiled=True),
        lax.all_gather(value_weight, "fsdp", axis=1, tiled=True),
        lax.all_gather(w_out, "fsdp", axis=1, tiled=True),
        lax.all_gather(w_gate, "fsdp", axis=1, tiled=True),
        lax.all_gather(w_up, "fsdp", axis=1, tiled=True),
        lax.all_gather(w_down, "fsdp", axis=1, tiled=True),
        lax.all_gather(gains, "fsdp", axis=1, tiled=True),
    )
    matrices = (
        lax.all_gather(columns[0], "dp", axis=0, tiled=True),
        lax.all_gather(columns[1], "dp", axis=0, tiled=True),
        lax.all_gather(columns[2], "dp", axis=0, tiled=True),
        lax.all_gather(columns[3], "dp", axis=0, tiled=True),
        lax.all_gather(columns[4], "dp", axis=0, tiled=True),
        lax.all_gather(columns[5], "dp", axis=0, tiled=True),
        lax.all_gather(columns[6], "dp", axis=0, tiled=True),
    )
    return (matrices, columns[7].astype(jnp.float32))


def times_transpose(left, right):
    return jnp.einsum("rk,jk->rj", left, right, preferred_element_type=jnp.float32)


def rows_product(left, right):
    return jnp.einsum("rd,rk->dk", left, right, preferred_element_type=jnp.float32)


def local(
    tokens, cotangent, counts, w_query, key_weight, value_weight, w_out, w_gate, w_up, w_down, gains
):
    group_counts = lax.all_gather(counts, "fsdp", axis=1, tiled=True)
    device = lax.axis_index("fsdp")
    slot_capacity = tokens.shape[1]
    key_value_width = KEY_HEADS * HEAD_WIDTH
    device_share = QUERY_HEADS // KEY_HEADS
    kept_weights, kept_gain = kept_fetch(
        w_query, key_weight, value_weight, w_out, w_gate, w_up, w_down, gains
    )
    outputs = []
    grad_inputs = []
    saved = [[] for index_unused in range(11)]
    gain_one_total = jnp.zeros((MODEL_WIDTH,), jnp.float32)
    gain_two_total = jnp.zeros((MODEL_WIDTH,), jnp.float32)
    for micro_idx in range(tokens.shape[0]):
        matrices, gain_pair = (kept_weights, kept_gain)
        full_query, full_key, full_value, full_out, full_gate, full_up, full_down = matrices
        inputs = tokens[micro_idx].astype(jnp.float32)
        allowed, query_pos = build_mask(group_counts[micro_idx], device, slot_capacity)
        cosine_table, sine_values = rope_tables(query_pos, HEAD_WIDTH)
        first_normed, scale_one = normalize(inputs, gain_pair[0])
        normed_low = first_normed.astype(jnp.bfloat16)
        reduced_query = apply_rotation(
            jnp.dot(normed_low, full_query, preferred_element_type=jnp.float32).reshape(
                slot_capacity, QUERY_HEADS, HEAD_WIDTH
            ),
            cosine_table,
            sine_values,
        ).astype(jnp.bfloat16)
        key_low = (
            apply_rotation(
                jnp.dot(normed_low, full_key, preferred_element_type=jnp.float32).reshape(
                    slot_capacity, KEY_HEADS, HEAD_WIDTH
                ),
                cosine_table,
                sine_values,
            )
            .astype(jnp.bfloat16)
            .reshape(slot_capacity, key_value_width)
        )
        value_low = jnp.dot(normed_low, full_value, preferred_element_type=jnp.float32).astype(
            jnp.bfloat16
        )
        grouped_keys, grouped_values = (
            lax.all_gather(key_low, "fsdp", axis=0, tiled=True),
            lax.all_gather(value_low, "fsdp", axis=0, tiled=True),
        )
        heads_of_key = grouped_keys.reshape(-1, KEY_HEADS, HEAD_WIDTH)
        heads_of_value = grouped_values.reshape(-1, KEY_HEADS, HEAD_WIDTH)
        heads_of_query = reduced_query.reshape(slot_capacity, KEY_HEADS, device_share, HEAD_WIDTH)
        scores = (
            jnp.einsum(
                "qngd,knd->ngqk", heads_of_query, heads_of_key, preferred_element_type=jnp.float32
            )
            * SCORE_SCALE
        )
        masked = jnp.where(allowed, scores, -1e30)
        row_top = jnp.max(masked, -1, keepdims=True)
        exponent = jnp.where(allowed, jnp.exp(masked - row_top), 0.0)
        row_total = jnp.sum(exponent, -1, keepdims=True)
        prob_low = (exponent / row_total).astype(jnp.bfloat16)
        log_total = row_top + jnp.log(row_total)
        mixed_heads = jnp.einsum(
            "ngqk,knd->qngd", prob_low, heads_of_value, preferred_element_type=jnp.float32
        ).reshape(slot_capacity, MODEL_WIDTH)
        attended = mixed_heads.astype(jnp.bfloat16)
        hidden_state = inputs + jnp.dot(attended, full_out, preferred_element_type=jnp.float32)
        normed_two, scale_two = normalize(hidden_state, gain_pair[1])
        normed_two_low = normed_two.astype(jnp.bfloat16)
        gate_act = jnp.dot(normed_two_low, full_gate, preferred_element_type=jnp.float32)
        upward = jnp.dot(normed_two_low, full_up, preferred_element_type=jnp.float32)
        sigmoid_gate = jax.nn.sigmoid(gate_act)
        product = (gate_act * sigmoid_gate * upward).astype(jnp.bfloat16)
        outputs.append(
            (hidden_state + jnp.dot(product, full_down, preferred_element_type=jnp.float32)).astype(
                jnp.bfloat16
            )
        )
        matrices, gain_pair = (kept_weights, kept_gain)
        full_query, full_key, full_value, full_out, full_gate, full_up, full_down = matrices
        grad_low = cotangent[micro_idx]
        grad_product = times_transpose(grad_low, full_down)
        grad_gate = (
            grad_product * upward * sigmoid_gate * (1.0 + gate_act * (1.0 - sigmoid_gate))
        ).astype(jnp.bfloat16)
        grad_upward = (grad_product * gate_act * sigmoid_gate).astype(jnp.bfloat16)
        grad_normed_two = times_transpose(grad_gate, full_gate) + times_transpose(
            grad_upward, full_up
        )
        gain_two_total = gain_two_total + jnp.sum(grad_normed_two * hidden_state * scale_two, 0)
        grad_hidden = grad_low.astype(jnp.float32) + norm_back(
            hidden_state, scale_two, gain_pair[1], grad_normed_two
        )
        grad_branch = grad_hidden.astype(jnp.bfloat16)
        mixed_gradient = times_transpose(grad_branch, full_out).astype(jnp.bfloat16)
        head_gradient = mixed_gradient.reshape(slot_capacity, KEY_HEADS, device_share, HEAD_WIDTH)
        again_scores = (
            jnp.einsum(
                "qngd,knd->ngqk", heads_of_query, heads_of_key, preferred_element_type=jnp.float32
            )
            * SCORE_SCALE
        )
        probability = jnp.where(allowed, jnp.exp(again_scores - log_total), 0.0)
        grad_prob = jnp.einsum(
            "qngd,knd->ngqk", head_gradient, heads_of_value, preferred_element_type=jnp.float32
        )
        row_delta = jnp.sum(probability * grad_prob, -1, keepdims=True)
        grad_scores = (probability * (grad_prob - row_delta)).astype(jnp.bfloat16)
        grad_query_rot = (
            jnp.einsum(
                "ngqk,knd->qngd", grad_scores, heads_of_key, preferred_element_type=jnp.float32
            ).reshape(slot_capacity, QUERY_HEADS, HEAD_WIDTH)
            * SCORE_SCALE
        )
        key_part = (
            jnp.einsum(
                "ngqk,qngd->knd", grad_scores, heads_of_query, preferred_element_type=jnp.float32
            ).reshape(-1, key_value_width)
            * SCORE_SCALE
        )
        value_part = jnp.einsum(
            "ngqk,qngd->knd",
            probability.astype(jnp.bfloat16),
            head_gradient,
            preferred_element_type=jnp.float32,
        ).reshape(-1, key_value_width)
        key_gradient, value_grad = (
            lax.psum_scatter(
                key_part.astype(jnp.bfloat16), "fsdp", scatter_dimension=0, tiled=True
            ).astype(jnp.float32),
            lax.psum_scatter(
                value_part.astype(jnp.bfloat16), "fsdp", scatter_dimension=0, tiled=True
            ).astype(jnp.float32),
        )
        grad_query = (
            apply_rotation(grad_query_rot, cosine_table, -sine_values)
            .astype(jnp.bfloat16)
            .reshape(slot_capacity, MODEL_WIDTH)
        )
        grad_key = (
            apply_rotation(
                key_gradient.reshape(slot_capacity, KEY_HEADS, HEAD_WIDTH),
                cosine_table,
                -sine_values,
            )
            .astype(jnp.bfloat16)
            .reshape(slot_capacity, key_value_width)
        )
        grad_value = value_grad.astype(jnp.bfloat16)
        grad_normed_one = (
            times_transpose(grad_query, full_query)
            + times_transpose(grad_key, full_key)
            + times_transpose(grad_value, full_value)
        )
        gain_one_total = gain_one_total + jnp.sum(grad_normed_one * inputs * scale_one, 0)
        grad_inputs.append(
            grad_hidden + norm_back(inputs, scale_one, gain_pair[0], grad_normed_one)
        )
        kept_rows = (
            normed_low,
            grad_query,
            grad_key,
            grad_value,
            attended,
            grad_branch,
            normed_two_low,
            grad_gate,
            grad_upward,
            product,
            grad_low,
        )
        for slot_index in range(11):
            saved[slot_index].append(kept_rows[slot_index])
    joined = [jnp.concatenate(column_list, 0) for column_list in saved]
    gain_terms = jnp.stack([gain_one_total, gain_two_total], 0)
    slices = (
        lax.all_to_all(joined[1], "fsdp", split_axis=1, concat_axis=0, tiled=True),
        lax.all_to_all(joined[2], "fsdp", split_axis=1, concat_axis=0, tiled=True),
        lax.all_to_all(joined[3], "fsdp", split_axis=1, concat_axis=0, tiled=True),
        lax.all_to_all(joined[5], "fsdp", split_axis=1, concat_axis=0, tiled=True),
        lax.all_to_all(joined[7], "fsdp", split_axis=1, concat_axis=0, tiled=True),
        lax.all_to_all(joined[8], "fsdp", split_axis=1, concat_axis=0, tiled=True),
        lax.all_to_all(joined[10], "fsdp", split_axis=1, concat_axis=0, tiled=True),
    )
    pieces = (
        lax.all_gather(joined[0], "fsdp", axis=0, tiled=True),
        lax.all_gather(joined[4], "fsdp", axis=0, tiled=True),
        lax.all_gather(joined[6], "fsdp", axis=0, tiled=True),
        lax.all_gather(joined[9], "fsdp", axis=0, tiled=True),
    )
    picked = [member for member in slices]
    gain_part = lax.psum_scatter(gain_terms, "fsdp", scatter_dimension=1, tiled=True)
    summed_rows = (
        lax.psum_scatter(
            rows_product(pieces[0], picked[0]).astype(jnp.bfloat16),
            "dp",
            scatter_dimension=0,
            tiled=True,
        ).astype(jnp.float32),
        lax.psum_scatter(
            rows_product(pieces[0], picked[1]).astype(jnp.bfloat16),
            "dp",
            scatter_dimension=0,
            tiled=True,
        ).astype(jnp.float32),
        lax.psum_scatter(
            rows_product(pieces[0], picked[2]).astype(jnp.bfloat16),
            "dp",
            scatter_dimension=0,
            tiled=True,
        ).astype(jnp.float32),
        lax.psum_scatter(
            rows_product(pieces[1], picked[3]).astype(jnp.bfloat16),
            "dp",
            scatter_dimension=0,
            tiled=True,
        ).astype(jnp.float32),
        lax.psum_scatter(
            rows_product(pieces[2], picked[4]).astype(jnp.bfloat16),
            "dp",
            scatter_dimension=0,
            tiled=True,
        ).astype(jnp.float32),
        lax.psum_scatter(
            rows_product(pieces[2], picked[5]).astype(jnp.bfloat16),
            "dp",
            scatter_dimension=0,
            tiled=True,
        ).astype(jnp.float32),
        lax.psum_scatter(
            rows_product(pieces[3], picked[6]).astype(jnp.bfloat16),
            "dp",
            scatter_dimension=0,
            tiled=True,
        ).astype(jnp.float32),
    )
    gain_grad = lax.psum(gain_part, "dp")
    return (
        jnp.stack(outputs, 0),
        jnp.stack(grad_inputs, 0),
        summed_rows[0],
        summed_rows[1],
        summed_rows[2],
        summed_rows[3],
        summed_rows[4],
        summed_rows[5],
        summed_rows[6],
        gain_grad,
    )


def swap_core(value):
    return lax.ppermute(value, "fsdp", [(j, j ^ 1) for j in range(8)])


def swap_dp(value, mask):
    return lax.ppermute(value, "dp", [(j, j ^ mask) for j in range(4)])


def shift_z(value, step):
    return lax.ppermute(value, "fsdp", [(j, (j + 2 * step) % 8) for j in range(8)])


def shift_z_up(value, step):
    return lax.ppermute(value, "fsdp", [(j, j + 2 * step) for j in range(8) if j + 2 * step < 8])


def shift_z_down(value, step):
    return lax.ppermute(value, "fsdp", [(j, j - 2 * step) for j in range(8) if j - 2 * step >= 0])


def add_low(*terms):
    total = terms[0].astype(jnp.float32)
    for term in terms[1:]:
        total = total + term.astype(jnp.float32)
    return total.astype(jnp.bfloat16)


def product_nn(left, right):
    return lax.dot_general(
        left, right, (((1,), (0,)), ((), ())), preferred_element_type=jnp.float32
    )


def product_nt(left, right):
    return lax.dot_general(
        left, right, (((1,), (1,)), ((), ())), preferred_element_type=jnp.float32
    )


def product_tn(left, right):
    return lax.dot_general(
        left, right, (((0,), (0,)), ((), ())), preferred_element_type=jnp.float32
    )


VMEM = pl.BlockSpec(memory_space=pltpu.VMEM)
SMEM = pl.BlockSpec(memory_space=pltpu.SMEM)
ANY = pl.BlockSpec(memory_space=pl.ANY)


def run(body, name, ins, in_specs, outs, out_specs, scratch, flops, megabytes):
    moved = sum(v.size * v.dtype.itemsize for v in ins)
    moved += sum(v.size * v.dtype.itemsize for v in outs)
    return pl.pallas_call(
        body,
        out_shape=tuple(outs),
        in_specs=in_specs,
        out_specs=tuple(out_specs),
        scratch_shapes=scratch,
        compiler_params=pltpu.CompilerParams(vmem_limit_bytes=megabytes * 1024 * 1024),
        cost_estimate=pl.CostEstimate(flops=flops, bytes_accessed=moved, transcendentals=0),
        name=name,
    )(*ins)


def struct(shape, dtype=jnp.bfloat16):
    return jax.ShapeDtypeStruct(shape, dtype)


def column_index(ids_ref, core_rel, s):
    return 2 * lax.rem(ids_ref[1] - s + 4, 4) + (ids_ref[2] ^ core_rel)


def start_row(index, size):
    return pl.ds(pl.multiple_of(index * size, 8), size)


def project_kernel(
    ids_ref, own_ref, other_ref, n1_ref, cos_ref, sin_ref, q_ref, kv_ref, proj_ref, turned_ref
):
    width = n1_ref.shape[0] * n1_ref.shape[1]
    kv_width = KEY_HEADS * HEAD_WIDTH
    q_cols, k_cols = width // 8, kv_width // 8
    for core_rel, w_ref in ((0, own_ref), (1, other_ref)):

        def body(s, carry, core_rel=core_rel, w_ref=w_ref):
            f = column_index(ids_ref, core_rel, s)
            total = product_nn(w_ref[s], n1_ref[ids_ref[0]])
            for k in range(1, 4):
                total += product_nn(w_ref[k * 4 + s], n1_ref[ids_ref[0] ^ k])
            proj_ref[start_row(f, q_cols), :] = total[:q_cols]
            proj_ref[pl.ds(pl.multiple_of(width + f * k_cols, 8), k_cols), :] = total[
                q_cols : q_cols + k_cols
            ]
            proj_ref[pl.ds(pl.multiple_of(width + kv_width + f * k_cols, 8), k_cols), :] = total[
                q_cols + k_cols : q_cols + 2 * k_cols
            ]
            return carry

        lax.fori_loop(0, 4, body, 0)
    cosine, sine = cos_ref[...], sin_ref[...]
    half = HEAD_WIDTH // 2

    def heads(head, carry):
        front = proj_ref[pl.ds(pl.multiple_of(head * HEAD_WIDTH, 8), half), :]
        back = proj_ref[pl.ds(pl.multiple_of(head * HEAD_WIDTH + half, 8), half), :]
        q_ref[head, :half, :] = (
            (front * cosine - back * sine).astype(jnp.bfloat16) * SCORE_SCALE
        ).astype(jnp.bfloat16)
        q_ref[head, half:, :] = (
            (back * cosine + front * sine).astype(jnp.bfloat16) * SCORE_SCALE
        ).astype(jnp.bfloat16)
        return carry

    lax.fori_loop(0, QUERY_HEADS, heads, 0)
    for head in range(KEY_HEADS):
        base = width + head * HEAD_WIDTH
        front = proj_ref[base : base + half, :]
        back = proj_ref[base + half : base + 2 * half, :]
        turned_ref[head * HEAD_WIDTH : head * HEAD_WIDTH + half, :] = front * cosine - back * sine
        turned_ref[head * HEAD_WIDTH + half : (head + 1) * HEAD_WIDTH, :] = (
            back * cosine + front * sine
        )
    turned_ref[kv_width:, :] = proj_ref[width + kv_width :, :]
    kv_ref[...] = turned_ref[...].T.astype(jnp.bfloat16)


def stage_heads(mb, cap, own_ref, other_ref, k_ref, v_ref):
    kv_width = KEY_HEADS * HEAD_WIDTH
    for core_rel, source in ((0, own_ref), (1, other_ref)):
        for s in range(4):
            block = core_rel * 4 + s
            rows = source[s, mb * cap : (mb + 1) * cap, :]
            for n in range(KEY_HEADS):
                lanes = n * HEAD_WIDTH
                k_ref[n, block * cap : (block + 1) * cap, :] = rows[:, lanes : lanes + HEAD_WIDTH]
                lanes += kv_width
                v_ref[n, block * cap : (block + 1) * cap, :] = rows[:, lanes : lanes + HEAD_WIDTH]


def stage_bias(ids_ref, counts_ref, mb, cap, share, bias_ref):
    slot = ids_ref[3]
    own_count = counts_ref[mb * 8 + slot]
    key = lax.broadcasted_iota(jnp.int32, (cap, cap), 0)
    query = lax.broadcasted_iota(jnp.int32, (cap, cap), 1)
    query_used = query < own_count
    for core_rel in range(2):
        for s in range(4):
            block = core_rel * 4 + s
            f = column_index(ids_ref, core_rel, s)
            count = counts_ref[mb * 8 + f]
            reach = jnp.where(f < slot, cap, jnp.where(f == slot, 0, -2 * cap))
            self_off = jnp.where(f == slot, 0, 2 * cap)
            allowed = (query_used & (key < count) & (key <= query + reach)) | (
                key == query + self_off
            )
            tile = jnp.where(allowed, 0.0, -1e30)
            for g in range(share):
                bias_ref[block * cap : (block + 1) * cap, g * cap : (g + 1) * cap] = tile


def join_heads(ref, n, share, mb, cap):
    return jnp.concatenate(
        [ref[share * n + g, :, mb * cap : (mb + 1) * cap] for g in range(share)], 1
    )


def attend_kernel(
    ids_ref, counts_ref, q_ref, own_ref, other_ref, att_ref, lse_ref, k_ref, v_ref, bias_ref
):
    cap = q_ref.shape[2] // 2
    share = QUERY_HEADS // KEY_HEADS
    for mb in range(2):
        stage_heads(mb, cap, own_ref, other_ref, k_ref, v_ref)
        stage_bias(ids_ref, counts_ref, mb, cap, share, bias_ref)

        def body(n, carry, mb=mb):
            scores = product_nn(k_ref[n], join_heads(q_ref, n, share, mb, cap)) + bias_ref[...]
            top = jnp.max(scores, 0, keepdims=True)
            exponent = jnp.exp(scores - top)
            total = jnp.sum(exponent, 0, keepdims=True)
            mixed = product_tn(v_ref[n], exponent.astype(jnp.bfloat16)) / total
            mixed = mixed.astype(jnp.bfloat16)
            for g in range(share):
                att_ref[share * n + g, :, mb * cap : (mb + 1) * cap] = mixed[
                    :, g * cap : (g + 1) * cap
                ]
            lse_ref[mb * KEY_HEADS + n] = top + jnp.log(total)
            return carry

        lax.fori_loop(0, KEY_HEADS, body, 0)


def attend_back_kernel(
    ids_ref,
    counts_ref,
    q_ref,
    do_ref,
    own_ref,
    other_ref,
    lse_ref,
    cos_ref,
    sin_ref,
    dq_ref,
    dkv_own_ref,
    dkv_other_ref,
    k_ref,
    v_ref,
    bias_ref,
    dk_ref,
    dv_ref,
):
    cap = q_ref.shape[2] // 2
    share = QUERY_HEADS // KEY_HEADS
    half = HEAD_WIDTH // 2
    kv_width = KEY_HEADS * HEAD_WIDTH
    for mb in range(2):
        stage_heads(mb, cap, own_ref, other_ref, k_ref, v_ref)
        stage_bias(ids_ref, counts_ref, mb, cap, share, bias_ref)
        cosine = jnp.concatenate([cos_ref[:, mb * cap : (mb + 1) * cap]] * share, 1)
        sine = jnp.concatenate([sin_ref[:, mb * cap : (mb + 1) * cap]] * share, 1)

        def body(n, carry, mb=mb, cosine=cosine, sine=sine):
            query = join_heads(q_ref, n, share, mb, cap)
            grad = join_heads(do_ref, n, share, mb, cap)
            keys = k_ref[n]
            prob = jnp.exp(
                product_nn(keys, query) + bias_ref[...] - lse_ref[mb * KEY_HEADS + n]
            )
            dprob = product_nn(v_ref[n], grad)
            delta = jnp.sum(prob * dprob, 0, keepdims=True)
            dscore = (prob * (dprob - delta)).astype(jnp.bfloat16)
            dq = product_tn(keys, dscore) * SCORE_SCALE
            front, back = dq[:half], dq[half:]
            turned = jnp.concatenate(
                [front * cosine + back * sine, back * cosine - front * sine], 0
            ).astype(jnp.bfloat16)
            for g in range(share):
                dq_ref[share * n + g, :, mb * cap : (mb + 1) * cap] = turned[
                    :, g * cap : (g + 1) * cap
                ]
            dk_ref[n] = product_nt(dscore, query).astype(jnp.bfloat16)
            dv_ref[n] = product_nt(prob.astype(jnp.bfloat16), grad).astype(jnp.bfloat16)
            return carry

        lax.fori_loop(0, KEY_HEADS, body, 0)
        for core_rel, target in ((0, dkv_own_ref), (1, dkv_other_ref)):
            for s in range(4):
                block = core_rel * 4 + s
                for n in range(KEY_HEADS):
                    lanes = n * HEAD_WIDTH
                    target[s, mb * cap : (mb + 1) * cap, lanes : lanes + HEAD_WIDTH] = dk_ref[
                        n, block * cap : (block + 1) * cap, :
                    ]
                    lanes += kv_width
                    target[s, mb * cap : (mb + 1) * cap, lanes : lanes + HEAD_WIDTH] = dv_ref[
                        n, block * cap : (block + 1) * cap, :
                    ]


def hidden_kernel(ids_ref, own_ref, other_ref, att_ref, x_ref, gain_ref, h_ref, n2_ref):
    q_cols = h_ref.shape[0] // 8
    for core_rel, w_ref in ((0, own_ref), (1, other_ref)):

        def body(s, carry, core_rel=core_rel, w_ref=w_ref):
            f = column_index(ids_ref, core_rel, s)
            total = product_nn(w_ref[s], att_ref[ids_ref[0]])
            for k in range(1, 4):
                total += product_nn(w_ref[k * 4 + s], att_ref[ids_ref[0] ^ k])
            h_ref[start_row(f, q_cols), :] = total[:q_cols]
            return carry

        lax.fori_loop(0, 4, body, 0)
    h = h_ref[...] + x_ref[...].astype(jnp.float32)
    h_ref[...] = h
    n2_ref[...] = (h * mean_square(h) * gain_ref[...]).astype(jnp.bfloat16)


def turn_point_kernel(
    ids_ref,
    parts_ref,
    arrived_ref,
    h_ref,
    dy_ref,
    gain_ref,
    own_ref,
    other_ref,
    att_ref,
    out_ref,
    dh_ref,
    grad_own_ref,
    grad_other_ref,
    do_ref,
    gain_grad_ref,
    da_ref,
    mixed_ref,
):
    rows = h_ref.shape[1]
    q_cols = h_ref.shape[0] // 8
    h = h_ref[...]
    out_ref[...] = (
        h + parts_ref[0, :, :rows] + arrived_ref[0].astype(jnp.float32)
    ).astype(jnp.bfloat16)
    dn = parts_ref[1, :, :rows] + arrived_ref[1].astype(jnp.float32)
    rms = mean_square(h)
    gain_grad_ref[...] = jnp.sum(dn * h * rms, 1, keepdims=True)
    weighted = dn * gain_ref[...]
    dh = (
        dy_ref[...].astype(jnp.float32)
        + rms * weighted
        - h * (rms * rms * rms * jnp.mean(weighted * h, 0, keepdims=True))
    )
    dh_ref[...] = dh
    da_ref[...] = dh
    mixed_ref[...] = jnp.zeros_like(mixed_ref)
    for core_rel, w_ref, grad_ref in ((0, own_ref, grad_own_ref), (1, other_ref, grad_other_ref)):

        def body(s, carry, core_rel=core_rel, w_ref=w_ref, grad_ref=grad_ref):
            f = column_index(ids_ref, core_rel, s)
            piece = jnp.concatenate(
                [da_ref[start_row(f, q_cols), :], jnp.zeros((8, rows), jnp.float32)], 0
            ).astype(jnp.bfloat16)
            for k in range(4):
                i = ids_ref[0] ^ k
                mixed_ref[i] += product_tn(w_ref[k * 4 + s], piece)
                grad_ref[k * 4 + s] = product_nt(piece, att_ref[i]).astype(jnp.bfloat16)
            return carry

        lax.fori_loop(0, 4, body, 0)
    do_ref[...] = mixed_ref[...].astype(jnp.bfloat16)


def finish_kernel(
    ids_ref,
    own_ref,
    other_ref,
    n1_ref,
    dq_ref,
    dkv_ref,
    cos_ref,
    sin_ref,
    dh_ref,
    x_ref,
    gain_ref,
    tokens_ref,
    grad_own_ref,
    grad_other_ref,
    gain_grad_ref,
    d_ref,
    dn_ref,
):
    width, rows = dh_ref.shape
    kv_width = KEY_HEADS * HEAD_WIDTH
    q_cols, k_cols = width // 8, kv_width // 8
    half = HEAD_WIDTH // 2
    cosine, sine = cos_ref[...], sin_ref[...]
    d_ref[:width, :] = dq_ref[...].astype(jnp.float32)
    d_ref[width:, :] = dkv_ref[...].T
    for head in range(KEY_HEADS):
        base = width + head * HEAD_WIDTH
        front = d_ref[base : base + half, :]
        back = d_ref[base + half : base + 2 * half, :]
        d_ref[base : base + half, :] = front * cosine + back * sine
        d_ref[base + half : base + 2 * half, :] = back * cosine - front * sine
    dn_ref[...] = jnp.zeros_like(dn_ref)
    for core_rel, w_ref, grad_ref in ((0, own_ref, grad_own_ref), (1, other_ref, grad_other_ref)):

        def body(s, carry, core_rel=core_rel, w_ref=w_ref, grad_ref=grad_ref):
            f = column_index(ids_ref, core_rel, s)
            piece = jnp.concatenate(
                [
                    d_ref[start_row(f, q_cols), :],
                    d_ref[pl.ds(pl.multiple_of(width + f * k_cols, 8), k_cols), :],
                    d_ref[pl.ds(pl.multiple_of(width + kv_width + f * k_cols, 8), k_cols), :],
                    jnp.zeros((8, rows), jnp.float32),
                ],
                0,
            ).astype(jnp.bfloat16)
            for k in range(4):
                i = ids_ref[0] ^ k
                dn_ref[i] += product_tn(w_ref[k * 4 + s], piece)
                grad_ref[k * 4 + s] = product_nt(piece, n1_ref[i]).astype(jnp.bfloat16)
            return carry

        lax.fori_loop(0, 4, body, 0)
    x = x_ref[...].astype(jnp.float32)
    rms = mean_square(x)
    dn = dn_ref[...].reshape(width, rows)
    gain_grad_ref[...] = jnp.sum(dn * x * rms, 1, keepdims=True)
    weighted = dn * gain_ref[...]
    tokens_ref[...] = (
        dh_ref[...]
        + rms * weighted
        - x * (rms * rms * rms * jnp.mean(weighted * x, 0, keepdims=True))
    )


def mlp_kernel(*refs):
    ids_ref, normed_ref, dy_ref = refs[:3]
    pieces = refs[3:13]
    parts_ref = refs[13]
    grads = refs[14:24]
    w_ref, grad_ref, gu_ref, prod_ref, dgu_ref, sem_in, sem_out = refs[24:]
    dp_id = ids_ref[0]
    z_id = ids_ref[1]
    half = prod_ref.shape[1]
    block = normed_ref.shape[1]

    def views(ref, group):
        low = 2 * group
        return [
            ref.at[pl.ds(low, 2)],
            ref.at[pl.ds(4 + low, 2)],
            ref.at[pl.ds(8 + low, 2)],
            ref.at[12 + low],
            ref.at[13 + low],
        ]

    loads = []
    for group in range(2):
        for j, target in enumerate(views(w_ref, group)):
            index = group * 5 + j
            loads.append(pltpu.make_async_copy(pieces[index], target, sem_in.at[index]))
    for load in loads:
        load.start()
    for group in range(2):
        for load in loads[group * 5 : group * 5 + 5]:
            load.wait()

        def forward(s, carry):
            m = lax.rem(z_id - s + 4, 4)
            total = product_nn(w_ref[s, : 2 * half, :], normed_ref[dp_id])
            for k in range(1, 4):
                total += product_nn(w_ref[k * 4 + s, : 2 * half, :], normed_ref[dp_id ^ k])
            gu_ref[m] = total
            gate = total[:half]
            prod_ref[m] = (gate * jax.nn.sigmoid(gate) * total[half:]).astype(jnp.bfloat16)
            return carry

        lax.fori_loop(2 * group, 2 * group + 2, forward, 0)
    parts_ref[...] = jnp.zeros_like(parts_ref)

    def middle(k, carry):
        m = dp_id ^ k
        product = prod_ref[m]
        dprod = jnp.zeros(product.shape, jnp.float32)
        for s in range(4):
            zz = lax.rem(z_id - s + 4, 4)
            weight = w_ref[k * 4 + s, 2 * half : 3 * half, :]
            dy = dy_ref[zz]
            dprod += product_nn(weight, dy)
            parts_ref[0, pl.ds(pl.multiple_of(zz * block, 16), block), :] += product_tn(
                weight, product
            )
            grad_ref[k * 4 + s, 2 * half :, :] = product_nt(product, dy).astype(jnp.bfloat16)
        gate = gu_ref[m, :half, :]
        up = gu_ref[m, half:, :]
        sig = jax.nn.sigmoid(gate)
        dgu_ref[m, :half, :] = (dprod * up * sig * (1.0 + gate * (1.0 - sig))).astype(jnp.bfloat16)
        dgu_ref[m, half:, :] = (dprod * gate * sig).astype(jnp.bfloat16)
        return carry

    lax.fori_loop(0, 4, middle, 0)

    def backward(s, carry):
        m = lax.rem(z_id - s + 4, 4)
        dgu = dgu_ref[m]
        for k in range(4):
            i = dp_id ^ k
            parts_ref[1, pl.ds(pl.multiple_of(i * block, 16), block), :] += product_tn(
                w_ref[k * 4 + s, : 2 * half, :], dgu
            )
            grad_ref[k * 4 + s, : 2 * half, :] = product_nt(dgu, normed_ref[i]).astype(
                jnp.bfloat16
            )
        return carry

    stores = []
    for group in range(2):
        lax.fori_loop(2 * group, 2 * group + 2, backward, 0)
        for j, source in enumerate(views(grad_ref, group)):
            index = group * 5 + j
            store = pltpu.make_async_copy(source, grads[index], sem_out.at[index])
            store.start()
            stores.append(store)
    for store in stores:
        store.wait()


def mean_square(values):
    return lax.rsqrt(jnp.mean(values * values, 0, keepdims=True) + EPSILON)


def fast(
    tokens, cotangent, counts, w_query, key_weight, value_weight, w_out, w_gate, w_up, w_down, gains
):
    dp_id = lax.axis_index("dp")
    slot = lax.axis_index("fsdp")
    z_id = slot // 2
    core_id = slot % 2
    ids = jnp.stack([dp_id, z_id, core_id, slot]).astype(jnp.int32)
    batches, cap, width = tokens.shape
    rows = batches * cap
    block = w_query.shape[0]
    q_cols, k_cols = w_query.shape[1], key_weight.shape[1]
    half = w_gate.shape[1]
    kv_width = KEY_HEADS * HEAD_WIDTH
    share = QUERY_HEADS // KEY_HEADS
    depth = 3 * half
    o1, o2, o3 = q_cols, q_cols + k_cols, q_cols + 2 * k_cols

    extra = jnp.zeros((8, block), jnp.bfloat16)
    extra = extra.at[0].set(gains.reshape(-1))
    extra = extra.at[1, :batches].set(counts[:, 0].astype(jnp.bfloat16))
    first_piece = jnp.concatenate([w_query.T, key_weight.T, value_weight.T, extra], 0)
    chain = [first_piece]
    for _ in range(3):
        chain.append(shift_z(chain[-1], 1))
    along = jnp.stack(chain, 0)

    down_halves = w_down.reshape(2, half, -1)
    own_down = lax.dynamic_index_in_dim(down_halves, core_id, 0, keepdims=False)
    other_down = swap_core(
        lax.dynamic_index_in_dim(down_halves, 1 - core_id, 0, keepdims=False)
    )
    down = jnp.where(
        core_id == 0,
        jnp.concatenate([own_down, other_down], 1),
        jnp.concatenate([other_down, own_down], 1),
    )
    out_rows = jnp.concatenate([w_out.T, jnp.zeros((8, block), jnp.bfloat16)], 0)
    mlp_piece = jnp.concatenate([w_gate.T, w_up.T, down, out_rows], 0)
    mlp_piece, along = lax.optimization_barrier((mlp_piece, along))

    extras = along[:, o3 : o3 + 2, :]
    other_extras = swap_core(extras)
    from_x = swap_dp(along, 1)
    from_y = swap_dp(along, 2)
    first_own = jnp.concatenate(
        [along, from_x, from_y, swap_dp(from_x[:2], 2), swap_dp(from_y[2:], 1)], 0
    )
    first_other = swap_core(first_own)

    mlp_chain = [mlp_piece]
    for _ in range(3):
        mlp_chain.append(shift_z(mlp_chain[-1], 1))
    pieces, out_pieces = [], [[], [], [], []]
    for group in range(2):
        own = jnp.stack(mlp_chain[2 * group : 2 * group + 2], 0)
        if group == 0:
            own, first_other = lax.optimization_barrier((own, first_other))
        by_x = swap_dp(own, 1)
        by_y = swap_dp(own, 2)
        far_a = swap_dp(by_x[0], 2)
        far_b = swap_dp(by_y[1], 1)
        pieces += [own, by_x, by_y, far_a, far_b]
        for k, part in enumerate((own, by_x, by_y, jnp.stack([far_a, far_b], 0))):
            out_pieces[k].append(part[:, depth:])
    out_own = jnp.concatenate([part for pair in out_pieces for part in pair], 0)
    out_other = swap_core(out_own)

    by_core = jnp.where(
        core_id == 0, jnp.stack([extras, other_extras], 1), jnp.stack([other_extras, extras], 1)
    )
    by_core = by_core[::-1]
    by_core = lax.dynamic_slice_in_dim(jnp.concatenate([by_core, by_core], 0), 3 - z_id, 4, 0)
    gain = by_core[:, :, 0, :].reshape(8, 2, q_cols).transpose(0, 2, 1).reshape(width, 2)
    gain = gain.astype(jnp.float32)
    gain_one, gain_two = gain[:, :1], gain[:, 1:]
    group_counts = by_core[:, :, 1, :batches].reshape(8, batches).astype(jnp.int32)
    flat_counts = group_counts.T.reshape(-1)
    before = jnp.sum(
        jnp.where(jnp.arange(8, dtype=jnp.int32)[:, None] < slot, group_counts, 0), 0
    )
    position = (before[:, None] + jnp.arange(cap, dtype=jnp.int32)[None, :]).reshape(-1)
    cosine, sine = rope_tables(position, HEAD_WIDTH)
    cosine, sine = cosine[:, 0, :].T, sine[:, 0, :].T

    dy = cotangent.reshape(rows, width).T
    dy_pair = jnp.concatenate([dy, swap_core(dy)], 1).reshape(4, block, 2 * rows)
    x = tokens.reshape(rows, width).T
    x_wide = x.astype(jnp.float32)
    n1 = (x_wide * mean_square(x_wide) * gain_one).astype(jnp.bfloat16).reshape(4, block, rows)

    query, kv = run(
        project_kernel,
        "project",
        (ids, first_own, first_other, n1, cosine, sine),
        [SMEM] + [VMEM] * 5,
        (struct((QUERY_HEADS, HEAD_WIDTH, rows)), struct((rows, 2 * kv_width))),
        [VMEM] * 2,
        [
            pltpu.VMEM((width + 2 * kv_width, rows), jnp.float32),
            pltpu.VMEM((2 * kv_width, rows), jnp.float32),
        ],
        2 * (width + 2 * kv_width) * width * rows,
        32,
    )
    kv_chain = [kv]
    for _ in range(3):
        kv_chain.append(shift_z_up(kv_chain[-1], 1))
    kv_own = jnp.stack(kv_chain, 0)
    kv_other = swap_core(kv_own)
    pair_flops = 2 * QUERY_HEADS * HEAD_WIDTH * rows * 8 * cap
    head_scratch = [
        pltpu.VMEM((KEY_HEADS, 8 * cap, HEAD_WIDTH), jnp.bfloat16),
        pltpu.VMEM((KEY_HEADS, 8 * cap, HEAD_WIDTH), jnp.bfloat16),
        pltpu.VMEM((8 * cap, share * cap), jnp.float32),
    ]
    attended, lse = run(
        attend_kernel,
        "attend",
        (ids, flat_counts, query, kv_own, kv_other),
        [SMEM, SMEM] + [VMEM] * 3,
        (
            struct((QUERY_HEADS, HEAD_WIDTH, rows)),
            struct((2 * KEY_HEADS, 1, share * cap), jnp.float32),
        ),
        [VMEM] * 2,
        head_scratch,
        8 * pair_flops,
        40,
    )
    attended = attended.reshape(4, block, rows)
    h, n2 = run(
        hidden_kernel,
        "hidden",
        (ids, out_own, out_other, attended, x, gain_two),
        [SMEM] + [VMEM] * 5,
        (struct((width, rows), jnp.float32), struct((width, rows))),
        [VMEM] * 2,
        [],
        2 * width * width * rows,
        32,
    )
    n2_pair = jnp.concatenate([n2, swap_core(n2)], 1).reshape(4, block, 2 * rows)
    one, two = struct((depth, block)), struct((2, depth, block))
    results = run(
        mlp_kernel,
        "mlp",
        (ids, n2_pair, dy_pair, *pieces),
        [SMEM, VMEM, VMEM] + [ANY] * 10,
        [struct((2, width, 2 * rows), jnp.float32)] + [two, two, two, one, one] * 2,
        [VMEM] + [ANY] * 10,
        [
            pltpu.VMEM((16, mlp_piece.shape[0], block), jnp.bfloat16),
            pltpu.VMEM((16, depth, block), jnp.bfloat16),
            pltpu.VMEM((4, 2 * half, 2 * rows), jnp.float32),
            pltpu.VMEM((4, half, 2 * rows), jnp.bfloat16),
            pltpu.VMEM((4, 2 * half, 2 * rows), jnp.bfloat16),
            pltpu.SemaphoreType.DMA((10,)),
            pltpu.SemaphoreType.DMA((10,)),
        ],
        18 * 16 * half * block * 2 * rows,
        56,
    )
    parts, mlp_grads = results[0], results[1:]
    arrived = swap_core(parts[:, :, rows:].astype(jnp.bfloat16))
    output, dh, out_grad_own, out_grad_other, mixed_gradient, gain_two_grad = run(
        turn_point_kernel,
        "turn_point",
        (ids, parts, arrived, h, dy, gain_two, out_own, out_other, attended),
        [SMEM] + [VMEM] * 8,
        (
            struct((width, rows)),
            struct((width, rows), jnp.float32),
            struct(out_own.shape),
            struct(out_own.shape),
            struct((4, block, rows)),
            struct((width, 1), jnp.float32),
        ),
        [VMEM] * 6,
        [
            pltpu.VMEM((width, rows), jnp.float32),
            pltpu.VMEM((4, block, rows), jnp.float32),
        ],
        4 * width * width * rows,
        40,
    )
    output = output.T.reshape(batches, cap, width)

    mlp_total = None
    for group in range(2):
        home, to_x, to_y, far_a, far_b = mlp_grads[group * 5 : group * 5 + 5]
        via_y = swap_dp(far_a, 2)
        via_x = swap_dp(far_b, 1)
        to_x = jnp.stack([add_low(to_x[0], via_y), to_x[1]], 0)
        to_y = jnp.stack([to_y[0], add_low(to_y[1], via_x)], 0)
        summed = add_low(home, swap_dp(to_x, 1), swap_dp(to_y, 2))
        for j in range(2):
            s = 2 * group + j
            part = summed[j] if s == 0 else shift_z(summed[j], -s)
            part = part.astype(jnp.float32)
            mlp_total = part if mlp_total is None else mlp_total + part
    grad_gate = mlp_total[:half].T
    grad_up = mlp_total[half : 2 * half].T
    down_total = mlp_total[2 * half :]
    left, right = down_total[:, :q_cols], down_total[:, q_cols:]
    keep = jnp.where(core_id == 0, left, right)
    give = jnp.where(core_id == 0, right, left).astype(jnp.bfloat16)
    taken = swap_core(give).astype(jnp.float32)
    grad_down = jnp.where(
        core_id == 0, jnp.concatenate([keep, taken], 0), jnp.concatenate([taken, keep], 0)
    )

    def reduce_all(own, other):
        mine = add_low(own, swap_core(other))
        home, to_x, to_y, far = mine[:4], mine[4:8], mine[8:12], mine[12:]
        via_y = swap_dp(far[:2], 2)
        via_x = swap_dp(far[2:], 1)
        to_x = jnp.concatenate([add_low(to_x[:2], via_y), to_x[2:]], 0)
        to_y = jnp.concatenate([to_y[:2], add_low(to_y[2:], via_x)], 0)
        summed = add_low(home, swap_dp(to_x, 1), swap_dp(to_y, 2))
        total = summed[0].astype(jnp.float32)
        for s in (1, 2, 3):
            total = total + shift_z(summed[s], -s).astype(jnp.float32)
        return total

    grad_out = reduce_all(out_grad_own, out_grad_other)[:q_cols].T

    dq, dkv_own, dkv_other = run(
        attend_back_kernel,
        "attend_back",
        (
            ids,
            flat_counts,
            query,
            mixed_gradient.reshape(QUERY_HEADS, HEAD_WIDTH, rows),
            kv_own,
            kv_other,
            lse,
            cosine,
            sine,
        ),
        [SMEM, SMEM] + [VMEM] * 7,
        (
            struct((QUERY_HEADS, HEAD_WIDTH, rows)),
            struct((4, rows, 2 * kv_width)),
            struct((4, rows, 2 * kv_width)),
        ),
        [VMEM] * 3,
        head_scratch
        + [
            pltpu.VMEM((KEY_HEADS, 8 * cap, HEAD_WIDTH), jnp.bfloat16),
            pltpu.VMEM((KEY_HEADS, 8 * cap, HEAD_WIDTH), jnp.bfloat16),
        ],
        20 * pair_flops,
        48,
    )
    dkv = add_low(dkv_own, swap_core(dkv_other))
    dkv_total = dkv[0].astype(jnp.float32)
    for s in (1, 2, 3):
        dkv_total = dkv_total + shift_z_down(dkv[s], s).astype(jnp.float32)

    grad_tokens, first_grad_own, first_grad_other, gain_one_grad = run(
        finish_kernel,
        "finish",
        (
            ids,
            first_own,
            first_other,
            n1,
            dq.reshape(width, rows),
            dkv_total,
            cosine,
            sine,
            dh,
            x,
            gain_one,
        ),
        [SMEM] + [VMEM] * 10,
        (
            struct((width, rows), jnp.float32),
            struct(first_own.shape),
            struct(first_own.shape),
            struct((width, 1), jnp.float32),
        ),
        [VMEM] * 4,
        [
            pltpu.VMEM((width + 2 * kv_width, rows), jnp.float32),
            pltpu.VMEM((4, block, rows), jnp.float32),
        ],
        4 * (width + 2 * kv_width) * width * rows,
        48,
    )
    grad_tokens = grad_tokens.T.reshape(batches, cap, width)
    first_total = reduce_all(first_grad_own, first_grad_other)
    gain_total = jnp.concatenate([gain_one_grad, gain_two_grad], 1).T
    gain_total = gain_total + swap_core(gain_total)
    gain_total = gain_total + swap_dp(gain_total, 1)
    gain_total = gain_total + swap_dp(gain_total, 2)
    for mask in (2, 4):
        gain_total = gain_total + lax.ppermute(
            gain_total, "fsdp", [(j, j ^ mask) for j in range(8)]
        )
    gain_grad = lax.dynamic_slice_in_dim(gain_total, slot * q_cols, q_cols, 1)
    return (
        output,
        grad_tokens,
        first_total[:o1].T,
        first_total[o1:o2].T,
        first_total[o2:o3].T,
        grad_out,
        grad_gate,
        grad_up,
        grad_down,
        gain_grad,
    )


def solution(mesh):
    in_specs = (
        P(None, ("dp", "fsdp"), None),
        P(None, ("dp", "fsdp"), None),
        P(None, ("dp", "fsdp")),
        P("dp", "fsdp"),
        P("dp", "fsdp"),
        P("dp", "fsdp"),
        P("dp", "fsdp"),
        P("dp", "fsdp"),
        P("dp", "fsdp"),
        P("dp", "fsdp"),
        P(None, "fsdp"),
    )
    out_specs = (
        P(None, ("dp", "fsdp"), None),
        P(None, ("dp", "fsdp"), None),
        P("dp", "fsdp"),
        P("dp", "fsdp"),
        P("dp", "fsdp"),
        P("dp", "fsdp"),
        P("dp", "fsdp"),
        P("dp", "fsdp"),
        P("dp", "fsdp"),
        P(None, "fsdp"),
    )
    square = mesh.shape["dp"] == 4 and mesh.shape["fsdp"] == 8
    return jax.shard_map(
        fast if square else local, mesh=mesh, in_specs=in_specs, out_specs=out_specs, check_vma=False)
```

```python
import functools

import jax
import jax.numpy as jnp
from jax import lax
from jax.experimental import pallas as pl
from jax.experimental.pallas import tpu as pltpu
from jax.sharding import PartitionSpec as P

MODEL_WIDTH = 960
QUERY_HEADS = 15
KEY_HEADS = 5
HEAD_WIDTH = 64


EPSILON = 1e-05
ROPE_BASE = 100000.0
SCORE_SCALE = 0.125


def rope_tables(position, head_size):
    half_size = head_size // 2
    frequency = ROPE_BASE ** (-(jnp.arange(half_size, dtype=jnp.float32) * 2.0) / head_size)
    angles = position.astype(jnp.float32)[:, None] * frequency[None, :]
    return (jnp.cos(angles)[:, None, :], jnp.sin(angles)[:, None, :])


def apply_rotation(values, cosine_table, sine_values):
    half_size = values.shape[-1] // 2
    front_half = values[..., :half_size]
    back_half = values[..., half_size:]
    return jnp.concatenate(
        [
            front_half * cosine_table - back_half * sine_values,
            back_half * cosine_table + front_half * sine_values,
        ],
        -1,
    )


def normalize(values, gain_row):
    inv_rms = lax.rsqrt(jnp.mean(values * values, -1, keepdims=True) + EPSILON)
    return (values * inv_rms * gain_row, inv_rms)


def norm_back(values, inv_rms, gain_row, incoming):
    weighted = incoming * gain_row
    return inv_rms * weighted - values * inv_rms * inv_rms * inv_rms * jnp.mean(
        weighted * values, -1, keepdims=True
    )


def build_mask(count_row, device, slot_capacity):
    group_width = count_row.shape[0]
    local_slot = jnp.arange(slot_capacity, dtype=jnp.int32)
    offsets = jnp.cumsum(count_row) - count_row
    is_mine = jnp.arange(group_width, dtype=jnp.int32) == device
    own_offset = jnp.sum(jnp.where(is_mine, offsets, 0))
    own_count = jnp.sum(jnp.where(is_mine, count_row, 0))
    query_pos = own_offset + local_slot
    query_valid = local_slot < own_count
    key_pos = (offsets[:, None] + local_slot[None, :]).reshape(-1)
    key_valid = (local_slot[None, :] < count_row[:, None]).reshape(-1)
    slot_ids = jnp.arange(group_width * slot_capacity, dtype=jnp.int32)
    own_slots = device * slot_capacity + local_slot
    allowed = query_valid[:, None] & key_valid[None, :] & (
        key_pos[None, :] <= query_pos[:, None]
    ) | (slot_ids[None, :] == own_slots[:, None])
    return (allowed, query_pos)


def kept_fetch(w_query, key_weight, value_weight, w_out, w_gate, w_up, w_down, gains):
    columns = (
        lax.all_gather(w_query, "fsdp", axis=1, tiled=True),
        lax.all_gather(key_weight, "fsdp", axis=1, tiled=True),
        lax.all_gather(value_weight, "fsdp", axis=1, tiled=True),
        lax.all_gather(w_out, "fsdp", axis=1, tiled=True),
        lax.all_gather(w_gate, "fsdp", axis=1, tiled=True),
        lax.all_gather(w_up, "fsdp", axis=1, tiled=True),
        lax.all_gather(w_down, "fsdp", axis=1, tiled=True),
        lax.all_gather(gains, "fsdp", axis=1, tiled=True),
    )
    matrices = (
        lax.all_gather(columns[0], "dp", axis=0, tiled=True),
        lax.all_gather(columns[1], "dp", axis=0, tiled=True),
        lax.all_gather(columns[2], "dp", axis=0, tiled=True),
        lax.all_gather(columns[3], "dp", axis=0, tiled=True),
        lax.all_gather(columns[4], "dp", axis=0, tiled=True),
        lax.all_gather(columns[5], "dp", axis=0, tiled=True),
        lax.all_gather(columns[6], "dp", axis=0, tiled=True),
    )
    return (matrices, columns[7].astype(jnp.float32))


def times_transpose(left, right):
    return jnp.einsum("rk,jk->rj", left, right, preferred_element_type=jnp.float32)


def rows_product(left, right):
    return jnp.einsum("rd,rk->dk", left, right, preferred_element_type=jnp.float32)


def local(
    tokens, cotangent, counts, w_query, key_weight, value_weight, w_out, w_gate, w_up, w_down, gains
):
    group_counts = lax.all_gather(counts, "fsdp", axis=1, tiled=True)
    device = lax.axis_index("fsdp")
    slot_capacity = tokens.shape[1]
    key_value_width = KEY_HEADS * HEAD_WIDTH
    device_share = QUERY_HEADS // KEY_HEADS
    kept_weights, kept_gain = kept_fetch(
        w_query, key_weight, value_weight, w_out, w_gate, w_up, w_down, gains
    )
    outputs = []
    grad_inputs = []
    saved = [[] for index_unused in range(11)]
    gain_one_total = jnp.zeros((MODEL_WIDTH,), jnp.float32)
    gain_two_total = jnp.zeros((MODEL_WIDTH,), jnp.float32)
    for micro_idx in range(tokens.shape[0]):
        matrices, gain_pair = (kept_weights, kept_gain)
        full_query, full_key, full_value, full_out, full_gate, full_up, full_down = matrices
        inputs = tokens[micro_idx].astype(jnp.float32)
        allowed, query_pos = build_mask(group_counts[micro_idx], device, slot_capacity)
        cosine_table, sine_values = rope_tables(query_pos, HEAD_WIDTH)
        first_normed, scale_one = normalize(inputs, gain_pair[0])
        normed_low = first_normed.astype(jnp.bfloat16)
        reduced_query = apply_rotation(
            jnp.dot(normed_low, full_query, preferred_element_type=jnp.float32).reshape(
                slot_capacity, QUERY_HEADS, HEAD_WIDTH
            ),
            cosine_table,
            sine_values,
        ).astype(jnp.bfloat16)
        key_low = (
            apply_rotation(
                jnp.dot(normed_low, full_key, preferred_element_type=jnp.float32).reshape(
                    slot_capacity, KEY_HEADS, HEAD_WIDTH
                ),
                cosine_table,
                sine_values,
            )
            .astype(jnp.bfloat16)
            .reshape(slot_capacity, key_value_width)
        )
        value_low = jnp.dot(normed_low, full_value, preferred_element_type=jnp.float32).astype(
            jnp.bfloat16
        )
        grouped_keys, grouped_values = (
            lax.all_gather(key_low, "fsdp", axis=0, tiled=True),
            lax.all_gather(value_low, "fsdp", axis=0, tiled=True),
        )
        heads_of_key = grouped_keys.reshape(-1, KEY_HEADS, HEAD_WIDTH)
        heads_of_value = grouped_values.reshape(-1, KEY_HEADS, HEAD_WIDTH)
        heads_of_query = reduced_query.reshape(slot_capacity, KEY_HEADS, device_share, HEAD_WIDTH)
        scores = (
            jnp.einsum(
                "qngd,knd->ngqk", heads_of_query, heads_of_key, preferred_element_type=jnp.float32
            )
            * SCORE_SCALE
        )
        masked = jnp.where(allowed, scores, -1e30)
        row_top = jnp.max(masked, -1, keepdims=True)
        exponent = jnp.where(allowed, jnp.exp(masked - row_top), 0.0)
        row_total = jnp.sum(exponent, -1, keepdims=True)
        prob_low = (exponent / row_total).astype(jnp.bfloat16)
        log_total = row_top + jnp.log(row_total)
        mixed_heads = jnp.einsum(
            "ngqk,knd->qngd", prob_low, heads_of_value, preferred_element_type=jnp.float32
        ).reshape(slot_capacity, MODEL_WIDTH)
        attended = mixed_heads.astype(jnp.bfloat16)
        hidden_state = inputs + jnp.dot(attended, full_out, preferred_element_type=jnp.float32)
        normed_two, scale_two = normalize(hidden_state, gain_pair[1])
        normed_two_low = normed_two.astype(jnp.bfloat16)
        gate_act = jnp.dot(normed_two_low, full_gate, preferred_element_type=jnp.float32)
        upward = jnp.dot(normed_two_low, full_up, preferred_element_type=jnp.float32)
        sigmoid_gate = jax.nn.sigmoid(gate_act)
        product = (gate_act * sigmoid_gate * upward).astype(jnp.bfloat16)
        outputs.append(
            (hidden_state + jnp.dot(product, full_down, preferred_element_type=jnp.float32)).astype(
                jnp.bfloat16
            )
        )
        matrices, gain_pair = (kept_weights, kept_gain)
        full_query, full_key, full_value, full_out, full_gate, full_up, full_down = matrices
        grad_low = cotangent[micro_idx]
        grad_product = times_transpose(grad_low, full_down)
        grad_gate = (
            grad_product * upward * sigmoid_gate * (1.0 + gate_act * (1.0 - sigmoid_gate))
        ).astype(jnp.bfloat16)
        grad_upward = (grad_product * gate_act * sigmoid_gate).astype(jnp.bfloat16)
        grad_normed_two = times_transpose(grad_gate, full_gate) + times_transpose(
            grad_upward, full_up
        )
        gain_two_total = gain_two_total + jnp.sum(grad_normed_two * hidden_state * scale_two, 0)
        grad_hidden = grad_low.astype(jnp.float32) + norm_back(
            hidden_state, scale_two, gain_pair[1], grad_normed_two
        )
        grad_branch = grad_hidden.astype(jnp.bfloat16)
        mixed_gradient = times_transpose(grad_branch, full_out).astype(jnp.bfloat16)
        head_gradient = mixed_gradient.reshape(slot_capacity, KEY_HEADS, device_share, HEAD_WIDTH)
        again_scores = (
            jnp.einsum(
                "qngd,knd->ngqk", heads_of_query, heads_of_key, preferred_element_type=jnp.float32
            )
            * SCORE_SCALE
        )
        probability = jnp.where(allowed, jnp.exp(again_scores - log_total), 0.0)
        grad_prob = jnp.einsum(
            "qngd,knd->ngqk", head_gradient, heads_of_value, preferred_element_type=jnp.float32
        )
        row_delta = jnp.sum(probability * grad_prob, -1, keepdims=True)
        grad_scores = (probability * (grad_prob - row_delta)).astype(jnp.bfloat16)
        grad_query_rot = (
            jnp.einsum(
                "ngqk,knd->qngd", grad_scores, heads_of_key, preferred_element_type=jnp.float32
            ).reshape(slot_capacity, QUERY_HEADS, HEAD_WIDTH)
            * SCORE_SCALE
        )
        key_part = (
            jnp.einsum(
                "ngqk,qngd->knd", grad_scores, heads_of_query, preferred_element_type=jnp.float32
            ).reshape(-1, key_value_width)
            * SCORE_SCALE
        )
        value_part = jnp.einsum(
            "ngqk,qngd->knd",
            probability.astype(jnp.bfloat16),
            head_gradient,
            preferred_element_type=jnp.float32,
        ).reshape(-1, key_value_width)
        key_gradient, value_grad = (
            lax.psum_scatter(
                key_part.astype(jnp.bfloat16), "fsdp", scatter_dimension=0, tiled=True
            ).astype(jnp.float32),
            lax.psum_scatter(
                value_part.astype(jnp.bfloat16), "fsdp", scatter_dimension=0, tiled=True
            ).astype(jnp.float32),
        )
        grad_query = (
            apply_rotation(grad_query_rot, cosine_table, -sine_values)
            .astype(jnp.bfloat16)
            .reshape(slot_capacity, MODEL_WIDTH)
        )
        grad_key = (
            apply_rotation(
                key_gradient.reshape(slot_capacity, KEY_HEADS, HEAD_WIDTH),
                cosine_table,
                -sine_values,
            )
            .astype(jnp.bfloat16)
            .reshape(slot_capacity, key_value_width)
        )
        grad_value = value_grad.astype(jnp.bfloat16)
        grad_normed_one = (
            times_transpose(grad_query, full_query)
            + times_transpose(grad_key, full_key)
            + times_transpose(grad_value, full_value)
        )
        gain_one_total = gain_one_total + jnp.sum(grad_normed_one * inputs * scale_one, 0)
        grad_inputs.append(
            grad_hidden + norm_back(inputs, scale_one, gain_pair[0], grad_normed_one)
        )
        kept_rows = (
            normed_low,
            grad_query,
            grad_key,
            grad_value,
            attended,
            grad_branch,
            normed_two_low,
            grad_gate,
            grad_upward,
            product,
            grad_low,
        )
        for slot_index in range(11):
            saved[slot_index].append(kept_rows[slot_index])
    joined = [jnp.concatenate(column_list, 0) for column_list in saved]
    gain_terms = jnp.stack([gain_one_total, gain_two_total], 0)
    slices = (
        lax.all_to_all(joined[1], "fsdp", split_axis=1, concat_axis=0, tiled=True),
        lax.all_to_all(joined[2], "fsdp", split_axis=1, concat_axis=0, tiled=True),
        lax.all_to_all(joined[3], "fsdp", split_axis=1, concat_axis=0, tiled=True),
        lax.all_to_all(joined[5], "fsdp", split_axis=1, concat_axis=0, tiled=True),
        lax.all_to_all(joined[7], "fsdp", split_axis=1, concat_axis=0, tiled=True),
        lax.all_to_all(joined[8], "fsdp", split_axis=1, concat_axis=0, tiled=True),
        lax.all_to_all(joined[10], "fsdp", split_axis=1, concat_axis=0, tiled=True),
    )
    pieces = (
        lax.all_gather(joined[0], "fsdp", axis=0, tiled=True),
        lax.all_gather(joined[4], "fsdp", axis=0, tiled=True),
        lax.all_gather(joined[6], "fsdp", axis=0, tiled=True),
        lax.all_gather(joined[9], "fsdp", axis=0, tiled=True),
    )
    picked = [member for member in slices]
    gain_part = lax.psum_scatter(gain_terms, "fsdp", scatter_dimension=1, tiled=True)
    summed_rows = (
        lax.psum_scatter(
            rows_product(pieces[0], picked[0]).astype(jnp.bfloat16),
            "dp",
            scatter_dimension=0,
            tiled=True,
        ).astype(jnp.float32),
        lax.psum_scatter(
            rows_product(pieces[0], picked[1]).astype(jnp.bfloat16),
            "dp",
            scatter_dimension=0,
            tiled=True,
        ).astype(jnp.float32),
        lax.psum_scatter(
            rows_product(pieces[0], picked[2]).astype(jnp.bfloat16),
            "dp",
            scatter_dimension=0,
            tiled=True,
        ).astype(jnp.float32),
        lax.psum_scatter(
            rows_product(pieces[1], picked[3]).astype(jnp.bfloat16),
            "dp",
            scatter_dimension=0,
            tiled=True,
        ).astype(jnp.float32),
        lax.psum_scatter(
            rows_product(pieces[2], picked[4]).astype(jnp.bfloat16),
            "dp",
            scatter_dimension=0,
            tiled=True,
        ).astype(jnp.float32),
        lax.psum_scatter(
            rows_product(pieces[2], picked[5]).astype(jnp.bfloat16),
            "dp",
            scatter_dimension=0,
            tiled=True,
        ).astype(jnp.float32),
        lax.psum_scatter(
            rows_product(pieces[3], picked[6]).astype(jnp.bfloat16),
            "dp",
            scatter_dimension=0,
            tiled=True,
        ).astype(jnp.float32),
    )
    gain_grad = lax.psum(gain_part, "dp")
    return (
        jnp.stack(outputs, 0),
        jnp.stack(grad_inputs, 0),
        summed_rows[0],
        summed_rows[1],
        summed_rows[2],
        summed_rows[3],
        summed_rows[4],
        summed_rows[5],
        summed_rows[6],
        gain_grad,
    )


def swap_core(value):
    return lax.ppermute(value, "fsdp", [(j, j ^ 1) for j in range(8)])


def swap_dp(value, mask):
    return lax.ppermute(value, "dp", [(j, j ^ mask) for j in range(4)])


def shift_z(value, step):
    return lax.ppermute(value, "fsdp", [(j, (j + 2 * step) % 8) for j in range(8)])


def shift_z_up(value, step):
    return lax.ppermute(value, "fsdp", [(j, j + 2 * step) for j in range(8) if j + 2 * step < 8])


def shift_z_down(value, step):
    return lax.ppermute(value, "fsdp", [(j, j - 2 * step) for j in range(8) if j - 2 * step >= 0])


def add_low(*terms):
    total = terms[0].astype(jnp.float32)
    for term in terms[1:]:
        total = total + term.astype(jnp.float32)
    return total.astype(jnp.bfloat16)


def product_nn(left, right):
    return lax.dot_general(
        left, right, (((1,), (0,)), ((), ())), preferred_element_type=jnp.float32
    )


def product_nt(left, right):
    return lax.dot_general(
        left, right, (((1,), (1,)), ((), ())), preferred_element_type=jnp.float32
    )


def product_tn(left, right):
    return lax.dot_general(
        left, right, (((0,), (0,)), ((), ())), preferred_element_type=jnp.float32
    )


VMEM = pl.BlockSpec(memory_space=pltpu.VMEM)
SMEM = pl.BlockSpec(memory_space=pltpu.SMEM)
ANY = pl.BlockSpec(memory_space=pl.ANY)


def run(body, name, ins, in_specs, outs, out_specs, scratch, flops, megabytes):
    moved = sum(v.size * v.dtype.itemsize for v in ins)
    moved += sum(v.size * v.dtype.itemsize for v in outs)
    return pl.pallas_call(
        body,
        out_shape=tuple(outs),
        in_specs=in_specs,
        out_specs=tuple(out_specs),
        scratch_shapes=scratch,
        compiler_params=pltpu.CompilerParams(vmem_limit_bytes=megabytes * 1024 * 1024),
        cost_estimate=pl.CostEstimate(flops=flops, bytes_accessed=moved, transcendentals=0),
        name=name,
    )(*ins)


def struct(shape, dtype=jnp.bfloat16):
    return jax.ShapeDtypeStruct(shape, dtype)


def column_index(ids_ref, core_rel, s):
    return 2 * lax.rem(ids_ref[1] - s + 4, 4) + (ids_ref[2] ^ core_rel)


def start_row(index, size):
    return pl.ds(pl.multiple_of(index * size, 8), size)


def after(value, *others):
    return lax.optimization_barrier((value,) + others)[0]


def pack_first_kernel(counts_ref, wq_ref, wk_ref, wv_ref, gains_ref, out_ref):
    block = wq_ref.shape[0]
    gains = gains_ref[...].astype(jnp.float32)
    row = lax.broadcasted_iota(jnp.int32, (8, block), 0)
    lane = lax.broadcasted_iota(jnp.int32, (8, block), 1)
    first = jnp.concatenate([gains[:1], gains[1:]], 1)
    used = jnp.where(
        lane == 0,
        counts_ref[0, 0].astype(jnp.float32),
        jnp.where(lane == 1, counts_ref[1, 0].astype(jnp.float32), 0.0),
    )
    extra = jnp.where(row == 0, first, jnp.where(row == 1, used, 0.0))
    full = jnp.concatenate(
        [
            wq_ref[...].astype(jnp.float32).T,
            extra,
            wk_ref[...].astype(jnp.float32).T,
            wv_ref[...].astype(jnp.float32).T,
        ],
        0,
    )
    out_ref[...] = jnp.zeros_like(out_ref)
    out_ref[:, :block] = full.astype(jnp.bfloat16)


def pack_mlp_kernel(ids_ref, wg_ref, wu_ref, wd_ref, other_ref, wo_ref, out_ref):
    block, half = wg_ref.shape
    core = ids_ref[2]
    out_ref[...] = jnp.zeros_like(out_ref)
    out_ref[:half, :block] = wg_ref[...].astype(jnp.float32).T.astype(jnp.bfloat16)
    out_ref[half : 2 * half, :block] = wu_ref[...].astype(jnp.float32).T.astype(jnp.bfloat16)
    own = wd_ref[pl.ds(pl.multiple_of(core * half, 16), half), :]
    other = other_ref[...]
    low = jnp.where(core == 0, own, other)
    high = jnp.where(core == 0, other, own)
    out_ref[2 * half : 3 * half, :block] = jnp.concatenate([low, high], 1)
    out_ref[3 * half :, :block] = jnp.concatenate(
        [wo_ref[...].astype(jnp.float32).T, jnp.zeros((8, block), jnp.float32)], 0
    ).astype(jnp.bfloat16)


def turn_in_kernel(x_ref, dy_ref, xt_ref, dyt_ref):
    xt_ref[...] = x_ref[...].astype(jnp.float32).T.astype(jnp.bfloat16)
    dyt_ref[...] = dy_ref[...].astype(jnp.float32).T.astype(jnp.bfloat16)


def fill_relative(ids_ref, source_ref, target_ref):
    block, lanes = source_ref.shape[1:]
    wide = target_ref.shape[0] // 4
    for k in range(4):
        target_ref[k * wide : k * wide + block, :] = source_ref[ids_ref[0] ^ k]
        target_ref[k * wide + block : (k + 1) * wide, :] = jnp.zeros(
            (wide - block, lanes), target_ref.dtype
        )


def wide_rows(refs, s, low, high):
    along, by_x, by_y, far_a, far_b = refs
    far = far_a if s < 2 else far_b
    return jnp.concatenate(
        [along[s, low:high], by_x[s, low:high], by_y[s, low:high], far[s % 2, low:high]], 1
    )


def project_kernel(*refs):
    ids_ref, own, other = refs[0], refs[1:6], refs[6:11]
    n1_ref, cos_ref, sin_ref, q_ref, kv_ref, proj_ref, turned_ref, rel_ref = refs[11:]
    width = n1_ref.shape[0] * n1_ref.shape[1]
    kv_width = KEY_HEADS * HEAD_WIDTH
    q_cols, k_cols = width // 8, kv_width // 8
    depth = own[0].shape[1]
    fill_relative(ids_ref, n1_ref, rel_ref)
    for core_rel, weights in ((0, own), (1, other)):
        for s in range(4):
            f = column_index(ids_ref, core_rel, s)
            total = product_nn(wide_rows(weights, s, 0, depth), rel_ref[...])
            proj_ref[start_row(f, q_cols), :] = total[:q_cols]
            proj_ref[pl.ds(pl.multiple_of(width + f * k_cols, 8), k_cols), :] = total[
                q_cols + 8 : q_cols + 8 + k_cols
            ]
            proj_ref[pl.ds(pl.multiple_of(width + kv_width + f * k_cols, 8), k_cols), :] = total[
                q_cols + 8 + k_cols :
            ]
    cosine, sine = cos_ref[...], sin_ref[...]
    half = HEAD_WIDTH // 2

    def heads(head, carry):
        front = proj_ref[pl.ds(pl.multiple_of(head * HEAD_WIDTH, 8), half), :]
        back = proj_ref[pl.ds(pl.multiple_of(head * HEAD_WIDTH + half, 8), half), :]
        q_ref[head, :half, :] = (
            (front * cosine - back * sine).astype(jnp.bfloat16) * SCORE_SCALE
        ).astype(jnp.bfloat16)
        q_ref[head, half:, :] = (
            (back * cosine + front * sine).astype(jnp.bfloat16) * SCORE_SCALE
        ).astype(jnp.bfloat16)
        return carry

    lax.fori_loop(0, QUERY_HEADS, heads, 0)
    for head in range(KEY_HEADS):
        base = width + head * HEAD_WIDTH
        front = proj_ref[base : base + half, :]
        back = proj_ref[base + half : base + 2 * half, :]
        turned_ref[head * HEAD_WIDTH : head * HEAD_WIDTH + half, :] = front * cosine - back * sine
        turned_ref[head * HEAD_WIDTH + half : (head + 1) * HEAD_WIDTH, :] = (
            back * cosine + front * sine
        )
    turned_ref[kv_width:, :] = proj_ref[width + kv_width :, :]
    kv_ref[...] = turned_ref[...].T.astype(jnp.bfloat16)


def stage_heads(mb, cap, blocks, k_ref, v_ref):
    kv_width = KEY_HEADS * HEAD_WIDTH
    for block, source in enumerate(blocks):
        rows = source[mb * cap : (mb + 1) * cap, :]
        for n in range(KEY_HEADS):
            lanes = n * HEAD_WIDTH
            k_ref[n, block * cap : (block + 1) * cap, :] = rows[:, lanes : lanes + HEAD_WIDTH]
            lanes += kv_width
            v_ref[n, block * cap : (block + 1) * cap, :] = rows[:, lanes : lanes + HEAD_WIDTH]


def stage_bias(ids_ref, counts_ref, mb, cap, share, bias_ref):
    slot = ids_ref[3]
    own_count = counts_ref[mb * 8 + slot]
    key = lax.broadcasted_iota(jnp.int32, (cap, cap), 0)
    query = lax.broadcasted_iota(jnp.int32, (cap, cap), 1)
    query_used = query < own_count
    for core_rel in range(2):
        for s in range(4):
            block = core_rel * 4 + s
            f = column_index(ids_ref, core_rel, s)
            count = counts_ref[mb * 8 + f]
            reach = jnp.where(f < slot, cap, jnp.where(f == slot, 0, -2 * cap))
            self_off = jnp.where(f == slot, 0, 2 * cap)
            allowed = (query_used & (key < count) & (key <= query + reach)) | (
                key == query + self_off
            )
            tile = jnp.where(allowed, 0.0, -1e30)
            for g in range(share):
                bias_ref[block * cap : (block + 1) * cap, g * cap : (g + 1) * cap] = tile


def join_heads(ref, n, share, mb, cap):
    return jnp.concatenate(
        [ref[share * n + g, :, mb * cap : (mb + 1) * cap] for g in range(share)], 1
    )


def attend_kernel(*refs):
    ids_ref, counts_ref, q_ref = refs[:3]
    blocks = refs[3:11]
    att_ref, lse_ref, k_ref, v_ref, bias_ref = refs[11:]
    cap = q_ref.shape[2] // 2
    share = QUERY_HEADS // KEY_HEADS
    for mb in range(2):
        stage_heads(mb, cap, blocks, k_ref, v_ref)
        stage_bias(ids_ref, counts_ref, mb, cap, share, bias_ref)

        def body(n, carry, mb=mb):
            scores = product_nn(k_ref[n], join_heads(q_ref, n, share, mb, cap)) + bias_ref[...]
            top = jnp.max(scores, 0, keepdims=True)
            exponent = jnp.exp(scores - top)
            total = jnp.sum(exponent, 0, keepdims=True)
            mixed = product_tn(v_ref[n], exponent.astype(jnp.bfloat16)) / total
            mixed = mixed.astype(jnp.bfloat16)
            for g in range(share):
                att_ref[share * n + g, :, mb * cap : (mb + 1) * cap] = mixed[
                    :, g * cap : (g + 1) * cap
                ]
            lse_ref[mb * KEY_HEADS + n] = top + jnp.log(total)
            return carry

        lax.fori_loop(0, KEY_HEADS, body, 0)


def attend_back_kernel(mb, *refs):
    ids_ref, counts_ref, q_ref, do_ref = refs[:4]
    blocks = refs[4:12]
    lse_ref, cos_ref, sin_ref, dq_ref = refs[12:16]
    targets = refs[16:24]
    k_ref, v_ref, bias_ref, dk_ref, dv_ref = refs[24:]
    cap = q_ref.shape[2] // 2
    share = QUERY_HEADS // KEY_HEADS
    half = HEAD_WIDTH // 2
    kv_width = KEY_HEADS * HEAD_WIDTH
    stage_heads(mb, cap, blocks, k_ref, v_ref)
    stage_bias(ids_ref, counts_ref, mb, cap, share, bias_ref)
    cosine = jnp.concatenate([cos_ref[:, mb * cap : (mb + 1) * cap]] * share, 1)
    sine = jnp.concatenate([sin_ref[:, mb * cap : (mb + 1) * cap]] * share, 1)

    def body(n, carry):
        query = join_heads(q_ref, n, share, mb, cap)
        grad = join_heads(do_ref, n, share, mb, cap)
        keys = k_ref[n]
        prob = jnp.exp(product_nn(keys, query) + bias_ref[...] - lse_ref[mb * KEY_HEADS + n])
        dprob = product_nn(v_ref[n], grad)
        delta = jnp.sum(prob * dprob, 0, keepdims=True)
        dscore = (prob * (dprob - delta)).astype(jnp.bfloat16)
        dq = product_tn(keys, dscore) * SCORE_SCALE
        front, back = dq[:half], dq[half:]
        turned = jnp.concatenate(
            [front * cosine + back * sine, back * cosine - front * sine], 0
        ).astype(jnp.bfloat16)
        for g in range(share):
            dq_ref[share * n + g] = turned[:, g * cap : (g + 1) * cap]
        dk_ref[n] = product_nt(dscore, query).astype(jnp.bfloat16)
        dv_ref[n] = product_nt(prob.astype(jnp.bfloat16), grad).astype(jnp.bfloat16)
        return carry

    lax.fori_loop(0, KEY_HEADS, body, 0)
    for block, target in enumerate(targets):
        for n in range(KEY_HEADS):
            lanes = n * HEAD_WIDTH
            target[:, lanes : lanes + HEAD_WIDTH] = dk_ref[n, block * cap : (block + 1) * cap, :]
            lanes += kv_width
            target[:, lanes : lanes + HEAD_WIDTH] = dv_ref[n, block * cap : (block + 1) * cap, :]


def collect_kernel(*refs):
    pieces, out_ref, sem = refs[:16], refs[16], refs[17]
    rows, wide = out_ref.shape[1], pieces[0].shape[1]
    copies = []
    for k in range(4):
        for s in range(4):
            copies.append(
                pltpu.make_async_copy(
                    pieces[k * 4 + s].at[pl.ds(pieces[0].shape[0] - rows, rows)],
                    out_ref.at[s, :, pl.ds(k * wide, wide)],
                    sem.at[k * 4 + s],
                )
            )
    for copy in copies:
        copy.start()
    for copy in copies:
        copy.wait()


def hidden_kernel(ids_ref, own_ref, other_ref, att_ref, x_ref, gain_ref, h_ref, n2_ref, rel_ref):
    q_cols = h_ref.shape[0] // 8
    fill_relative(ids_ref, att_ref, rel_ref)
    for core_rel, w_ref in ((0, own_ref), (1, other_ref)):
        for s in range(4):
            f = column_index(ids_ref, core_rel, s)
            h_ref[start_row(f, q_cols), :] = product_nn(w_ref[s], rel_ref[...])[:q_cols]
    h = h_ref[...] + x_ref[...].astype(jnp.float32)
    h_ref[...] = h
    n2_ref[...] = (h * mean_square(h) * gain_ref[...]).astype(jnp.bfloat16)


def turn_point_kernel(
    ids_ref,
    parts_ref,
    arrived_ref,
    h_ref,
    dy_ref,
    gain_ref,
    own_ref,
    other_ref,
    out_ref,
    dh_ref,
    do_ref,
    gain_grad_ref,
    pieces_ref,
    da_ref,
):
    width, rows = h_ref.shape
    q_cols = width // 8
    block = do_ref.shape[1]
    wide = own_ref.shape[2] // 4
    h = h_ref[...]
    out_ref[...] = (h + parts_ref[0] + arrived_ref[0].astype(jnp.float32)).astype(jnp.bfloat16)
    dn = parts_ref[1] + arrived_ref[1].astype(jnp.float32)
    rms = mean_square(h)
    gain_grad_ref[...] = jnp.sum(dn * h * rms, 1, keepdims=True)
    weighted = dn * gain_ref[...]
    dh = (
        dy_ref[...].astype(jnp.float32)
        + rms * weighted
        - h * (rms * rms * rms * jnp.mean(weighted * h, 0, keepdims=True))
    )
    dh_ref[...] = dh
    da_ref[...] = dh
    spread(ids_ref, da_ref, pieces_ref, q_cols)
    half = pieces_ref.shape[0] // 2
    mixed = product_tn(own_ref[...].reshape(half, 4 * wide), pieces_ref[:half, :])
    mixed += product_tn(other_ref[...].reshape(half, 4 * wide), pieces_ref[half:, :])
    mixed = mixed.astype(jnp.bfloat16)
    for k in range(4):
        do_ref[ids_ref[0] ^ k] = mixed[k * wide : k * wide + block]


def spread(ids_ref, source_ref, target_ref, cols):
    rows = source_ref.shape[1]
    for core_rel in range(2):
        for s in range(4):
            f = column_index(ids_ref, core_rel, s)
            low = (core_rel * 4 + s) * (cols + 8)
            target_ref[low : low + cols + 8, :] = jnp.concatenate(
                [source_ref[start_row(f, cols), :], jnp.zeros((8, rows), jnp.float32)], 0
            ).astype(jnp.bfloat16)


def finish_q_kernel(*refs):
    ids_ref, own, other = refs[0], refs[1:6], refs[6:11]
    n1_ref, att_ref, dq_a_ref, dq_b_ref, pieces_ref, dn_ref = refs[11:17]
    grads = refs[17:25]
    n1_rel, att_rel, d_ref, dq_ref = refs[25:]
    cap = dq_a_ref.shape[1]
    width = dq_a_ref.shape[0]
    q_cols = width // 8
    depth = q_cols + 8
    block = n1_ref.shape[1]
    wide = n1_rel.shape[0] // 4
    d_ref[:, :cap] = dq_a_ref[...].astype(jnp.float32)
    d_ref[:, cap:] = dq_b_ref[...].astype(jnp.float32)
    spread(ids_ref, d_ref, dq_ref, q_cols)
    fill_relative(ids_ref, n1_ref, n1_rel)
    fill_relative(ids_ref, att_ref, att_rel)
    weights = jnp.concatenate(
        [wide_rows(w, s, 0, depth) for w in (own, other) for s in range(4)], 0
    )
    dn = product_tn(weights, dq_ref[...])
    for k in range(4):
        dn_ref[ids_ref[0] ^ k] = dn[k * wide : k * wide + block]
    for core_rel in range(2):
        for s in range(4):
            low = (core_rel * 4 + s) * depth
            gq = product_nt(dq_ref[low : low + depth, :], n1_rel[...]).astype(jnp.bfloat16)
            go = product_nt(pieces_ref[low : low + depth, :], att_rel[...]).astype(jnp.bfloat16)
            for k in range(4):
                target = grads[core_rel * 4 + k]
                target[s, :depth, :] = gq[:, k * wide : (k + 1) * wide]
                target[s, depth:, :] = go[:, k * wide : (k + 1) * wide]


def finish_kv_kernel(*refs):
    ids_ref, own, other = refs[0], refs[1:6], refs[6:11]
    n1_ref, dkv_a_ref, dkv_b_ref, cos_ref, sin_ref, dn_ref, dh_ref, x_ref, gain_ref = refs[11:20]
    tokens_ref, gain_grad_ref = refs[20:22]
    grads = refs[22:30]
    n1_rel, d_ref, dkv_ref = refs[30:]
    width, rows = dh_ref.shape
    cap = rows // 2
    kv_width = KEY_HEADS * HEAD_WIDTH
    q_cols, k_cols = width // 8, kv_width // 8
    half = HEAD_WIDTH // 2
    block = n1_ref.shape[1]
    wide = n1_rel.shape[0] // 4
    cosine, sine = cos_ref[...], sin_ref[...]
    d_ref[:, :cap] = dkv_a_ref[...].T
    d_ref[:, cap:] = dkv_b_ref[...].T
    for head in range(KEY_HEADS):
        base = head * HEAD_WIDTH
        front = d_ref[base : base + half, :]
        back = d_ref[base + half : base + 2 * half, :]
        d_ref[base : base + half, :] = front * cosine + back * sine
        d_ref[base + half : base + 2 * half, :] = back * cosine - front * sine
    for core_rel in range(2):
        for s in range(4):
            f = column_index(ids_ref, core_rel, s)
            low = (core_rel * 4 + s) * 2 * k_cols
            dkv_ref[low : low + 2 * k_cols, :] = jnp.concatenate(
                [
                    d_ref[start_row(f, k_cols), :],
                    d_ref[pl.ds(pl.multiple_of(kv_width + f * k_cols, 8), k_cols), :],
                ],
                0,
            ).astype(jnp.bfloat16)
    fill_relative(ids_ref, n1_ref, n1_rel)
    low = q_cols + 8
    weights = jnp.concatenate(
        [wide_rows(w, s, low, low + 2 * k_cols) for w in (own, other) for s in range(4)], 0
    )
    dn = product_tn(weights, dkv_ref[...])
    for k in range(4):
        i = ids_ref[0] ^ k
        tokens_ref[pl.ds(pl.multiple_of(i * block, 16), block), :] = (
            dn[k * wide : k * wide + block] + dn_ref[i]
        )
    for core_rel in range(2):
        for s in range(4):
            low = (core_rel * 4 + s) * 2 * k_cols
            got = product_nt(dkv_ref[low : low + 2 * k_cols, :], n1_rel[...]).astype(jnp.bfloat16)
            for k in range(4):
                grads[core_rel * 4 + k][s] = got[:, k * wide : (k + 1) * wide]
    x = x_ref[...].astype(jnp.float32)
    rms = mean_square(x)
    dn = tokens_ref[...]
    gain_grad_ref[...] = jnp.sum(dn * x * rms, 1, keepdims=True)
    weighted = dn * gain_ref[...]
    tokens_ref[...] = (
        dh_ref[...]
        + rms * weighted
        - x * (rms * rms * rms * jnp.mean(weighted * x, 0, keepdims=True))
    )


def mlp_kernel(*refs):
    ids_ref, n2_own, n2_other, dy_own, dy_other = refs[:5]
    pieces = refs[5:21]
    keep_ref, send_ref = refs[21:23]
    grads = refs[23:39]
    wgu, wdn, ggu, gdn, gu_ref, prod_ref, dgu_ref, n2_rel, dy_rel, sem_in, sem_out = refs[39:]
    dp_id = ids_ref[0]
    z_id = ids_ref[1]
    block, rows = n2_own.shape[1:]
    pair = 2 * rows
    wide = pieces[0].shape[1]
    half = prod_ref.shape[0] // 4
    loads = []
    for s in range(4):
        for k in range(4):
            piece = pieces[k * 4 + s]
            lanes = pl.ds(k * wide, wide)
            loads.append(
                pltpu.make_async_copy(
                    piece.at[pl.ds(0, 2 * half)],
                    wgu.at[pl.ds(s * 2 * half, 2 * half), lanes],
                    sem_in.at[0, k * 4 + s],
                )
            )
    for k in range(4):
        for s in range(4):
            loads.append(
                pltpu.make_async_copy(
                    pieces[k * 4 + s].at[pl.ds(2 * half, half)],
                    wdn.at[pl.ds(k * half, half), pl.ds(s * wide, wide)],
                    sem_in.at[1, k * 4 + s],
                )
            )
    for load in loads:
        load.start()
    pad = jnp.zeros((wide - block, pair), jnp.bfloat16)
    for j in range(4):
        i = dp_id ^ j
        zz = lax.rem(z_id - j + 4, 4)
        n2_rel[j * wide : j * wide + block, :] = jnp.concatenate([n2_own[i], n2_other[i]], 1)
        dy_rel[j * wide : j * wide + block, :] = jnp.concatenate([dy_own[zz], dy_other[zz]], 1)
        n2_rel[j * wide + block : (j + 1) * wide, :] = pad
        dy_rel[j * wide + block : (j + 1) * wide, :] = pad
    for load in loads[:16]:
        load.wait()

    def rows_of(index, size):
        return pl.ds(pl.multiple_of(index * size, 16), size)

    def forward(s, carry):
        m = lax.rem(z_id - s + 4, 4)
        k = m ^ dp_id
        total = product_nn(wgu[rows_of(s, 2 * half), :], n2_rel[...])
        gu_ref[rows_of(k, 2 * half), :] = total
        gate = total[:half]
        prod_ref[rows_of(k, half), :] = (gate * jax.nn.sigmoid(gate) * total[half:]).astype(
            jnp.bfloat16
        )
        return carry

    lax.fori_loop(0, 4, forward, 0)
    for load in loads[16:]:
        load.wait()

    def middle(k, carry):
        s = lax.rem(z_id - (dp_id ^ k) + 4, 4)
        dprod = product_nn(wdn[rows_of(k, half), :], dy_rel[...])
        gdn[rows_of(k, half), :] = product_nt(prod_ref[rows_of(k, half), :], dy_rel[...]).astype(
            jnp.bfloat16
        )
        total = gu_ref[rows_of(k, 2 * half), :]
        gate, up = total[:half], total[half:]
        sig = jax.nn.sigmoid(gate)
        dgu_ref[rows_of(s, 2 * half), :] = jnp.concatenate(
            [dprod * up * sig * (1.0 + gate * (1.0 - sig)), dprod * gate * sig], 0
        ).astype(jnp.bfloat16)
        return carry

    lax.fori_loop(0, 4, middle, 0)

    def backward(s, carry):
        ggu[rows_of(s, 2 * half), :] = product_nt(
            dgu_ref[rows_of(s, 2 * half), :], n2_rel[...]
        ).astype(jnp.bfloat16)
        return carry

    stores = []
    for k in range(4):
        for s in range(4):
            stores.append(
                pltpu.make_async_copy(
                    gdn.at[pl.ds(k * half, half), pl.ds(s * wide, wide)],
                    grads[k * 4 + s].at[pl.ds(2 * half, half)],
                    sem_out.at[1, k * 4 + s],
                )
            )
    for store in stores:
        store.start()
    lax.fori_loop(0, 4, backward, 0)
    late = []
    for k in range(4):
        for s in range(4):
            late.append(
                pltpu.make_async_copy(
                    ggu.at[pl.ds(s * 2 * half, 2 * half), pl.ds(k * wide, wide)],
                    grads[k * 4 + s].at[pl.ds(0, 2 * half)],
                    sem_out.at[0, k * 4 + s],
                )
            )
    for store in late:
        store.start()
    for j in range(4):
        lanes = slice(j * wide, (j + 1) * wide)
        out = product_tn(wdn[:, lanes], prod_ref[...])[:block]
        zz = rows_of(lax.rem(z_id - j + 4, 4), block)
        keep_ref[0, zz, :] = out[:, :rows]
        send_ref[0, zz, :] = out[:, rows:].astype(jnp.bfloat16)
        dn = product_tn(wgu[:, lanes], dgu_ref[...])[:block]
        i = rows_of(dp_id ^ j, block)
        keep_ref[1, i, :] = dn[:, :rows]
        send_ref[1, i, :] = dn[:, rows:].astype(jnp.bfloat16)
    for store in stores + late:
        store.wait()


def mean_square(values):
    return lax.rsqrt(jnp.mean(values * values, 0, keepdims=True) + EPSILON)


def fast(
    tokens, cotangent, counts, w_query, key_weight, value_weight, w_out, w_gate, w_up, w_down, gains
):
    dp_id = lax.axis_index("dp")
    slot = lax.axis_index("fsdp")
    z_id = slot // 2
    core_id = slot % 2
    ids = jnp.stack([dp_id, z_id, core_id, slot]).astype(jnp.int32)
    batches, cap, width = tokens.shape
    rows = batches * cap
    block = w_query.shape[0]
    wide = -(-block // 128) * 128
    q_cols, k_cols = w_query.shape[1], key_weight.shape[1]
    half = w_gate.shape[1]
    kv_width = KEY_HEADS * HEAD_WIDTH
    share = QUERY_HEADS // KEY_HEADS
    q_rows = q_cols + 8
    depth = q_rows + 2 * k_cols
    mlp_rows = 3 * half + q_rows

    (first_piece,) = run(
        pack_first_kernel,
        "pack_first",
        (counts, w_query, key_weight, value_weight, gains),
        [SMEM] + [VMEM] * 4,
        [struct((depth, wide))],
        [VMEM],
        [],
        0,
        16,
    )
    chain = [first_piece]
    for _ in range(3):
        chain.append(shift_z(chain[-1], 1))
    down_halves = w_down.reshape(2, half, -1)
    other_down = swap_core(
        lax.dynamic_index_in_dim(down_halves, 1 - core_id, 0, keepdims=False)
    )
    (mlp_piece,) = run(
        pack_mlp_kernel,
        "pack_mlp",
        (ids, w_gate, w_up, w_down, other_down, w_out),
        [SMEM] + [VMEM] * 5,
        [struct((mlp_rows, wide))],
        [VMEM],
        [],
        0,
        16,
    )
    x, dy = run(
        turn_in_kernel,
        "turn_in",
        (tokens.reshape(rows, width), cotangent.reshape(rows, width)),
        [VMEM] * 2,
        [struct((width, rows))] * 2,
        [VMEM] * 2,
        [],
        0,
        16,
    )
    dy_other = swap_core(dy)

    along = jnp.stack(chain, 0)
    extras = along[:, q_cols : q_cols + 2, :block]
    other_extras = swap_core(extras)
    from_x = swap_dp(along, 1)
    from_y = swap_dp(along, 2)
    first_own = [along, from_x, from_y, swap_dp(from_x[:2], 2), swap_dp(from_y[2:], 1)]
    first_other = [swap_core(piece) for piece in first_own]

    def spread_square(piece):
        return swap_dp(piece, 1), swap_dp(piece, 2)

    mlp_chain = [mlp_piece, shift_z(after(mlp_piece, along), 1)]
    for _ in range(2):
        mlp_chain.append(shift_z(mlp_chain[-1], 1))
    by_square = [spread_square(mlp_piece)]
    by_square.append(spread_square(after(mlp_chain[1], first_own[3], first_own[4])))

    by_core = jnp.where(
        core_id == 0, jnp.stack([extras, other_extras], 1), jnp.stack([other_extras, extras], 1)
    )
    by_core = by_core[::-1]
    by_core = lax.dynamic_slice_in_dim(jnp.concatenate([by_core, by_core], 0), 3 - z_id, 4, 0)
    gain = by_core[:, :, 0, :].reshape(8, 2, q_cols).transpose(0, 2, 1).reshape(width, 2)
    gain = gain.astype(jnp.float32)
    gain_one, gain_two = gain[:, :1], gain[:, 1:]
    group_counts = by_core[:, :, 1, :batches].reshape(8, batches).astype(jnp.int32)
    flat_counts = group_counts.T.reshape(-1)
    before = jnp.sum(
        jnp.where(jnp.arange(8, dtype=jnp.int32)[:, None] < slot, group_counts, 0), 0
    )
    position = (before[:, None] + jnp.arange(cap, dtype=jnp.int32)[None, :]).reshape(-1)
    cosine, sine = rope_tables(position, HEAD_WIDTH)
    cosine, sine = cosine[:, 0, :].T, sine[:, 0, :].T
    x_wide = x.astype(jnp.float32)
    n1 = (x_wide * mean_square(x_wide) * gain_one).astype(jnp.bfloat16).reshape(4, block, rows)

    query, kv = run(
        project_kernel,
        "project",
        (ids, *first_own, *first_other, n1, cosine, sine),
        [SMEM] + [VMEM] * 13,
        (struct((QUERY_HEADS, HEAD_WIDTH, rows)), struct((rows, 2 * kv_width))),
        [VMEM] * 2,
        [
            pltpu.VMEM((width + 2 * kv_width, rows), jnp.float32),
            pltpu.VMEM((2 * kv_width, rows), jnp.float32),
            pltpu.VMEM((4 * wide, rows), jnp.bfloat16),
        ],
        2 * (width + 2 * kv_width) * width * rows,
        24,
    )
    kv_own, kv_other = [kv], [swap_core(kv)]
    for _ in range(3):
        kv_own.append(shift_z_up(kv_own[-1], 1))
        kv_other.append(swap_core(kv_own[-1]))

    by_square.append(spread_square(after(mlp_chain[2], kv)))
    far_zero = swap_dp(after(by_square[0][0], kv), 2)
    far_one = swap_dp(after(by_square[1][1], kv), 1)
    by_square.append(spread_square(after(mlp_chain[3], kv_own[1])))
    far_two = swap_dp(after(by_square[2][0], kv_own[2]), 2)
    far_three = swap_dp(after(by_square[3][1], kv_own[3]), 1)
    pieces = mlp_chain + [p[0] for p in by_square] + [p[1] for p in by_square]
    pieces += [far_zero, far_one, far_two, far_three]

    pair_flops = 2 * QUERY_HEADS * HEAD_WIDTH * rows * 8 * cap
    head_scratch = [
        pltpu.VMEM((KEY_HEADS, 8 * cap, HEAD_WIDTH), jnp.bfloat16),
        pltpu.VMEM((KEY_HEADS, 8 * cap, HEAD_WIDTH), jnp.bfloat16),
        pltpu.VMEM((8 * cap, share * cap), jnp.float32),
    ]
    attended, lse = run(
        attend_kernel,
        "attend",
        (ids, flat_counts, query, *kv_own, *kv_other),
        [SMEM, SMEM] + [VMEM] * 9,
        (
            struct((QUERY_HEADS, HEAD_WIDTH, rows)),
            struct((2 * KEY_HEADS, 1, share * cap), jnp.float32),
        ),
        [VMEM] * 2,
        head_scratch,
        8 * pair_flops,
        28,
    )
    attended = attended.reshape(4, block, rows)
    (out_own,) = run(
        collect_kernel,
        "collect",
        tuple(pieces),
        [ANY] * 16,
        [struct((4, q_rows, 4 * wide))],
        [VMEM],
        [pltpu.SemaphoreType.DMA((16,))],
        0,
        8,
    )
    out_other = swap_core(out_own)
    h, n2 = run(
        hidden_kernel,
        "hidden",
        (ids, out_own, out_other, attended, x, gain_two),
        [SMEM] + [VMEM] * 5,
        (struct((width, rows), jnp.float32), struct((width, rows))),
        [VMEM] * 2,
        [pltpu.VMEM((4 * wide, rows), jnp.bfloat16)],
        2 * width * width * rows,
        24,
    )
    n2_other = swap_core(n2)
    blocks = (4, block, rows)
    results = run(
        mlp_kernel,
        "mlp",
        (
            ids,
            n2.reshape(blocks),
            n2_other.reshape(blocks),
            dy.reshape(blocks),
            dy_other.reshape(blocks),
            *pieces,
        ),
        [SMEM] + [VMEM] * 4 + [ANY] * 16,
        [struct((2, width, rows), jnp.float32), struct((2, width, rows))]
        + [struct((3 * half, wide))] * 16,
        [VMEM] * 2 + [ANY] * 16,
        [
            pltpu.VMEM((8 * half, 4 * wide), jnp.bfloat16),
            pltpu.VMEM((4 * half, 4 * wide), jnp.bfloat16),
            pltpu.VMEM((8 * half, 4 * wide), jnp.bfloat16),
            pltpu.VMEM((4 * half, 4 * wide), jnp.bfloat16),
            pltpu.VMEM((8 * half, 2 * rows), jnp.float32),
            pltpu.VMEM((4 * half, 2 * rows), jnp.bfloat16),
            pltpu.VMEM((8 * half, 2 * rows), jnp.bfloat16),
            pltpu.VMEM((4 * wide, 2 * rows), jnp.bfloat16),
            pltpu.VMEM((4 * wide, 2 * rows), jnp.bfloat16),
            pltpu.SemaphoreType.DMA((2, 16)),
            pltpu.SemaphoreType.DMA((2, 16)),
        ],
        18 * 16 * half * block * 2 * rows,
        56,
    )
    keep, send, grads = results[0], results[1], results[2:]
    arrived = swap_core(send)
    home, to_x, to_y, far = grads[:4], grads[4:8], grads[8:12], grads[12:]

    def first_leg(group, *deps):
        a, b = 2 * group, 2 * group + 1
        return (
            swap_dp(after(far[a], *deps), 2),
            swap_dp(after(far[b], *deps), 1),
            swap_dp(after(to_x[b], *deps), 1),
            swap_dp(after(to_y[a], *deps), 2),
        )

    def second_leg(group, legs, *deps):
        a, b = 2 * group, 2 * group + 1
        via_y, via_x = after(legs[0], *deps), after(legs[1], *deps)
        x_a = swap_dp(add_low(to_x[a], via_y), 1)
        y_b = swap_dp(add_low(to_y[b], via_x), 2)
        return x_a, y_b

    legs_one = first_leg(1)
    output, dh, mixed_gradient, gain_two_grad, da_pieces = run(
        turn_point_kernel,
        "turn_point",
        (ids, keep, arrived, h, dy, gain_two, out_own, out_other),
        [SMEM] + [VMEM] * 7,
        (
            struct((width, rows)),
            struct((width, rows), jnp.float32),
            struct(blocks),
            struct((width, 1), jnp.float32),
            struct((8 * q_rows, rows)),
        ),
        [VMEM] * 5,
        [pltpu.VMEM((width, rows), jnp.float32)],
        2 * width * width * rows,
        24,
    )
    output = output.T.reshape(batches, cap, width)
    legs_zero = first_leg(0, mixed_gradient)
    turned_one = second_leg(1, legs_one, mixed_gradient)

    def attend_back(mb):
        return run(
            functools.partial(attend_back_kernel, mb),
            "attend_back",
            (
                ids,
                flat_counts,
                query,
                mixed_gradient.reshape(QUERY_HEADS, HEAD_WIDTH, rows),
                *kv_own,
                *kv_other,
                lse,
                cosine,
                sine,
            ),
            [SMEM, SMEM] + [VMEM] * 13,
            [struct((QUERY_HEADS, HEAD_WIDTH, cap))] + [struct((cap, 2 * kv_width))] * 8,
            [VMEM] * 9,
            head_scratch
            + [
                pltpu.VMEM((KEY_HEADS, 8 * cap, HEAD_WIDTH), jnp.bfloat16),
                pltpu.VMEM((KEY_HEADS, 8 * cap, HEAD_WIDTH), jnp.bfloat16),
            ],
            10 * pair_flops,
            28,
        )

    def reduce_kv(own, other):
        summed = [add_low(own[s], swap_core(other[s])) for s in (3, 2, 1, 0)][::-1]
        total = summed[0].astype(jnp.float32)
        for s in (3, 2, 1):
            total = total + shift_z_down(summed[s], s).astype(jnp.float32)
        return total

    back_a = attend_back(0)
    dkv_a = reduce_kv(back_a[1:5], back_a[5:9])
    summed_three = add_low(home[3], legs_one[2], after(turned_one[1], back_a[0]))
    summed_two = add_low(home[2], turned_one[0], legs_one[3])
    turned_zero = second_leg(0, legs_zero, back_a[0])
    hop = shift_z(summed_three, -1)
    back_b = attend_back(1)
    dkv_b = reduce_kv(back_b[1:5], back_b[5:9])
    hop = shift_z(add_low(summed_two, after(hop, back_b[0])), -1)
    summed_one = add_low(home[1], legs_zero[2], after(turned_zero[1], back_b[0]))
    hop = shift_z(add_low(summed_one, hop), -1)
    mlp_total = (
        home[0].astype(jnp.float32)
        + turned_zero[0].astype(jnp.float32)
        + legs_zero[3].astype(jnp.float32)
        + hop.astype(jnp.float32)
    )
    grad_gate = mlp_total[:half, :block].T
    grad_up = mlp_total[half : 2 * half, :block].T
    down_total = mlp_total[2 * half :, :block]
    left, right = down_total[:, :q_cols], down_total[:, q_cols:]
    stay = jnp.where(core_id == 0, left, right)
    give = jnp.where(core_id == 0, right, left).astype(jnp.bfloat16)
    taken = swap_core(give).astype(jnp.float32)
    grad_down = jnp.where(
        core_id == 0, jnp.concatenate([stay, taken], 0), jnp.concatenate([taken, stay], 0)
    )

    def reduce_all(parts):
        mine = [add_low(parts[k], swap_core(parts[4 + k])) for k in range(4)]
        summed = [mine[0]] + [swap_dp(mine[k], k) for k in (1, 2, 3)]
        out = [add_low(*[piece[s] for piece in summed]) for s in range(4)]
        total = out[0].astype(jnp.float32)
        for s in (1, 2, 3):
            total = total + shift_z(out[s], -s).astype(jnp.float32)
        return total

    q_results = run(
        finish_q_kernel,
        "finish_q",
        (
            ids,
            *first_own,
            *first_other,
            n1,
            attended,
            back_a[0].reshape(width, cap),
            back_b[0].reshape(width, cap),
            da_pieces,
        ),
        [SMEM] + [VMEM] * 15,
        [struct(blocks, jnp.float32)] + [struct((4, 2 * q_rows, wide))] * 8,
        [VMEM] * 9,
        [
            pltpu.VMEM((4 * wide, rows), jnp.bfloat16),
            pltpu.VMEM((4 * wide, rows), jnp.bfloat16),
            pltpu.VMEM((width, rows), jnp.float32),
            pltpu.VMEM((8 * q_rows, rows), jnp.bfloat16),
        ],
        6 * width * width * rows,
        32,
    )
    dn_q = q_results[0]
    q_out_total = reduce_all(q_results[1:])
    grad_query = q_out_total[:q_cols, :block].T
    grad_out = q_out_total[q_rows : q_rows + q_cols, :block].T

    kv_results = run(
        finish_kv_kernel,
        "finish_kv",
        (
            ids,
            *first_own,
            *first_other,
            n1,
            dkv_a,
            dkv_b,
            cosine,
            sine,
            dn_q,
            dh,
            x,
            gain_one,
        ),
        [SMEM] + [VMEM] * 19,
        [struct((width, rows), jnp.float32), struct((width, 1), jnp.float32)]
        + [struct((4, 2 * k_cols, wide))] * 8,
        [VMEM] * 10,
        [
            pltpu.VMEM((4 * wide, rows), jnp.bfloat16),
            pltpu.VMEM((2 * kv_width, rows), jnp.float32),
            pltpu.VMEM((16 * k_cols, rows), jnp.bfloat16),
        ],
        8 * kv_width * width * rows,
        32,
    )
    grad_tokens = kv_results[0].T.reshape(batches, cap, width)
    kv_total = reduce_all(kv_results[2:])
    gain_total = jnp.concatenate([kv_results[1], gain_two_grad], 1).T
    gain_total = gain_total + swap_core(gain_total)
    gain_total = (gain_total + swap_dp(gain_total, 1)) + (
        swap_dp(gain_total, 2) + swap_dp(gain_total, 3)
    )
    gain_total = (gain_total + shift_z(gain_total, 2)) + (
        shift_z(gain_total, 1) + shift_z(gain_total, -1)
    )
    gain_grad = lax.dynamic_slice_in_dim(gain_total, slot * q_cols, q_cols, 1)
    return (
        output,
        grad_tokens,
        grad_query,
        kv_total[:k_cols, :block].T,
        kv_total[k_cols:, :block].T,
        grad_out,
        grad_gate,
        grad_up,
        grad_down,
        gain_grad,
    )


def solution(mesh):
    in_specs = (
        P(None, ("dp", "fsdp"), None),
        P(None, ("dp", "fsdp"), None),
        P(None, ("dp", "fsdp")),
        P("dp", "fsdp"),
        P("dp", "fsdp"),
        P("dp", "fsdp"),
        P("dp", "fsdp"),
        P("dp", "fsdp"),
        P("dp", "fsdp"),
        P("dp", "fsdp"),
        P(None, "fsdp"),
    )
    out_specs = (
        P(None, ("dp", "fsdp"), None),
        P(None, ("dp", "fsdp"), None),
        P("dp", "fsdp"),
        P("dp", "fsdp"),
        P("dp", "fsdp"),
        P("dp", "fsdp"),
        P("dp", "fsdp"),
        P("dp", "fsdp"),
        P("dp", "fsdp"),
        P(None, "fsdp"),
    )
    square = mesh.shape["dp"] == 4 and mesh.shape["fsdp"] == 8
    return jax.shard_map(
        fast if square else local, mesh=mesh, in_specs=in_specs, out_specs=out_specs, check_vma=False)
```

```python
import functools

import jax
import jax.numpy as jnp
from jax import lax
from jax.experimental import pallas as pl
from jax.experimental.pallas import tpu as pltpu
from jax.sharding import PartitionSpec as P

MODEL_WIDTH = 960
QUERY_HEADS = 15
KEY_HEADS = 5
HEAD_WIDTH = 64


EPSILON = 1e-05
ROPE_BASE = 100000.0
SCORE_SCALE = 0.125


def rope_tables(position, head_size):
    half_size = head_size // 2
    frequency = ROPE_BASE ** (-(jnp.arange(half_size, dtype=jnp.float32) * 2.0) / head_size)
    angles = position.astype(jnp.float32)[:, None] * frequency[None, :]
    return (jnp.cos(angles)[:, None, :], jnp.sin(angles)[:, None, :])


def apply_rotation(values, cosine_table, sine_values):
    half_size = values.shape[-1] // 2
    front_half = values[..., :half_size]
    back_half = values[..., half_size:]
    return jnp.concatenate(
        [
            front_half * cosine_table - back_half * sine_values,
            back_half * cosine_table + front_half * sine_values,
        ],
        -1,
    )


def normalize(values, gain_row):
    inv_rms = lax.rsqrt(jnp.mean(values * values, -1, keepdims=True) + EPSILON)
    return (values * inv_rms * gain_row, inv_rms)


def norm_back(values, inv_rms, gain_row, incoming):
    weighted = incoming * gain_row
    return inv_rms * weighted - values * inv_rms * inv_rms * inv_rms * jnp.mean(
        weighted * values, -1, keepdims=True
    )


def build_mask(count_row, device, slot_capacity):
    group_width = count_row.shape[0]
    local_slot = jnp.arange(slot_capacity, dtype=jnp.int32)
    offsets = jnp.cumsum(count_row) - count_row
    is_mine = jnp.arange(group_width, dtype=jnp.int32) == device
    own_offset = jnp.sum(jnp.where(is_mine, offsets, 0))
    own_count = jnp.sum(jnp.where(is_mine, count_row, 0))
    query_pos = own_offset + local_slot
    query_valid = local_slot < own_count
    key_pos = (offsets[:, None] + local_slot[None, :]).reshape(-1)
    key_valid = (local_slot[None, :] < count_row[:, None]).reshape(-1)
    slot_ids = jnp.arange(group_width * slot_capacity, dtype=jnp.int32)
    own_slots = device * slot_capacity + local_slot
    allowed = query_valid[:, None] & key_valid[None, :] & (
        key_pos[None, :] <= query_pos[:, None]
    ) | (slot_ids[None, :] == own_slots[:, None])
    return (allowed, query_pos)


def kept_fetch(w_query, key_weight, value_weight, w_out, w_gate, w_up, w_down, gains):
    columns = (
        lax.all_gather(w_query, "fsdp", axis=1, tiled=True),
        lax.all_gather(key_weight, "fsdp", axis=1, tiled=True),
        lax.all_gather(value_weight, "fsdp", axis=1, tiled=True),
        lax.all_gather(w_out, "fsdp", axis=1, tiled=True),
        lax.all_gather(w_gate, "fsdp", axis=1, tiled=True),
        lax.all_gather(w_up, "fsdp", axis=1, tiled=True),
        lax.all_gather(w_down, "fsdp", axis=1, tiled=True),
        lax.all_gather(gains, "fsdp", axis=1, tiled=True),
    )
    matrices = (
        lax.all_gather(columns[0], "dp", axis=0, tiled=True),
        lax.all_gather(columns[1], "dp", axis=0, tiled=True),
        lax.all_gather(columns[2], "dp", axis=0, tiled=True),
        lax.all_gather(columns[3], "dp", axis=0, tiled=True),
        lax.all_gather(columns[4], "dp", axis=0, tiled=True),
        lax.all_gather(columns[5], "dp", axis=0, tiled=True),
        lax.all_gather(columns[6], "dp", axis=0, tiled=True),
    )
    return (matrices, columns[7].astype(jnp.float32))


def times_transpose(left, right):
    return jnp.einsum("rk,jk->rj", left, right, preferred_element_type=jnp.float32)


def rows_product(left, right):
    return jnp.einsum("rd,rk->dk", left, right, preferred_element_type=jnp.float32)


def local(
    tokens, cotangent, counts, w_query, key_weight, value_weight, w_out, w_gate, w_up, w_down, gains
):
    group_counts = lax.all_gather(counts, "fsdp", axis=1, tiled=True)
    device = lax.axis_index("fsdp")
    slot_capacity = tokens.shape[1]
    key_value_width = KEY_HEADS * HEAD_WIDTH
    device_share = QUERY_HEADS // KEY_HEADS
    kept_weights, kept_gain = kept_fetch(
        w_query, key_weight, value_weight, w_out, w_gate, w_up, w_down, gains
    )
    outputs = []
    grad_inputs = []
    saved = [[] for index_unused in range(11)]
    gain_one_total = jnp.zeros((MODEL_WIDTH,), jnp.float32)
    gain_two_total = jnp.zeros((MODEL_WIDTH,), jnp.float32)
    for micro_idx in range(tokens.shape[0]):
        matrices, gain_pair = (kept_weights, kept_gain)
        full_query, full_key, full_value, full_out, full_gate, full_up, full_down = matrices
        inputs = tokens[micro_idx].astype(jnp.float32)
        allowed, query_pos = build_mask(group_counts[micro_idx], device, slot_capacity)
        cosine_table, sine_values = rope_tables(query_pos, HEAD_WIDTH)
        first_normed, scale_one = normalize(inputs, gain_pair[0])
        normed_low = first_normed.astype(jnp.bfloat16)
        reduced_query = apply_rotation(
            jnp.dot(normed_low, full_query, preferred_element_type=jnp.float32).reshape(
                slot_capacity, QUERY_HEADS, HEAD_WIDTH
            ),
            cosine_table,
            sine_values,
        ).astype(jnp.bfloat16)
        key_low = (
            apply_rotation(
                jnp.dot(normed_low, full_key, preferred_element_type=jnp.float32).reshape(
                    slot_capacity, KEY_HEADS, HEAD_WIDTH
                ),
                cosine_table,
                sine_values,
            )
            .astype(jnp.bfloat16)
            .reshape(slot_capacity, key_value_width)
        )
        value_low = jnp.dot(normed_low, full_value, preferred_element_type=jnp.float32).astype(
            jnp.bfloat16
        )
        grouped_keys, grouped_values = (
            lax.all_gather(key_low, "fsdp", axis=0, tiled=True),
            lax.all_gather(value_low, "fsdp", axis=0, tiled=True),
        )
        heads_of_key = grouped_keys.reshape(-1, KEY_HEADS, HEAD_WIDTH)
        heads_of_value = grouped_values.reshape(-1, KEY_HEADS, HEAD_WIDTH)
        heads_of_query = reduced_query.reshape(slot_capacity, KEY_HEADS, device_share, HEAD_WIDTH)
        scores = (
            jnp.einsum(
                "qngd,knd->ngqk", heads_of_query, heads_of_key, preferred_element_type=jnp.float32
            )
            * SCORE_SCALE
        )
        masked = jnp.where(allowed, scores, -1e30)
        row_top = jnp.max(masked, -1, keepdims=True)
        exponent = jnp.where(allowed, jnp.exp(masked - row_top), 0.0)
        row_total = jnp.sum(exponent, -1, keepdims=True)
        prob_low = (exponent / row_total).astype(jnp.bfloat16)
        log_total = row_top + jnp.log(row_total)
        mixed_heads = jnp.einsum(
            "ngqk,knd->qngd", prob_low, heads_of_value, preferred_element_type=jnp.float32
        ).reshape(slot_capacity, MODEL_WIDTH)
        attended = mixed_heads.astype(jnp.bfloat16)
        hidden_state = inputs + jnp.dot(attended, full_out, preferred_element_type=jnp.float32)
        normed_two, scale_two = normalize(hidden_state, gain_pair[1])
        normed_two_low = normed_two.astype(jnp.bfloat16)
        gate_act = jnp.dot(normed_two_low, full_gate, preferred_element_type=jnp.float32)
        upward = jnp.dot(normed_two_low, full_up, preferred_element_type=jnp.float32)
        sigmoid_gate = jax.nn.sigmoid(gate_act)
        product = (gate_act * sigmoid_gate * upward).astype(jnp.bfloat16)
        outputs.append(
            (hidden_state + jnp.dot(product, full_down, preferred_element_type=jnp.float32)).astype(
                jnp.bfloat16
            )
        )
        matrices, gain_pair = (kept_weights, kept_gain)
        full_query, full_key, full_value, full_out, full_gate, full_up, full_down = matrices
        grad_low = cotangent[micro_idx]
        grad_product = times_transpose(grad_low, full_down)
        grad_gate = (
            grad_product * upward * sigmoid_gate * (1.0 + gate_act * (1.0 - sigmoid_gate))
        ).astype(jnp.bfloat16)
        grad_upward = (grad_product * gate_act * sigmoid_gate).astype(jnp.bfloat16)
        grad_normed_two = times_transpose(grad_gate, full_gate) + times_transpose(
            grad_upward, full_up
        )
        gain_two_total = gain_two_total + jnp.sum(grad_normed_two * hidden_state * scale_two, 0)
        grad_hidden = grad_low.astype(jnp.float32) + norm_back(
            hidden_state, scale_two, gain_pair[1], grad_normed_two
        )
        grad_branch = grad_hidden.astype(jnp.bfloat16)
        mixed_gradient = times_transpose(grad_branch, full_out).astype(jnp.bfloat16)
        head_gradient = mixed_gradient.reshape(slot_capacity, KEY_HEADS, device_share, HEAD_WIDTH)
        again_scores = (
            jnp.einsum(
                "qngd,knd->ngqk", heads_of_query, heads_of_key, preferred_element_type=jnp.float32
            )
            * SCORE_SCALE
        )
        probability = jnp.where(allowed, jnp.exp(again_scores - log_total), 0.0)
        grad_prob = jnp.einsum(
            "qngd,knd->ngqk", head_gradient, heads_of_value, preferred_element_type=jnp.float32
        )
        row_delta = jnp.sum(probability * grad_prob, -1, keepdims=True)
        grad_scores = (probability * (grad_prob - row_delta)).astype(jnp.bfloat16)
        grad_query_rot = (
            jnp.einsum(
                "ngqk,knd->qngd", grad_scores, heads_of_key, preferred_element_type=jnp.float32
            ).reshape(slot_capacity, QUERY_HEADS, HEAD_WIDTH)
            * SCORE_SCALE
        )
        key_part = (
            jnp.einsum(
                "ngqk,qngd->knd", grad_scores, heads_of_query, preferred_element_type=jnp.float32
            ).reshape(-1, key_value_width)
            * SCORE_SCALE
        )
        value_part = jnp.einsum(
            "ngqk,qngd->knd",
            probability.astype(jnp.bfloat16),
            head_gradient,
            preferred_element_type=jnp.float32,
        ).reshape(-1, key_value_width)
        key_gradient, value_grad = (
            lax.psum_scatter(
                key_part.astype(jnp.bfloat16), "fsdp", scatter_dimension=0, tiled=True
            ).astype(jnp.float32),
            lax.psum_scatter(
                value_part.astype(jnp.bfloat16), "fsdp", scatter_dimension=0, tiled=True
            ).astype(jnp.float32),
        )
        grad_query = (
            apply_rotation(grad_query_rot, cosine_table, -sine_values)
            .astype(jnp.bfloat16)
            .reshape(slot_capacity, MODEL_WIDTH)
        )
        grad_key = (
            apply_rotation(
                key_gradient.reshape(slot_capacity, KEY_HEADS, HEAD_WIDTH),
                cosine_table,
                -sine_values,
            )
            .astype(jnp.bfloat16)
            .reshape(slot_capacity, key_value_width)
        )
        grad_value = value_grad.astype(jnp.bfloat16)
        grad_normed_one = (
            times_transpose(grad_query, full_query)
            + times_transpose(grad_key, full_key)
            + times_transpose(grad_value, full_value)
        )
        gain_one_total = gain_one_total + jnp.sum(grad_normed_one * inputs * scale_one, 0)
        grad_inputs.append(
            grad_hidden + norm_back(inputs, scale_one, gain_pair[0], grad_normed_one)
        )
        kept_rows = (
            normed_low,
            grad_query,
            grad_key,
            grad_value,
            attended,
            grad_branch,
            normed_two_low,
            grad_gate,
            grad_upward,
            product,
            grad_low,
        )
        for slot_index in range(11):
            saved[slot_index].append(kept_rows[slot_index])
    joined = [jnp.concatenate(column_list, 0) for column_list in saved]
    gain_terms = jnp.stack([gain_one_total, gain_two_total], 0)
    slices = (
        lax.all_to_all(joined[1], "fsdp", split_axis=1, concat_axis=0, tiled=True),
        lax.all_to_all(joined[2], "fsdp", split_axis=1, concat_axis=0, tiled=True),
        lax.all_to_all(joined[3], "fsdp", split_axis=1, concat_axis=0, tiled=True),
        lax.all_to_all(joined[5], "fsdp", split_axis=1, concat_axis=0, tiled=True),
        lax.all_to_all(joined[7], "fsdp", split_axis=1, concat_axis=0, tiled=True),
        lax.all_to_all(joined[8], "fsdp", split_axis=1, concat_axis=0, tiled=True),
        lax.all_to_all(joined[10], "fsdp", split_axis=1, concat_axis=0, tiled=True),
    )
    pieces = (
        lax.all_gather(joined[0], "fsdp", axis=0, tiled=True),
        lax.all_gather(joined[4], "fsdp", axis=0, tiled=True),
        lax.all_gather(joined[6], "fsdp", axis=0, tiled=True),
        lax.all_gather(joined[9], "fsdp", axis=0, tiled=True),
    )
    picked = [member for member in slices]
    gain_part = lax.psum_scatter(gain_terms, "fsdp", scatter_dimension=1, tiled=True)
    summed_rows = (
        lax.psum_scatter(
            rows_product(pieces[0], picked[0]).astype(jnp.bfloat16),
            "dp",
            scatter_dimension=0,
            tiled=True,
        ).astype(jnp.float32),
        lax.psum_scatter(
            rows_product(pieces[0], picked[1]).astype(jnp.bfloat16),
            "dp",
            scatter_dimension=0,
            tiled=True,
        ).astype(jnp.float32),
        lax.psum_scatter(
            rows_product(pieces[0], picked[2]).astype(jnp.bfloat16),
            "dp",
            scatter_dimension=0,
            tiled=True,
        ).astype(jnp.float32),
        lax.psum_scatter(
            rows_product(pieces[1], picked[3]).astype(jnp.bfloat16),
            "dp",
            scatter_dimension=0,
            tiled=True,
        ).astype(jnp.float32),
        lax.psum_scatter(
            rows_product(pieces[2], picked[4]).astype(jnp.bfloat16),
            "dp",
            scatter_dimension=0,
            tiled=True,
        ).astype(jnp.float32),
        lax.psum_scatter(
            rows_product(pieces[2], picked[5]).astype(jnp.bfloat16),
            "dp",
            scatter_dimension=0,
            tiled=True,
        ).astype(jnp.float32),
        lax.psum_scatter(
            rows_product(pieces[3], picked[6]).astype(jnp.bfloat16),
            "dp",
            scatter_dimension=0,
            tiled=True,
        ).astype(jnp.float32),
    )
    gain_grad = lax.psum(gain_part, "dp")
    return (
        jnp.stack(outputs, 0),
        jnp.stack(grad_inputs, 0),
        summed_rows[0],
        summed_rows[1],
        summed_rows[2],
        summed_rows[3],
        summed_rows[4],
        summed_rows[5],
        summed_rows[6],
        gain_grad,
    )


def swap_core(value):
    return lax.ppermute(value, "fsdp", [(j, j ^ 1) for j in range(8)])


def swap_dp(value, mask):
    return lax.ppermute(value, "dp", [(j, j ^ mask) for j in range(4)])


def shift_z(value, step):
    return lax.ppermute(value, "fsdp", [(j, (j + 2 * step) % 8) for j in range(8)])


def shift_z_up(value, step):
    return lax.ppermute(value, "fsdp", [(j, j + 2 * step) for j in range(8) if j + 2 * step < 8])


def shift_z_down(value, step):
    return lax.ppermute(value, "fsdp", [(j, j - 2 * step) for j in range(8) if j - 2 * step >= 0])


def add_low(*terms):
    total = terms[0].astype(jnp.float32)
    for term in terms[1:]:
        total = total + term.astype(jnp.float32)
    return total.astype(jnp.bfloat16)


def product_nn(left, right):
    return lax.dot_general(
        left, right, (((1,), (0,)), ((), ())), preferred_element_type=jnp.float32
    )


def product_nt(left, right):
    return lax.dot_general(
        left, right, (((1,), (1,)), ((), ())), preferred_element_type=jnp.float32
    )


def product_tn(left, right):
    return lax.dot_general(
        left, right, (((0,), (0,)), ((), ())), preferred_element_type=jnp.float32
    )


VMEM = pl.BlockSpec(memory_space=pltpu.VMEM)
SMEM = pl.BlockSpec(memory_space=pltpu.SMEM)
ANY = pl.BlockSpec(memory_space=pl.ANY)


def run(body, name, ins, in_specs, outs, out_specs, scratch, flops, megabytes):
    moved = sum(v.size * v.dtype.itemsize for v in ins)
    moved += sum(v.size * v.dtype.itemsize for v in outs)
    return pl.pallas_call(
        body,
        out_shape=tuple(outs),
        in_specs=in_specs,
        out_specs=tuple(out_specs),
        scratch_shapes=scratch,
        compiler_params=pltpu.CompilerParams(vmem_limit_bytes=megabytes * 1024 * 1024),
        cost_estimate=pl.CostEstimate(flops=flops, bytes_accessed=moved, transcendentals=0),
        name=name,
    )(*ins)


def struct(shape, dtype=jnp.bfloat16):
    return jax.ShapeDtypeStruct(shape, dtype)


def column_index(ids_ref, core_rel, s):
    return 2 * lax.rem(ids_ref[1] - s + 4, 4) + (ids_ref[2] ^ core_rel)


def start_row(index, size):
    return pl.ds(pl.multiple_of(index * size, 8), size)


def after(value, *others):
    return lax.optimization_barrier((value,) + others)[0]


def pack_first_kernel(counts_ref, wq_ref, wk_ref, wv_ref, gains_ref, out_ref):
    block = wq_ref.shape[0]
    gains = gains_ref[...].astype(jnp.float32)
    row = lax.broadcasted_iota(jnp.int32, (8, block), 0)
    lane = lax.broadcasted_iota(jnp.int32, (8, block), 1)
    first = jnp.concatenate([gains[:1], gains[1:]], 1)
    used = jnp.where(
        lane == 0,
        counts_ref[0, 0].astype(jnp.float32),
        jnp.where(lane == 1, counts_ref[1, 0].astype(jnp.float32), 0.0),
    )
    extra = jnp.where(row == 0, first, jnp.where(row == 1, used, 0.0))
    full = jnp.concatenate(
        [
            wq_ref[...].astype(jnp.float32).T,
            extra,
            wk_ref[...].astype(jnp.float32).T,
            wv_ref[...].astype(jnp.float32).T,
        ],
        0,
    )
    out_ref[...] = jnp.zeros_like(out_ref)
    out_ref[:, :block] = full.astype(jnp.bfloat16)


def pack_mlp_kernel(ids_ref, wg_ref, wu_ref, wd_ref, other_ref, wo_ref, out_ref):
    block, half = wg_ref.shape
    core = ids_ref[2]
    out_ref[...] = jnp.zeros_like(out_ref)
    out_ref[:half, :block] = wg_ref[...].astype(jnp.float32).T.astype(jnp.bfloat16)
    out_ref[half : 2 * half, :block] = wu_ref[...].astype(jnp.float32).T.astype(jnp.bfloat16)
    own = wd_ref[pl.ds(pl.multiple_of(core * half, 16), half), :]
    other = other_ref[...]
    low = jnp.where(core == 0, own, other)
    high = jnp.where(core == 0, other, own)
    out_ref[2 * half : 3 * half, :block] = jnp.concatenate([low, high], 1)
    out_ref[3 * half :, :block] = jnp.concatenate(
        [wo_ref[...].astype(jnp.float32).T, jnp.zeros((8, block), jnp.float32)], 0
    ).astype(jnp.bfloat16)


def turn_in_kernel(x_ref, dy_ref, xt_ref, dyt_ref):
    xt_ref[...] = x_ref[...].astype(jnp.float32).T.astype(jnp.bfloat16)
    dyt_ref[...] = jnp.zeros_like(dyt_ref)
    dyt_ref[:, : dy_ref.shape[0]] = dy_ref[...].astype(jnp.float32).T.astype(jnp.bfloat16)


def fill_relative(ids_ref, target_ref, *sources):
    block, lanes = sources[0].shape[1], target_ref.shape[1]
    wide = target_ref.shape[0] // 4
    for k in range(4):
        parts = [source[ids_ref[0] ^ k] for source in sources]
        target_ref[k * wide : k * wide + block, :] = (
            parts[0] if len(parts) == 1 else jnp.concatenate(parts, 1)
        )
        target_ref[k * wide + block : (k + 1) * wide, :] = jnp.zeros(
            (wide - block, lanes), target_ref.dtype
        )


def wide_rows(refs, s, low, high):
    along, by_x, by_y, far_a, far_b = refs
    far = far_a if s < 2 else far_b
    return jnp.concatenate(
        [along[s, low:high], by_x[s, low:high], by_y[s, low:high], far[s % 2, low:high]], 1
    )


def project_kernel(*refs):
    ids_ref, own, other = refs[0], refs[1:6], refs[6:11]
    n1_ref, cos_ref, sin_ref, q_ref, kv_ref, proj_ref, turned_ref, rel_ref = refs[11:]
    width = n1_ref.shape[0] * n1_ref.shape[1]
    kv_width = KEY_HEADS * HEAD_WIDTH
    q_cols, k_cols = width // 8, kv_width // 8
    depth = own[0].shape[1]
    fill_relative(ids_ref, rel_ref, n1_ref)
    for core_rel, weights in ((0, own), (1, other)):
        for s in range(4):
            f = column_index(ids_ref, core_rel, s)
            total = product_nn(wide_rows(weights, s, 0, depth), rel_ref[...])
            proj_ref[start_row(f, q_cols), :] = total[:q_cols]
            proj_ref[pl.ds(pl.multiple_of(width + f * k_cols, 8), k_cols), :] = total[
                q_cols + 8 : q_cols + 8 + k_cols
            ]
            proj_ref[pl.ds(pl.multiple_of(width + kv_width + f * k_cols, 8), k_cols), :] = total[
                q_cols + 8 + k_cols :
            ]
    cosine, sine = cos_ref[...], sin_ref[...]
    half = HEAD_WIDTH // 2

    def heads(head, carry):
        front = proj_ref[pl.ds(pl.multiple_of(head * HEAD_WIDTH, 8), half), :]
        back = proj_ref[pl.ds(pl.multiple_of(head * HEAD_WIDTH + half, 8), half), :]
        q_ref[head, :half, :] = (
            (front * cosine - back * sine).astype(jnp.bfloat16) * SCORE_SCALE
        ).astype(jnp.bfloat16)
        q_ref[head, half:, :] = (
            (back * cosine + front * sine).astype(jnp.bfloat16) * SCORE_SCALE
        ).astype(jnp.bfloat16)
        return carry

    lax.fori_loop(0, QUERY_HEADS, heads, 0)
    for head in range(KEY_HEADS):
        base = width + head * HEAD_WIDTH
        front = proj_ref[base : base + half, :]
        back = proj_ref[base + half : base + 2 * half, :]
        turned_ref[head * HEAD_WIDTH : head * HEAD_WIDTH + half, :] = front * cosine - back * sine
        turned_ref[head * HEAD_WIDTH + half : (head + 1) * HEAD_WIDTH, :] = (
            back * cosine + front * sine
        )
    turned_ref[kv_width:, :] = proj_ref[width + kv_width :, :]
    kv_ref[...] = turned_ref[...].T.astype(jnp.bfloat16)


def stage_heads(mb, cap, blocks, k_ref, v_ref):
    kv_width = KEY_HEADS * HEAD_WIDTH
    for block, source in enumerate(blocks):
        rows = source[mb * cap : (mb + 1) * cap, :]
        for n in range(KEY_HEADS):
            lanes = n * HEAD_WIDTH
            k_ref[n, block * cap : (block + 1) * cap, :] = rows[:, lanes : lanes + HEAD_WIDTH]
            lanes += kv_width
            v_ref[n, block * cap : (block + 1) * cap, :] = rows[:, lanes : lanes + HEAD_WIDTH]


def stage_bias(ids_ref, counts_ref, mb, cap, share, bias_ref):
    slot = ids_ref[3]
    own_count = counts_ref[mb * 8 + slot]
    key = lax.broadcasted_iota(jnp.int32, (cap, cap), 0)
    query = lax.broadcasted_iota(jnp.int32, (cap, cap), 1)
    query_used = query < own_count
    for core_rel in range(2):
        for s in range(4):
            block = core_rel * 4 + s
            f = column_index(ids_ref, core_rel, s)
            count = counts_ref[mb * 8 + f]
            reach = jnp.where(f < slot, cap, jnp.where(f == slot, 0, -2 * cap))
            self_off = jnp.where(f == slot, 0, 2 * cap)
            allowed = (query_used & (key < count) & (key <= query + reach)) | (
                key == query + self_off
            )
            tile = jnp.where(allowed, 0.0, -1e30)
            for g in range(share):
                bias_ref[block * cap : (block + 1) * cap, g * cap : (g + 1) * cap] = tile


def join_heads(ref, n, share, mb, cap):
    return jnp.concatenate(
        [ref[share * n + g, :, mb * cap : (mb + 1) * cap] for g in range(share)], 1
    )


def attend_kernel(mb, *refs):
    ids_ref, counts_ref, q_ref = refs[:3]
    blocks = refs[3:11]
    att_ref, lse_ref, k_ref, v_ref, bias_ref = refs[11:]
    cap = q_ref.shape[2] // 2
    share = QUERY_HEADS // KEY_HEADS
    stage_heads(mb, cap, blocks, k_ref, v_ref)
    stage_bias(ids_ref, counts_ref, mb, cap, share, bias_ref)

    def body(n, carry):
        scores = product_nn(k_ref[n], join_heads(q_ref, n, share, mb, cap)) + bias_ref[...]
        top = jnp.max(scores, 0, keepdims=True)
        exponent = jnp.exp(scores - top)
        total = jnp.sum(exponent, 0, keepdims=True)
        mixed = product_tn(v_ref[n], exponent.astype(jnp.bfloat16)) / total
        mixed = mixed.astype(jnp.bfloat16)
        for g in range(share):
            att_ref[share * n + g] = mixed[:, g * cap : (g + 1) * cap]
        lse_ref[n] = top + jnp.log(total)
        return carry

    lax.fori_loop(0, KEY_HEADS, body, 0)


def attend_back_kernel(mb, *refs):
    ids_ref, counts_ref, q_ref, do_ref = refs[:4]
    blocks = refs[4:12]
    lse_ref, cos_ref, sin_ref, dq_ref = refs[12:16]
    targets = refs[16:24]
    k_ref, v_ref, bias_ref, dk_ref, dv_ref = refs[24:]
    cap = q_ref.shape[2] // 2
    share = QUERY_HEADS // KEY_HEADS
    half = HEAD_WIDTH // 2
    kv_width = KEY_HEADS * HEAD_WIDTH
    stage_heads(mb, cap, blocks, k_ref, v_ref)
    stage_bias(ids_ref, counts_ref, mb, cap, share, bias_ref)
    cosine = jnp.concatenate([cos_ref[:, mb * cap : (mb + 1) * cap]] * share, 1)
    sine = jnp.concatenate([sin_ref[:, mb * cap : (mb + 1) * cap]] * share, 1)

    def body(n, carry):
        query = join_heads(q_ref, n, share, mb, cap)
        grad = join_heads(do_ref, n, share, mb, cap)
        keys = k_ref[n]
        prob = jnp.exp(product_nn(keys, query) + bias_ref[...] - lse_ref[n])
        dprob = product_nn(v_ref[n], grad)
        delta = jnp.sum(prob * dprob, 0, keepdims=True)
        dscore = (prob * (dprob - delta)).astype(jnp.bfloat16)
        dq = product_tn(keys, dscore) * SCORE_SCALE
        front, back = dq[:half], dq[half:]
        turned = jnp.concatenate(
            [front * cosine + back * sine, back * cosine - front * sine], 0
        ).astype(jnp.bfloat16)
        for g in range(share):
            dq_ref[share * n + g] = turned[:, g * cap : (g + 1) * cap]
        dk_ref[n] = product_nt(dscore, query).astype(jnp.bfloat16)
        dv_ref[n] = product_nt(prob.astype(jnp.bfloat16), grad).astype(jnp.bfloat16)
        return carry

    lax.fori_loop(0, KEY_HEADS, body, 0)
    for block, target in enumerate(targets):
        for n in range(KEY_HEADS):
            lanes = n * HEAD_WIDTH
            target[:, lanes : lanes + HEAD_WIDTH] = dk_ref[n, block * cap : (block + 1) * cap, :]
            lanes += kv_width
            target[:, lanes : lanes + HEAD_WIDTH] = dv_ref[n, block * cap : (block + 1) * cap, :]


def collect_kernel(*refs):
    pieces, out_ref, sem = refs[:16], refs[16], refs[17]
    rows, wide = out_ref.shape[1], pieces[0].shape[1]
    copies = []
    for k in range(4):
        for s in range(4):
            copies.append(
                pltpu.make_async_copy(
                    pieces[k * 4 + s].at[pl.ds(pieces[0].shape[0] - rows, rows)],
                    out_ref.at[s, :, pl.ds(k * wide, wide)],
                    sem.at[k * 4 + s],
                )
            )
    for copy in copies:
        copy.start()
    for copy in copies:
        copy.wait()


def hidden_kernel(
    ids_ref, own_ref, other_ref, att_a_ref, att_b_ref, x_ref, gain_ref, h_ref, n2_ref, rel_ref
):
    q_cols, rows = h_ref.shape[0] // 8, h_ref.shape[1]
    fill_relative(ids_ref, rel_ref, att_a_ref, att_b_ref)
    for core_rel, w_ref in ((0, own_ref), (1, other_ref)):
        for s in range(4):
            f = column_index(ids_ref, core_rel, s)
            h_ref[start_row(f, q_cols), :] = product_nn(w_ref[s], rel_ref[...])[:q_cols]
    h = h_ref[...] + x_ref[...].astype(jnp.float32)
    h_ref[...] = h
    n2_ref[...] = jnp.zeros_like(n2_ref)
    n2_ref[:, :rows] = (h * mean_square(h) * gain_ref[...]).astype(jnp.bfloat16)


def turn_point_kernel(
    ids_ref,
    parts_ref,
    arrived_ref,
    h_ref,
    dy_ref,
    gain_ref,
    own_ref,
    other_ref,
    out_ref,
    dh_ref,
    do_ref,
    gain_grad_ref,
    pieces_ref,
    da_ref,
):
    width, rows = h_ref.shape
    q_cols = width // 8
    block = do_ref.shape[1]
    wide = own_ref.shape[2] // 4
    h = h_ref[...]
    out_ref[...] = (h + parts_ref[0] + arrived_ref[0, :, :rows].astype(jnp.float32)).astype(
        jnp.bfloat16
    )
    dn = parts_ref[1] + arrived_ref[1, :, :rows].astype(jnp.float32)
    rms = mean_square(h)
    gain_grad_ref[...] = jnp.sum(dn * h * rms, 1, keepdims=True)
    weighted = dn * gain_ref[...]
    dh = (
        dy_ref[:, :rows].astype(jnp.float32)
        + rms * weighted
        - h * (rms * rms * rms * jnp.mean(weighted * h, 0, keepdims=True))
    )
    dh_ref[...] = dh
    da_ref[...] = dh
    spread(ids_ref, da_ref, pieces_ref, q_cols)
    half = pieces_ref.shape[0] // 2
    mixed = product_tn(own_ref[...].reshape(half, 4 * wide), pieces_ref[:half, :])
    mixed += product_tn(other_ref[...].reshape(half, 4 * wide), pieces_ref[half:, :])
    mixed = mixed.astype(jnp.bfloat16)
    for k in range(4):
        do_ref[ids_ref[0] ^ k] = mixed[k * wide : k * wide + block]


def spread(ids_ref, source_ref, target_ref, cols):
    rows = source_ref.shape[1]
    for core_rel in range(2):
        for s in range(4):
            f = column_index(ids_ref, core_rel, s)
            low = (core_rel * 4 + s) * (cols + 8)
            target_ref[low : low + cols + 8, :] = jnp.concatenate(
                [source_ref[start_row(f, cols), :], jnp.zeros((8, rows), jnp.float32)], 0
            ).astype(jnp.bfloat16)


def out_grad_kernel(ids_ref, att_a_ref, att_b_ref, pieces_ref, *refs):
    grads, att_rel = refs[:8], refs[8]
    depth = pieces_ref.shape[0] // 8
    wide = att_rel.shape[0] // 4
    fill_relative(ids_ref, att_rel, att_a_ref, att_b_ref)
    for core_rel in range(2):
        for s in range(4):
            low = (core_rel * 4 + s) * depth
            got = product_nt(pieces_ref[low : low + depth, :], att_rel[...]).astype(jnp.bfloat16)
            for k in range(4):
                grads[core_rel * 4 + k][s] = got[:, k * wide : (k + 1) * wide]


def finish_q_kernel(*refs):
    ids_ref, own, other = refs[0], refs[1:6], refs[6:11]
    n1_ref, dq_a_ref, dq_b_ref = refs[11:14]
    out_grads = refs[14:22]
    dn_ref, grads = refs[22], refs[23:31]
    n1_rel, d_ref, dq_ref = refs[31:]
    cap = dq_a_ref.shape[1]
    width = dq_a_ref.shape[0]
    q_cols = width // 8
    depth = q_cols + 8
    block = n1_ref.shape[1]
    wide = n1_rel.shape[0] // 4
    d_ref[:, :cap] = dq_a_ref[...].astype(jnp.float32)
    d_ref[:, cap:] = dq_b_ref[...].astype(jnp.float32)
    spread(ids_ref, d_ref, dq_ref, q_cols)
    fill_relative(ids_ref, n1_rel, n1_ref)
    weights = jnp.concatenate(
        [wide_rows(w, s, 0, depth) for w in (own, other) for s in range(4)], 0
    )
    dn = product_tn(weights, dq_ref[...])
    for k in range(4):
        dn_ref[ids_ref[0] ^ k] = dn[k * wide : k * wide + block]
    for core_rel in range(2):
        for s in range(4):
            low = (core_rel * 4 + s) * depth
            gq = product_nt(dq_ref[low : low + depth, :], n1_rel[...]).astype(jnp.bfloat16)
            for k in range(4):
                target = grads[core_rel * 4 + k]
                target[s, :depth, :] = gq[:, k * wide : (k + 1) * wide]
                target[s, depth:, :] = out_grads[core_rel * 4 + k][s]


def finish_kv_kernel(*refs):
    ids_ref, own, other = refs[0], refs[1:6], refs[6:11]
    n1_ref, dkv_a_ref, dkv_b_ref, cos_ref, sin_ref, dn_ref, dh_ref, x_ref, gain_ref = refs[11:20]
    tokens_ref, gain_grad_ref = refs[20:22]
    grads = refs[22:30]
    n1_rel, d_ref, dkv_ref = refs[30:]
    width, rows = dh_ref.shape
    cap = rows // 2
    kv_width = KEY_HEADS * HEAD_WIDTH
    q_cols, k_cols = width // 8, kv_width // 8
    half = HEAD_WIDTH // 2
    block = n1_ref.shape[1]
    wide = n1_rel.shape[0] // 4
    cosine, sine = cos_ref[...], sin_ref[...]
    d_ref[:, :cap] = dkv_a_ref[...].T
    d_ref[:, cap:] = dkv_b_ref[...].T
    for head in range(KEY_HEADS):
        base = head * HEAD_WIDTH
        front = d_ref[base : base + half, :]
        back = d_ref[base + half : base + 2 * half, :]
        d_ref[base : base + half, :] = front * cosine + back * sine
        d_ref[base + half : base + 2 * half, :] = back * cosine - front * sine
    for core_rel in range(2):
        for s in range(4):
            f = column_index(ids_ref, core_rel, s)
            low = (core_rel * 4 + s) * 2 * k_cols
            dkv_ref[low : low + 2 * k_cols, :] = jnp.concatenate(
                [
                    d_ref[start_row(f, k_cols), :],
                    d_ref[pl.ds(pl.multiple_of(kv_width + f * k_cols, 8), k_cols), :],
                ],
                0,
            ).astype(jnp.bfloat16)
    fill_relative(ids_ref, n1_rel, n1_ref)
    low = q_cols + 8
    weights = jnp.concatenate(
        [wide_rows(w, s, low, low + 2 * k_cols) for w in (own, other) for s in range(4)], 0
    )
    dn = product_tn(weights, dkv_ref[...])
    for k in range(4):
        i = ids_ref[0] ^ k
        tokens_ref[pl.ds(pl.multiple_of(i * block, 16), block), :] = (
            dn[k * wide : k * wide + block] + dn_ref[i]
        )
    for core_rel in range(2):
        for s in range(4):
            low = (core_rel * 4 + s) * 2 * k_cols
            got = product_nt(dkv_ref[low : low + 2 * k_cols, :], n1_rel[...]).astype(jnp.bfloat16)
            for k in range(4):
                grads[core_rel * 4 + k][s] = got[:, k * wide : (k + 1) * wide]
    x = x_ref[...].astype(jnp.float32)
    rms = mean_square(x)
    dn = tokens_ref[...]
    gain_grad_ref[...] = jnp.sum(dn * x * rms, 1, keepdims=True)
    weighted = dn * gain_ref[...]
    tokens_ref[...] = (
        dh_ref[...]
        + rms * weighted
        - x * (rms * rms * rms * jnp.mean(weighted * x, 0, keepdims=True))
    )


def mlp_kernel(*refs):
    ids_ref, n2_own, n2_other, dy_own, dy_other = refs[:5]
    pieces = refs[5:21]
    keep_ref, send_ref = refs[21:23]
    grads = refs[23:39]
    wgu, wdn, gu_ref, prod_ref, dgu_ref, n2_rel, dy_rel, sem_in, sem_out = refs[39:]
    dp_id = ids_ref[0]
    z_id = ids_ref[1]
    block, rows = keep_ref.shape[1] // 4, keep_ref.shape[2]
    pair = 2 * rows
    wide = pieces[0].shape[1]
    half = prod_ref.shape[0] // 4

    def gate_up_part(ref, piece, k, s):
        return piece.at[pl.ds(0, 2 * half)], ref.at[
            pl.ds(s * 2 * half, 2 * half), pl.ds(k * wide, wide)
        ]

    def down_part(ref, piece, k, s):
        return piece.at[pl.ds(2 * half, half)], ref.at[
            pl.ds(k * half, half), pl.ds(s * wide, wide)
        ]

    loads, more_loads = [], []
    for s in range(4):
        for k in range(4):
            source, target = gate_up_part(wgu, pieces[k * 4 + s], k, s)
            loads.append(pltpu.make_async_copy(source, target, sem_in.at[0, k * 4 + s]))
            source, target = down_part(wdn, pieces[k * 4 + s], k, s)
            more_loads.append(pltpu.make_async_copy(source, target, sem_in.at[1, k * 4 + s]))
    for load in loads + more_loads:
        load.start()
    pad = jnp.zeros((wide - block, pair), jnp.bfloat16)
    for j in range(4):
        i = dp_id ^ j
        zz = lax.rem(z_id - j + 4, 4)
        n2_rel[j * wide : j * wide + block, :] = jnp.concatenate(
            [n2_own[i][:, :rows], n2_other[i][:, :rows]], 1
        )
        dy_rel[j * wide : j * wide + block, :] = jnp.concatenate(
            [dy_own[zz][:, :rows], dy_other[zz][:, :rows]], 1
        )
        n2_rel[j * wide + block : (j + 1) * wide, :] = pad
        dy_rel[j * wide + block : (j + 1) * wide, :] = pad

    def rows_of(index, size):
        return pl.ds(pl.multiple_of(index * size, 16), size)

    for s in range(4):
        for load in loads[4 * s : 4 * s + 4]:
            load.wait()
        k = lax.rem(z_id - s + 4, 4) ^ dp_id
        total = product_nn(wgu[s * 2 * half : (s + 1) * 2 * half, :], n2_rel[...])
        gu_ref[rows_of(k, 2 * half), :] = total
        gate = total[:half]
        prod_ref[rows_of(k, half), :] = (gate * jax.nn.sigmoid(gate) * total[half:]).astype(
            jnp.bfloat16
        )
    for load in more_loads:
        load.wait()
    for k in range(4):
        s = lax.rem(z_id - (dp_id ^ k) + 4, 4)
        dprod = product_nn(wdn[k * half : (k + 1) * half, :], dy_rel[...])
        gate = gu_ref[k * 2 * half : k * 2 * half + half, :]
        up = gu_ref[k * 2 * half + half : (k + 1) * 2 * half, :]
        sig = jax.nn.sigmoid(gate)
        dgu_ref[rows_of(s, 2 * half), :] = jnp.concatenate(
            [dprod * up * sig * (1.0 + gate * (1.0 - sig)), dprod * gate * sig], 0
        ).astype(jnp.bfloat16)
    for j in range(4):
        lanes = slice(j * wide, (j + 1) * wide)
        out = product_tn(wdn[:, lanes], prod_ref[...])[:block]
        zz = rows_of(lax.rem(z_id - j + 4, 4), block)
        keep_ref[0, zz, :] = out[:, :rows]
        send_ref[0, zz, :rows] = out[:, rows:].astype(jnp.bfloat16)
    for k in range(4):
        here = slice(k * half, (k + 1) * half)
        wdn[here, :] = product_nt(prod_ref[here, :], dy_rel[...]).astype(jnp.bfloat16)
    stores = []
    for k in range(4):
        for s in range(4):
            target, source = down_part(wdn, grads[k * 4 + s], k, s)
            stores.append(pltpu.make_async_copy(source, target, sem_out.at[1, k * 4 + s]))
    for store in stores:
        store.start()
    for j in range(4):
        lanes = slice(j * wide, (j + 1) * wide)
        dn = product_tn(wgu[:, lanes], dgu_ref[...])[:block]
        i = rows_of(dp_id ^ j, block)
        keep_ref[1, i, :] = dn[:, :rows]
        send_ref[1, i, :rows] = dn[:, rows:].astype(jnp.bfloat16)
    send_ref[:, :, rows:] = jnp.zeros((2, 4 * block, send_ref.shape[2] - rows), jnp.bfloat16)
    for s in range(4):
        here = slice(s * 2 * half, (s + 1) * 2 * half)
        wgu[here, :] = product_nt(dgu_ref[here, :], n2_rel[...]).astype(jnp.bfloat16)
        for k in range(4):
            target, source = gate_up_part(wgu, grads[k * 4 + s], k, s)
            store = pltpu.make_async_copy(source, target, sem_out.at[0, k * 4 + s])
            store.start()
            stores.append(store)
    for store in stores:
        store.wait()


def mean_square(values):
    return lax.rsqrt(jnp.mean(values * values, 0, keepdims=True) + EPSILON)


def fast(
    tokens, cotangent, counts, w_query, key_weight, value_weight, w_out, w_gate, w_up, w_down, gains
):
    dp_id = lax.axis_index("dp")
    slot = lax.axis_index("fsdp")
    z_id = slot // 2
    core_id = slot % 2
    ids = jnp.stack([dp_id, z_id, core_id, slot]).astype(jnp.int32)
    batches, cap, width = tokens.shape
    rows = batches * cap
    block = w_query.shape[0]
    wide = -(-block // 128) * 128
    q_cols, k_cols = w_query.shape[1], key_weight.shape[1]
    half = w_gate.shape[1]
    kv_width = KEY_HEADS * HEAD_WIDTH
    share = QUERY_HEADS // KEY_HEADS
    q_rows = q_cols + 8
    depth = q_rows + 2 * k_cols
    mlp_rows = 3 * half + q_rows
    padded = -(-rows // 128) * 128

    (first_piece,) = run(
        pack_first_kernel,
        "pack_first",
        (counts, w_query, key_weight, value_weight, gains),
        [SMEM] + [VMEM] * 4,
        [struct((depth, wide))],
        [VMEM],
        [],
        0,
        16,
    )
    chain = [first_piece] + [shift_z(first_piece, step) for step in (1, 2, 3)]
    down_halves = w_down.reshape(2, half, -1)
    other_down = swap_core(
        lax.dynamic_index_in_dim(down_halves, 1 - core_id, 0, keepdims=False)
    )
    (mlp_piece,) = run(
        pack_mlp_kernel,
        "pack_mlp",
        (ids, w_gate, w_up, w_down, other_down, w_out),
        [SMEM] + [VMEM] * 5,
        [struct((mlp_rows, wide))],
        [VMEM],
        [],
        0,
        16,
    )
    x, dy = run(
        turn_in_kernel,
        "turn_in",
        (tokens.reshape(rows, width), cotangent.reshape(rows, width)),
        [VMEM] * 2,
        [struct((width, rows)), struct((width, padded))],
        [VMEM] * 2,
        [],
        0,
        16,
    )
    dy_other = swap_core(dy)

    along = jnp.stack(chain, 0)
    extras = along[:, q_cols : q_cols + 2, :block]
    other_extras = swap_core(extras)
    x_zero, y_zero = swap_dp(mlp_piece, 1), swap_dp(mlp_piece, 2)
    along_next = after(along, x_zero, y_zero)
    from_x = swap_dp(along_next, 1)
    from_y = swap_dp(along_next, 2)
    first_own = [along, from_x, from_y, swap_dp(from_x[:2], 2), swap_dp(from_y[2:], 1)]
    first_other = [swap_core(piece) for piece in first_own]

    z_one = shift_z(after(mlp_piece, along), 1)
    z_two = shift_z(z_one, 1)
    z_three = shift_z(z_two, 1)
    far_zero = swap_dp(after(x_zero, *first_own[3:]), 2)
    z_one_next = after(z_one, *first_own[3:])
    x_one, y_one = swap_dp(z_one_next, 1), swap_dp(z_one_next, 2)

    by_core = jnp.where(
        core_id == 0, jnp.stack([extras, other_extras], 1), jnp.stack([other_extras, extras], 1)
    )
    by_core = by_core[::-1]
    by_core = lax.dynamic_slice_in_dim(jnp.concatenate([by_core, by_core], 0), 3 - z_id, 4, 0)
    gain = by_core[:, :, 0, :].reshape(8, 2, q_cols).transpose(0, 2, 1).reshape(width, 2)
    gain = gain.astype(jnp.float32)
    gain_one, gain_two = gain[:, :1], gain[:, 1:]
    group_counts = by_core[:, :, 1, :batches].reshape(8, batches).astype(jnp.int32)
    flat_counts = group_counts.T.reshape(-1)
    before = jnp.sum(
        jnp.where(jnp.arange(8, dtype=jnp.int32)[:, None] < slot, group_counts, 0), 0
    )
    position = (before[:, None] + jnp.arange(cap, dtype=jnp.int32)[None, :]).reshape(-1)
    cosine, sine = rope_tables(position, HEAD_WIDTH)
    cosine, sine = cosine[:, 0, :].T, sine[:, 0, :].T
    x_wide = x.astype(jnp.float32)
    n1 = (x_wide * mean_square(x_wide) * gain_one).astype(jnp.bfloat16).reshape(4, block, rows)
    n1_next = after(n1, z_one)

    query, kv = run(
        project_kernel,
        "project",
        (ids, *first_own, *first_other, n1_next, cosine, sine),
        [SMEM] + [VMEM] * 13,
        (struct((QUERY_HEADS, HEAD_WIDTH, rows)), struct((rows, 2 * kv_width))),
        [VMEM] * 2,
        [
            pltpu.VMEM((width + 2 * kv_width, rows), jnp.float32),
            pltpu.VMEM((2 * kv_width, rows), jnp.float32),
            pltpu.VMEM((4 * wide, rows), jnp.bfloat16),
        ],
        2 * (width + 2 * kv_width) * width * rows,
        24,
    )
    kv_next = after(kv, z_two)
    kv_own = [kv] + [shift_z_up(kv_next, step) for step in (1, 2, 3)]
    kv_other = [swap_core(piece) for piece in kv_own]
    z_two_next, x_zero_next = after(z_two, kv), after(y_one, kv)
    x_two, y_two = swap_dp(z_two_next, 1), swap_dp(z_two_next, 2)
    far_one = swap_dp(x_zero_next, 1)
    x_three, y_three = swap_dp(z_three, 1), swap_dp(z_three, 2)
    far_two = swap_dp(x_two, 2)
    far_three = swap_dp(y_three, 1)
    pieces = [mlp_piece, z_one, z_two, z_three]
    pieces += [x_zero, x_one, x_two, x_three]
    pieces += [y_zero, y_one, y_two, y_three]
    pieces += [far_zero, far_one, far_two, far_three]

    pair_flops = 2 * QUERY_HEADS * HEAD_WIDTH * rows * 8 * cap
    head_scratch = [
        pltpu.VMEM((KEY_HEADS, 8 * cap, HEAD_WIDTH), jnp.bfloat16),
        pltpu.VMEM((KEY_HEADS, 8 * cap, HEAD_WIDTH), jnp.bfloat16),
        pltpu.VMEM((8 * cap, share * cap), jnp.float32),
    ]
    def attend(mb, queries):
        return run(
            functools.partial(attend_kernel, mb),
            "attend",
            (ids, flat_counts, queries, *kv_own, *kv_other),
            [SMEM, SMEM] + [VMEM] * 9,
            (
                struct((QUERY_HEADS, HEAD_WIDTH, cap)),
                struct((KEY_HEADS, 1, share * cap), jnp.float32),
            ),
            [VMEM] * 2,
            head_scratch,
            4 * pair_flops,
            24,
        )

    att_a, lse_a = attend(0, after(query, x_one, y_one, far_zero, x_two, y_two, z_three))
    att_b, lse_b = attend(1, after(query, x_three, y_three, far_one, far_two, att_a))
    att_a = att_a.reshape(4, block, cap)
    att_b = att_b.reshape(4, block, cap)
    lse = (lse_a, lse_b)
    blocks = (4, block, rows)
    wide_blocks = (4, block, padded)
    (out_own,) = run(
        collect_kernel,
        "collect",
        tuple(pieces),
        [ANY] * 16,
        [struct((4, q_rows, 4 * wide))],
        [VMEM],
        [pltpu.SemaphoreType.DMA((16,))],
        0,
        8,
    )
    out_other = swap_core(out_own)
    h, n2 = run(
        hidden_kernel,
        "hidden",
        (ids, out_own, out_other, att_a, att_b, x, gain_two),
        [SMEM] + [VMEM] * 6,
        (struct((width, rows), jnp.float32), struct((width, padded))),
        [VMEM] * 2,
        [pltpu.VMEM((4 * wide, rows), jnp.bfloat16)],
        2 * width * width * rows,
        24,
    )
    n2_other = swap_core(n2)
    results = run(
        mlp_kernel,
        "mlp",
        (
            ids,
            n2.reshape(wide_blocks),
            n2_other.reshape(wide_blocks),
            dy.reshape(wide_blocks),
            dy_other.reshape(wide_blocks),
            *pieces,
        ),
        [SMEM] + [VMEM] * 4 + [ANY] * 16,
        [struct((2, width, rows), jnp.float32), struct((2, width, padded))]
        + [struct((3 * half, wide))] * 16,
        [VMEM] * 2 + [ANY] * 16,
        [
            pltpu.VMEM((8 * half, 4 * wide), jnp.bfloat16),
            pltpu.VMEM((4 * half, 4 * wide), jnp.bfloat16),
            pltpu.VMEM((8 * half, 2 * rows), jnp.float32),
            pltpu.VMEM((4 * half, 2 * rows), jnp.bfloat16),
            pltpu.VMEM((8 * half, 2 * rows), jnp.bfloat16),
            pltpu.VMEM((4 * wide, 2 * rows), jnp.bfloat16),
            pltpu.VMEM((4 * wide, 2 * rows), jnp.bfloat16),
            pltpu.SemaphoreType.DMA((2, 16)),
            pltpu.SemaphoreType.DMA((2, 16)),
        ],
        18 * 16 * half * block * 2 * rows,
        44,
    )
    keep, send, grads = results[0], results[1], results[2:]
    arrived = swap_core(send)
    home, to_x, to_y, far = grads[:4], grads[4:8], grads[8:12], grads[12:]

    def first_leg(group, *deps):
        a, b = 2 * group, 2 * group + 1
        return (
            swap_dp(after(far[a], *deps), 2),
            swap_dp(after(far[b], *deps), 1),
            swap_dp(after(to_x[b], *deps), 1),
            swap_dp(after(to_y[a], *deps), 2),
        )

    def second_leg(group, legs, *deps):
        a, b = 2 * group, 2 * group + 1
        via_y, via_x = after(legs[0], *deps), after(legs[1], *deps)
        x_a = swap_dp(add_low(to_x[a], via_y), 1)
        y_b = swap_dp(add_low(to_y[b], via_x), 2)
        return x_a, y_b

    legs_one = first_leg(1)
    output, dh, mixed_gradient, gain_two_grad, da_pieces = run(
        turn_point_kernel,
        "turn_point",
        (ids, keep, arrived, h, dy, gain_two, out_own, out_other),
        [SMEM] + [VMEM] * 7,
        (
            struct((width, rows)),
            struct((width, rows), jnp.float32),
            struct(blocks),
            struct((width, 1), jnp.float32),
            struct((8 * q_rows, rows)),
        ),
        [VMEM] * 5,
        [pltpu.VMEM((width, rows), jnp.float32)],
        2 * width * width * rows,
        24,
    )
    output = output.T.reshape(batches, cap, width)
    legs_zero = first_leg(0, mixed_gradient)
    turned_one = second_leg(1, legs_one, mixed_gradient)

    def attend_back(mb, mixed):
        return run(
            functools.partial(attend_back_kernel, mb),
            "attend_back",
            (
                ids,
                flat_counts,
                query,
                mixed.reshape(QUERY_HEADS, HEAD_WIDTH, rows),
                *kv_own,
                *kv_other,
                lse[mb],
                cosine,
                sine,
            ),
            [SMEM, SMEM] + [VMEM] * 13,
            [struct((QUERY_HEADS, HEAD_WIDTH, cap))] + [struct((cap, 2 * kv_width))] * 8,
            [VMEM] * 9,
            head_scratch
            + [
                pltpu.VMEM((KEY_HEADS, 8 * cap, HEAD_WIDTH), jnp.bfloat16),
                pltpu.VMEM((KEY_HEADS, 8 * cap, HEAD_WIDTH), jnp.bfloat16),
            ],
            10 * pair_flops,
            24,
        )

    def sum_cores(own, other):
        return [add_low(own[s], swap_core(other[s])) for s in (3, 2, 1, 0)][::-1]

    def sum_z(summed):
        total = summed[0].astype(jnp.float32)
        for s in (3, 2, 1):
            total = total + shift_z_down(summed[s], s).astype(jnp.float32)
        return total

    back_a = attend_back(0, after(mixed_gradient, *legs_one))
    out_grads = run(
        out_grad_kernel,
        "out_grad",
        (ids, att_a, att_b, after(da_pieces, back_a[0])),
        [SMEM] + [VMEM] * 3,
        [struct((4, q_rows, wide))] * 8,
        [VMEM] * 8,
        [pltpu.VMEM((4 * wide, rows), jnp.bfloat16)],
        2 * width * width * rows,
        16,
    )
    summed_a = sum_cores(back_a[1:5], back_a[5:9])
    dkv_a = sum_z(summed_a)
    back_b = attend_back(1, after(mixed_gradient, *summed_a, *turned_one, out_grads[0]))
    dkv_b = sum_z(sum_cores(back_b[1:5], back_b[5:9]))
    turned_zero = second_leg(0, legs_zero, back_b[0])
    summed_three = add_low(home[3], legs_one[2], after(turned_one[1], back_b[0]))
    summed_two = add_low(home[2], after(turned_one[0], back_b[0]), legs_one[3])
    hop = shift_z(summed_three, -1)
    hop = shift_z(add_low(summed_two, hop), -1)
    summed_one = add_low(home[1], legs_zero[2], turned_zero[1])
    hop = shift_z(add_low(summed_one, hop), -1)
    mlp_total = (
        home[0].astype(jnp.float32)
        + turned_zero[0].astype(jnp.float32)
        + legs_zero[3].astype(jnp.float32)
        + hop.astype(jnp.float32)
    )
    grad_gate = mlp_total[:half, :block].T
    grad_up = mlp_total[half : 2 * half, :block].T
    down_total = mlp_total[2 * half :, :block]
    left, right = down_total[:, :q_cols], down_total[:, q_cols:]
    stay = jnp.where(core_id == 0, left, right)
    give = jnp.where(core_id == 0, right, left).astype(jnp.bfloat16)
    taken = swap_core(give).astype(jnp.float32)
    grad_down = jnp.where(
        core_id == 0, jnp.concatenate([stay, taken], 0), jnp.concatenate([taken, stay], 0)
    )

    def reduce_all(parts):
        mine = [add_low(parts[k], swap_core(parts[4 + k])) for k in range(4)]
        summed = [mine[0]] + [swap_dp(mine[k], k) for k in (1, 2, 3)]
        out = [add_low(*[piece[s] for piece in summed]) for s in range(4)]
        total = out[0].astype(jnp.float32)
        for s in (1, 2, 3):
            total = total + shift_z(out[s], -s).astype(jnp.float32)
        return total

    q_results = run(
        finish_q_kernel,
        "finish_q",
        (
            ids,
            *first_own,
            *first_other,
            after(n1, dkv_a, *legs_zero),
            back_a[0].reshape(width, cap),
            back_b[0].reshape(width, cap),
            *out_grads,
        ),
        [SMEM] + [VMEM] * 21,
        [struct(blocks, jnp.float32)] + [struct((4, 2 * q_rows, wide))] * 8,
        [VMEM] * 9,
        [
            pltpu.VMEM((4 * wide, rows), jnp.bfloat16),
            pltpu.VMEM((width, rows), jnp.float32),
            pltpu.VMEM((8 * q_rows, rows), jnp.bfloat16),
        ],
        4 * width * width * rows,
        24,
    )
    dn_q = q_results[0]
    q_out_total = reduce_all(q_results[1:])
    grad_query = q_out_total[:q_cols, :block].T
    grad_out = q_out_total[q_rows : q_rows + q_cols, :block].T

    kv_results = run(
        finish_kv_kernel,
        "finish_kv",
        (
            ids,
            *first_own,
            *first_other,
            after(n1, *turned_zero),
            dkv_a,
            dkv_b,
            cosine,
            sine,
            dn_q,
            dh,
            x,
            gain_one,
        ),
        [SMEM] + [VMEM] * 19,
        [struct((width, rows), jnp.float32), struct((width, 1), jnp.float32)]
        + [struct((4, 2 * k_cols, wide))] * 8,
        [VMEM] * 10,
        [
            pltpu.VMEM((4 * wide, rows), jnp.bfloat16),
            pltpu.VMEM((2 * kv_width, rows), jnp.float32),
            pltpu.VMEM((16 * k_cols, rows), jnp.bfloat16),
        ],
        8 * kv_width * width * rows,
        24,
    )
    grad_tokens = kv_results[0].T.reshape(batches, cap, width)
    kv_total = reduce_all(kv_results[2:])
    gain_total = jnp.concatenate([kv_results[1], gain_two_grad], 1).T
    gain_total = gain_total + swap_core(gain_total)
    gain_total = (gain_total + swap_dp(gain_total, 1)) + (
        swap_dp(gain_total, 2) + swap_dp(gain_total, 3)
    )
    gain_total = (gain_total + shift_z(gain_total, 2)) + (
        shift_z(gain_total, 1) + shift_z(gain_total, -1)
    )
    gain_grad = lax.dynamic_slice_in_dim(gain_total, slot * q_cols, q_cols, 1)
    return (
        output,
        grad_tokens,
        grad_query,
        kv_total[:k_cols, :block].T,
        kv_total[k_cols:, :block].T,
        grad_out,
        grad_gate,
        grad_up,
        grad_down,
        gain_grad,
    )


def solution(mesh):
    in_specs = (
        P(None, ("dp", "fsdp"), None),
        P(None, ("dp", "fsdp"), None),
        P(None, ("dp", "fsdp")),
        P("dp", "fsdp"),
        P("dp", "fsdp"),
        P("dp", "fsdp"),
        P("dp", "fsdp"),
        P("dp", "fsdp"),
        P("dp", "fsdp"),
        P("dp", "fsdp"),
        P(None, "fsdp"),
    )
    out_specs = (
        P(None, ("dp", "fsdp"), None),
        P(None, ("dp", "fsdp"), None),
        P("dp", "fsdp"),
        P("dp", "fsdp"),
        P("dp", "fsdp"),
        P("dp", "fsdp"),
        P("dp", "fsdp"),
        P("dp", "fsdp"),
        P("dp", "fsdp"),
        P(None, "fsdp"),
    )
    square = mesh.shape["dp"] == 4 and mesh.shape["fsdp"] == 8
    return jax.shard_map(
        fast if square else local, mesh=mesh, in_specs=in_specs, out_specs=out_specs, check_vma=False)
```

```python
import functools

import jax
import jax.numpy as jnp
from jax import lax
from jax.experimental import pallas as pl
from jax.experimental.pallas import tpu as pltpu
from jax.sharding import PartitionSpec as P

MODEL_WIDTH = 960
QUERY_HEADS = 15
KEY_HEADS = 5
HEAD_WIDTH = 64


EPSILON = 1e-05
ROPE_BASE = 100000.0
SCORE_SCALE = 0.125


def rope_tables(position, head_size):
    half_size = head_size // 2
    frequency = ROPE_BASE ** (-(jnp.arange(half_size, dtype=jnp.float32) * 2.0) / head_size)
    angles = position.astype(jnp.float32)[:, None] * frequency[None, :]
    return (jnp.cos(angles)[:, None, :], jnp.sin(angles)[:, None, :])


def apply_rotation(values, cosine_table, sine_values):
    half_size = values.shape[-1] // 2
    front_half = values[..., :half_size]
    back_half = values[..., half_size:]
    return jnp.concatenate(
        [
            front_half * cosine_table - back_half * sine_values,
            back_half * cosine_table + front_half * sine_values,
        ],
        -1,
    )


def normalize(values, gain_row):
    inv_rms = lax.rsqrt(jnp.mean(values * values, -1, keepdims=True) + EPSILON)
    return (values * inv_rms * gain_row, inv_rms)


def norm_back(values, inv_rms, gain_row, incoming):
    weighted = incoming * gain_row
    return inv_rms * weighted - values * inv_rms * inv_rms * inv_rms * jnp.mean(
        weighted * values, -1, keepdims=True
    )


def build_mask(count_row, device, slot_capacity):
    group_width = count_row.shape[0]
    local_slot = jnp.arange(slot_capacity, dtype=jnp.int32)
    offsets = jnp.cumsum(count_row) - count_row
    is_mine = jnp.arange(group_width, dtype=jnp.int32) == device
    own_offset = jnp.sum(jnp.where(is_mine, offsets, 0))
    own_count = jnp.sum(jnp.where(is_mine, count_row, 0))
    query_pos = own_offset + local_slot
    query_valid = local_slot < own_count
    key_pos = (offsets[:, None] + local_slot[None, :]).reshape(-1)
    key_valid = (local_slot[None, :] < count_row[:, None]).reshape(-1)
    slot_ids = jnp.arange(group_width * slot_capacity, dtype=jnp.int32)
    own_slots = device * slot_capacity + local_slot
    allowed = query_valid[:, None] & key_valid[None, :] & (
        key_pos[None, :] <= query_pos[:, None]
    ) | (slot_ids[None, :] == own_slots[:, None])
    return (allowed, query_pos)


def kept_fetch(w_query, key_weight, value_weight, w_out, w_gate, w_up, w_down, gains):
    columns = (
        lax.all_gather(w_query, "fsdp", axis=1, tiled=True),
        lax.all_gather(key_weight, "fsdp", axis=1, tiled=True),
        lax.all_gather(value_weight, "fsdp", axis=1, tiled=True),
        lax.all_gather(w_out, "fsdp", axis=1, tiled=True),
        lax.all_gather(w_gate, "fsdp", axis=1, tiled=True),
        lax.all_gather(w_up, "fsdp", axis=1, tiled=True),
        lax.all_gather(w_down, "fsdp", axis=1, tiled=True),
        lax.all_gather(gains, "fsdp", axis=1, tiled=True),
    )
    matrices = (
        lax.all_gather(columns[0], "dp", axis=0, tiled=True),
        lax.all_gather(columns[1], "dp", axis=0, tiled=True),
        lax.all_gather(columns[2], "dp", axis=0, tiled=True),
        lax.all_gather(columns[3], "dp", axis=0, tiled=True),
        lax.all_gather(columns[4], "dp", axis=0, tiled=True),
        lax.all_gather(columns[5], "dp", axis=0, tiled=True),
        lax.all_gather(columns[6], "dp", axis=0, tiled=True),
    )
    return (matrices, columns[7].astype(jnp.float32))


def times_transpose(left, right):
    return jnp.einsum("rk,jk->rj", left, right, preferred_element_type=jnp.float32)


def rows_product(left, right):
    return jnp.einsum("rd,rk->dk", left, right, preferred_element_type=jnp.float32)


def local(
    tokens, cotangent, counts, w_query, key_weight, value_weight, w_out, w_gate, w_up, w_down, gains
):
    group_counts = lax.all_gather(counts, "fsdp", axis=1, tiled=True)
    device = lax.axis_index("fsdp")
    slot_capacity = tokens.shape[1]
    key_value_width = KEY_HEADS * HEAD_WIDTH
    device_share = QUERY_HEADS // KEY_HEADS
    kept_weights, kept_gain = kept_fetch(
        w_query, key_weight, value_weight, w_out, w_gate, w_up, w_down, gains
    )
    outputs = []
    grad_inputs = []
    saved = [[] for index_unused in range(11)]
    gain_one_total = jnp.zeros((MODEL_WIDTH,), jnp.float32)
    gain_two_total = jnp.zeros((MODEL_WIDTH,), jnp.float32)
    for micro_idx in range(tokens.shape[0]):
        matrices, gain_pair = (kept_weights, kept_gain)
        full_query, full_key, full_value, full_out, full_gate, full_up, full_down = matrices
        inputs = tokens[micro_idx].astype(jnp.float32)
        allowed, query_pos = build_mask(group_counts[micro_idx], device, slot_capacity)
        cosine_table, sine_values = rope_tables(query_pos, HEAD_WIDTH)
        first_normed, scale_one = normalize(inputs, gain_pair[0])
        normed_low = first_normed.astype(jnp.bfloat16)
        reduced_query = apply_rotation(
            jnp.dot(normed_low, full_query, preferred_element_type=jnp.float32).reshape(
                slot_capacity, QUERY_HEADS, HEAD_WIDTH
            ),
            cosine_table,
            sine_values,
        ).astype(jnp.bfloat16)
        key_low = (
            apply_rotation(
                jnp.dot(normed_low, full_key, preferred_element_type=jnp.float32).reshape(
                    slot_capacity, KEY_HEADS, HEAD_WIDTH
                ),
                cosine_table,
                sine_values,
            )
            .astype(jnp.bfloat16)
            .reshape(slot_capacity, key_value_width)
        )
        value_low = jnp.dot(normed_low, full_value, preferred_element_type=jnp.float32).astype(
            jnp.bfloat16
        )
        grouped_keys, grouped_values = (
            lax.all_gather(key_low, "fsdp", axis=0, tiled=True),
            lax.all_gather(value_low, "fsdp", axis=0, tiled=True),
        )
        heads_of_key = grouped_keys.reshape(-1, KEY_HEADS, HEAD_WIDTH)
        heads_of_value = grouped_values.reshape(-1, KEY_HEADS, HEAD_WIDTH)
        heads_of_query = reduced_query.reshape(slot_capacity, KEY_HEADS, device_share, HEAD_WIDTH)
        scores = (
            jnp.einsum(
                "qngd,knd->ngqk", heads_of_query, heads_of_key, preferred_element_type=jnp.float32
            )
            * SCORE_SCALE
        )
        masked = jnp.where(allowed, scores, -1e30)
        row_top = jnp.max(masked, -1, keepdims=True)
        exponent = jnp.where(allowed, jnp.exp(masked - row_top), 0.0)
        row_total = jnp.sum(exponent, -1, keepdims=True)
        prob_low = (exponent / row_total).astype(jnp.bfloat16)
        log_total = row_top + jnp.log(row_total)
        mixed_heads = jnp.einsum(
            "ngqk,knd->qngd", prob_low, heads_of_value, preferred_element_type=jnp.float32
        ).reshape(slot_capacity, MODEL_WIDTH)
        attended = mixed_heads.astype(jnp.bfloat16)
        hidden_state = inputs + jnp.dot(attended, full_out, preferred_element_type=jnp.float32)
        normed_two, scale_two = normalize(hidden_state, gain_pair[1])
        normed_two_low = normed_two.astype(jnp.bfloat16)
        gate_act = jnp.dot(normed_two_low, full_gate, preferred_element_type=jnp.float32)
        upward = jnp.dot(normed_two_low, full_up, preferred_element_type=jnp.float32)
        sigmoid_gate = jax.nn.sigmoid(gate_act)
        product = (gate_act * sigmoid_gate * upward).astype(jnp.bfloat16)
        outputs.append(
            (hidden_state + jnp.dot(product, full_down, preferred_element_type=jnp.float32)).astype(
                jnp.bfloat16
            )
        )
        matrices, gain_pair = (kept_weights, kept_gain)
        full_query, full_key, full_value, full_out, full_gate, full_up, full_down = matrices
        grad_low = cotangent[micro_idx]
        grad_product = times_transpose(grad_low, full_down)
        grad_gate = (
            grad_product * upward * sigmoid_gate * (1.0 + gate_act * (1.0 - sigmoid_gate))
        ).astype(jnp.bfloat16)
        grad_upward = (grad_product * gate_act * sigmoid_gate).astype(jnp.bfloat16)
        grad_normed_two = times_transpose(grad_gate, full_gate) + times_transpose(
            grad_upward, full_up
        )
        gain_two_total = gain_two_total + jnp.sum(grad_normed_two * hidden_state * scale_two, 0)
        grad_hidden = grad_low.astype(jnp.float32) + norm_back(
            hidden_state, scale_two, gain_pair[1], grad_normed_two
        )
        grad_branch = grad_hidden.astype(jnp.bfloat16)
        mixed_gradient = times_transpose(grad_branch, full_out).astype(jnp.bfloat16)
        head_gradient = mixed_gradient.reshape(slot_capacity, KEY_HEADS, device_share, HEAD_WIDTH)
        again_scores = (
            jnp.einsum(
                "qngd,knd->ngqk", heads_of_query, heads_of_key, preferred_element_type=jnp.float32
            )
            * SCORE_SCALE
        )
        probability = jnp.where(allowed, jnp.exp(again_scores - log_total), 0.0)
        grad_prob = jnp.einsum(
            "qngd,knd->ngqk", head_gradient, heads_of_value, preferred_element_type=jnp.float32
        )
        row_delta = jnp.sum(probability * grad_prob, -1, keepdims=True)
        grad_scores = (probability * (grad_prob - row_delta)).astype(jnp.bfloat16)
        grad_query_rot = (
            jnp.einsum(
                "ngqk,knd->qngd", grad_scores, heads_of_key, preferred_element_type=jnp.float32
            ).reshape(slot_capacity, QUERY_HEADS, HEAD_WIDTH)
            * SCORE_SCALE
        )
        key_part = (
            jnp.einsum(
                "ngqk,qngd->knd", grad_scores, heads_of_query, preferred_element_type=jnp.float32
            ).reshape(-1, key_value_width)
            * SCORE_SCALE
        )
        value_part = jnp.einsum(
            "ngqk,qngd->knd",
            probability.astype(jnp.bfloat16),
            head_gradient,
            preferred_element_type=jnp.float32,
        ).reshape(-1, key_value_width)
        key_gradient, value_grad = (
            lax.psum_scatter(
                key_part.astype(jnp.bfloat16), "fsdp", scatter_dimension=0, tiled=True
            ).astype(jnp.float32),
            lax.psum_scatter(
                value_part.astype(jnp.bfloat16), "fsdp", scatter_dimension=0, tiled=True
            ).astype(jnp.float32),
        )
        grad_query = (
            apply_rotation(grad_query_rot, cosine_table, -sine_values)
            .astype(jnp.bfloat16)
            .reshape(slot_capacity, MODEL_WIDTH)
        )
        grad_key = (
            apply_rotation(
                key_gradient.reshape(slot_capacity, KEY_HEADS, HEAD_WIDTH),
                cosine_table,
                -sine_values,
            )
            .astype(jnp.bfloat16)
            .reshape(slot_capacity, key_value_width)
        )
        grad_value = value_grad.astype(jnp.bfloat16)
        grad_normed_one = (
            times_transpose(grad_query, full_query)
            + times_transpose(grad_key, full_key)
            + times_transpose(grad_value, full_value)
        )
        gain_one_total = gain_one_total + jnp.sum(grad_normed_one * inputs * scale_one, 0)
        grad_inputs.append(
            grad_hidden + norm_back(inputs, scale_one, gain_pair[0], grad_normed_one)
        )
        kept_rows = (
            normed_low,
            grad_query,
            grad_key,
            grad_value,
            attended,
            grad_branch,
            normed_two_low,
            grad_gate,
            grad_upward,
            product,
            grad_low,
        )
        for slot_index in range(11):
            saved[slot_index].append(kept_rows[slot_index])
    joined = [jnp.concatenate(column_list, 0) for column_list in saved]
    gain_terms = jnp.stack([gain_one_total, gain_two_total], 0)
    slices = (
        lax.all_to_all(joined[1], "fsdp", split_axis=1, concat_axis=0, tiled=True),
        lax.all_to_all(joined[2], "fsdp", split_axis=1, concat_axis=0, tiled=True),
        lax.all_to_all(joined[3], "fsdp", split_axis=1, concat_axis=0, tiled=True),
        lax.all_to_all(joined[5], "fsdp", split_axis=1, concat_axis=0, tiled=True),
        lax.all_to_all(joined[7], "fsdp", split_axis=1, concat_axis=0, tiled=True),
        lax.all_to_all(joined[8], "fsdp", split_axis=1, concat_axis=0, tiled=True),
        lax.all_to_all(joined[10], "fsdp", split_axis=1, concat_axis=0, tiled=True),
    )
    pieces = (
        lax.all_gather(joined[0], "fsdp", axis=0, tiled=True),
        lax.all_gather(joined[4], "fsdp", axis=0, tiled=True),
        lax.all_gather(joined[6], "fsdp", axis=0, tiled=True),
        lax.all_gather(joined[9], "fsdp", axis=0, tiled=True),
    )
    picked = [member for member in slices]
    gain_part = lax.psum_scatter(gain_terms, "fsdp", scatter_dimension=1, tiled=True)
    summed_rows = (
        lax.psum_scatter(
            rows_product(pieces[0], picked[0]).astype(jnp.bfloat16),
            "dp",
            scatter_dimension=0,
            tiled=True,
        ).astype(jnp.float32),
        lax.psum_scatter(
            rows_product(pieces[0], picked[1]).astype(jnp.bfloat16),
            "dp",
            scatter_dimension=0,
            tiled=True,
        ).astype(jnp.float32),
        lax.psum_scatter(
            rows_product(pieces[0], picked[2]).astype(jnp.bfloat16),
            "dp",
            scatter_dimension=0,
            tiled=True,
        ).astype(jnp.float32),
        lax.psum_scatter(
            rows_product(pieces[1], picked[3]).astype(jnp.bfloat16),
            "dp",
            scatter_dimension=0,
            tiled=True,
        ).astype(jnp.float32),
        lax.psum_scatter(
            rows_product(pieces[2], picked[4]).astype(jnp.bfloat16),
            "dp",
            scatter_dimension=0,
            tiled=True,
        ).astype(jnp.float32),
        lax.psum_scatter(
            rows_product(pieces[2], picked[5]).astype(jnp.bfloat16),
            "dp",
            scatter_dimension=0,
            tiled=True,
        ).astype(jnp.float32),
        lax.psum_scatter(
            rows_product(pieces[3], picked[6]).astype(jnp.bfloat16),
            "dp",
            scatter_dimension=0,
            tiled=True,
        ).astype(jnp.float32),
    )
    gain_grad = lax.psum(gain_part, "dp")
    return (
        jnp.stack(outputs, 0),
        jnp.stack(grad_inputs, 0),
        summed_rows[0],
        summed_rows[1],
        summed_rows[2],
        summed_rows[3],
        summed_rows[4],
        summed_rows[5],
        summed_rows[6],
        gain_grad,
    )


def swap_core(value):
    return lax.ppermute(value, "fsdp", [(j, j ^ 1) for j in range(8)])


def swap_dp(value, mask):
    return lax.ppermute(value, "dp", [(j, j ^ mask) for j in range(4)])


def shift_z(value, step):
    return lax.ppermute(value, "fsdp", [(j, (j + 2 * step) % 8) for j in range(8)])


def shift_z_up(value, step):
    return lax.ppermute(value, "fsdp", [(j, j + 2 * step) for j in range(8) if j + 2 * step < 8])


def shift_z_down(value, step):
    return lax.ppermute(value, "fsdp", [(j, j - 2 * step) for j in range(8) if j - 2 * step >= 0])


def add_low(*terms):
    total = terms[0].astype(jnp.float32)
    for term in terms[1:]:
        total = total + term.astype(jnp.float32)
    return total.astype(jnp.bfloat16)


def product_nn(left, right):
    return lax.dot_general(
        left, right, (((1,), (0,)), ((), ())), preferred_element_type=jnp.float32
    )


def product_nt(left, right):
    return lax.dot_general(
        left, right, (((1,), (1,)), ((), ())), preferred_element_type=jnp.float32
    )


def product_tn(left, right):
    return lax.dot_general(
        left, right, (((0,), (0,)), ((), ())), preferred_element_type=jnp.float32
    )


VMEM = pl.BlockSpec(memory_space=pltpu.VMEM)
SMEM = pl.BlockSpec(memory_space=pltpu.SMEM)
ANY = pl.BlockSpec(memory_space=pl.ANY)


def run(body, name, ins, in_specs, outs, out_specs, scratch, flops, megabytes):
    moved = sum(v.size * v.dtype.itemsize for v in ins)
    moved += sum(v.size * v.dtype.itemsize for v in outs)
    return pl.pallas_call(
        body,
        out_shape=tuple(outs),
        in_specs=in_specs,
        out_specs=tuple(out_specs),
        scratch_shapes=scratch,
        compiler_params=pltpu.CompilerParams(vmem_limit_bytes=megabytes * 1024 * 1024),
        cost_estimate=pl.CostEstimate(flops=flops, bytes_accessed=moved, transcendentals=0),
        name=name,
    )(*ins)


def struct(shape, dtype=jnp.bfloat16):
    return jax.ShapeDtypeStruct(shape, dtype)


def column_index(ids_ref, core_rel, s):
    return 2 * lax.rem(ids_ref[1] - s + 4, 4) + (ids_ref[2] ^ core_rel)


def start_row(index, size):
    return pl.ds(pl.multiple_of(index * size, 8), size)


def after(value, *others):
    return lax.optimization_barrier((value,) + others)[0]


def pack_first_kernel(counts_ref, wq_ref, wk_ref, wv_ref, gains_ref, out_ref):
    block = wq_ref.shape[0]
    gains = gains_ref[...].astype(jnp.float32)
    row = lax.broadcasted_iota(jnp.int32, (8, block), 0)
    lane = lax.broadcasted_iota(jnp.int32, (8, block), 1)
    first = jnp.concatenate([gains[:1], gains[1:]], 1)
    used = jnp.where(
        lane == 0,
        counts_ref[0, 0].astype(jnp.float32),
        jnp.where(lane == 1, counts_ref[1, 0].astype(jnp.float32), 0.0),
    )
    extra = jnp.where(row == 0, first, jnp.where(row == 1, used, 0.0))
    full = jnp.concatenate(
        [
            wq_ref[...].astype(jnp.float32).T,
            extra,
            wk_ref[...].astype(jnp.float32).T,
            wv_ref[...].astype(jnp.float32).T,
        ],
        0,
    )
    out_ref[...] = jnp.zeros_like(out_ref)
    out_ref[:, :block] = full.astype(jnp.bfloat16)


def pack_mlp_kernel(ids_ref, wg_ref, wu_ref, wd_ref, other_ref, wo_ref, out_ref):
    block, half = wg_ref.shape
    core = ids_ref[2]
    out_ref[...] = jnp.zeros_like(out_ref)
    out_ref[:half, :block] = wg_ref[...].astype(jnp.float32).T.astype(jnp.bfloat16)
    out_ref[half : 2 * half, :block] = wu_ref[...].astype(jnp.float32).T.astype(jnp.bfloat16)
    own = wd_ref[pl.ds(pl.multiple_of(core * half, 16), half), :]
    other = other_ref[...]
    low = jnp.where(core == 0, own, other)
    high = jnp.where(core == 0, other, own)
    out_ref[2 * half : 3 * half, :block] = jnp.concatenate([low, high], 1)
    out_ref[3 * half :, :block] = jnp.concatenate(
        [wo_ref[...].astype(jnp.float32).T, jnp.zeros((8, block), jnp.float32)], 0
    ).astype(jnp.bfloat16)


def turn_in_kernel(x_ref, dy_ref, xt_ref, dyt_ref):
    xt_ref[...] = x_ref[...].astype(jnp.float32).T.astype(jnp.bfloat16)
    dyt_ref[...] = jnp.zeros_like(dyt_ref)
    dyt_ref[:, : dy_ref.shape[0]] = dy_ref[...].astype(jnp.float32).T.astype(jnp.bfloat16)


def fill_relative(ids_ref, target_ref, *sources):
    block, lanes = sources[0].shape[1], target_ref.shape[1]
    wide = target_ref.shape[0] // 4
    for k in range(4):
        parts = [source[ids_ref[0] ^ k] for source in sources]
        target_ref[k * wide : k * wide + block, :] = (
            parts[0] if len(parts) == 1 else jnp.concatenate(parts, 1)
        )
        target_ref[k * wide + block : (k + 1) * wide, :] = jnp.zeros(
            (wide - block, lanes), target_ref.dtype
        )


def wide_rows(refs, s, low, high):
    along, by_x, by_y, far_a, far_b = refs
    far = far_a if s < 2 else far_b
    return jnp.concatenate(
        [along[s, low:high], by_x[s, low:high], by_y[s, low:high], far[s % 2, low:high]], 1
    )


def project_kernel(*refs):
    ids_ref, own, other = refs[0], refs[1:6], refs[6:11]
    n1_ref, cos_ref, sin_ref, q_ref, kv_ref, proj_ref, turned_ref, rel_ref = refs[11:]
    width = n1_ref.shape[0] * n1_ref.shape[1]
    kv_width = KEY_HEADS * HEAD_WIDTH
    q_cols, k_cols = width // 8, kv_width // 8
    depth = own[0].shape[1]
    fill_relative(ids_ref, rel_ref, n1_ref)
    for core_rel, weights in ((0, own), (1, other)):
        for s in range(4):
            f = column_index(ids_ref, core_rel, s)
            total = product_nn(wide_rows(weights, s, 0, depth), rel_ref[...])
            proj_ref[start_row(f, q_cols), :] = total[:q_cols]
            proj_ref[pl.ds(pl.multiple_of(width + f * k_cols, 8), k_cols), :] = total[
                q_cols + 8 : q_cols + 8 + k_cols
            ]
            proj_ref[pl.ds(pl.multiple_of(width + kv_width + f * k_cols, 8), k_cols), :] = total[
                q_cols + 8 + k_cols :
            ]
    cosine, sine = cos_ref[...], sin_ref[...]
    half = HEAD_WIDTH // 2

    def heads(head, carry):
        front = proj_ref[pl.ds(pl.multiple_of(head * HEAD_WIDTH, 8), half), :]
        back = proj_ref[pl.ds(pl.multiple_of(head * HEAD_WIDTH + half, 8), half), :]
        q_ref[head, :half, :] = (
            (front * cosine - back * sine).astype(jnp.bfloat16) * SCORE_SCALE
        ).astype(jnp.bfloat16)
        q_ref[head, half:, :] = (
            (back * cosine + front * sine).astype(jnp.bfloat16) * SCORE_SCALE
        ).astype(jnp.bfloat16)
        return carry

    lax.fori_loop(0, QUERY_HEADS, heads, 0)
    for head in range(KEY_HEADS):
        base = width + head * HEAD_WIDTH
        front = proj_ref[base : base + half, :]
        back = proj_ref[base + half : base + 2 * half, :]
        turned_ref[head * HEAD_WIDTH : head * HEAD_WIDTH + half, :] = front * cosine - back * sine
        turned_ref[head * HEAD_WIDTH + half : (head + 1) * HEAD_WIDTH, :] = (
            back * cosine + front * sine
        )
    turned_ref[kv_width:, :] = proj_ref[width + kv_width :, :]
    kv_ref[...] = turned_ref[...].T.astype(jnp.bfloat16)


def stage_heads(mb, cap, blocks, k_ref, v_ref):
    kv_width = KEY_HEADS * HEAD_WIDTH
    for block, source in enumerate(blocks):
        rows = source[mb * cap : (mb + 1) * cap, :]
        for n in range(KEY_HEADS):
            lanes = n * HEAD_WIDTH
            k_ref[n, block * cap : (block + 1) * cap, :] = rows[:, lanes : lanes + HEAD_WIDTH]
            lanes += kv_width
            v_ref[n, block * cap : (block + 1) * cap, :] = rows[:, lanes : lanes + HEAD_WIDTH]


def stage_bias(ids_ref, counts_ref, mb, cap, share, bias_ref):
    slot = ids_ref[3]
    own_count = counts_ref[mb * 8 + slot]
    key = lax.broadcasted_iota(jnp.int32, (cap, cap), 0)
    query = lax.broadcasted_iota(jnp.int32, (cap, cap), 1)
    query_used = query < own_count
    for core_rel in range(2):
        for s in range(4):
            block = core_rel * 4 + s
            f = column_index(ids_ref, core_rel, s)
            count = counts_ref[mb * 8 + f]
            reach = jnp.where(f < slot, cap, jnp.where(f == slot, 0, -2 * cap))
            self_off = jnp.where(f == slot, 0, 2 * cap)
            allowed = (query_used & (key < count) & (key <= query + reach)) | (
                key == query + self_off
            )
            tile = jnp.where(allowed, 0.0, -1e30)
            for g in range(share):
                bias_ref[block * cap : (block + 1) * cap, g * cap : (g + 1) * cap] = tile


def join_heads(ref, n, share, mb, cap):
    return jnp.concatenate(
        [ref[share * n + g, :, mb * cap : (mb + 1) * cap] for g in range(share)], 1
    )


def attend_kernel(mb, *refs):
    ids_ref, counts_ref, q_ref = refs[:3]
    blocks = refs[3:11]
    att_ref, lse_ref, k_ref, v_ref, bias_ref = refs[11:]
    cap = q_ref.shape[2] // 2
    share = QUERY_HEADS // KEY_HEADS
    stage_heads(mb, cap, blocks, k_ref, v_ref)
    stage_bias(ids_ref, counts_ref, mb, cap, share, bias_ref)

    def body(n, carry):
        scores = product_nn(k_ref[n], join_heads(q_ref, n, share, mb, cap)) + bias_ref[...]
        top = jnp.max(scores, 0, keepdims=True)
        exponent = jnp.exp(scores - top)
        total = jnp.sum(exponent, 0, keepdims=True)
        mixed = product_tn(v_ref[n], exponent.astype(jnp.bfloat16)) / total
        mixed = mixed.astype(jnp.bfloat16)
        for g in range(share):
            att_ref[share * n + g] = mixed[:, g * cap : (g + 1) * cap]
        lse_ref[n] = top + jnp.log(total)
        return carry

    lax.fori_loop(0, KEY_HEADS, body, 0)


def attend_back_kernel(mb, *refs):
    ids_ref, counts_ref, q_ref, do_ref = refs[:4]
    blocks = refs[4:12]
    lse_ref, cos_ref, sin_ref, dq_ref = refs[12:16]
    targets = [ref.at[s] for ref in refs[16:18] for s in range(4)]
    k_ref, v_ref, bias_ref, dk_ref, dv_ref = refs[18:]
    cap = q_ref.shape[2] // 2
    share = QUERY_HEADS // KEY_HEADS
    half = HEAD_WIDTH // 2
    kv_width = KEY_HEADS * HEAD_WIDTH
    stage_heads(mb, cap, blocks, k_ref, v_ref)
    stage_bias(ids_ref, counts_ref, mb, cap, share, bias_ref)
    cosine = jnp.concatenate([cos_ref[:, mb * cap : (mb + 1) * cap]] * share, 1)
    sine = jnp.concatenate([sin_ref[:, mb * cap : (mb + 1) * cap]] * share, 1)

    def body(n, carry):
        query = join_heads(q_ref, n, share, mb, cap)
        grad = join_heads(do_ref, n, share, mb, cap)
        keys = k_ref[n]
        prob = jnp.exp(product_nn(keys, query) + bias_ref[...] - lse_ref[n])
        dprob = product_nn(v_ref[n], grad)
        delta = jnp.sum(prob * dprob, 0, keepdims=True)
        dscore = (prob * (dprob - delta)).astype(jnp.bfloat16)
        dq = product_tn(keys, dscore) * SCORE_SCALE
        front, back = dq[:half], dq[half:]
        turned = jnp.concatenate(
            [front * cosine + back * sine, back * cosine - front * sine], 0
        ).astype(jnp.bfloat16)
        for g in range(share):
            dq_ref[share * n + g] = turned[:, g * cap : (g + 1) * cap]
        dk_ref[n] = product_nt(dscore, query).astype(jnp.bfloat16)
        dv_ref[n] = product_nt(prob.astype(jnp.bfloat16), grad).astype(jnp.bfloat16)
        return carry

    lax.fori_loop(0, KEY_HEADS, body, 0)
    for block, target in enumerate(targets):
        for n in range(KEY_HEADS):
            lanes = n * HEAD_WIDTH
            target[:, lanes : lanes + HEAD_WIDTH] = dk_ref[n, block * cap : (block + 1) * cap, :]
            lanes += kv_width
            target[:, lanes : lanes + HEAD_WIDTH] = dv_ref[n, block * cap : (block + 1) * cap, :]


def collect_kernel(*refs):
    pieces, out_ref, sem = refs[:16], refs[16], refs[17]
    rows, wide = out_ref.shape[1], pieces[0].shape[1]
    copies = []
    for k in range(4):
        for s in range(4):
            copies.append(
                pltpu.make_async_copy(
                    pieces[k * 4 + s].at[pl.ds(pieces[0].shape[0] - rows, rows)],
                    out_ref.at[s, :, pl.ds(k * wide, wide)],
                    sem.at[k * 4 + s],
                )
            )
    for copy in copies:
        copy.start()
    for copy in copies:
        copy.wait()


def hidden_kernel(
    ids_ref, own_ref, other_ref, att_a_ref, att_b_ref, x_ref, gain_ref, h_ref, n2_ref, rel_ref
):
    q_cols, rows = h_ref.shape[0] // 8, h_ref.shape[1]
    fill_relative(ids_ref, rel_ref, att_a_ref, att_b_ref)
    for core_rel, w_ref in ((0, own_ref), (1, other_ref)):
        for s in range(4):
            f = column_index(ids_ref, core_rel, s)
            h_ref[start_row(f, q_cols), :] = product_nn(w_ref[s], rel_ref[...])[:q_cols]
    h = h_ref[...] + x_ref[...].astype(jnp.float32)
    h_ref[...] = h
    n2_ref[...] = jnp.zeros_like(n2_ref)
    n2_ref[:, :rows] = (h * mean_square(h) * gain_ref[...]).astype(jnp.bfloat16)


def turn_point_kernel(
    ids_ref,
    parts_ref,
    arrived_ref,
    h_ref,
    dy_ref,
    gain_ref,
    own_ref,
    other_ref,
    out_ref,
    dh_ref,
    do_ref,
    gain_grad_ref,
    pieces_ref,
    da_ref,
):
    width, rows = h_ref.shape
    q_cols = width // 8
    block = do_ref.shape[1]
    wide = own_ref.shape[2] // 4
    h = h_ref[...]
    out_ref[...] = (h + parts_ref[0] + arrived_ref[0, :, :rows].astype(jnp.float32)).astype(
        jnp.bfloat16
    )
    dn = parts_ref[1] + arrived_ref[1, :, :rows].astype(jnp.float32)
    rms = mean_square(h)
    gain_grad_ref[...] = jnp.sum(dn * h * rms, 1, keepdims=True)
    weighted = dn * gain_ref[...]
    dh = (
        dy_ref[:, :rows].astype(jnp.float32)
        + rms * weighted
        - h * (rms * rms * rms * jnp.mean(weighted * h, 0, keepdims=True))
    )
    dh_ref[...] = dh
    da_ref[...] = dh
    spread(ids_ref, da_ref, pieces_ref, q_cols)
    half = pieces_ref.shape[0] // 2
    mixed = product_tn(own_ref[...].reshape(half, 4 * wide), pieces_ref[:half, :])
    mixed += product_tn(other_ref[...].reshape(half, 4 * wide), pieces_ref[half:, :])
    mixed = mixed.astype(jnp.bfloat16)
    for k in range(4):
        do_ref[ids_ref[0] ^ k] = mixed[k * wide : k * wide + block]


def spread(ids_ref, source_ref, target_ref, cols):
    rows = source_ref.shape[1]
    for core_rel in range(2):
        for s in range(4):
            f = column_index(ids_ref, core_rel, s)
            low = (core_rel * 4 + s) * (cols + 8)
            target_ref[low : low + cols + 8, :] = jnp.concatenate(
                [source_ref[start_row(f, cols), :], jnp.zeros((8, rows), jnp.float32)], 0
            ).astype(jnp.bfloat16)


def targets_of(refs):
    return list(refs[:4]) + [refs[4].at[pl.ds(4 * k, 4)] for k in range(4)]


def out_grad_kernel(ids_ref, att_a_ref, att_b_ref, pieces_ref, *refs):
    grads, att_rel = targets_of(refs[:5]), refs[5]
    depth = pieces_ref.shape[0] // 8
    wide = att_rel.shape[0] // 4
    fill_relative(ids_ref, att_rel, att_a_ref, att_b_ref)
    for core_rel in range(2):
        for s in range(4):
            low = (core_rel * 4 + s) * depth
            got = product_nt(pieces_ref[low : low + depth, :], att_rel[...]).astype(jnp.bfloat16)
            for k in range(4):
                grads[core_rel * 4 + k][s] = got[:, k * wide : (k + 1) * wide]


def finish_q_kernel(*refs):
    ids_ref, own, other = refs[0], refs[1:6], refs[6:11]
    n1_ref, dq_a_ref, dq_b_ref = refs[11:14]
    out_grads = targets_of(refs[14:19])
    dn_ref, grads = refs[19], targets_of(refs[20:25])
    n1_rel, d_ref, dq_ref = refs[25:]
    cap = dq_a_ref.shape[1]
    width = dq_a_ref.shape[0]
    q_cols = width // 8
    depth = q_cols + 8
    block = n1_ref.shape[1]
    wide = n1_rel.shape[0] // 4
    d_ref[:, :cap] = dq_a_ref[...].astype(jnp.float32)
    d_ref[:, cap:] = dq_b_ref[...].astype(jnp.float32)
    spread(ids_ref, d_ref, dq_ref, q_cols)
    fill_relative(ids_ref, n1_rel, n1_ref)
    weights = jnp.concatenate(
        [wide_rows(w, s, 0, depth) for w in (own, other) for s in range(4)], 0
    )
    dn = product_tn(weights, dq_ref[...])
    for k in range(4):
        dn_ref[ids_ref[0] ^ k] = dn[k * wide : k * wide + block]
    for core_rel in range(2):
        for s in range(4):
            low = (core_rel * 4 + s) * depth
            gq = product_nt(dq_ref[low : low + depth, :], n1_rel[...]).astype(jnp.bfloat16)
            for k in range(4):
                target = grads[core_rel * 4 + k]
                target[s, :depth, :] = gq[:, k * wide : (k + 1) * wide]
                target[s, depth:, :] = out_grads[core_rel * 4 + k][s]


def kv_grad_kernel(
    ids_ref, n1_ref, dkv_a_ref, dkv_b_ref, cos_ref, sin_ref, dkv_ref, *refs
):
    grads = targets_of(refs[:5])
    n1_rel, d_ref = refs[5:]
    cap = dkv_a_ref.shape[0]
    kv_width = KEY_HEADS * HEAD_WIDTH
    k_cols = kv_width // 8
    half = HEAD_WIDTH // 2
    wide = n1_rel.shape[0] // 4
    cosine, sine = cos_ref[...], sin_ref[...]
    d_ref[:, :cap] = dkv_a_ref[...].T
    d_ref[:, cap:] = dkv_b_ref[...].T
    for head in range(KEY_HEADS):
        base = head * HEAD_WIDTH
        front = d_ref[base : base + half, :]
        back = d_ref[base + half : base + 2 * half, :]
        d_ref[base : base + half, :] = front * cosine + back * sine
        d_ref[base + half : base + 2 * half, :] = back * cosine - front * sine
    for core_rel in range(2):
        for s in range(4):
            f = column_index(ids_ref, core_rel, s)
            low = (core_rel * 4 + s) * 2 * k_cols
            dkv_ref[low : low + 2 * k_cols, :] = jnp.concatenate(
                [
                    d_ref[start_row(f, k_cols), :],
                    d_ref[pl.ds(pl.multiple_of(kv_width + f * k_cols, 8), k_cols), :],
                ],
                0,
            ).astype(jnp.bfloat16)
    fill_relative(ids_ref, n1_rel, n1_ref)
    for core_rel in range(2):
        for s in range(4):
            low = (core_rel * 4 + s) * 2 * k_cols
            got = product_nt(dkv_ref[low : low + 2 * k_cols, :], n1_rel[...]).astype(jnp.bfloat16)
            for k in range(4):
                grads[core_rel * 4 + k][s] = got[:, k * wide : (k + 1) * wide]


def finish_kernel(*refs):
    ids_ref, own, other = refs[0], refs[1:6], refs[6:11]
    dkv_ref, dn_ref, dh_ref, x_ref, gain_ref, tokens_ref, gain_grad_ref = refs[11:]
    width = dh_ref.shape[0]
    block = dn_ref.shape[1]
    kv_rows = dkv_ref.shape[0] // 8
    low = own[0].shape[1] - kv_rows
    wide = own[0].shape[2]
    weights = jnp.concatenate(
        [wide_rows(w, s, low, low + kv_rows) for w in (own, other) for s in range(4)], 0
    )
    dn = product_tn(weights, dkv_ref[...])
    for k in range(4):
        i = ids_ref[0] ^ k
        tokens_ref[pl.ds(pl.multiple_of(i * block, 16), block), :] = (
            dn[k * wide : k * wide + block] + dn_ref[i]
        )
    x = x_ref[...].astype(jnp.float32)
    rms = mean_square(x)
    dn = tokens_ref[...]
    gain_grad_ref[...] = jnp.sum(dn * x * rms, 1, keepdims=True)
    weighted = dn * gain_ref[...]
    tokens_ref[...] = (
        dh_ref[...]
        + rms * weighted
        - x * (rms * rms * rms * jnp.mean(weighted * x, 0, keepdims=True))
    )


def mlp_kernel(*refs):
    ids_ref, n2_own, n2_other, dy_own, dy_other = refs[:5]
    pieces = refs[5:21]
    keep_ref, send_ref = refs[21:23]
    grads = refs[23:39]
    wgu, wdn, gu_ref, prod_ref, dgu_ref, n2_rel, dy_rel, sem_in, sem_out = refs[39:]
    dp_id = ids_ref[0]
    z_id = ids_ref[1]
    block, rows = keep_ref.shape[1] // 4, keep_ref.shape[2]
    pair = 2 * rows
    wide = pieces[0].shape[1]
    half = prod_ref.shape[0] // 4

    def gate_up_part(ref, piece, k, s):
        return piece.at[pl.ds(0, 2 * half)], ref.at[
            pl.ds(s * 2 * half, 2 * half), pl.ds(k * wide, wide)
        ]

    def down_part(ref, piece, k, s):
        return piece.at[pl.ds(2 * half, half)], ref.at[
            pl.ds(k * half, half), pl.ds(s * wide, wide)
        ]

    loads, more_loads = [], []
    for s in range(4):
        for k in range(4):
            source, target = gate_up_part(wgu, pieces[k * 4 + s], k, s)
            loads.append(pltpu.make_async_copy(source, target, sem_in.at[0, k * 4 + s]))
            source, target = down_part(wdn, pieces[k * 4 + s], k, s)
            more_loads.append(pltpu.make_async_copy(source, target, sem_in.at[1, k * 4 + s]))
    for load in loads + more_loads:
        load.start()
    pad = jnp.zeros((wide - block, pair), jnp.bfloat16)
    for j in range(4):
        i = dp_id ^ j
        zz = lax.rem(z_id - j + 4, 4)
        n2_rel[j * wide : j * wide + block, :] = jnp.concatenate(
            [n2_own[i][:, :rows], n2_other[i][:, :rows]], 1
        )
        dy_rel[j * wide : j * wide + block, :] = jnp.concatenate(
            [dy_own[zz][:, :rows], dy_other[zz][:, :rows]], 1
        )
        n2_rel[j * wide + block : (j + 1) * wide, :] = pad
        dy_rel[j * wide + block : (j + 1) * wide, :] = pad

    def rows_of(index, size):
        return pl.ds(pl.multiple_of(index * size, 16), size)

    for s in range(4):
        for load in loads[4 * s : 4 * s + 4]:
            load.wait()
        k = lax.rem(z_id - s + 4, 4) ^ dp_id
        total = product_nn(wgu[s * 2 * half : (s + 1) * 2 * half, :], n2_rel[...])
        gu_ref[rows_of(k, 2 * half), :] = total
        gate = total[:half]
        prod_ref[rows_of(k, half), :] = (gate * jax.nn.sigmoid(gate) * total[half:]).astype(
            jnp.bfloat16
        )
    for load in more_loads:
        load.wait()
    for k in range(4):
        s = lax.rem(z_id - (dp_id ^ k) + 4, 4)
        dprod = product_nn(wdn[k * half : (k + 1) * half, :], dy_rel[...])
        gate = gu_ref[k * 2 * half : k * 2 * half + half, :]
        up = gu_ref[k * 2 * half + half : (k + 1) * 2 * half, :]
        sig = jax.nn.sigmoid(gate)
        dgu_ref[rows_of(s, 2 * half), :] = jnp.concatenate(
            [dprod * up * sig * (1.0 + gate * (1.0 - sig)), dprod * gate * sig], 0
        ).astype(jnp.bfloat16)
    for j in range(4):
        lanes = slice(j * wide, (j + 1) * wide)
        out = product_tn(wdn[:, lanes], prod_ref[...])[:block]
        zz = rows_of(lax.rem(z_id - j + 4, 4), block)
        keep_ref[0, zz, :] = out[:, :rows]
        send_ref[0, zz, :rows] = out[:, rows:].astype(jnp.bfloat16)
    for k in range(4):
        here = slice(k * half, (k + 1) * half)
        wdn[here, :] = product_nt(prod_ref[here, :], dy_rel[...]).astype(jnp.bfloat16)
    stores = []
    for k in range(4):
        for s in range(4):
            target, source = down_part(wdn, grads[k * 4 + s], k, s)
            stores.append(pltpu.make_async_copy(source, target, sem_out.at[1, k * 4 + s]))
    for store in stores:
        store.start()
    for j in range(4):
        lanes = slice(j * wide, (j + 1) * wide)
        dn = product_tn(wgu[:, lanes], dgu_ref[...])[:block]
        i = rows_of(dp_id ^ j, block)
        keep_ref[1, i, :] = dn[:, :rows]
        send_ref[1, i, :rows] = dn[:, rows:].astype(jnp.bfloat16)
    send_ref[:, :, rows:] = jnp.zeros((2, 4 * block, send_ref.shape[2] - rows), jnp.bfloat16)
    for s in range(4):
        here = slice(s * 2 * half, (s + 1) * 2 * half)
        wgu[here, :] = product_nt(dgu_ref[here, :], n2_rel[...]).astype(jnp.bfloat16)
        for k in range(4):
            target, source = gate_up_part(wgu, grads[k * 4 + s], k, s)
            store = pltpu.make_async_copy(source, target, sem_out.at[0, k * 4 + s])
            store.start()
            stores.append(store)
    for store in stores:
        store.wait()


def mean_square(values):
    return lax.rsqrt(jnp.mean(values * values, 0, keepdims=True) + EPSILON)


def fast(
    tokens, cotangent, counts, w_query, key_weight, value_weight, w_out, w_gate, w_up, w_down, gains
):
    dp_id = lax.axis_index("dp")
    slot = lax.axis_index("fsdp")
    z_id = slot // 2
    core_id = slot % 2
    ids = jnp.stack([dp_id, z_id, core_id, slot]).astype(jnp.int32)
    batches, cap, width = tokens.shape
    rows = batches * cap
    block = w_query.shape[0]
    wide = -(-block // 128) * 128
    q_cols, k_cols = w_query.shape[1], key_weight.shape[1]
    half = w_gate.shape[1]
    kv_width = KEY_HEADS * HEAD_WIDTH
    share = QUERY_HEADS // KEY_HEADS
    q_rows = q_cols + 8
    depth = q_rows + 2 * k_cols
    mlp_rows = 3 * half + q_rows
    padded = -(-rows // 128) * 128

    (first_piece,) = run(
        pack_first_kernel,
        "pack_first",
        (counts, w_query, key_weight, value_weight, gains),
        [SMEM] + [VMEM] * 4,
        [struct((depth, wide))],
        [VMEM],
        [],
        0,
        16,
    )
    chain = [first_piece] + [shift_z(first_piece, step) for step in (1, 2, 3)]
    down_halves = w_down.reshape(2, half, -1)
    other_down = swap_core(
        lax.dynamic_index_in_dim(down_halves, 1 - core_id, 0, keepdims=False)
    )
    (mlp_piece,) = run(
        pack_mlp_kernel,
        "pack_mlp",
        (ids, w_gate, w_up, w_down, other_down, w_out),
        [SMEM] + [VMEM] * 5,
        [struct((mlp_rows, wide))],
        [VMEM],
        [],
        0,
        16,
    )
    x, dy = run(
        turn_in_kernel,
        "turn_in",
        (tokens.reshape(rows, width), cotangent.reshape(rows, width)),
        [VMEM] * 2,
        [struct((width, rows)), struct((width, padded))],
        [VMEM] * 2,
        [],
        0,
        16,
    )

    along = jnp.stack(chain, 0)
    extras = along[:, q_cols : q_cols + 2, :block]
    other_extras = swap_core(extras)
    x_zero, y_zero = swap_dp(mlp_piece, 1), swap_dp(mlp_piece, 2)
    along_next = after(along, x_zero, y_zero)
    from_x = swap_dp(along_next, 1)
    from_y = swap_dp(along_next, 2)
    first_own = [along, from_x, from_y, swap_dp(from_x[:2], 2), swap_dp(from_y[2:], 1)]
    first_other = [swap_core(piece) for piece in first_own]

    z_one = shift_z(after(mlp_piece, along), 1)
    z_two = shift_z(z_one, 1)
    z_three = shift_z(z_two, 1)
    far_zero = swap_dp(after(x_zero, *first_own[3:]), 2)
    z_one_next = after(z_one, *first_own[3:])
    x_one = swap_dp(z_one_next, 1)

    by_core = jnp.where(
        core_id == 0, jnp.stack([extras, other_extras], 1), jnp.stack([other_extras, extras], 1)
    )
    by_core = by_core[::-1]
    by_core = lax.dynamic_slice_in_dim(jnp.concatenate([by_core, by_core], 0), 3 - z_id, 4, 0)
    gain = by_core[:, :, 0, :].reshape(8, 2, q_cols).transpose(0, 2, 1).reshape(width, 2)
    gain = gain.astype(jnp.float32)
    gain_one, gain_two = gain[:, :1], gain[:, 1:]
    group_counts = by_core[:, :, 1, :batches].reshape(8, batches).astype(jnp.int32)
    flat_counts = group_counts.T.reshape(-1)
    before = jnp.sum(
        jnp.where(jnp.arange(8, dtype=jnp.int32)[:, None] < slot, group_counts, 0), 0
    )
    position = (before[:, None] + jnp.arange(cap, dtype=jnp.int32)[None, :]).reshape(-1)
    cosine, sine = rope_tables(position, HEAD_WIDTH)
    cosine, sine = cosine[:, 0, :].T, sine[:, 0, :].T
    x_wide = x.astype(jnp.float32)
    n1 = (x_wide * mean_square(x_wide) * gain_one).astype(jnp.bfloat16).reshape(4, block, rows)
    n1_next = after(n1, z_two)

    query, kv = run(
        project_kernel,
        "project",
        (ids, *first_own, *first_other, n1_next, cosine, sine),
        [SMEM] + [VMEM] * 13,
        (struct((QUERY_HEADS, HEAD_WIDTH, rows)), struct((rows, 2 * kv_width))),
        [VMEM] * 2,
        [
            pltpu.VMEM((width + 2 * kv_width, rows), jnp.float32),
            pltpu.VMEM((2 * kv_width, rows), jnp.float32),
            pltpu.VMEM((4 * wide, rows), jnp.bfloat16),
        ],
        2 * (width + 2 * kv_width) * width * rows,
        24,
    )
    kv_zero = after(kv, x_one, far_zero)
    kv_one = shift_z_up(kv_zero, 1)
    x_two = swap_dp(after(z_two, kv_zero), 1)
    y_one = swap_dp(after(z_one, kv_zero), 2)
    wave = (kv_one, x_two, y_one, z_three)
    kv_two = shift_z_up(after(*wave), 1)
    far_one = swap_dp(after(y_one, *wave), 1)
    y_two = swap_dp(after(z_two, *wave), 2)
    wave = (kv_two, far_one, y_two)
    kv_three = shift_z_up(after(*wave), 1)
    x_three = swap_dp(after(z_three, *wave), 1)
    y_three = swap_dp(after(z_three, *wave), 2)
    wave = (kv_three, x_three, y_three)
    far_two = swap_dp(after(x_two, *wave), 2)
    far_three = swap_dp(after(y_three, *wave), 1)
    kv_own = [kv, kv_one, kv_two, kv_three]
    kv_other = [swap_core(piece) for piece in (kv_zero, kv_one, kv_two, kv_three)]
    pieces = [mlp_piece, z_one, z_two, z_three]
    pieces += [x_zero, x_one, x_two, x_three]
    pieces += [y_zero, y_one, y_two, y_three]
    pieces += [far_zero, far_one, far_two, far_three]

    pair_flops = 2 * QUERY_HEADS * HEAD_WIDTH * rows * 8 * cap
    head_scratch = [
        pltpu.VMEM((KEY_HEADS, 8 * cap, HEAD_WIDTH), jnp.bfloat16),
        pltpu.VMEM((KEY_HEADS, 8 * cap, HEAD_WIDTH), jnp.bfloat16),
        pltpu.VMEM((8 * cap, share * cap), jnp.float32),
    ]
    def attend(mb, queries):
        return run(
            functools.partial(attend_kernel, mb),
            "attend",
            (ids, flat_counts, queries, *kv_own, *kv_other),
            [SMEM, SMEM] + [VMEM] * 9,
            (
                struct((QUERY_HEADS, HEAD_WIDTH, cap)),
                struct((KEY_HEADS, 1, share * cap), jnp.float32),
            ),
            [VMEM] * 2,
            head_scratch,
            4 * pair_flops,
            24,
        )

    att_a, lse_a = attend(0, after(query, x_three, y_three))
    (out_own,) = run(
        collect_kernel,
        "collect",
        tuple(pieces[:15]) + (after(far_three, att_a),),
        [ANY] * 16,
        [struct((4, q_rows, 4 * wide))],
        [VMEM],
        [pltpu.SemaphoreType.DMA((16,))],
        0,
        8,
    )
    out_other = swap_core(out_own)
    dy_other = swap_core(after(dy, att_a))
    att_b, lse_b = attend(1, after(query, out_own))
    att_a = att_a.reshape(4, block, cap)
    att_b = att_b.reshape(4, block, cap)
    lse = (lse_a, lse_b)
    blocks = (4, block, rows)
    wide_blocks = (4, block, padded)
    h, n2 = run(
        hidden_kernel,
        "hidden",
        (ids, out_own, out_other, att_a, att_b, after(x, dy_other), gain_two),
        [SMEM] + [VMEM] * 6,
        (struct((width, rows), jnp.float32), struct((width, padded))),
        [VMEM] * 2,
        [pltpu.VMEM((4 * wide, rows), jnp.bfloat16)],
        2 * width * width * rows,
        24,
    )
    n2_other = swap_core(n2)
    results = run(
        mlp_kernel,
        "mlp",
        (
            ids,
            n2.reshape(wide_blocks),
            n2_other.reshape(wide_blocks),
            dy.reshape(wide_blocks),
            dy_other.reshape(wide_blocks),
            *pieces,
        ),
        [SMEM] + [VMEM] * 4 + [ANY] * 16,
        [struct((2, width, rows), jnp.float32), struct((2, width, padded))]
        + [struct((3 * half, wide))] * 16,
        [VMEM] * 2 + [ANY] * 16,
        [
            pltpu.VMEM((8 * half, 4 * wide), jnp.bfloat16),
            pltpu.VMEM((4 * half, 4 * wide), jnp.bfloat16),
            pltpu.VMEM((8 * half, 2 * rows), jnp.float32),
            pltpu.VMEM((4 * half, 2 * rows), jnp.bfloat16),
            pltpu.VMEM((8 * half, 2 * rows), jnp.bfloat16),
            pltpu.VMEM((4 * wide, 2 * rows), jnp.bfloat16),
            pltpu.VMEM((4 * wide, 2 * rows), jnp.bfloat16),
            pltpu.SemaphoreType.DMA((2, 16)),
            pltpu.SemaphoreType.DMA((2, 16)),
        ],
        18 * 16 * half * block * 2 * rows,
        44,
    )
    keep, send = results[:2]
    home, to_x, to_y, far = results[2:6], results[6:10], results[10:14], results[14:18]
    arrived = swap_core(send)
    via_three, via_two = swap_dp(far[3], 1), swap_dp(far[2], 2)

    output, dh, mixed_gradient, gain_two_grad, da_pieces = run(
        turn_point_kernel,
        "turn_point",
        (ids, keep, arrived, h, dy, gain_two, out_own, out_other),
        [SMEM] + [VMEM] * 7,
        (
            struct((width, rows)),
            struct((width, rows), jnp.float32),
            struct(blocks),
            struct((width, 1), jnp.float32),
            struct((8 * q_rows, rows)),
        ),
        [VMEM] * 5,
        [pltpu.VMEM((width, rows), jnp.float32)],
        2 * width * width * rows,
        24,
    )
    output = output.T.reshape(batches, cap, width)
    def attend_back(mb, mixed):
        return run(
            functools.partial(attend_back_kernel, mb),
            "attend_back",
            (
                ids,
                flat_counts,
                query,
                mixed.reshape(QUERY_HEADS, HEAD_WIDTH, rows),
                *kv_own,
                *kv_other,
                lse[mb],
                cosine,
                sine,
            ),
            [SMEM, SMEM] + [VMEM] * 13,
            [struct((QUERY_HEADS, HEAD_WIDTH, cap))] + [struct((4, cap, 2 * kv_width))] * 2,
            [VMEM] * 3,
            head_scratch
            + [
                pltpu.VMEM((KEY_HEADS, 8 * cap, HEAD_WIDTH), jnp.bfloat16),
                pltpu.VMEM((KEY_HEADS, 8 * cap, HEAD_WIDTH), jnp.bfloat16),
            ],
            10 * pair_flops,
            24,
        )

    def sum_cores(own, other):
        arrived = swap_core(other)
        return [add_low(own[s], arrived[s]) for s in range(4)]

    def sum_z(summed):
        total = summed[0].astype(jnp.float32)
        for s in (3, 2, 1):
            total = total + shift_z_down(summed[s], s).astype(jnp.float32)
        return total

    wave = (via_three, via_two, mixed_gradient)
    x_three, y_two = swap_dp(after(to_x[3], *wave), 1), swap_dp(after(to_y[2], *wave), 2)
    x_two = swap_dp(add_low(to_x[2], after(via_two, *wave)), 1)
    y_three = swap_dp(add_low(to_y[3], after(via_three, *wave)), 2)
    back_a = attend_back(0, after(mixed_gradient, *wave))
    wave = (back_a[0], x_three, y_two, x_two, y_three)
    via_one, via_zero = swap_dp(after(far[1], *wave), 1), swap_dp(after(far[0], *wave), 2)
    hop = shift_z(add_low(after(home[3], back_a[0]), x_three, y_three), -1)
    out_grads = run(
        out_grad_kernel,
        "out_grad",
        (ids, att_a, att_b, after(da_pieces, *wave)),
        [SMEM] + [VMEM] * 3,
        [struct((4, q_rows, wide))] * 4 + [struct((16, q_rows, wide))],
        [VMEM] * 5,
        [pltpu.VMEM((4 * wide, rows), jnp.bfloat16)],
        2 * width * width * rows,
        16,
    )
    summed_a = sum_cores(*back_a[1:])
    wave = (via_one, via_zero, hop, out_grads[0])
    dkv_a = sum_z([after(piece, *wave) for piece in summed_a])
    x_one, y_zero = swap_dp(after(to_x[1], *wave), 1), swap_dp(after(to_y[0], *wave), 2)
    back_b = attend_back(1, after(mixed_gradient, *summed_a, *wave))
    wave = (back_b[0], dkv_a, x_one, y_zero)
    x_zero = swap_dp(add_low(to_x[0], after(via_zero, *wave)), 1)
    y_one = swap_dp(add_low(to_y[1], after(via_one, *wave)), 2)
    summed_b = sum_cores(back_b[1], after(back_b[2], dkv_a, x_one, y_zero))
    parts_b = [shift_z_down(summed_b[s], s) for s in (1, 2, 3)]
    def sum_pair(parts):
        arrived = swap_core(parts[4])
        return [add_low(parts[k], arrived[4 * k : 4 * k + 4]) for k in range(4)]

    def reduce_all(mine):
        summed = [mine[0]] + [swap_dp(mine[k], k) for k in (1, 2, 3)]
        out = [add_low(*[piece[s] for piece in summed]) for s in range(4)]
        total = out[0].astype(jnp.float32)
        for s in (1, 2, 3):
            total = total + shift_z(out[s], -s).astype(jnp.float32)
        return total

    q_results = run(
        finish_q_kernel,
        "finish_q",
        (
            ids,
            *first_own,
            *first_other,
            after(n1, *wave, *summed_b),
            back_a[0].reshape(width, cap),
            back_b[0].reshape(width, cap),
            *out_grads,
        ),
        [SMEM] + [VMEM] * 18,
        [struct(blocks, jnp.float32)]
        + [struct((4, 2 * q_rows, wide))] * 4
        + [struct((16, 2 * q_rows, wide))],
        [VMEM] * 6,
        [
            pltpu.VMEM((4 * wide, rows), jnp.bfloat16),
            pltpu.VMEM((width, rows), jnp.float32),
            pltpu.VMEM((8 * q_rows, rows), jnp.bfloat16),
        ],
        4 * width * width * rows,
        24,
    )
    dn_q = q_results[0]
    dkv_b = after(summed_b[0], dn_q).astype(jnp.float32)
    for part in parts_b:
        dkv_b = dkv_b + part.astype(jnp.float32)
    hop = shift_z(add_low(home[2], x_two, y_two, after(hop, dkv_b)), -1)
    q_out_mine = sum_pair(q_results[1:])
    q_out_total = reduce_all(q_out_mine)
    grad_query = q_out_total[:q_cols, :block].T
    grad_out = q_out_total[q_rows : q_rows + q_cols, :block].T

    dkv_pieces, *kv_grads = run(
        kv_grad_kernel,
        "kv_grad",
        (ids, after(n1, x_zero, y_one, *q_out_mine), dkv_a, dkv_b, cosine, sine),
        [SMEM] + [VMEM] * 5,
        [struct((16 * k_cols, rows))]
        + [struct((4, 2 * k_cols, wide))] * 4
        + [struct((16, 2 * k_cols, wide))],
        [VMEM] * 6,
        [
            pltpu.VMEM((4 * wide, rows), jnp.bfloat16),
            pltpu.VMEM((2 * kv_width, rows), jnp.float32),
        ],
        4 * kv_width * width * rows,
        20,
    )
    grad_tokens, gain_one_grad = run(
        finish_kernel,
        "finish",
        (ids, *first_own, *first_other, dkv_pieces, dn_q, dh, x, gain_one),
        [SMEM] + [VMEM] * 15,
        [struct((width, rows), jnp.float32), struct((width, 1), jnp.float32)],
        [VMEM] * 2,
        [],
        4 * kv_width * width * rows,
        24,
    )
    grad_tokens = grad_tokens.T.reshape(batches, cap, width)
    hop = shift_z(add_low(home[1], x_one, y_one, after(hop, dkv_pieces)), -1)
    mlp_total = (
        home[0].astype(jnp.float32)
        + y_zero.astype(jnp.float32)
        + x_zero.astype(jnp.float32)
        + hop.astype(jnp.float32)
    )
    grad_gate = mlp_total[:half, :block].T
    grad_up = mlp_total[half : 2 * half, :block].T
    down_total = mlp_total[2 * half :, :block]
    left, right = down_total[:, :q_cols], down_total[:, q_cols:]
    stay = jnp.where(core_id == 0, left, right)
    give = jnp.where(core_id == 0, right, left).astype(jnp.bfloat16)
    taken = swap_core(give).astype(jnp.float32)
    grad_down = jnp.where(
        core_id == 0, jnp.concatenate([stay, taken], 0), jnp.concatenate([taken, stay], 0)
    )

    kv_mine = sum_pair(kv_grads)
    kv_total = reduce_all(kv_mine)
    gain_total = after(jnp.concatenate([gain_one_grad, gain_two_grad], 1).T, *kv_mine)
    gain_total = gain_total + swap_core(gain_total)
    gain_total = gain_total + swap_dp(gain_total, 1)
    gain_total = gain_total + swap_dp(gain_total, 2)
    for mask in (2, 4):
        gain_total = gain_total + lax.ppermute(
            gain_total, "fsdp", [(j, j ^ mask) for j in range(8)]
        )
    gain_grad = lax.dynamic_slice_in_dim(gain_total, slot * q_cols, q_cols, 1)
    return (
        output,
        grad_tokens,
        grad_query,
        kv_total[:k_cols, :block].T,
        kv_total[k_cols:, :block].T,
        grad_out,
        grad_gate,
        grad_up,
        grad_down,
        gain_grad,
    )


def solution(mesh):
    in_specs = (
        P(None, ("dp", "fsdp"), None),
        P(None, ("dp", "fsdp"), None),
        P(None, ("dp", "fsdp")),
        P("dp", "fsdp"),
        P("dp", "fsdp"),
        P("dp", "fsdp"),
        P("dp", "fsdp"),
        P("dp", "fsdp"),
        P("dp", "fsdp"),
        P("dp", "fsdp"),
        P(None, "fsdp"),
    )
    out_specs = (
        P(None, ("dp", "fsdp"), None),
        P(None, ("dp", "fsdp"), None),
        P("dp", "fsdp"),
        P("dp", "fsdp"),
        P("dp", "fsdp"),
        P("dp", "fsdp"),
        P("dp", "fsdp"),
        P("dp", "fsdp"),
        P("dp", "fsdp"),
        P(None, "fsdp"),
    )
    square = mesh.shape["dp"] == 4 and mesh.shape["fsdp"] == 8
    return jax.shard_map(
        fast if square else local, mesh=mesh, in_specs=in_specs, out_specs=out_specs, check_vma=False)
```

```python
import functools

import jax
import jax.numpy as jnp
from jax import lax
from jax.experimental import pallas as pl
from jax.experimental.pallas import tpu as pltpu
from jax.sharding import PartitionSpec as P

MODEL_WIDTH = 960
QUERY_HEADS = 15
KEY_HEADS = 5
HEAD_WIDTH = 64


EPSILON = 1e-05
ROPE_BASE = 100000.0
SCORE_SCALE = 0.125


def rope_tables(position, head_size):
    half_size = head_size // 2
    frequency = ROPE_BASE ** (-(jnp.arange(half_size, dtype=jnp.float32) * 2.0) / head_size)
    angles = position.astype(jnp.float32)[:, None] * frequency[None, :]
    return (jnp.cos(angles)[:, None, :], jnp.sin(angles)[:, None, :])


def apply_rotation(values, cosine_table, sine_values):
    half_size = values.shape[-1] // 2
    front_half = values[..., :half_size]
    back_half = values[..., half_size:]
    return jnp.concatenate(
        [
            front_half * cosine_table - back_half * sine_values,
            back_half * cosine_table + front_half * sine_values,
        ],
        -1,
    )


def normalize(values, gain_row):
    inv_rms = lax.rsqrt(jnp.mean(values * values, -1, keepdims=True) + EPSILON)
    return (values * inv_rms * gain_row, inv_rms)


def norm_back(values, inv_rms, gain_row, incoming):
    weighted = incoming * gain_row
    return inv_rms * weighted - values * inv_rms * inv_rms * inv_rms * jnp.mean(
        weighted * values, -1, keepdims=True
    )


def build_mask(count_row, device, slot_capacity):
    group_width = count_row.shape[0]
    local_slot = jnp.arange(slot_capacity, dtype=jnp.int32)
    offsets = jnp.cumsum(count_row) - count_row
    is_mine = jnp.arange(group_width, dtype=jnp.int32) == device
    own_offset = jnp.sum(jnp.where(is_mine, offsets, 0))
    own_count = jnp.sum(jnp.where(is_mine, count_row, 0))
    query_pos = own_offset + local_slot
    query_valid = local_slot < own_count
    key_pos = (offsets[:, None] + local_slot[None, :]).reshape(-1)
    key_valid = (local_slot[None, :] < count_row[:, None]).reshape(-1)
    slot_ids = jnp.arange(group_width * slot_capacity, dtype=jnp.int32)
    own_slots = device * slot_capacity + local_slot
    allowed = query_valid[:, None] & key_valid[None, :] & (
        key_pos[None, :] <= query_pos[:, None]
    ) | (slot_ids[None, :] == own_slots[:, None])
    return (allowed, query_pos)


def kept_fetch(w_query, key_weight, value_weight, w_out, w_gate, w_up, w_down, gains):
    columns = (
        lax.all_gather(w_query, "fsdp", axis=1, tiled=True),
        lax.all_gather(key_weight, "fsdp", axis=1, tiled=True),
        lax.all_gather(value_weight, "fsdp", axis=1, tiled=True),
        lax.all_gather(w_out, "fsdp", axis=1, tiled=True),
        lax.all_gather(w_gate, "fsdp", axis=1, tiled=True),
        lax.all_gather(w_up, "fsdp", axis=1, tiled=True),
        lax.all_gather(w_down, "fsdp", axis=1, tiled=True),
        lax.all_gather(gains, "fsdp", axis=1, tiled=True),
    )
    matrices = (
        lax.all_gather(columns[0], "dp", axis=0, tiled=True),
        lax.all_gather(columns[1], "dp", axis=0, tiled=True),
        lax.all_gather(columns[2], "dp", axis=0, tiled=True),
        lax.all_gather(columns[3], "dp", axis=0, tiled=True),
        lax.all_gather(columns[4], "dp", axis=0, tiled=True),
        lax.all_gather(columns[5], "dp", axis=0, tiled=True),
        lax.all_gather(columns[6], "dp", axis=0, tiled=True),
    )
    return (matrices, columns[7].astype(jnp.float32))


def times_transpose(left, right):
    return jnp.einsum("rk,jk->rj", left, right, preferred_element_type=jnp.float32)


def rows_product(left, right):
    return jnp.einsum("rd,rk->dk", left, right, preferred_element_type=jnp.float32)


def local(
    tokens, cotangent, counts, w_query, key_weight, value_weight, w_out, w_gate, w_up, w_down, gains
):
    group_counts = lax.all_gather(counts, "fsdp", axis=1, tiled=True)
    device = lax.axis_index("fsdp")
    slot_capacity = tokens.shape[1]
    key_value_width = KEY_HEADS * HEAD_WIDTH
    device_share = QUERY_HEADS // KEY_HEADS
    kept_weights, kept_gain = kept_fetch(
        w_query, key_weight, value_weight, w_out, w_gate, w_up, w_down, gains
    )
    outputs = []
    grad_inputs = []
    saved = [[] for index_unused in range(11)]
    gain_one_total = jnp.zeros((MODEL_WIDTH,), jnp.float32)
    gain_two_total = jnp.zeros((MODEL_WIDTH,), jnp.float32)
    for micro_idx in range(tokens.shape[0]):
        matrices, gain_pair = (kept_weights, kept_gain)
        full_query, full_key, full_value, full_out, full_gate, full_up, full_down = matrices
        inputs = tokens[micro_idx].astype(jnp.float32)
        allowed, query_pos = build_mask(group_counts[micro_idx], device, slot_capacity)
        cosine_table, sine_values = rope_tables(query_pos, HEAD_WIDTH)
        first_normed, scale_one = normalize(inputs, gain_pair[0])
        normed_low = first_normed.astype(jnp.bfloat16)
        reduced_query = apply_rotation(
            jnp.dot(normed_low, full_query, preferred_element_type=jnp.float32).reshape(
                slot_capacity, QUERY_HEADS, HEAD_WIDTH
            ),
            cosine_table,
            sine_values,
        ).astype(jnp.bfloat16)
        key_low = (
            apply_rotation(
                jnp.dot(normed_low, full_key, preferred_element_type=jnp.float32).reshape(
                    slot_capacity, KEY_HEADS, HEAD_WIDTH
                ),
                cosine_table,
                sine_values,
            )
            .astype(jnp.bfloat16)
            .reshape(slot_capacity, key_value_width)
        )
        value_low = jnp.dot(normed_low, full_value, preferred_element_type=jnp.float32).astype(
            jnp.bfloat16
        )
        grouped_keys, grouped_values = (
            lax.all_gather(key_low, "fsdp", axis=0, tiled=True),
            lax.all_gather(value_low, "fsdp", axis=0, tiled=True),
        )
        heads_of_key = grouped_keys.reshape(-1, KEY_HEADS, HEAD_WIDTH)
        heads_of_value = grouped_values.reshape(-1, KEY_HEADS, HEAD_WIDTH)
        heads_of_query = reduced_query.reshape(slot_capacity, KEY_HEADS, device_share, HEAD_WIDTH)
        scores = (
            jnp.einsum(
                "qngd,knd->ngqk", heads_of_query, heads_of_key, preferred_element_type=jnp.float32
            )
            * SCORE_SCALE
        )
        masked = jnp.where(allowed, scores, -1e30)
        row_top = jnp.max(masked, -1, keepdims=True)
        exponent = jnp.where(allowed, jnp.exp(masked - row_top), 0.0)
        row_total = jnp.sum(exponent, -1, keepdims=True)
        prob_low = (exponent / row_total).astype(jnp.bfloat16)
        log_total = row_top + jnp.log(row_total)
        mixed_heads = jnp.einsum(
            "ngqk,knd->qngd", prob_low, heads_of_value, preferred_element_type=jnp.float32
        ).reshape(slot_capacity, MODEL_WIDTH)
        attended = mixed_heads.astype(jnp.bfloat16)
        hidden_state = inputs + jnp.dot(attended, full_out, preferred_element_type=jnp.float32)
        normed_two, scale_two = normalize(hidden_state, gain_pair[1])
        normed_two_low = normed_two.astype(jnp.bfloat16)
        gate_act = jnp.dot(normed_two_low, full_gate, preferred_element_type=jnp.float32)
        upward = jnp.dot(normed_two_low, full_up, preferred_element_type=jnp.float32)
        sigmoid_gate = jax.nn.sigmoid(gate_act)
        product = (gate_act * sigmoid_gate * upward).astype(jnp.bfloat16)
        outputs.append(
            (hidden_state + jnp.dot(product, full_down, preferred_element_type=jnp.float32)).astype(
                jnp.bfloat16
            )
        )
        matrices, gain_pair = (kept_weights, kept_gain)
        full_query, full_key, full_value, full_out, full_gate, full_up, full_down = matrices
        grad_low = cotangent[micro_idx]
        grad_product = times_transpose(grad_low, full_down)
        grad_gate = (
            grad_product * upward * sigmoid_gate * (1.0 + gate_act * (1.0 - sigmoid_gate))
        ).astype(jnp.bfloat16)
        grad_upward = (grad_product * gate_act * sigmoid_gate).astype(jnp.bfloat16)
        grad_normed_two = times_transpose(grad_gate, full_gate) + times_transpose(
            grad_upward, full_up
        )
        gain_two_total = gain_two_total + jnp.sum(grad_normed_two * hidden_state * scale_two, 0)
        grad_hidden = grad_low.astype(jnp.float32) + norm_back(
            hidden_state, scale_two, gain_pair[1], grad_normed_two
        )
        grad_branch = grad_hidden.astype(jnp.bfloat16)
        mixed_gradient = times_transpose(grad_branch, full_out).astype(jnp.bfloat16)
        head_gradient = mixed_gradient.reshape(slot_capacity, KEY_HEADS, device_share, HEAD_WIDTH)
        again_scores = (
            jnp.einsum(
                "qngd,knd->ngqk", heads_of_query, heads_of_key, preferred_element_type=jnp.float32
            )
            * SCORE_SCALE
        )
        probability = jnp.where(allowed, jnp.exp(again_scores - log_total), 0.0)
        grad_prob = jnp.einsum(
            "qngd,knd->ngqk", head_gradient, heads_of_value, preferred_element_type=jnp.float32
        )
        row_delta = jnp.sum(probability * grad_prob, -1, keepdims=True)
        grad_scores = (probability * (grad_prob - row_delta)).astype(jnp.bfloat16)
        grad_query_rot = (
            jnp.einsum(
                "ngqk,knd->qngd", grad_scores, heads_of_key, preferred_element_type=jnp.float32
            ).reshape(slot_capacity, QUERY_HEADS, HEAD_WIDTH)
            * SCORE_SCALE
        )
        key_part = (
            jnp.einsum(
                "ngqk,qngd->knd", grad_scores, heads_of_query, preferred_element_type=jnp.float32
            ).reshape(-1, key_value_width)
            * SCORE_SCALE
        )
        value_part = jnp.einsum(
            "ngqk,qngd->knd",
            probability.astype(jnp.bfloat16),
            head_gradient,
            preferred_element_type=jnp.float32,
        ).reshape(-1, key_value_width)
        key_gradient, value_grad = (
            lax.psum_scatter(
                key_part.astype(jnp.bfloat16), "fsdp", scatter_dimension=0, tiled=True
            ).astype(jnp.float32),
            lax.psum_scatter(
                value_part.astype(jnp.bfloat16), "fsdp", scatter_dimension=0, tiled=True
            ).astype(jnp.float32),
        )
        grad_query = (
            apply_rotation(grad_query_rot, cosine_table, -sine_values)
            .astype(jnp.bfloat16)
            .reshape(slot_capacity, MODEL_WIDTH)
        )
        grad_key = (
            apply_rotation(
                key_gradient.reshape(slot_capacity, KEY_HEADS, HEAD_WIDTH),
                cosine_table,
                -sine_values,
            )
            .astype(jnp.bfloat16)
            .reshape(slot_capacity, key_value_width)
        )
        grad_value = value_grad.astype(jnp.bfloat16)
        grad_normed_one = (
            times_transpose(grad_query, full_query)
            + times_transpose(grad_key, full_key)
            + times_transpose(grad_value, full_value)
        )
        gain_one_total = gain_one_total + jnp.sum(grad_normed_one * inputs * scale_one, 0)
        grad_inputs.append(
            grad_hidden + norm_back(inputs, scale_one, gain_pair[0], grad_normed_one)
        )
        kept_rows = (
            normed_low,
            grad_query,
            grad_key,
            grad_value,
            attended,
            grad_branch,
            normed_two_low,
            grad_gate,
            grad_upward,
            product,
            grad_low,
        )
        for slot_index in range(11):
            saved[slot_index].append(kept_rows[slot_index])
    joined = [jnp.concatenate(column_list, 0) for column_list in saved]
    gain_terms = jnp.stack([gain_one_total, gain_two_total], 0)
    slices = (
        lax.all_to_all(joined[1], "fsdp", split_axis=1, concat_axis=0, tiled=True),
        lax.all_to_all(joined[2], "fsdp", split_axis=1, concat_axis=0, tiled=True),
        lax.all_to_all(joined[3], "fsdp", split_axis=1, concat_axis=0, tiled=True),
        lax.all_to_all(joined[5], "fsdp", split_axis=1, concat_axis=0, tiled=True),
        lax.all_to_all(joined[7], "fsdp", split_axis=1, concat_axis=0, tiled=True),
        lax.all_to_all(joined[8], "fsdp", split_axis=1, concat_axis=0, tiled=True),
        lax.all_to_all(joined[10], "fsdp", split_axis=1, concat_axis=0, tiled=True),
    )
    pieces = (
        lax.all_gather(joined[0], "fsdp", axis=0, tiled=True),
        lax.all_gather(joined[4], "fsdp", axis=0, tiled=True),
        lax.all_gather(joined[6], "fsdp", axis=0, tiled=True),
        lax.all_gather(joined[9], "fsdp", axis=0, tiled=True),
    )
    picked = [member for member in slices]
    gain_part = lax.psum_scatter(gain_terms, "fsdp", scatter_dimension=1, tiled=True)
    summed_rows = (
        lax.psum_scatter(
            rows_product(pieces[0], picked[0]).astype(jnp.bfloat16),
            "dp",
            scatter_dimension=0,
            tiled=True,
        ).astype(jnp.float32),
        lax.psum_scatter(
            rows_product(pieces[0], picked[1]).astype(jnp.bfloat16),
            "dp",
            scatter_dimension=0,
            tiled=True,
        ).astype(jnp.float32),
        lax.psum_scatter(
            rows_product(pieces[0], picked[2]).astype(jnp.bfloat16),
            "dp",
            scatter_dimension=0,
            tiled=True,
        ).astype(jnp.float32),
        lax.psum_scatter(
            rows_product(pieces[1], picked[3]).astype(jnp.bfloat16),
            "dp",
            scatter_dimension=0,
            tiled=True,
        ).astype(jnp.float32),
        lax.psum_scatter(
            rows_product(pieces[2], picked[4]).astype(jnp.bfloat16),
            "dp",
            scatter_dimension=0,
            tiled=True,
        ).astype(jnp.float32),
        lax.psum_scatter(
            rows_product(pieces[2], picked[5]).astype(jnp.bfloat16),
            "dp",
            scatter_dimension=0,
            tiled=True,
        ).astype(jnp.float32),
        lax.psum_scatter(
            rows_product(pieces[3], picked[6]).astype(jnp.bfloat16),
            "dp",
            scatter_dimension=0,
            tiled=True,
        ).astype(jnp.float32),
    )
    gain_grad = lax.psum(gain_part, "dp")
    return (
        jnp.stack(outputs, 0),
        jnp.stack(grad_inputs, 0),
        summed_rows[0],
        summed_rows[1],
        summed_rows[2],
        summed_rows[3],
        summed_rows[4],
        summed_rows[5],
        summed_rows[6],
        gain_grad,
    )


def swap_core(value):
    return lax.ppermute(value, "fsdp", [(j, j ^ 1) for j in range(8)])


def swap_dp(value, mask):
    return lax.ppermute(value, "dp", [(j, j ^ mask) for j in range(4)])


def shift_z(value, step):
    return lax.ppermute(value, "fsdp", [(j, (j + 2 * step) % 8) for j in range(8)])


def shift_z_up(value, step):
    return lax.ppermute(value, "fsdp", [(j, j + 2 * step) for j in range(8) if j + 2 * step < 8])


def shift_z_down(value, step):
    return lax.ppermute(value, "fsdp", [(j, j - 2 * step) for j in range(8) if j - 2 * step >= 0])


def add_low(*terms):
    total = terms[0].astype(jnp.float32)
    for term in terms[1:]:
        total = total + term.astype(jnp.float32)
    return total.astype(jnp.bfloat16)


def product_nn(left, right):
    return lax.dot_general(
        left, right, (((1,), (0,)), ((), ())), preferred_element_type=jnp.float32
    )


def product_nt(left, right):
    return lax.dot_general(
        left, right, (((1,), (1,)), ((), ())), preferred_element_type=jnp.float32
    )


def product_tn(left, right):
    return lax.dot_general(
        left, right, (((0,), (0,)), ((), ())), preferred_element_type=jnp.float32
    )


VMEM = pl.BlockSpec(memory_space=pltpu.VMEM)
SMEM = pl.BlockSpec(memory_space=pltpu.SMEM)
ANY = pl.BlockSpec(memory_space=pl.ANY)


def run(body, name, ins, in_specs, outs, out_specs, scratch, flops, megabytes):
    moved = sum(v.size * v.dtype.itemsize for v in ins)
    moved += sum(v.size * v.dtype.itemsize for v in outs)
    return pl.pallas_call(
        body,
        out_shape=tuple(outs),
        in_specs=in_specs,
        out_specs=tuple(out_specs),
        scratch_shapes=scratch,
        compiler_params=pltpu.CompilerParams(vmem_limit_bytes=megabytes * 1024 * 1024),
        cost_estimate=pl.CostEstimate(flops=flops, bytes_accessed=moved, transcendentals=0),
        name=name,
    )(*ins)


def struct(shape, dtype=jnp.bfloat16):
    return jax.ShapeDtypeStruct(shape, dtype)


def column_index(ids_ref, core_rel, s):
    return 2 * lax.rem(ids_ref[1] - s + 4, 4) + (ids_ref[2] ^ core_rel)


def start_row(index, size):
    return pl.ds(pl.multiple_of(index * size, 8), size)


def after(value, *others):
    return lax.optimization_barrier((value,) + others)[0]


def pack_first_kernel(counts_ref, wq_ref, wk_ref, wv_ref, gains_ref, out_ref):
    block = wq_ref.shape[0]
    gains = gains_ref[...].astype(jnp.float32)
    row = lax.broadcasted_iota(jnp.int32, (8, block), 0)
    lane = lax.broadcasted_iota(jnp.int32, (8, block), 1)
    first = jnp.concatenate([gains[:1], gains[1:]], 1)
    used = jnp.where(
        lane == 0,
        counts_ref[0, 0].astype(jnp.float32),
        jnp.where(lane == 1, counts_ref[1, 0].astype(jnp.float32), 0.0),
    )
    extra = jnp.where(row == 0, first, jnp.where(row == 1, used, 0.0))
    full = jnp.concatenate(
        [
            wq_ref[...].astype(jnp.float32).T,
            extra,
            wk_ref[...].astype(jnp.float32),
            wv_ref[...].astype(jnp.float32),
        ],
        0,
    )
    out_ref[...] = jnp.zeros_like(out_ref)
    out_ref[:, :block] = full.astype(jnp.bfloat16)


def pack_mlp_kernel(ids_ref, wg_ref, wu_ref, wd_ref, other_ref, wo_ref, out_ref):
    half, block = wg_ref.shape
    core = ids_ref[2]
    out_ref[...] = jnp.zeros_like(out_ref)
    out_ref[:half, :block] = wg_ref[...]
    out_ref[half : 2 * half, :block] = wu_ref[...]
    down = wd_ref[...].astype(jnp.float32)
    own = jnp.where(core == 0, down[:, :half], down[:, half:])
    other = other_ref[:, :half].astype(jnp.float32)
    low = jnp.where(core == 0, own, other)
    high = jnp.where(core == 0, other, own)
    out_ref[2 * half : 3 * half, :block] = jnp.concatenate([low, high], 0).T.astype(jnp.bfloat16)
    out_ref[3 * half :, :block] = jnp.concatenate(
        [wo_ref[...].astype(jnp.float32).T, jnp.zeros((8, block), jnp.float32)], 0
    ).astype(jnp.bfloat16)


def turn_in_kernel(x_ref, dy_ref, xt_ref, dyt_ref):
    xt_ref[...] = x_ref[...].astype(jnp.float32).T.astype(jnp.bfloat16)
    dyt_ref[...] = jnp.zeros_like(dyt_ref)
    dyt_ref[:, : dy_ref.shape[0]] = dy_ref[...].astype(jnp.float32).T.astype(jnp.bfloat16)


def fill_relative(ids_ref, target_ref, *sources):
    block, lanes = sources[0].shape[1], target_ref.shape[1]
    wide = target_ref.shape[0] // 4
    for k in range(4):
        parts = [source[ids_ref[0] ^ k] for source in sources]
        target_ref[k * wide : k * wide + block, :] = (
            parts[0] if len(parts) == 1 else jnp.concatenate(parts, 1)
        )
        target_ref[k * wide + block : (k + 1) * wide, :] = jnp.zeros(
            (wide - block, lanes), target_ref.dtype
        )


def wide_rows(refs, s, low, high):
    along, by_x, by_y, far_a, far_b = refs
    far = far_a if s < 2 else far_b
    return jnp.concatenate(
        [along[s, low:high], by_x[s, low:high], by_y[s, low:high], far[s % 2, low:high]], 1
    )


def project_kernel(*refs):
    ids_ref, own, other = refs[0], refs[1:6], refs[6:11]
    n1_ref, cos_ref, sin_ref, q_ref, kv_ref, proj_ref, turned_ref, rel_ref = refs[11:]
    width = n1_ref.shape[0] * n1_ref.shape[1]
    kv_width = KEY_HEADS * HEAD_WIDTH
    q_cols, k_cols = width // 8, kv_width // 8
    depth = own[0].shape[1]
    fill_relative(ids_ref, rel_ref, n1_ref)
    for core_rel, weights in ((0, own), (1, other)):
        for s in range(4):
            f = column_index(ids_ref, core_rel, s)
            total = product_nn(wide_rows(weights, s, 0, depth), rel_ref[...])
            proj_ref[start_row(f, q_cols), :] = total[:q_cols]
            proj_ref[pl.ds(pl.multiple_of(width + f * k_cols, 8), k_cols), :] = total[
                q_cols + 8 : q_cols + 8 + k_cols
            ]
            proj_ref[pl.ds(pl.multiple_of(width + kv_width + f * k_cols, 8), k_cols), :] = total[
                q_cols + 8 + k_cols :
            ]
    cosine, sine = cos_ref[...], sin_ref[...]
    half = HEAD_WIDTH // 2

    def heads(head, carry):
        front = proj_ref[pl.ds(pl.multiple_of(head * HEAD_WIDTH, 8), half), :]
        back = proj_ref[pl.ds(pl.multiple_of(head * HEAD_WIDTH + half, 8), half), :]
        q_ref[head, :half, :] = (
            (front * cosine - back * sine).astype(jnp.bfloat16) * SCORE_SCALE
        ).astype(jnp.bfloat16)
        q_ref[head, half:, :] = (
            (back * cosine + front * sine).astype(jnp.bfloat16) * SCORE_SCALE
        ).astype(jnp.bfloat16)
        return carry

    lax.fori_loop(0, QUERY_HEADS, heads, 0)
    for head in range(KEY_HEADS):
        base = width + head * HEAD_WIDTH
        front = proj_ref[base : base + half, :]
        back = proj_ref[base + half : base + 2 * half, :]
        turned_ref[head * HEAD_WIDTH : head * HEAD_WIDTH + half, :] = front * cosine - back * sine
        turned_ref[head * HEAD_WIDTH + half : (head + 1) * HEAD_WIDTH, :] = (
            back * cosine + front * sine
        )
    turned_ref[kv_width:, :] = proj_ref[width + kv_width :, :]
    kv_ref[...] = turned_ref[...].T.astype(jnp.bfloat16)


def stage_heads(mb, cap, blocks, k_ref, v_ref):
    kv_width = KEY_HEADS * HEAD_WIDTH
    for block, source in enumerate(blocks):
        rows = source[mb * cap : (mb + 1) * cap, :]
        for n in range(KEY_HEADS):
            lanes = n * HEAD_WIDTH
            k_ref[n, block * cap : (block + 1) * cap, :] = rows[:, lanes : lanes + HEAD_WIDTH]
            lanes += kv_width
            v_ref[n, block * cap : (block + 1) * cap, :] = rows[:, lanes : lanes + HEAD_WIDTH]


def stage_bias(ids_ref, counts_ref, mb, cap, share, bias_ref):
    slot = ids_ref[3]
    own_count = counts_ref[mb * 8 + slot]
    key = lax.broadcasted_iota(jnp.int32, (cap, cap), 0)
    query = lax.broadcasted_iota(jnp.int32, (cap, cap), 1)
    query_used = query < own_count
    for core_rel in range(2):
        for s in range(4):
            block = core_rel * 4 + s
            f = column_index(ids_ref, core_rel, s)
            count = counts_ref[mb * 8 + f]
            reach = jnp.where(f < slot, cap, jnp.where(f == slot, 0, -2 * cap))
            self_off = jnp.where(f == slot, 0, 2 * cap)
            allowed = (query_used & (key < count) & (key <= query + reach)) | (
                key == query + self_off
            )
            tile = jnp.where(allowed, 0.0, -1e30)
            for g in range(share):
                bias_ref[block * cap : (block + 1) * cap, g * cap : (g + 1) * cap] = tile


def join_heads(ref, n, share, mb, cap):
    return jnp.concatenate(
        [ref[share * n + g, :, mb * cap : (mb + 1) * cap] for g in range(share)], 1
    )


def attend_kernel(mb, *refs):
    ids_ref, counts_ref, q_ref = refs[:3]
    blocks = refs[3:11]
    att_ref, lse_ref, k_ref, v_ref, bias_ref = refs[11:]
    cap = q_ref.shape[2] // 2
    share = QUERY_HEADS // KEY_HEADS
    stage_heads(mb, cap, blocks, k_ref, v_ref)
    stage_bias(ids_ref, counts_ref, mb, cap, share, bias_ref)

    def body(n, carry):
        scores = product_nn(k_ref[n], join_heads(q_ref, n, share, mb, cap)) + bias_ref[...]
        top = jnp.max(scores, 0, keepdims=True)
        exponent = jnp.exp(scores - top)
        total = jnp.sum(exponent, 0, keepdims=True)
        mixed = product_tn(v_ref[n], exponent.astype(jnp.bfloat16)) / total
        mixed = mixed.astype(jnp.bfloat16)
        for g in range(share):
            att_ref[share * n + g] = mixed[:, g * cap : (g + 1) * cap]
        lse_ref[n] = top + jnp.log(total)
        return carry

    lax.fori_loop(0, KEY_HEADS, body, 0)


def attend_back_kernel(mb, *refs):
    ids_ref, counts_ref, q_ref, do_ref = refs[:4]
    blocks = refs[4:12]
    lse_ref, cos_ref, sin_ref, dq_ref = refs[12:16]
    targets = [ref.at[s] for ref in refs[16:18] for s in range(4)]
    k_ref, v_ref, bias_ref, dk_ref, dv_ref = refs[18:]
    cap = q_ref.shape[2] // 2
    share = QUERY_HEADS // KEY_HEADS
    half = HEAD_WIDTH // 2
    kv_width = KEY_HEADS * HEAD_WIDTH
    stage_heads(mb, cap, blocks, k_ref, v_ref)
    stage_bias(ids_ref, counts_ref, mb, cap, share, bias_ref)
    cosine = jnp.concatenate([cos_ref[:, mb * cap : (mb + 1) * cap]] * share, 1)
    sine = jnp.concatenate([sin_ref[:, mb * cap : (mb + 1) * cap]] * share, 1)

    def body(n, carry):
        query = join_heads(q_ref, n, share, mb, cap)
        grad = join_heads(do_ref, n, share, mb, cap)
        keys = k_ref[n]
        prob = jnp.exp(product_nn(keys, query) + bias_ref[...] - lse_ref[n])
        dprob = product_nn(v_ref[n], grad)
        delta = jnp.sum(prob * dprob, 0, keepdims=True)
        dscore = (prob * (dprob - delta)).astype(jnp.bfloat16)
        dq = product_tn(keys, dscore) * SCORE_SCALE
        front, back = dq[:half], dq[half:]
        turned = jnp.concatenate(
            [front * cosine + back * sine, back * cosine - front * sine], 0
        ).astype(jnp.bfloat16)
        for g in range(share):
            dq_ref[share * n + g] = turned[:, g * cap : (g + 1) * cap]
        dk_ref[n] = product_nt(dscore, query).astype(jnp.bfloat16)
        dv_ref[n] = product_nt(prob.astype(jnp.bfloat16), grad).astype(jnp.bfloat16)
        return carry

    lax.fori_loop(0, KEY_HEADS, body, 0)
    for block, target in enumerate(targets):
        for n in range(KEY_HEADS):
            lanes = n * HEAD_WIDTH
            target[:, lanes : lanes + HEAD_WIDTH] = dk_ref[n, block * cap : (block + 1) * cap, :]
            lanes += kv_width
            target[:, lanes : lanes + HEAD_WIDTH] = dv_ref[n, block * cap : (block + 1) * cap, :]


def collect_kernel(*refs):
    pieces, out_ref, sem = refs[:16], refs[16], refs[17]
    rows, wide = out_ref.shape[1], pieces[0].shape[1]
    copies = []
    for k in range(4):
        for s in range(4):
            copies.append(
                pltpu.make_async_copy(
                    pieces[k * 4 + s].at[pl.ds(pieces[0].shape[0] - rows, rows)],
                    out_ref.at[s, :, pl.ds(k * wide, wide)],
                    sem.at[k * 4 + s],
                )
            )
    for copy in copies:
        copy.start()
    for copy in copies:
        copy.wait()


def hidden_kernel(
    ids_ref, own_ref, other_ref, att_a_ref, att_b_ref, x_ref, gain_ref, h_ref, n2_ref, rel_ref
):
    q_cols, rows = h_ref.shape[0] // 8, h_ref.shape[1]
    fill_relative(ids_ref, rel_ref, att_a_ref, att_b_ref)
    for core_rel, w_ref in ((0, own_ref), (1, other_ref)):
        for s in range(4):
            f = column_index(ids_ref, core_rel, s)
            h_ref[start_row(f, q_cols), :] = product_nn(w_ref[s], rel_ref[...])[:q_cols]
    h = h_ref[...] + x_ref[...].astype(jnp.float32)
    h_ref[...] = h
    n2_ref[...] = jnp.zeros_like(n2_ref)
    n2_ref[:, :rows] = (h * mean_square(h) * gain_ref[...]).astype(jnp.bfloat16)


def turn_point_kernel(
    ids_ref,
    parts_ref,
    arrived_ref,
    h_ref,
    dy_ref,
    gain_ref,
    own_ref,
    other_ref,
    out_ref,
    dh_ref,
    do_ref,
    gain_grad_ref,
    pieces_ref,
    da_ref,
):
    width, rows = h_ref.shape
    q_cols = width // 8
    block = do_ref.shape[1]
    wide = own_ref.shape[2] // 4
    h = h_ref[...]
    out_ref[...] = (h + parts_ref[0] + arrived_ref[0, :, :rows].astype(jnp.float32)).astype(
        jnp.bfloat16
    )
    dn = parts_ref[1] + arrived_ref[1, :, :rows].astype(jnp.float32)
    rms = mean_square(h)
    gain_grad_ref[...] = jnp.sum(dn * h * rms, 1, keepdims=True)
    weighted = dn * gain_ref[...]
    dh = (
        dy_ref[:, :rows].astype(jnp.float32)
        + rms * weighted
        - h * (rms * rms * rms * jnp.mean(weighted * h, 0, keepdims=True))
    )
    dh_ref[...] = dh
    da_ref[...] = dh
    spread(ids_ref, da_ref, pieces_ref, q_cols)
    half = pieces_ref.shape[0] // 2
    mixed = product_tn(own_ref[...].reshape(half, 4 * wide), pieces_ref[:half, :])
    mixed += product_tn(other_ref[...].reshape(half, 4 * wide), pieces_ref[half:, :])
    mixed = mixed.astype(jnp.bfloat16)
    for k in range(4):
        do_ref[ids_ref[0] ^ k] = mixed[k * wide : k * wide + block]


def spread(ids_ref, source_ref, target_ref, cols):
    rows = source_ref.shape[1]
    for core_rel in range(2):
        for s in range(4):
            f = column_index(ids_ref, core_rel, s)
            low = (core_rel * 4 + s) * (cols + 8)
            target_ref[low : low + cols + 8, :] = jnp.concatenate(
                [source_ref[start_row(f, cols), :], jnp.zeros((8, rows), jnp.float32)], 0
            ).astype(jnp.bfloat16)


def targets_of(refs):
    return list(refs[:4]) + [refs[4].at[pl.ds(4 * k, 4)] for k in range(4)]


def out_grad_kernel(ids_ref, att_a_ref, att_b_ref, pieces_ref, *refs):
    grads, att_rel = targets_of(refs[:5]), refs[5]
    depth = pieces_ref.shape[0] // 8
    wide = att_rel.shape[0] // 4
    fill_relative(ids_ref, att_rel, att_a_ref, att_b_ref)
    for core_rel in range(2):
        for s in range(4):
            low = (core_rel * 4 + s) * depth
            got = product_nt(pieces_ref[low : low + depth, :], att_rel[...]).astype(jnp.bfloat16)
            for k in range(4):
                grads[core_rel * 4 + k][s] = got[:, k * wide : (k + 1) * wide]


def finish_q_kernel(*refs):
    ids_ref, own, other = refs[0], refs[1:6], refs[6:11]
    n1_ref, dq_a_ref, dq_b_ref = refs[11:14]
    out_grads = targets_of(refs[14:19])
    dn_ref, grads = refs[19], targets_of(refs[20:25])
    n1_rel, d_ref, dq_ref = refs[25:]
    cap = dq_a_ref.shape[1]
    width = dq_a_ref.shape[0]
    q_cols = width // 8
    depth = q_cols + 8
    block = n1_ref.shape[1]
    wide = n1_rel.shape[0] // 4
    d_ref[:, :cap] = dq_a_ref[...].astype(jnp.float32)
    d_ref[:, cap:] = dq_b_ref[...].astype(jnp.float32)
    spread(ids_ref, d_ref, dq_ref, q_cols)
    fill_relative(ids_ref, n1_rel, n1_ref)
    weights = jnp.concatenate(
        [wide_rows(w, s, 0, depth) for w in (own, other) for s in range(4)], 0
    )
    dn = product_tn(weights, dq_ref[...])
    for k in range(4):
        dn_ref[ids_ref[0] ^ k] = dn[k * wide : k * wide + block]
    for core_rel in range(2):
        for s in range(4):
            low = (core_rel * 4 + s) * depth
            gq = product_nt(dq_ref[low : low + depth, :], n1_rel[...]).astype(jnp.bfloat16)
            for k in range(4):
                target = grads[core_rel * 4 + k]
                target[s, :depth, :] = gq[:, k * wide : (k + 1) * wide]
                target[s, depth:, :] = out_grads[core_rel * 4 + k][s]


def kv_grad_kernel(
    ids_ref, n1_ref, dkv_a_ref, dkv_b_ref, cos_ref, sin_ref, dkv_ref, *refs
):
    grads = targets_of(refs[:5])
    n1_rel, d_ref = refs[5:]
    cap = dkv_a_ref.shape[0]
    kv_width = KEY_HEADS * HEAD_WIDTH
    k_cols = kv_width // 8
    half = HEAD_WIDTH // 2
    wide = n1_rel.shape[0] // 4
    cosine, sine = cos_ref[...], sin_ref[...]
    d_ref[:, :cap] = dkv_a_ref[...].T
    d_ref[:, cap:] = dkv_b_ref[...].T
    for head in range(KEY_HEADS):
        base = head * HEAD_WIDTH
        front = d_ref[base : base + half, :]
        back = d_ref[base + half : base + 2 * half, :]
        d_ref[base : base + half, :] = front * cosine + back * sine
        d_ref[base + half : base + 2 * half, :] = back * cosine - front * sine
    for core_rel in range(2):
        for s in range(4):
            f = column_index(ids_ref, core_rel, s)
            low = (core_rel * 4 + s) * 2 * k_cols
            dkv_ref[low : low + 2 * k_cols, :] = jnp.concatenate(
                [
                    d_ref[start_row(f, k_cols), :],
                    d_ref[pl.ds(pl.multiple_of(kv_width + f * k_cols, 8), k_cols), :],
                ],
                0,
            ).astype(jnp.bfloat16)
    fill_relative(ids_ref, n1_rel, n1_ref)
    for core_rel in range(2):
        for s in range(4):
            low = (core_rel * 4 + s) * 2 * k_cols
            got = product_nt(dkv_ref[low : low + 2 * k_cols, :], n1_rel[...]).astype(jnp.bfloat16)
            for k in range(4):
                grads[core_rel * 4 + k][s] = got[:, k * wide : (k + 1) * wide]


def finish_kernel(*refs):
    ids_ref, own, other = refs[0], refs[1:6], refs[6:11]
    dkv_ref, dn_ref, dh_ref, x_ref, gain_ref, tokens_ref, gain_grad_ref = refs[11:]
    width = dh_ref.shape[0]
    block = dn_ref.shape[1]
    kv_rows = dkv_ref.shape[0] // 8
    low = own[0].shape[1] - kv_rows
    wide = own[0].shape[2]
    weights = jnp.concatenate(
        [wide_rows(w, s, low, low + kv_rows) for w in (own, other) for s in range(4)], 0
    )
    dn = product_tn(weights, dkv_ref[...])
    for k in range(4):
        i = ids_ref[0] ^ k
        tokens_ref[pl.ds(pl.multiple_of(i * block, 16), block), :] = (
            dn[k * wide : k * wide + block] + dn_ref[i]
        )
    x = x_ref[...].astype(jnp.float32)
    rms = mean_square(x)
    dn = tokens_ref[...]
    gain_grad_ref[...] = jnp.sum(dn * x * rms, 1, keepdims=True)
    weighted = dn * gain_ref[...]
    tokens_ref[...] = (
        dh_ref[...]
        + rms * weighted
        - x * (rms * rms * rms * jnp.mean(weighted * x, 0, keepdims=True))
    )


def mlp_kernel(*refs):
    ids_ref, n2_own, n2_other, dy_own, dy_other = refs[:5]
    pieces = refs[5:21]
    keep_ref, send_ref = refs[21:23]
    grads = refs[23:39]
    wgu, wdn, gu_ref, prod_ref, dgu_ref, n2_rel, dy_rel, sem_in, sem_out = refs[39:]
    dp_id = ids_ref[0]
    z_id = ids_ref[1]
    block, rows = keep_ref.shape[1] // 4, keep_ref.shape[2]
    pair = 2 * rows
    wide = pieces[0].shape[1]
    half = prod_ref.shape[0] // 4

    def gate_up_part(ref, piece, k, s):
        return piece.at[pl.ds(0, 2 * half)], ref.at[
            pl.ds(s * 2 * half, 2 * half), pl.ds(k * wide, wide)
        ]

    def down_part(ref, piece, k, s):
        return piece.at[pl.ds(2 * half, half)], ref.at[
            pl.ds(k * half, half), pl.ds(s * wide, wide)
        ]

    loads, more_loads = [], []
    for s in range(4):
        for k in range(4):
            source, target = gate_up_part(wgu, pieces[k * 4 + s], k, s)
            loads.append(pltpu.make_async_copy(source, target, sem_in.at[0, k * 4 + s]))
            source, target = down_part(wdn, pieces[k * 4 + s], k, s)
            more_loads.append(pltpu.make_async_copy(source, target, sem_in.at[1, k * 4 + s]))
    for load in loads + more_loads:
        load.start()
    pad = jnp.zeros((wide - block, pair), jnp.bfloat16)
    for j in range(4):
        i = dp_id ^ j
        zz = lax.rem(z_id - j + 4, 4)
        n2_rel[j * wide : j * wide + block, :] = jnp.concatenate(
            [n2_own[i][:, :rows], n2_other[i][:, :rows]], 1
        )
        dy_rel[j * wide : j * wide + block, :] = jnp.concatenate(
            [dy_own[zz][:, :rows], dy_other[zz][:, :rows]], 1
        )
        n2_rel[j * wide + block : (j + 1) * wide, :] = pad
        dy_rel[j * wide + block : (j + 1) * wide, :] = pad

    def rows_of(index, size):
        return pl.ds(pl.multiple_of(index * size, 16), size)

    for s in range(4):
        for load in loads[4 * s : 4 * s + 4]:
            load.wait()
        k = lax.rem(z_id - s + 4, 4) ^ dp_id
        total = product_nn(wgu[s * 2 * half : (s + 1) * 2 * half, :], n2_rel[...])
        gu_ref[rows_of(k, 2 * half), :] = total
        gate = total[:half]
        prod_ref[rows_of(k, half), :] = (gate * jax.nn.sigmoid(gate) * total[half:]).astype(
            jnp.bfloat16
        )
    for load in more_loads:
        load.wait()
    for k in range(4):
        s = lax.rem(z_id - (dp_id ^ k) + 4, 4)
        dprod = product_nn(wdn[k * half : (k + 1) * half, :], dy_rel[...])
        gate = gu_ref[k * 2 * half : k * 2 * half + half, :]
        up = gu_ref[k * 2 * half + half : (k + 1) * 2 * half, :]
        sig = jax.nn.sigmoid(gate)
        dgu_ref[rows_of(s, 2 * half), :] = jnp.concatenate(
            [dprod * up * sig * (1.0 + gate * (1.0 - sig)), dprod * gate * sig], 0
        ).astype(jnp.bfloat16)
    for j in range(4):
        lanes = slice(j * wide, (j + 1) * wide)
        out = product_tn(wdn[:, lanes], prod_ref[...])[:block]
        zz = rows_of(lax.rem(z_id - j + 4, 4), block)
        keep_ref[0, zz, :] = out[:, :rows]
        send_ref[0, zz, :rows] = out[:, rows:].astype(jnp.bfloat16)
    for k in range(4):
        here = slice(k * half, (k + 1) * half)
        wdn[here, :] = product_nt(prod_ref[here, :], dy_rel[...]).astype(jnp.bfloat16)
    stores = []
    for k in range(4):
        for s in range(4):
            target, source = down_part(wdn, grads[k * 4 + s], k, s)
            stores.append(pltpu.make_async_copy(source, target, sem_out.at[1, k * 4 + s]))
    for store in stores:
        store.start()
    for j in range(4):
        lanes = slice(j * wide, (j + 1) * wide)
        dn = product_tn(wgu[:, lanes], dgu_ref[...])[:block]
        i = rows_of(dp_id ^ j, block)
        keep_ref[1, i, :] = dn[:, :rows]
        send_ref[1, i, :rows] = dn[:, rows:].astype(jnp.bfloat16)
    send_ref[:, :, rows:] = jnp.zeros((2, 4 * block, send_ref.shape[2] - rows), jnp.bfloat16)
    for s in range(4):
        here = slice(s * 2 * half, (s + 1) * 2 * half)
        wgu[here, :] = product_nt(dgu_ref[here, :], n2_rel[...]).astype(jnp.bfloat16)
        for k in range(4):
            target, source = gate_up_part(wgu, grads[k * 4 + s], k, s)
            store = pltpu.make_async_copy(source, target, sem_out.at[0, k * 4 + s])
            store.start()
            stores.append(store)
    for store in stores:
        store.wait()


def mean_square(values):
    return lax.rsqrt(jnp.mean(values * values, 0, keepdims=True) + EPSILON)


def fast(
    tokens, cotangent, counts, w_query, key_weight, value_weight, w_out, w_gate, w_up, w_down, gains
):
    dp_id = lax.axis_index("dp")
    slot = lax.axis_index("fsdp")
    z_id = slot // 2
    core_id = slot % 2
    ids = jnp.stack([dp_id, z_id, core_id, slot]).astype(jnp.int32)
    batches, cap, width = tokens.shape
    rows = batches * cap
    block = w_query.shape[0]
    wide = -(-block // 128) * 128
    q_cols, k_cols = w_query.shape[1], key_weight.shape[1]
    half = w_gate.shape[1]
    kv_width = KEY_HEADS * HEAD_WIDTH
    share = QUERY_HEADS // KEY_HEADS
    q_rows = q_cols + 8
    depth = q_rows + 2 * k_cols
    mlp_rows = 3 * half + q_rows
    padded = -(-rows // 128) * 128

    (first_piece,) = run(
        pack_first_kernel,
        "pack_first",
        (counts, w_query, key_weight.T, value_weight.T, gains),
        [SMEM] + [VMEM] * 4,
        [struct((depth, wide))],
        [VMEM],
        [],
        0,
        16,
    )
    chain = [first_piece] + [shift_z(first_piece, step) for step in (1, 2, 3)]
    down = w_down.T
    give = jnp.where(core_id == 0, down[:, half:], down[:, :half])
    other_down = swap_core(jnp.pad(give, ((0, 0), (0, -half % 128))))
    (mlp_piece,) = run(
        pack_mlp_kernel,
        "pack_mlp",
        (ids, w_gate.T, w_up.T, down, other_down, w_out),
        [SMEM] + [VMEM] * 5,
        [struct((mlp_rows, wide))],
        [VMEM],
        [],
        0,
        16,
    )
    x, dy = run(
        turn_in_kernel,
        "turn_in",
        (tokens.reshape(rows, width), cotangent.reshape(rows, width)),
        [VMEM] * 2,
        [struct((width, rows)), struct((width, padded))],
        [VMEM] * 2,
        [],
        0,
        16,
    )

    along = jnp.stack(chain, 0)
    extras = along[:, q_cols : q_cols + 2, :block]
    other_extras = swap_core(extras)
    from_x = swap_dp(along, 1)
    from_y = swap_dp(along, 2)
    first_own = [along, from_x, from_y, swap_dp(from_x[:2], 2), swap_dp(from_y[2:], 1)]
    first_other = [swap_core(piece) for piece in first_own]

    z_one = shift_z(after(mlp_piece, along), 1)
    z_two = shift_z(z_one, 1)
    z_three = shift_z(z_two, 1)
    mlp_next = after(mlp_piece, *first_own[3:])
    x_zero, y_zero = swap_dp(mlp_next, 1), swap_dp(mlp_next, 2)

    by_core = jnp.where(
        core_id == 0, jnp.stack([extras, other_extras], 1), jnp.stack([other_extras, extras], 1)
    )
    by_core = by_core[::-1]
    by_core = lax.dynamic_slice_in_dim(jnp.concatenate([by_core, by_core], 0), 3 - z_id, 4, 0)
    gain = by_core[:, :, 0, :].reshape(8, 2, q_cols).transpose(0, 2, 1).reshape(width, 2)
    gain = gain.astype(jnp.float32)
    gain_one, gain_two = gain[:, :1], gain[:, 1:]
    group_counts = by_core[:, :, 1, :batches].reshape(8, batches).astype(jnp.int32)
    flat_counts = group_counts.T.reshape(-1)
    before = jnp.sum(
        jnp.where(jnp.arange(8, dtype=jnp.int32)[:, None] < slot, group_counts, 0), 0
    )
    position = (before[:, None] + jnp.arange(cap, dtype=jnp.int32)[None, :]).reshape(-1)
    cosine, sine = rope_tables(position, HEAD_WIDTH)
    cosine, sine = cosine[:, 0, :].T, sine[:, 0, :].T
    x_wide = x.astype(jnp.float32)
    n1 = (x_wide * mean_square(x_wide) * gain_one).astype(jnp.bfloat16).reshape(4, block, rows)
    n1_next = after(n1, z_two)

    query, kv = run(
        project_kernel,
        "project",
        (ids, *first_own, *first_other, n1_next, cosine, sine),
        [SMEM] + [VMEM] * 13,
        (struct((QUERY_HEADS, HEAD_WIDTH, rows)), struct((rows, 2 * kv_width))),
        [VMEM] * 2,
        [
            pltpu.VMEM((width + 2 * kv_width, rows), jnp.float32),
            pltpu.VMEM((2 * kv_width, rows), jnp.float32),
            pltpu.VMEM((4 * wide, rows), jnp.bfloat16),
        ],
        2 * (width + 2 * kv_width) * width * rows,
        24,
    )
    kv_zero = after(kv, x_zero, y_zero)
    kv_one = shift_z_up(kv_zero, 1)
    x_one = swap_dp(after(z_one, kv_zero), 1)
    far_zero = swap_dp(after(x_zero, kv_zero), 2)
    wave = (kv_one, x_one, far_zero, z_three)
    kv_two = shift_z_up(after(*wave), 1)
    x_two = swap_dp(after(z_two, *wave), 1)
    y_one = swap_dp(after(z_one, *wave), 2)
    wave = (kv_two, x_two, y_one)
    kv_three = shift_z_up(after(*wave), 1)
    far_one = swap_dp(after(y_one, *wave), 1)
    y_two = swap_dp(after(z_two, *wave), 2)
    wave = (kv_three, far_one, y_two)
    x_three = swap_dp(after(z_three, *wave), 1)
    y_three = swap_dp(after(z_three, *wave), 2)
    kv_own = [kv, kv_one, kv_two, kv_three]
    kv_other = [swap_core(piece) for piece in (kv_zero, kv_one, kv_two, kv_three)]
    pair_flops = 2 * QUERY_HEADS * HEAD_WIDTH * rows * 8 * cap
    head_scratch = [
        pltpu.VMEM((KEY_HEADS, 8 * cap, HEAD_WIDTH), jnp.bfloat16),
        pltpu.VMEM((KEY_HEADS, 8 * cap, HEAD_WIDTH), jnp.bfloat16),
        pltpu.VMEM((8 * cap, share * cap), jnp.float32),
    ]
    def attend(mb, queries):
        return run(
            functools.partial(attend_kernel, mb),
            "attend",
            (ids, flat_counts, queries, *kv_own, *kv_other),
            [SMEM, SMEM] + [VMEM] * 9,
            (
                struct((QUERY_HEADS, HEAD_WIDTH, cap)),
                struct((KEY_HEADS, 1, share * cap), jnp.float32),
            ),
            [VMEM] * 2,
            head_scratch,
            4 * pair_flops,
            24,
        )

    att_a, lse_a = attend(0, after(query, far_one, y_two))
    wave = (att_a, x_three, y_three)
    far_two = swap_dp(after(x_two, *wave), 2)
    far_three = swap_dp(after(y_three, *wave), 1)
    dy_other = swap_core(after(dy, att_a))
    att_b, lse_b = attend(1, after(query, *wave))
    pieces = [mlp_piece, z_one, z_two, z_three]
    pieces += [x_zero, x_one, x_two, x_three]
    pieces += [y_zero, y_one, y_two, y_three]
    pieces += [far_zero, far_one, far_two, far_three]
    (out_own,) = run(
        collect_kernel,
        "collect",
        tuple(pieces[:15]) + (after(far_three, att_b),),
        [ANY] * 16,
        [struct((4, q_rows, 4 * wide))],
        [VMEM],
        [pltpu.SemaphoreType.DMA((16,))],
        0,
        8,
    )
    out_other = swap_core(out_own)
    att_a = att_a.reshape(4, block, cap)
    att_b = att_b.reshape(4, block, cap)
    lse = (lse_a, lse_b)
    blocks = (4, block, rows)
    wide_blocks = (4, block, padded)
    h, n2 = run(
        hidden_kernel,
        "hidden",
        (ids, out_own, out_other, att_a, att_b, after(x, dy_other), gain_two),
        [SMEM] + [VMEM] * 6,
        (struct((width, rows), jnp.float32), struct((width, padded))),
        [VMEM] * 2,
        [pltpu.VMEM((4 * wide, rows), jnp.bfloat16)],
        2 * width * width * rows,
        24,
    )
    n2_other = swap_core(n2)
    results = run(
        mlp_kernel,
        "mlp",
        (
            ids,
            n2.reshape(wide_blocks),
            n2_other.reshape(wide_blocks),
            dy.reshape(wide_blocks),
            dy_other.reshape(wide_blocks),
            *pieces,
        ),
        [SMEM] + [VMEM] * 4 + [ANY] * 16,
        [struct((2, width, rows), jnp.float32), struct((2, width, padded))]
        + [struct((3 * half, wide))] * 16,
        [VMEM] * 2 + [ANY] * 16,
        [
            pltpu.VMEM((8 * half, 4 * wide), jnp.bfloat16),
            pltpu.VMEM((4 * half, 4 * wide), jnp.bfloat16),
            pltpu.VMEM((8 * half, 2 * rows), jnp.float32),
            pltpu.VMEM((4 * half, 2 * rows), jnp.bfloat16),
            pltpu.VMEM((8 * half, 2 * rows), jnp.bfloat16),
            pltpu.VMEM((4 * wide, 2 * rows), jnp.bfloat16),
            pltpu.VMEM((4 * wide, 2 * rows), jnp.bfloat16),
            pltpu.SemaphoreType.DMA((2, 16)),
            pltpu.SemaphoreType.DMA((2, 16)),
        ],
        18 * 16 * half * block * 2 * rows,
        44,
    )
    keep, send = results[:2]
    home, to_x, to_y, far = results[2:6], results[6:10], results[10:14], results[14:18]
    arrived = swap_core(send)

    output, dh, mixed_gradient, gain_two_grad, da_pieces = run(
        turn_point_kernel,
        "turn_point",
        (ids, keep, arrived, h, dy, gain_two, out_own, out_other),
        [SMEM] + [VMEM] * 7,
        (
            struct((width, rows)),
            struct((width, rows), jnp.float32),
            struct(blocks),
            struct((width, 1), jnp.float32),
            struct((8 * q_rows, rows)),
        ),
        [VMEM] * 5,
        [pltpu.VMEM((width, rows), jnp.float32)],
        2 * width * width * rows,
        24,
    )
    output = output.T.reshape(batches, cap, width)
    def attend_back(mb, mixed):
        return run(
            functools.partial(attend_back_kernel, mb),
            "attend_back",
            (
                ids,
                flat_counts,
                query,
                mixed.reshape(QUERY_HEADS, HEAD_WIDTH, rows),
                *kv_own,
                *kv_other,
                lse[mb],
                cosine,
                sine,
            ),
            [SMEM, SMEM] + [VMEM] * 13,
            [struct((QUERY_HEADS, HEAD_WIDTH, cap))] + [struct((4, cap, 2 * kv_width))] * 2,
            [VMEM] * 3,
            head_scratch
            + [
                pltpu.VMEM((KEY_HEADS, 8 * cap, HEAD_WIDTH), jnp.bfloat16),
                pltpu.VMEM((KEY_HEADS, 8 * cap, HEAD_WIDTH), jnp.bfloat16),
            ],
            10 * pair_flops,
            24,
        )

    def sum_cores(own, other):
        arrived = swap_core(other)
        return [add_low(own[s], arrived[s]) for s in range(4)]

    def sum_z(summed):
        total = summed[0].astype(jnp.float32)
        for s in (3, 2, 1):
            total = total + shift_z_down(summed[s], s).astype(jnp.float32)
        return total

    via_three = swap_dp(after(far[3], mixed_gradient), 1)
    via_two = swap_dp(after(far[2], mixed_gradient), 2)
    x_three = swap_dp(after(to_x[3], mixed_gradient), 1)
    y_two = swap_dp(after(to_y[2], mixed_gradient), 2)
    back_a = attend_back(0, mixed_gradient)
    wave = (back_a[0], via_three, via_two, x_three, y_two)
    x_two = swap_dp(add_low(to_x[2], after(via_two, *wave)), 1)
    y_three = swap_dp(add_low(to_y[3], after(via_three, *wave)), 2)
    via_one, via_zero = swap_dp(after(far[1], *wave), 1), swap_dp(after(far[0], *wave), 2)
    out_grads = run(
        out_grad_kernel,
        "out_grad",
        (ids, att_a, att_b, after(da_pieces, *wave)),
        [SMEM] + [VMEM] * 3,
        [struct((4, q_rows, wide))] * 4 + [struct((16, q_rows, wide))],
        [VMEM] * 5,
        [pltpu.VMEM((4 * wide, rows), jnp.bfloat16)],
        2 * width * width * rows,
        16,
    )
    summed_a = sum_cores(*back_a[1:])
    wave = (x_two, y_three, out_grads[0])
    dkv_a = sum_z([after(piece, *wave) for piece in summed_a])
    back_b = attend_back(1, after(mixed_gradient, *summed_a, *wave))
    wave = (back_b[0], dkv_a, via_one, via_zero)
    x_one, y_zero = swap_dp(after(to_x[1], *wave), 1), swap_dp(after(to_y[0], *wave), 2)
    summed_b = sum_cores(back_b[1], after(back_b[2], *wave))
    parts_b = [shift_z_down(summed_b[s], s) for s in (1, 2, 3)]

    def sum_pair(parts):
        arrived = swap_core(parts[4])
        return [add_low(parts[k], arrived[4 * k : 4 * k + 4]) for k in range(4)]

    def share_square(mine):
        return [mine[0]] + [swap_dp(mine[k], k) for k in (1, 2, 3)]

    def reduce_all(summed):
        out = [add_low(*[piece[s] for piece in summed]) for s in range(4)]
        total = out[0].astype(jnp.float32)
        for s in (1, 2, 3):
            total = total + shift_z(out[s], -s).astype(jnp.float32)
        return total

    q_results = run(
        finish_q_kernel,
        "finish_q",
        (
            ids,
            *first_own,
            *first_other,
            after(n1, *wave),
            back_a[0].reshape(width, cap),
            back_b[0].reshape(width, cap),
            *out_grads,
        ),
        [SMEM] + [VMEM] * 18,
        [struct(blocks, jnp.float32)]
        + [struct((4, 2 * q_rows, wide))] * 4
        + [struct((16, 2 * q_rows, wide))],
        [VMEM] * 6,
        [
            pltpu.VMEM((4 * wide, rows), jnp.bfloat16),
            pltpu.VMEM((width, rows), jnp.float32),
            pltpu.VMEM((8 * q_rows, rows), jnp.bfloat16),
        ],
        4 * width * width * rows,
        24,
    )
    dn_q = q_results[0]
    dkv_b = summed_b[0].astype(jnp.float32)
    for part in parts_b:
        dkv_b = dkv_b + part.astype(jnp.float32)
    x_zero = swap_dp(add_low(to_x[0], after(via_zero, dkv_b)), 1)
    y_one = swap_dp(add_low(to_y[1], after(via_one, dkv_b)), 2)
    hop = shift_z(add_low(after(home[3], dkv_b), x_three, y_three), -1)
    q_out_mine = sum_pair(q_results[1:])
    q_out_shared = share_square(q_out_mine)
    q_out_total = reduce_all(q_out_shared)
    grad_query = q_out_total[:q_cols, :block].T
    grad_out = q_out_total[q_rows : q_rows + q_cols, :block].T

    dkv_pieces, *kv_grads = run(
        kv_grad_kernel,
        "kv_grad",
        (ids, after(n1, x_one, y_zero, *q_out_mine), dkv_a, dkv_b, cosine, sine),
        [SMEM] + [VMEM] * 5,
        [struct((16 * k_cols, rows))]
        + [struct((4, 2 * k_cols, wide))] * 4
        + [struct((16, 2 * k_cols, wide))],
        [VMEM] * 6,
        [
            pltpu.VMEM((4 * wide, rows), jnp.bfloat16),
            pltpu.VMEM((2 * kv_width, rows), jnp.float32),
        ],
        4 * kv_width * width * rows,
        20,
    )
    grad_tokens, gain_one_grad = run(
        finish_kernel,
        "finish",
        (ids, *first_own, *first_other, dkv_pieces, dn_q, dh, after(x, x_zero, y_one), gain_one),
        [SMEM] + [VMEM] * 15,
        [struct((width, rows), jnp.float32), struct((width, 1), jnp.float32)],
        [VMEM] * 2,
        [],
        4 * kv_width * width * rows,
        24,
    )
    grad_tokens = grad_tokens.T.reshape(batches, cap, width)
    kv_mine = sum_pair(kv_grads)
    hop = shift_z(add_low(home[2], x_two, y_two, after(hop, dkv_pieces)), -1)
    hop = shift_z(add_low(home[1], x_one, y_one, after(hop, *kv_mine)), -1)
    mlp_total = (
        home[0].astype(jnp.float32)
        + y_zero.astype(jnp.float32)
        + x_zero.astype(jnp.float32)
        + hop.astype(jnp.float32)
    )
    grad_gate = mlp_total[:half, :block].T
    grad_up = mlp_total[half : 2 * half, :block].T
    down_total = mlp_total[2 * half :, :block]
    left, right = down_total[:, :q_cols], down_total[:, q_cols:]
    stay = jnp.where(core_id == 0, left, right)
    give = jnp.where(core_id == 0, right, left).astype(jnp.bfloat16)
    taken = swap_core(give).astype(jnp.float32)
    grad_down = jnp.where(
        core_id == 0, jnp.concatenate([stay, taken], 0), jnp.concatenate([taken, stay], 0)
    )

    kv_total = reduce_all(share_square(kv_mine))
    gain_total = after(jnp.concatenate([gain_one_grad, gain_two_grad], 1).T, *kv_mine)
    gain_total = gain_total + swap_core(gain_total)
    gain_total = gain_total + swap_dp(gain_total, 1)
    gain_total = gain_total + swap_dp(gain_total, 2)
    for mask in (2, 4):
        gain_total = gain_total + lax.ppermute(
            gain_total, "fsdp", [(j, j ^ mask) for j in range(8)]
        )
    gain_grad = lax.dynamic_slice_in_dim(gain_total, slot * q_cols, q_cols, 1)
    return (
        output,
        grad_tokens,
        grad_query,
        kv_total[:k_cols, :block].T,
        kv_total[k_cols:, :block].T,
        grad_out,
        grad_gate,
        grad_up,
        grad_down,
        gain_grad,
    )


def solution(mesh):
    in_specs = (
        P(None, ("dp", "fsdp"), None),
        P(None, ("dp", "fsdp"), None),
        P(None, ("dp", "fsdp")),
        P("dp", "fsdp"),
        P("dp", "fsdp"),
        P("dp", "fsdp"),
        P("dp", "fsdp"),
        P("dp", "fsdp"),
        P("dp", "fsdp"),
        P("dp", "fsdp"),
        P(None, "fsdp"),
    )
    out_specs = (
        P(None, ("dp", "fsdp"), None),
        P(None, ("dp", "fsdp"), None),
        P("dp", "fsdp"),
        P("dp", "fsdp"),
        P("dp", "fsdp"),
        P("dp", "fsdp"),
        P("dp", "fsdp"),
        P("dp", "fsdp"),
        P("dp", "fsdp"),
        P(None, "fsdp"),
    )
    square = mesh.shape["dp"] == 4 and mesh.shape["fsdp"] == 8
    return jax.shard_map(
        fast if square else local, mesh=mesh, in_specs=in_specs, out_specs=out_specs, check_vma=False)
```

```python
import functools

import jax
import jax.numpy as jnp
from jax import lax
from jax.experimental import pallas as pl
from jax.experimental.pallas import tpu as pltpu
from jax.sharding import PartitionSpec as P

MODEL_WIDTH = 960
QUERY_HEADS = 15
KEY_HEADS = 5
HEAD_WIDTH = 64


EPSILON = 1e-05
ROPE_BASE = 100000.0
SCORE_SCALE = 0.125


def rope_tables(position, head_size):
    half_size = head_size // 2
    frequency = ROPE_BASE ** (-(jnp.arange(half_size, dtype=jnp.float32) * 2.0) / head_size)
    angles = position.astype(jnp.float32)[:, None] * frequency[None, :]
    return (jnp.cos(angles)[:, None, :], jnp.sin(angles)[:, None, :])


def apply_rotation(values, cosine_table, sine_values):
    half_size = values.shape[-1] // 2
    front_half = values[..., :half_size]
    back_half = values[..., half_size:]
    return jnp.concatenate(
        [
            front_half * cosine_table - back_half * sine_values,
            back_half * cosine_table + front_half * sine_values,
        ],
        -1,
    )


def normalize(values, gain_row):
    inv_rms = lax.rsqrt(jnp.mean(values * values, -1, keepdims=True) + EPSILON)
    return (values * inv_rms * gain_row, inv_rms)


def norm_back(values, inv_rms, gain_row, incoming):
    weighted = incoming * gain_row
    return inv_rms * weighted - values * inv_rms * inv_rms * inv_rms * jnp.mean(
        weighted * values, -1, keepdims=True
    )


def build_mask(count_row, device, slot_capacity):
    group_width = count_row.shape[0]
    local_slot = jnp.arange(slot_capacity, dtype=jnp.int32)
    offsets = jnp.cumsum(count_row) - count_row
    is_mine = jnp.arange(group_width, dtype=jnp.int32) == device
    own_offset = jnp.sum(jnp.where(is_mine, offsets, 0))
    own_count = jnp.sum(jnp.where(is_mine, count_row, 0))
    query_pos = own_offset + local_slot
    query_valid = local_slot < own_count
    key_pos = (offsets[:, None] + local_slot[None, :]).reshape(-1)
    key_valid = (local_slot[None, :] < count_row[:, None]).reshape(-1)
    slot_ids = jnp.arange(group_width * slot_capacity, dtype=jnp.int32)
    own_slots = device * slot_capacity + local_slot
    allowed = query_valid[:, None] & key_valid[None, :] & (
        key_pos[None, :] <= query_pos[:, None]
    ) | (slot_ids[None, :] == own_slots[:, None])
    return (allowed, query_pos)


def kept_fetch(w_query, key_weight, value_weight, w_out, w_gate, w_up, w_down, gains):
    columns = (
        lax.all_gather(w_query, "fsdp", axis=1, tiled=True),
        lax.all_gather(key_weight, "fsdp", axis=1, tiled=True),
        lax.all_gather(value_weight, "fsdp", axis=1, tiled=True),
        lax.all_gather(w_out, "fsdp", axis=1, tiled=True),
        lax.all_gather(w_gate, "fsdp", axis=1, tiled=True),
        lax.all_gather(w_up, "fsdp", axis=1, tiled=True),
        lax.all_gather(w_down, "fsdp", axis=1, tiled=True),
        lax.all_gather(gains, "fsdp", axis=1, tiled=True),
    )
    matrices = (
        lax.all_gather(columns[0], "dp", axis=0, tiled=True),
        lax.all_gather(columns[1], "dp", axis=0, tiled=True),
        lax.all_gather(columns[2], "dp", axis=0, tiled=True),
        lax.all_gather(columns[3], "dp", axis=0, tiled=True),
        lax.all_gather(columns[4], "dp", axis=0, tiled=True),
        lax.all_gather(columns[5], "dp", axis=0, tiled=True),
        lax.all_gather(columns[6], "dp", axis=0, tiled=True),
    )
    return (matrices, columns[7].astype(jnp.float32))


def times_transpose(left, right):
    return jnp.einsum("rk,jk->rj", left, right, preferred_element_type=jnp.float32)


def rows_product(left, right):
    return jnp.einsum("rd,rk->dk", left, right, preferred_element_type=jnp.float32)


def local(
    tokens, cotangent, counts, w_query, key_weight, value_weight, w_out, w_gate, w_up, w_down, gains
):
    group_counts = lax.all_gather(counts, "fsdp", axis=1, tiled=True)
    device = lax.axis_index("fsdp")
    slot_capacity = tokens.shape[1]
    key_value_width = KEY_HEADS * HEAD_WIDTH
    device_share = QUERY_HEADS // KEY_HEADS
    kept_weights, kept_gain = kept_fetch(
        w_query, key_weight, value_weight, w_out, w_gate, w_up, w_down, gains
    )
    outputs = []
    grad_inputs = []
    saved = [[] for index_unused in range(11)]
    gain_one_total = jnp.zeros((MODEL_WIDTH,), jnp.float32)
    gain_two_total = jnp.zeros((MODEL_WIDTH,), jnp.float32)
    for micro_idx in range(tokens.shape[0]):
        matrices, gain_pair = (kept_weights, kept_gain)
        full_query, full_key, full_value, full_out, full_gate, full_up, full_down = matrices
        inputs = tokens[micro_idx].astype(jnp.float32)
        allowed, query_pos = build_mask(group_counts[micro_idx], device, slot_capacity)
        cosine_table, sine_values = rope_tables(query_pos, HEAD_WIDTH)
        first_normed, scale_one = normalize(inputs, gain_pair[0])
        normed_low = first_normed.astype(jnp.bfloat16)
        reduced_query = apply_rotation(
            jnp.dot(normed_low, full_query, preferred_element_type=jnp.float32).reshape(
                slot_capacity, QUERY_HEADS, HEAD_WIDTH
            ),
            cosine_table,
            sine_values,
        ).astype(jnp.bfloat16)
        key_low = (
            apply_rotation(
                jnp.dot(normed_low, full_key, preferred_element_type=jnp.float32).reshape(
                    slot_capacity, KEY_HEADS, HEAD_WIDTH
                ),
                cosine_table,
                sine_values,
            )
            .astype(jnp.bfloat16)
            .reshape(slot_capacity, key_value_width)
        )
        value_low = jnp.dot(normed_low, full_value, preferred_element_type=jnp.float32).astype(
            jnp.bfloat16
        )
        grouped_keys, grouped_values = (
            lax.all_gather(key_low, "fsdp", axis=0, tiled=True),
            lax.all_gather(value_low, "fsdp", axis=0, tiled=True),
        )
        heads_of_key = grouped_keys.reshape(-1, KEY_HEADS, HEAD_WIDTH)
        heads_of_value = grouped_values.reshape(-1, KEY_HEADS, HEAD_WIDTH)
        heads_of_query = reduced_query.reshape(slot_capacity, KEY_HEADS, device_share, HEAD_WIDTH)
        scores = (
            jnp.einsum(
                "qngd,knd->ngqk", heads_of_query, heads_of_key, preferred_element_type=jnp.float32
            )
            * SCORE_SCALE
        )
        masked = jnp.where(allowed, scores, -1e30)
        row_top = jnp.max(masked, -1, keepdims=True)
        exponent = jnp.where(allowed, jnp.exp(masked - row_top), 0.0)
        row_total = jnp.sum(exponent, -1, keepdims=True)
        prob_low = (exponent / row_total).astype(jnp.bfloat16)
        log_total = row_top + jnp.log(row_total)
        mixed_heads = jnp.einsum(
            "ngqk,knd->qngd", prob_low, heads_of_value, preferred_element_type=jnp.float32
        ).reshape(slot_capacity, MODEL_WIDTH)
        attended = mixed_heads.astype(jnp.bfloat16)
        hidden_state = inputs + jnp.dot(attended, full_out, preferred_element_type=jnp.float32)
        normed_two, scale_two = normalize(hidden_state, gain_pair[1])
        normed_two_low = normed_two.astype(jnp.bfloat16)
        gate_act = jnp.dot(normed_two_low, full_gate, preferred_element_type=jnp.float32)
        upward = jnp.dot(normed_two_low, full_up, preferred_element_type=jnp.float32)
        sigmoid_gate = jax.nn.sigmoid(gate_act)
        product = (gate_act * sigmoid_gate * upward).astype(jnp.bfloat16)
        outputs.append(
            (hidden_state + jnp.dot(product, full_down, preferred_element_type=jnp.float32)).astype(
                jnp.bfloat16
            )
        )
        matrices, gain_pair = (kept_weights, kept_gain)
        full_query, full_key, full_value, full_out, full_gate, full_up, full_down = matrices
        grad_low = cotangent[micro_idx]
        grad_product = times_transpose(grad_low, full_down)
        grad_gate = (
            grad_product * upward * sigmoid_gate * (1.0 + gate_act * (1.0 - sigmoid_gate))
        ).astype(jnp.bfloat16)
        grad_upward = (grad_product * gate_act * sigmoid_gate).astype(jnp.bfloat16)
        grad_normed_two = times_transpose(grad_gate, full_gate) + times_transpose(
            grad_upward, full_up
        )
        gain_two_total = gain_two_total + jnp.sum(grad_normed_two * hidden_state * scale_two, 0)
        grad_hidden = grad_low.astype(jnp.float32) + norm_back(
            hidden_state, scale_two, gain_pair[1], grad_normed_two
        )
        grad_branch = grad_hidden.astype(jnp.bfloat16)
        mixed_gradient = times_transpose(grad_branch, full_out).astype(jnp.bfloat16)
        head_gradient = mixed_gradient.reshape(slot_capacity, KEY_HEADS, device_share, HEAD_WIDTH)
        again_scores = (
            jnp.einsum(
                "qngd,knd->ngqk", heads_of_query, heads_of_key, preferred_element_type=jnp.float32
            )
            * SCORE_SCALE
        )
        probability = jnp.where(allowed, jnp.exp(again_scores - log_total), 0.0)
        grad_prob = jnp.einsum(
            "qngd,knd->ngqk", head_gradient, heads_of_value, preferred_element_type=jnp.float32
        )
        row_delta = jnp.sum(probability * grad_prob, -1, keepdims=True)
        grad_scores = (probability * (grad_prob - row_delta)).astype(jnp.bfloat16)
        grad_query_rot = (
            jnp.einsum(
                "ngqk,knd->qngd", grad_scores, heads_of_key, preferred_element_type=jnp.float32
            ).reshape(slot_capacity, QUERY_HEADS, HEAD_WIDTH)
            * SCORE_SCALE
        )
        key_part = (
            jnp.einsum(
                "ngqk,qngd->knd", grad_scores, heads_of_query, preferred_element_type=jnp.float32
            ).reshape(-1, key_value_width)
            * SCORE_SCALE
        )
        value_part = jnp.einsum(
            "ngqk,qngd->knd",
            probability.astype(jnp.bfloat16),
            head_gradient,
            preferred_element_type=jnp.float32,
        ).reshape(-1, key_value_width)
        key_gradient, value_grad = (
            lax.psum_scatter(
                key_part.astype(jnp.bfloat16), "fsdp", scatter_dimension=0, tiled=True
            ).astype(jnp.float32),
            lax.psum_scatter(
                value_part.astype(jnp.bfloat16), "fsdp", scatter_dimension=0, tiled=True
            ).astype(jnp.float32),
        )
        grad_query = (
            apply_rotation(grad_query_rot, cosine_table, -sine_values)
            .astype(jnp.bfloat16)
            .reshape(slot_capacity, MODEL_WIDTH)
        )
        grad_key = (
            apply_rotation(
                key_gradient.reshape(slot_capacity, KEY_HEADS, HEAD_WIDTH),
                cosine_table,
                -sine_values,
            )
            .astype(jnp.bfloat16)
            .reshape(slot_capacity, key_value_width)
        )
        grad_value = value_grad.astype(jnp.bfloat16)
        grad_normed_one = (
            times_transpose(grad_query, full_query)
            + times_transpose(grad_key, full_key)
            + times_transpose(grad_value, full_value)
        )
        gain_one_total = gain_one_total + jnp.sum(grad_normed_one * inputs * scale_one, 0)
        grad_inputs.append(
            grad_hidden + norm_back(inputs, scale_one, gain_pair[0], grad_normed_one)
        )
        kept_rows = (
            normed_low,
            grad_query,
            grad_key,
            grad_value,
            attended,
            grad_branch,
            normed_two_low,
            grad_gate,
            grad_upward,
            product,
            grad_low,
        )
        for slot_index in range(11):
            saved[slot_index].append(kept_rows[slot_index])
    joined = [jnp.concatenate(column_list, 0) for column_list in saved]
    gain_terms = jnp.stack([gain_one_total, gain_two_total], 0)
    slices = (
        lax.all_to_all(joined[1], "fsdp", split_axis=1, concat_axis=0, tiled=True),
        lax.all_to_all(joined[2], "fsdp", split_axis=1, concat_axis=0, tiled=True),
        lax.all_to_all(joined[3], "fsdp", split_axis=1, concat_axis=0, tiled=True),
        lax.all_to_all(joined[5], "fsdp", split_axis=1, concat_axis=0, tiled=True),
        lax.all_to_all(joined[7], "fsdp", split_axis=1, concat_axis=0, tiled=True),
        lax.all_to_all(joined[8], "fsdp", split_axis=1, concat_axis=0, tiled=True),
        lax.all_to_all(joined[10], "fsdp", split_axis=1, concat_axis=0, tiled=True),
    )
    pieces = (
        lax.all_gather(joined[0], "fsdp", axis=0, tiled=True),
        lax.all_gather(joined[4], "fsdp", axis=0, tiled=True),
        lax.all_gather(joined[6], "fsdp", axis=0, tiled=True),
        lax.all_gather(joined[9], "fsdp", axis=0, tiled=True),
    )
    picked = [member for member in slices]
    gain_part = lax.psum_scatter(gain_terms, "fsdp", scatter_dimension=1, tiled=True)
    summed_rows = (
        lax.psum_scatter(
            rows_product(pieces[0], picked[0]).astype(jnp.bfloat16),
            "dp",
            scatter_dimension=0,
            tiled=True,
        ).astype(jnp.float32),
        lax.psum_scatter(
            rows_product(pieces[0], picked[1]).astype(jnp.bfloat16),
            "dp",
            scatter_dimension=0,
            tiled=True,
        ).astype(jnp.float32),
        lax.psum_scatter(
            rows_product(pieces[0], picked[2]).astype(jnp.bfloat16),
            "dp",
            scatter_dimension=0,
            tiled=True,
        ).astype(jnp.float32),
        lax.psum_scatter(
            rows_product(pieces[1], picked[3]).astype(jnp.bfloat16),
            "dp",
            scatter_dimension=0,
            tiled=True,
        ).astype(jnp.float32),
        lax.psum_scatter(
            rows_product(pieces[2], picked[4]).astype(jnp.bfloat16),
            "dp",
            scatter_dimension=0,
            tiled=True,
        ).astype(jnp.float32),
        lax.psum_scatter(
            rows_product(pieces[2], picked[5]).astype(jnp.bfloat16),
            "dp",
            scatter_dimension=0,
            tiled=True,
        ).astype(jnp.float32),
        lax.psum_scatter(
            rows_product(pieces[3], picked[6]).astype(jnp.bfloat16),
            "dp",
            scatter_dimension=0,
            tiled=True,
        ).astype(jnp.float32),
    )
    gain_grad = lax.psum(gain_part, "dp")
    return (
        jnp.stack(outputs, 0),
        jnp.stack(grad_inputs, 0),
        summed_rows[0],
        summed_rows[1],
        summed_rows[2],
        summed_rows[3],
        summed_rows[4],
        summed_rows[5],
        summed_rows[6],
        gain_grad,
    )


def swap_core(value):
    return lax.ppermute(value, "fsdp", [(j, j ^ 1) for j in range(8)])


def swap_dp(value, mask):
    return lax.ppermute(value, "dp", [(j, j ^ mask) for j in range(4)])


def shift_z(value, step):
    return lax.ppermute(value, "fsdp", [(j, (j + 2 * step) % 8) for j in range(8)])


def shift_z_up(value, step):
    return lax.ppermute(value, "fsdp", [(j, j + 2 * step) for j in range(8) if j + 2 * step < 8])


def shift_z_down(value, step):
    return lax.ppermute(value, "fsdp", [(j, j - 2 * step) for j in range(8) if j - 2 * step >= 0])


def add_low(*terms):
    total = terms[0].astype(jnp.float32)
    for term in terms[1:]:
        total = total + term.astype(jnp.float32)
    return total.astype(jnp.bfloat16)


def product_nn(left, right):
    return lax.dot_general(
        left, right, (((1,), (0,)), ((), ())), preferred_element_type=jnp.float32
    )


def product_nt(left, right):
    return lax.dot_general(
        left, right, (((1,), (1,)), ((), ())), preferred_element_type=jnp.float32
    )


def product_tn(left, right):
    return lax.dot_general(
        left, right, (((0,), (0,)), ((), ())), preferred_element_type=jnp.float32
    )


VMEM = pl.BlockSpec(memory_space=pltpu.VMEM)
SMEM = pl.BlockSpec(memory_space=pltpu.SMEM)
HBM = pl.BlockSpec(memory_space=pltpu.HBM)


def run(body, name, ins, in_specs, outs, out_specs, scratch, flops, megabytes):
    moved = sum(v.size * v.dtype.itemsize for v in ins)
    moved += sum(v.size * v.dtype.itemsize for v in outs)
    return pl.pallas_call(
        body,
        out_shape=tuple(outs),
        in_specs=in_specs,
        out_specs=tuple(out_specs),
        scratch_shapes=scratch,
        compiler_params=pltpu.CompilerParams(vmem_limit_bytes=megabytes * 1024 * 1024),
        cost_estimate=pl.CostEstimate(flops=flops, bytes_accessed=moved, transcendentals=0),
        name=name,
    )(*ins)


def struct(shape, dtype=jnp.bfloat16):
    return jax.ShapeDtypeStruct(shape, dtype)


def column_index(ids_ref, core_rel, s):
    return 2 * lax.rem(ids_ref[1] - s + 4, 4) + (ids_ref[2] ^ core_rel)


def start_row(index, size):
    return pl.ds(pl.multiple_of(index * size, 8), size)


def after(value, *others):
    return lax.optimization_barrier((value,) + others)[0]


def pack_first_kernel(counts_ref, wq_ref, wk_ref, wv_ref, gains_ref, out_ref):
    block = wq_ref.shape[0]
    gains = gains_ref[...].astype(jnp.float32)
    row = lax.broadcasted_iota(jnp.int32, (8, block), 0)
    lane = lax.broadcasted_iota(jnp.int32, (8, block), 1)
    first = jnp.concatenate([gains[:1], gains[1:]], 1)
    used = jnp.where(
        lane == 0,
        counts_ref[0, 0].astype(jnp.float32),
        jnp.where(lane == 1, counts_ref[1, 0].astype(jnp.float32), 0.0),
    )
    extra = jnp.where(row == 0, first, jnp.where(row == 1, used, 0.0))
    full = jnp.concatenate(
        [
            wq_ref[...].astype(jnp.float32).T,
            extra,
            wk_ref[...].astype(jnp.float32),
            wv_ref[...].astype(jnp.float32),
        ],
        0,
    )
    out_ref[...] = jnp.zeros_like(out_ref)
    out_ref[:, :block] = full.astype(jnp.bfloat16)


def pack_mlp_kernel(ids_ref, wg_ref, wu_ref, wd_ref, other_ref, wo_ref, out_ref):
    half, block = wg_ref.shape
    core = ids_ref[2]
    out_ref[...] = jnp.zeros_like(out_ref)
    out_ref[:half, :block] = wg_ref[...]
    out_ref[half : 2 * half, :block] = wu_ref[...]
    down = wd_ref[...].astype(jnp.float32)
    own = jnp.where(core == 0, down[:, :half], down[:, half:])
    other = other_ref[:, :half].astype(jnp.float32)
    low = jnp.where(core == 0, own, other)
    high = jnp.where(core == 0, other, own)
    out_ref[2 * half : 3 * half, :block] = jnp.concatenate([low, high], 0).T.astype(jnp.bfloat16)
    out_ref[3 * half :, :block] = jnp.concatenate(
        [wo_ref[...].astype(jnp.float32).T, jnp.zeros((8, block), jnp.float32)], 0
    ).astype(jnp.bfloat16)


def turn_in_kernel(x_ref, dy_ref, xt_ref, dyt_ref):
    xt_ref[...] = x_ref[...].astype(jnp.float32).T.astype(jnp.bfloat16)
    dyt_ref[...] = jnp.zeros_like(dyt_ref)
    dyt_ref[:, : dy_ref.shape[0]] = dy_ref[...].astype(jnp.float32).T.astype(jnp.bfloat16)


def fill_relative(ids_ref, target_ref, *sources):
    block, lanes = sources[0].shape[1], target_ref.shape[1]
    wide = target_ref.shape[0] // 4
    for k in range(4):
        parts = [source[ids_ref[0] ^ k] for source in sources]
        target_ref[k * wide : k * wide + block, :] = (
            parts[0] if len(parts) == 1 else jnp.concatenate(parts, 1)
        )
        target_ref[k * wide + block : (k + 1) * wide, :] = jnp.zeros(
            (wide - block, lanes), target_ref.dtype
        )


def wide_rows(refs, s, low, high):
    along, by_x, by_y, far_a, far_b = refs
    far = far_a if s < 2 else far_b
    return jnp.concatenate(
        [along[s, low:high], by_x[s, low:high], by_y[s, low:high], far[s % 2, low:high]], 1
    )


def project_kernel(*refs):
    ids_ref, own, other = refs[0], refs[1:6], refs[6:11]
    n1_ref, cos_ref, sin_ref, q_ref, kv_ref, all_ref, proj_ref, turned_ref, rel_ref = refs[11:]
    width = n1_ref.shape[0] * n1_ref.shape[1]
    kv_width = KEY_HEADS * HEAD_WIDTH
    q_cols, k_cols = width // 8, kv_width // 8
    depth = own[0].shape[1]
    fill_relative(ids_ref, rel_ref, n1_ref)
    for core_rel, weights in ((0, own), (1, other)):
        for s in range(4):
            f = column_index(ids_ref, core_rel, s)
            all_ref[core_rel * 4 + s] = wide_rows(weights, s, 0, depth)
            total = product_nn(all_ref[core_rel * 4 + s], rel_ref[...])
            proj_ref[start_row(f, q_cols), :] = total[:q_cols]
            proj_ref[pl.ds(pl.multiple_of(width + f * k_cols, 8), k_cols), :] = total[
                q_cols + 8 : q_cols + 8 + k_cols
            ]
            proj_ref[pl.ds(pl.multiple_of(width + kv_width + f * k_cols, 8), k_cols), :] = total[
                q_cols + 8 + k_cols :
            ]
    cosine, sine = cos_ref[...], sin_ref[...]
    half = HEAD_WIDTH // 2

    def heads(head, carry):
        front = proj_ref[pl.ds(pl.multiple_of(head * HEAD_WIDTH, 8), half), :]
        back = proj_ref[pl.ds(pl.multiple_of(head * HEAD_WIDTH + half, 8), half), :]
        q_ref[head, :half, :] = (
            (front * cosine - back * sine).astype(jnp.bfloat16) * SCORE_SCALE
        ).astype(jnp.bfloat16)
        q_ref[head, half:, :] = (
            (back * cosine + front * sine).astype(jnp.bfloat16) * SCORE_SCALE
        ).astype(jnp.bfloat16)
        return carry

    lax.fori_loop(0, QUERY_HEADS, heads, 0)
    for head in range(KEY_HEADS):
        base = width + head * HEAD_WIDTH
        front = proj_ref[base : base + half, :]
        back = proj_ref[base + half : base + 2 * half, :]
        turned_ref[head * HEAD_WIDTH : head * HEAD_WIDTH + half, :] = front * cosine - back * sine
        turned_ref[head * HEAD_WIDTH + half : (head + 1) * HEAD_WIDTH, :] = (
            back * cosine + front * sine
        )
    turned_ref[kv_width:, :] = proj_ref[width + kv_width :, :]
    kv_ref[...] = turned_ref[...].T.astype(jnp.bfloat16)


def stage_heads(mb, cap, blocks, k_ref, v_ref):
    kv_width = KEY_HEADS * HEAD_WIDTH
    for block, source in enumerate(blocks):
        rows = source[mb * cap : (mb + 1) * cap, :]
        for n in range(KEY_HEADS):
            lanes = n * HEAD_WIDTH
            k_ref[n, block * cap : (block + 1) * cap, :] = rows[:, lanes : lanes + HEAD_WIDTH]
            lanes += kv_width
            v_ref[n, block * cap : (block + 1) * cap, :] = rows[:, lanes : lanes + HEAD_WIDTH]


def stage_bias(ids_ref, counts_ref, mb, cap, share, bias_ref):
    slot = ids_ref[3]
    own_count = counts_ref[mb * 8 + slot]
    key = lax.broadcasted_iota(jnp.int32, (cap, cap), 0)
    query = lax.broadcasted_iota(jnp.int32, (cap, cap), 1)
    query_used = query < own_count
    for core_rel in range(2):
        for s in range(4):
            block = core_rel * 4 + s
            f = column_index(ids_ref, core_rel, s)
            count = counts_ref[mb * 8 + f]
            reach = jnp.where(f < slot, cap, jnp.where(f == slot, 0, -2 * cap))
            self_off = jnp.where(f == slot, 0, 2 * cap)
            allowed = (query_used & (key < count) & (key <= query + reach)) | (
                key == query + self_off
            )
            tile = jnp.where(allowed, 0.0, -1e30)
            for g in range(share):
                bias_ref[block * cap : (block + 1) * cap, g * cap : (g + 1) * cap] = tile


def join_heads(ref, n, share, mb, cap):
    return jnp.concatenate(
        [ref[share * n + g, :, mb * cap : (mb + 1) * cap] for g in range(share)], 1
    )


def attend_kernel(mb, *refs):
    ids_ref, counts_ref, q_ref = refs[:3]
    blocks = refs[3:11]
    att_ref, lse_ref, k_ref, v_ref, bias_ref = refs[11:]
    cap = q_ref.shape[2] // 2
    share = QUERY_HEADS // KEY_HEADS
    stage_heads(mb, cap, blocks, k_ref, v_ref)
    stage_bias(ids_ref, counts_ref, mb, cap, share, bias_ref)

    def body(n, carry):
        scores = product_nn(k_ref[n], join_heads(q_ref, n, share, mb, cap)) + bias_ref[...]
        top = jnp.max(scores, 0, keepdims=True)
        exponent = jnp.exp(scores - top)
        total = jnp.sum(exponent, 0, keepdims=True)
        mixed = product_tn(v_ref[n], exponent.astype(jnp.bfloat16)) / total
        mixed = mixed.astype(jnp.bfloat16)
        for g in range(share):
            att_ref[share * n + g] = mixed[:, g * cap : (g + 1) * cap]
        lse_ref[n] = top + jnp.log(total)
        return carry

    lax.fori_loop(0, KEY_HEADS, body, 0)


def attend_back_kernel(mb, *refs):
    ids_ref, counts_ref, q_ref, do_ref, k_ref, v_ref, lse_ref, cos_ref, sin_ref = refs[:9]
    dq_ref = refs[9]
    targets = [ref.at[s] for ref in refs[10:12] for s in range(4)]
    bias_ref, dk_ref, dv_ref = refs[12:]
    cap = q_ref.shape[2] // 2
    share = QUERY_HEADS // KEY_HEADS
    half = HEAD_WIDTH // 2
    kv_width = KEY_HEADS * HEAD_WIDTH
    stage_bias(ids_ref, counts_ref, mb, cap, share, bias_ref)
    cosine = jnp.concatenate([cos_ref[:, mb * cap : (mb + 1) * cap]] * share, 1)
    sine = jnp.concatenate([sin_ref[:, mb * cap : (mb + 1) * cap]] * share, 1)

    def body(n, carry):
        query = join_heads(q_ref, n, share, mb, cap)
        grad = join_heads(do_ref, n, share, mb, cap)
        keys = k_ref[n]
        prob = jnp.exp(product_nn(keys, query) + bias_ref[...] - lse_ref[n])
        dprob = product_nn(v_ref[n], grad)
        delta = jnp.sum(prob * dprob, 0, keepdims=True)
        dscore = (prob * (dprob - delta)).astype(jnp.bfloat16)
        dq = product_tn(keys, dscore) * SCORE_SCALE
        front, back = dq[:half], dq[half:]
        turned = jnp.concatenate(
            [front * cosine + back * sine, back * cosine - front * sine], 0
        ).astype(jnp.bfloat16)
        for g in range(share):
            dq_ref[share * n + g] = turned[:, g * cap : (g + 1) * cap]
        dk_ref[n] = product_nt(dscore, query).astype(jnp.bfloat16)
        dv_ref[n] = product_nt(prob.astype(jnp.bfloat16), grad).astype(jnp.bfloat16)
        return carry

    lax.fori_loop(0, KEY_HEADS, body, 0)
    for block, target in enumerate(targets):
        for n in range(KEY_HEADS):
            lanes = n * HEAD_WIDTH
            target[:, lanes : lanes + HEAD_WIDTH] = dk_ref[n, block * cap : (block + 1) * cap, :]
            lanes += kv_width
            target[:, lanes : lanes + HEAD_WIDTH] = dv_ref[n, block * cap : (block + 1) * cap, :]


def collect_kernel(*refs):
    pieces, out_ref, sem = refs[:16], refs[16], refs[17]
    rows, wide = out_ref.shape[1], pieces[0].shape[1]
    copies = []
    for k in range(4):
        for s in range(4):
            copies.append(
                pltpu.make_async_copy(
                    pieces[k * 4 + s].at[pl.ds(pieces[0].shape[0] - rows, rows)],
                    out_ref.at[s, :, pl.ds(k * wide, wide)],
                    sem.at[k * 4 + s],
                )
            )
    for copy in copies:
        copy.start()
    for copy in copies:
        copy.wait()


def hidden_kernel(
    ids_ref, own_ref, other_ref, att_a_ref, att_b_ref, x_ref, gain_ref, h_ref, n2_ref, rel_ref
):
    q_cols, rows = h_ref.shape[0] // 8, h_ref.shape[1]
    fill_relative(ids_ref, rel_ref, att_a_ref, att_b_ref)
    for core_rel, w_ref in ((0, own_ref), (1, other_ref)):
        for s in range(4):
            f = column_index(ids_ref, core_rel, s)
            h_ref[start_row(f, q_cols), :] = product_nn(w_ref[s], rel_ref[...])[:q_cols]
    h = h_ref[...] + x_ref[...].astype(jnp.float32)
    h_ref[...] = h
    n2_ref[...] = jnp.zeros_like(n2_ref)
    n2_ref[:, :rows] = (h * mean_square(h) * gain_ref[...]).astype(jnp.bfloat16)


def turn_point_kernel(
    ids_ref,
    parts_ref,
    arrived_ref,
    h_ref,
    dy_ref,
    gain_ref,
    own_ref,
    other_ref,
    out_ref,
    dh_ref,
    do_ref,
    gain_grad_ref,
    pieces_ref,
    da_ref,
):
    width, rows = h_ref.shape
    q_cols = width // 8
    block = do_ref.shape[1]
    wide = own_ref.shape[2] // 4
    h = h_ref[...]
    out_ref[...] = (h + parts_ref[0] + arrived_ref[0, :, :rows].astype(jnp.float32)).astype(
        jnp.bfloat16
    )
    dn = parts_ref[1] + arrived_ref[1, :, :rows].astype(jnp.float32)
    rms = mean_square(h)
    gain_grad_ref[...] = jnp.sum(dn * h * rms, 1, keepdims=True)
    weighted = dn * gain_ref[...]
    dh = (
        dy_ref[:, :rows].astype(jnp.float32)
        + rms * weighted
        - h * (rms * rms * rms * jnp.mean(weighted * h, 0, keepdims=True))
    )
    dh_ref[...] = dh
    da_ref[...] = dh
    spread(ids_ref, da_ref, pieces_ref, q_cols)
    half = pieces_ref.shape[0] // 2
    mixed = product_tn(own_ref[...].reshape(half, 4 * wide), pieces_ref[:half, :])
    mixed += product_tn(other_ref[...].reshape(half, 4 * wide), pieces_ref[half:, :])
    mixed = mixed.astype(jnp.bfloat16)
    for k in range(4):
        do_ref[ids_ref[0] ^ k] = mixed[k * wide : k * wide + block]


def spread(ids_ref, source_ref, target_ref, cols):
    rows = source_ref.shape[1]
    for core_rel in range(2):
        for s in range(4):
            f = column_index(ids_ref, core_rel, s)
            low = (core_rel * 4 + s) * (cols + 8)
            target_ref[low : low + cols + 8, :] = jnp.concatenate(
                [source_ref[start_row(f, cols), :], jnp.zeros((8, rows), jnp.float32)], 0
            ).astype(jnp.bfloat16)


def targets_of(refs):
    return list(refs[:4]) + [refs[4].at[pl.ds(4 * k, 4)] for k in range(4)]


def out_grad_kernel(ids_ref, att_a_ref, att_b_ref, pieces_ref, *refs):
    grads, att_rel = targets_of(refs[:5]), refs[5]
    depth = pieces_ref.shape[0] // 8
    wide = att_rel.shape[0] // 4
    fill_relative(ids_ref, att_rel, att_a_ref, att_b_ref)
    for core_rel in range(2):
        for s in range(4):
            low = (core_rel * 4 + s) * depth
            got = product_nt(pieces_ref[low : low + depth, :], att_rel[...]).astype(jnp.bfloat16)
            for k in range(4):
                grads[core_rel * 4 + k][s] = got[:, k * wide : (k + 1) * wide]


def finish_q_kernel(*refs):
    ids_ref, all_ref, n1_ref, dq_a_ref, dq_b_ref = refs[:5]
    out_grads = targets_of(refs[5:10])
    dn_ref, grads = refs[10], targets_of(refs[11:16])
    n1_rel, d_ref, dq_ref = refs[16:]
    cap = dq_a_ref.shape[1]
    width = dq_a_ref.shape[0]
    q_cols = width // 8
    depth = q_cols + 8
    block = n1_ref.shape[1]
    wide = n1_rel.shape[0] // 4
    d_ref[:, :cap] = dq_a_ref[...].astype(jnp.float32)
    d_ref[:, cap:] = dq_b_ref[...].astype(jnp.float32)
    spread(ids_ref, d_ref, dq_ref, q_cols)
    fill_relative(ids_ref, n1_rel, n1_ref)
    weights = jnp.concatenate([all_ref[j, :depth, :] for j in range(8)], 0)
    dn = product_tn(weights, dq_ref[...])
    for k in range(4):
        dn_ref[ids_ref[0] ^ k] = dn[k * wide : k * wide + block]
    for core_rel in range(2):
        for s in range(4):
            low = (core_rel * 4 + s) * depth
            gq = product_nt(dq_ref[low : low + depth, :], n1_rel[...]).astype(jnp.bfloat16)
            for k in range(4):
                target = grads[core_rel * 4 + k]
                target[s, :depth, :] = gq[:, k * wide : (k + 1) * wide]
                target[s, depth:, :] = out_grads[core_rel * 4 + k][s]


def kv_grad_kernel(
    ids_ref, n1_ref, dkv_a_ref, dkv_b_ref, cos_ref, sin_ref, dkv_ref, *refs
):
    grads = targets_of(refs[:5])
    n1_rel, d_ref = refs[5:]
    cap = dkv_a_ref.shape[0]
    kv_width = KEY_HEADS * HEAD_WIDTH
    k_cols = kv_width // 8
    half = HEAD_WIDTH // 2
    wide = n1_rel.shape[0] // 4
    cosine, sine = cos_ref[...], sin_ref[...]
    d_ref[:, :cap] = dkv_a_ref[...].T
    d_ref[:, cap:] = dkv_b_ref[...].T
    for head in range(KEY_HEADS):
        base = head * HEAD_WIDTH
        front = d_ref[base : base + half, :]
        back = d_ref[base + half : base + 2 * half, :]
        d_ref[base : base + half, :] = front * cosine + back * sine
        d_ref[base + half : base + 2 * half, :] = back * cosine - front * sine
    for core_rel in range(2):
        for s in range(4):
            f = column_index(ids_ref, core_rel, s)
            low = (core_rel * 4 + s) * 2 * k_cols
            dkv_ref[low : low + 2 * k_cols, :] = jnp.concatenate(
                [
                    d_ref[start_row(f, k_cols), :],
                    d_ref[pl.ds(pl.multiple_of(kv_width + f * k_cols, 8), k_cols), :],
                ],
                0,
            ).astype(jnp.bfloat16)
    fill_relative(ids_ref, n1_rel, n1_ref)
    for core_rel in range(2):
        for s in range(4):
            low = (core_rel * 4 + s) * 2 * k_cols
            got = product_nt(dkv_ref[low : low + 2 * k_cols, :], n1_rel[...]).astype(jnp.bfloat16)
            for k in range(4):
                grads[core_rel * 4 + k][s] = got[:, k * wide : (k + 1) * wide]


def finish_kernel(*refs):
    ids_ref, all_ref, dkv_ref, dn_ref, dh_ref, x_ref, gain_ref = refs[:7]
    tokens_ref, gain_grad_ref = refs[7:]
    width = dh_ref.shape[0]
    block = dn_ref.shape[1]
    kv_rows = dkv_ref.shape[0] // 8
    low = all_ref.shape[1] - kv_rows
    wide = all_ref.shape[2] // 4
    weights = jnp.concatenate([all_ref[j, low:, :] for j in range(8)], 0)
    dn = product_tn(weights, dkv_ref[...])
    for k in range(4):
        i = ids_ref[0] ^ k
        tokens_ref[pl.ds(pl.multiple_of(i * block, 16), block), :] = (
            dn[k * wide : k * wide + block] + dn_ref[i]
        )
    x = x_ref[...].astype(jnp.float32)
    rms = mean_square(x)
    dn = tokens_ref[...]
    gain_grad_ref[...] = jnp.sum(dn * x * rms, 1, keepdims=True)
    weighted = dn * gain_ref[...]
    tokens_ref[...] = (
        dh_ref[...]
        + rms * weighted
        - x * (rms * rms * rms * jnp.mean(weighted * x, 0, keepdims=True))
    )


def mlp_kernel(*refs):
    ids_ref, n2_own, n2_other, dy_own, dy_other = refs[:5]
    pieces = refs[5:21]
    keep_ref, send_ref = refs[21:23]
    grads = refs[23:39]
    wgu, wdn, gu_ref, prod_ref, dgu_ref, n2_rel, dy_rel, sem_in, sem_out = refs[39:]
    dp_id = ids_ref[0]
    z_id = ids_ref[1]
    block, rows = keep_ref.shape[1] // 4, keep_ref.shape[2]
    pair = 2 * rows
    wide = pieces[0].shape[1]
    half = prod_ref.shape[0] // 4

    def gate_up_part(ref, piece, k, s):
        return piece.at[pl.ds(0, 2 * half)], ref.at[
            pl.ds(s * 2 * half, 2 * half), pl.ds(k * wide, wide)
        ]

    def down_part(ref, piece, k, s):
        return piece.at[pl.ds(2 * half, half)], ref.at[
            pl.ds(k * half, half), pl.ds(s * wide, wide)
        ]

    loads, more_loads = [], []
    for s in range(4):
        for k in range(4):
            source, target = gate_up_part(wgu, pieces[k * 4 + s], k, s)
            loads.append(pltpu.make_async_copy(source, target, sem_in.at[0, k * 4 + s]))
            source, target = down_part(wdn, pieces[k * 4 + s], k, s)
            more_loads.append(pltpu.make_async_copy(source, target, sem_in.at[1, k * 4 + s]))
    for load in loads + more_loads:
        load.start()
    pad = jnp.zeros((wide - block, pair), jnp.bfloat16)
    for j in range(4):
        i = dp_id ^ j
        zz = lax.rem(z_id - j + 4, 4)
        n2_rel[j * wide : j * wide + block, :] = jnp.concatenate(
            [n2_own[i][:, :rows], n2_other[i][:, :rows]], 1
        )
        dy_rel[j * wide : j * wide + block, :] = jnp.concatenate(
            [dy_own[zz][:, :rows], dy_other[zz][:, :rows]], 1
        )
        n2_rel[j * wide + block : (j + 1) * wide, :] = pad
        dy_rel[j * wide + block : (j + 1) * wide, :] = pad

    def rows_of(index, size):
        return pl.ds(pl.multiple_of(index * size, 16), size)

    for s in range(4):
        for load in loads[4 * s : 4 * s + 4]:
            load.wait()
        k = lax.rem(z_id - s + 4, 4) ^ dp_id
        total = product_nn(wgu[s * 2 * half : (s + 1) * 2 * half, :], n2_rel[...])
        gu_ref[rows_of(k, 2 * half), :] = total
        gate = total[:half]
        prod_ref[rows_of(k, half), :] = (gate * jax.nn.sigmoid(gate) * total[half:]).astype(
            jnp.bfloat16
        )
    for load in more_loads:
        load.wait()
    for k in range(4):
        s = lax.rem(z_id - (dp_id ^ k) + 4, 4)
        dprod = product_nn(wdn[k * half : (k + 1) * half, :], dy_rel[...])
        gate = gu_ref[k * 2 * half : k * 2 * half + half, :]
        up = gu_ref[k * 2 * half + half : (k + 1) * 2 * half, :]
        sig = jax.nn.sigmoid(gate)
        dgu_ref[rows_of(s, 2 * half), :] = jnp.concatenate(
            [dprod * up * sig * (1.0 + gate * (1.0 - sig)), dprod * gate * sig], 0
        ).astype(jnp.bfloat16)
    for j in range(4):
        lanes = slice(j * wide, (j + 1) * wide)
        out = product_tn(wdn[:, lanes], prod_ref[...])[:block]
        zz = rows_of(lax.rem(z_id - j + 4, 4), block)
        keep_ref[0, zz, :] = out[:, :rows]
        send_ref[0, zz, :rows] = out[:, rows:].astype(jnp.bfloat16)
    for k in range(4):
        here = slice(k * half, (k + 1) * half)
        wdn[here, :] = product_nt(prod_ref[here, :], dy_rel[...]).astype(jnp.bfloat16)
    stores = []
    for k in range(4):
        for s in range(4):
            target, source = down_part(wdn, grads[k * 4 + s], k, s)
            stores.append(pltpu.make_async_copy(source, target, sem_out.at[1, k * 4 + s]))
    for store in stores:
        store.start()
    for j in range(4):
        lanes = slice(j * wide, (j + 1) * wide)
        dn = product_tn(wgu[:, lanes], dgu_ref[...])[:block]
        i = rows_of(dp_id ^ j, block)
        keep_ref[1, i, :] = dn[:, :rows]
        send_ref[1, i, :rows] = dn[:, rows:].astype(jnp.bfloat16)
    send_ref[:, :, rows:] = jnp.zeros((2, 4 * block, send_ref.shape[2] - rows), jnp.bfloat16)
    for s in range(4):
        here = slice(s * 2 * half, (s + 1) * 2 * half)
        wgu[here, :] = product_nt(dgu_ref[here, :], n2_rel[...]).astype(jnp.bfloat16)
        for k in range(4):
            target, source = gate_up_part(wgu, grads[k * 4 + s], k, s)
            store = pltpu.make_async_copy(source, target, sem_out.at[0, k * 4 + s])
            store.start()
            stores.append(store)
    for store in stores:
        store.wait()


def mean_square(values):
    return lax.rsqrt(jnp.mean(values * values, 0, keepdims=True) + EPSILON)


def fast(
    tokens, cotangent, counts, w_query, key_weight, value_weight, w_out, w_gate, w_up, w_down, gains
):
    dp_id = lax.axis_index("dp")
    slot = lax.axis_index("fsdp")
    z_id = slot // 2
    core_id = slot % 2
    ids = jnp.stack([dp_id, z_id, core_id, slot]).astype(jnp.int32)
    batches, cap, width = tokens.shape
    rows = batches * cap
    block = w_query.shape[0]
    wide = -(-block // 128) * 128
    q_cols, k_cols = w_query.shape[1], key_weight.shape[1]
    half = w_gate.shape[1]
    kv_width = KEY_HEADS * HEAD_WIDTH
    share = QUERY_HEADS // KEY_HEADS
    q_rows = q_cols + 8
    depth = q_rows + 2 * k_cols
    mlp_rows = 3 * half + q_rows
    padded = -(-rows // 128) * 128

    (first_piece,) = run(
        pack_first_kernel,
        "pack_first",
        (counts, w_query, key_weight.T, value_weight.T, gains),
        [SMEM] + [VMEM] * 4,
        [struct((depth, wide))],
        [VMEM],
        [],
        0,
        16,
    )
    chain = [first_piece] + [shift_z(first_piece, step) for step in (1, 2, 3)]
    down = w_down.T
    give = jnp.where(core_id == 0, down[:, half:], down[:, :half])
    other_down = swap_core(jnp.pad(give, ((0, 0), (0, -half % 128))))
    (mlp_piece,) = run(
        pack_mlp_kernel,
        "pack_mlp",
        (ids, w_gate.T, w_up.T, down, other_down, w_out),
        [SMEM] + [VMEM] * 5,
        [struct((mlp_rows, wide))],
        [VMEM],
        [],
        0,
        16,
    )
    x, dy = run(
        turn_in_kernel,
        "turn_in",
        (tokens.reshape(rows, width), cotangent.reshape(rows, width)),
        [VMEM] * 2,
        [struct((width, rows)), struct((width, padded))],
        [VMEM] * 2,
        [],
        0,
        16,
    )

    along = jnp.stack(chain, 0)
    extras = along[:, q_cols : q_cols + 2, :block]
    other_extras = swap_core(extras)
    from_x = swap_dp(along, 1)
    from_y = swap_dp(along, 2)
    first_own = [along, from_x, from_y, swap_dp(from_x[:2], 2), swap_dp(from_y[2:], 1)]
    first_other = [swap_core(piece) for piece in first_own]

    z_one = shift_z(after(mlp_piece, along), 1)
    z_two = shift_z(z_one, 1)
    z_three = shift_z(z_two, 1)
    mlp_next = after(mlp_piece, *first_own[3:])
    x_zero, y_zero = swap_dp(mlp_next, 1), swap_dp(mlp_next, 2)

    by_core = jnp.where(
        core_id == 0, jnp.stack([extras, other_extras], 1), jnp.stack([other_extras, extras], 1)
    )
    by_core = by_core[::-1]
    by_core = lax.dynamic_slice_in_dim(jnp.concatenate([by_core, by_core], 0), 3 - z_id, 4, 0)
    gain = by_core[:, :, 0, :].reshape(8, 2, q_cols).transpose(0, 2, 1).reshape(width, 2)
    gain = gain.astype(jnp.float32)
    gain_one, gain_two = gain[:, :1], gain[:, 1:]
    group_counts = by_core[:, :, 1, :batches].reshape(8, batches).astype(jnp.int32)
    flat_counts = group_counts.T.reshape(-1)
    before = jnp.sum(
        jnp.where(jnp.arange(8, dtype=jnp.int32)[:, None] < slot, group_counts, 0), 0
    )
    position = (before[:, None] + jnp.arange(cap, dtype=jnp.int32)[None, :]).reshape(-1)
    cosine, sine = rope_tables(position, HEAD_WIDTH)
    cosine, sine = cosine[:, 0, :].T, sine[:, 0, :].T
    x_wide = x.astype(jnp.float32)
    n1 = (x_wide * mean_square(x_wide) * gain_one).astype(jnp.bfloat16).reshape(4, block, rows)
    n1_next = after(n1, z_two, flat_counts, gain_one, gain_two)

    query, kv, first_all = run(
        project_kernel,
        "project",
        (ids, *first_own, *first_other, n1_next, cosine, sine),
        [SMEM] + [VMEM] * 13,
        (
            struct((QUERY_HEADS, HEAD_WIDTH, rows)),
            struct((rows, 2 * kv_width)),
            struct((8, depth, 4 * wide)),
        ),
        [VMEM] * 3,
        [
            pltpu.VMEM((width + 2 * kv_width, rows), jnp.float32),
            pltpu.VMEM((2 * kv_width, rows), jnp.float32),
            pltpu.VMEM((4 * wide, rows), jnp.bfloat16),
        ],
        2 * (width + 2 * kv_width) * width * rows,
        20,
    )
    kv_zero = after(kv, x_zero, y_zero)
    kv_one = shift_z_up(kv_zero, 1)
    x_one = swap_dp(after(z_one, kv_zero), 1)
    far_zero = swap_dp(after(x_zero, kv_zero), 2)
    wave = (kv_one, x_one, far_zero, z_three)
    kv_two = shift_z_up(after(*wave), 1)
    x_two = swap_dp(after(z_two, *wave), 1)
    y_one = swap_dp(after(z_one, *wave), 2)
    wave = (kv_two, x_two, y_one)
    kv_three = shift_z_up(after(*wave), 1)
    far_one = swap_dp(after(y_one, *wave), 1)
    y_two = swap_dp(after(z_two, *wave), 2)
    wave = (kv_three, far_one, y_two)
    x_three = swap_dp(after(z_three, *wave), 1)
    y_three = swap_dp(after(z_three, *wave), 2)
    kv_own = [kv, kv_one, kv_two, kv_three]
    kv_other = [swap_core(piece) for piece in (kv_zero, kv_one, kv_two, kv_three)]
    pair_flops = 2 * QUERY_HEADS * HEAD_WIDTH * rows * 8 * cap
    bias_scratch = pltpu.VMEM((8 * cap, share * cap), jnp.float32)
    def attend(mb, queries):
        return run(
            functools.partial(attend_kernel, mb),
            "attend",
            (ids, flat_counts, queries, *kv_own, *kv_other),
            [SMEM, SMEM] + [VMEM] * 9,
            (
                struct((QUERY_HEADS, HEAD_WIDTH, cap)),
                struct((KEY_HEADS, 1, share * cap), jnp.float32),
                struct((KEY_HEADS, 8 * cap, HEAD_WIDTH)),
                struct((KEY_HEADS, 8 * cap, HEAD_WIDTH)),
            ),
            [VMEM] * 4,
            [bias_scratch],
            4 * pair_flops,
            20,
        )

    att_a, lse_a, *heads_a = attend(0, after(query, far_one, y_two))
    wave = (att_a, x_three, y_three)
    far_two = swap_dp(after(x_two, *wave), 2)
    far_three = swap_dp(after(y_three, *wave), 1)
    dy_other = swap_core(after(dy, att_a))
    att_b, lse_b, *heads_b = attend(1, after(query, *wave))
    pieces = [mlp_piece, z_one, z_two, z_three]
    pieces += [x_zero, x_one, x_two, x_three]
    pieces += [y_zero, y_one, y_two, y_three]
    pieces += [far_zero, far_one, far_two, far_three]
    (out_own,) = run(
        collect_kernel,
        "collect",
        tuple(pieces[:15]) + (after(far_three, att_b),),
        [HBM] * 16,
        [struct((4, q_rows, 4 * wide))],
        [VMEM],
        [pltpu.SemaphoreType.DMA((16,))],
        0,
        8,
    )
    out_other = swap_core(out_own)
    att_a = att_a.reshape(4, block, cap)
    att_b = att_b.reshape(4, block, cap)
    lse = (lse_a, lse_b)
    blocks = (4, block, rows)
    wide_blocks = (4, block, padded)
    h, n2 = run(
        hidden_kernel,
        "hidden",
        (ids, out_own, out_other, att_a, att_b, after(x, dy_other), gain_two),
        [SMEM] + [VMEM] * 6,
        (struct((width, rows), jnp.float32), struct((width, padded))),
        [VMEM] * 2,
        [pltpu.VMEM((4 * wide, rows), jnp.bfloat16)],
        2 * width * width * rows,
        16,
    )
    n2_other = swap_core(n2)
    results = run(
        mlp_kernel,
        "mlp",
        (
            ids,
            n2.reshape(wide_blocks),
            n2_other.reshape(wide_blocks),
            dy.reshape(wide_blocks),
            dy_other.reshape(wide_blocks),
            *pieces,
        ),
        [SMEM] + [VMEM] * 4 + [HBM] * 16,
        [struct((2, width, rows), jnp.float32), struct((2, width, padded))]
        + [struct((3 * half, wide))] * 16,
        [VMEM] * 2 + [HBM] * 16,
        [
            pltpu.VMEM((8 * half, 4 * wide), jnp.bfloat16),
            pltpu.VMEM((4 * half, 4 * wide), jnp.bfloat16),
            pltpu.VMEM((8 * half, 2 * rows), jnp.float32),
            pltpu.VMEM((4 * half, 2 * rows), jnp.bfloat16),
            pltpu.VMEM((8 * half, 2 * rows), jnp.bfloat16),
            pltpu.VMEM((4 * wide, 2 * rows), jnp.bfloat16),
            pltpu.VMEM((4 * wide, 2 * rows), jnp.bfloat16),
            pltpu.SemaphoreType.DMA((2, 16)),
            pltpu.SemaphoreType.DMA((2, 16)),
        ],
        18 * 16 * half * block * 2 * rows,
        40,
    )
    keep, send = results[:2]
    home, to_x, to_y, far = results[2:6], results[6:10], results[10:14], results[14:18]
    arrived = swap_core(send)

    output, dh, mixed_gradient, gain_two_grad, da_pieces = run(
        turn_point_kernel,
        "turn_point",
        (ids, keep, arrived, h, dy, gain_two, out_own, out_other),
        [SMEM] + [VMEM] * 7,
        (
            struct((width, rows)),
            struct((width, rows), jnp.float32),
            struct(blocks),
            struct((width, 1), jnp.float32),
            struct((8 * q_rows, rows)),
        ),
        [VMEM] * 5,
        [pltpu.VMEM((width, rows), jnp.float32)],
        2 * width * width * rows,
        22,
    )
    output = output.T.reshape(batches, cap, width)
    def attend_back(mb, mixed):
        return run(
            functools.partial(attend_back_kernel, mb),
            "attend_back",
            (
                ids,
                flat_counts,
                query,
                mixed.reshape(QUERY_HEADS, HEAD_WIDTH, rows),
                *(heads_a, heads_b)[mb],
                lse[mb],
                cosine,
                sine,
            ),
            [SMEM, SMEM] + [VMEM] * 7,
            [struct((QUERY_HEADS, HEAD_WIDTH, cap))] + [struct((4, cap, 2 * kv_width))] * 2,
            [VMEM] * 3,
            [
                bias_scratch,
                pltpu.VMEM((KEY_HEADS, 8 * cap, HEAD_WIDTH), jnp.bfloat16),
                pltpu.VMEM((KEY_HEADS, 8 * cap, HEAD_WIDTH), jnp.bfloat16),
            ],
            10 * pair_flops,
            24,
        )

    def sum_cores(own, other):
        arrived = swap_core(other)
        return [add_low(own[s], arrived[s]) for s in range(4)]

    def sum_z(summed):
        total = summed[0].astype(jnp.float32)
        for s in (3, 2, 1):
            total = total + shift_z_down(summed[s], s).astype(jnp.float32)
        return total

    via_three = swap_dp(after(far[3], mixed_gradient), 1)
    via_two = swap_dp(after(far[2], mixed_gradient), 2)
    x_three = swap_dp(after(to_x[3], mixed_gradient), 1)
    y_two = swap_dp(after(to_y[2], mixed_gradient), 2)
    back_a = attend_back(0, mixed_gradient)
    wave = (back_a[0], via_three, via_two, x_three, y_two)
    x_two = swap_dp(add_low(to_x[2], after(via_two, *wave)), 1)
    y_three = swap_dp(add_low(to_y[3], after(via_three, *wave)), 2)
    via_one, via_zero = swap_dp(after(far[1], *wave), 1), swap_dp(after(far[0], *wave), 2)
    out_grads = run(
        out_grad_kernel,
        "out_grad",
        (ids, att_a, att_b, after(da_pieces, *wave)),
        [SMEM] + [VMEM] * 3,
        [struct((4, q_rows, wide))] * 4 + [struct((16, q_rows, wide))],
        [VMEM] * 5,
        [pltpu.VMEM((4 * wide, rows), jnp.bfloat16)],
        2 * width * width * rows,
        14,
    )
    summed_a = sum_cores(*back_a[1:])
    wave = (x_two, y_three, out_grads[0])
    dkv_a = sum_z([after(piece, *wave) for piece in summed_a])
    back_b = attend_back(1, after(mixed_gradient, *summed_a, *wave))
    wave = (back_b[0], dkv_a, via_one, via_zero)
    x_one, y_zero = swap_dp(after(to_x[1], *wave), 1), swap_dp(after(to_y[0], *wave), 2)
    summed_b = sum_cores(back_b[1], after(back_b[2], *wave))
    parts_b = [shift_z_down(summed_b[s], s) for s in (1, 2, 3)]

    def sum_pair(parts):
        arrived = swap_core(parts[4])
        return [add_low(parts[k], arrived[4 * k : 4 * k + 4]) for k in range(4)]

    def share_square(mine):
        return [mine[0]] + [swap_dp(mine[k], k) for k in (1, 2, 3)]

    def reduce_all(summed):
        out = [add_low(*[piece[s] for piece in summed]) for s in range(4)]
        total = out[0].astype(jnp.float32)
        for s in (1, 2, 3):
            total = total + shift_z(out[s], -s).astype(jnp.float32)
        return total

    q_results = run(
        finish_q_kernel,
        "finish_q",
        (
            ids,
            first_all,
            after(n1, *wave),
            back_a[0].reshape(width, cap),
            back_b[0].reshape(width, cap),
            *out_grads,
        ),
        [SMEM] + [VMEM] * 9,
        [struct(blocks, jnp.float32)]
        + [struct((4, 2 * q_rows, wide))] * 4
        + [struct((16, 2 * q_rows, wide))],
        [VMEM] * 6,
        [
            pltpu.VMEM((4 * wide, rows), jnp.bfloat16),
            pltpu.VMEM((width, rows), jnp.float32),
            pltpu.VMEM((8 * q_rows, rows), jnp.bfloat16),
        ],
        4 * width * width * rows,
        22,
    )
    dn_q = q_results[0]
    dkv_b = summed_b[0].astype(jnp.float32)
    for part in parts_b:
        dkv_b = dkv_b + part.astype(jnp.float32)
    x_zero = swap_dp(add_low(to_x[0], after(via_zero, dkv_b)), 1)
    y_one = swap_dp(add_low(to_y[1], after(via_one, dkv_b)), 2)
    hop = shift_z(add_low(after(home[3], dkv_b), x_three, y_three), -1)
    q_out_mine = sum_pair(q_results[1:])
    q_out_shared = share_square(q_out_mine)
    q_out_total = reduce_all(q_out_shared)
    grad_query = q_out_total[:q_cols, :block].T
    grad_out = q_out_total[q_rows : q_rows + q_cols, :block].T

    dkv_pieces, *kv_grads = run(
        kv_grad_kernel,
        "kv_grad",
        (ids, after(n1, x_one, y_zero, *q_out_mine), dkv_a, dkv_b, cosine, sine),
        [SMEM] + [VMEM] * 5,
        [struct((16 * k_cols, rows))]
        + [struct((4, 2 * k_cols, wide))] * 4
        + [struct((16, 2 * k_cols, wide))],
        [VMEM] * 6,
        [
            pltpu.VMEM((4 * wide, rows), jnp.bfloat16),
            pltpu.VMEM((2 * kv_width, rows), jnp.float32),
        ],
        4 * kv_width * width * rows,
        14,
    )
    grad_tokens, gain_one_grad = run(
        finish_kernel,
        "finish",
        (ids, first_all, dkv_pieces, dn_q, dh, after(x, x_zero, y_one), gain_one),
        [SMEM] + [VMEM] * 6,
        [struct((width, rows), jnp.float32), struct((width, 1), jnp.float32)],
        [VMEM] * 2,
        [],
        4 * kv_width * width * rows,
        20,
    )
    grad_tokens = grad_tokens.T.reshape(batches, cap, width)
    kv_mine = sum_pair(kv_grads)
    hop = shift_z(add_low(home[2], x_two, y_two, after(hop, dkv_pieces)), -1)
    hop = shift_z(add_low(home[1], x_one, y_one, after(hop, *kv_mine)), -1)
    mlp_total = (
        home[0].astype(jnp.float32)
        + y_zero.astype(jnp.float32)
        + x_zero.astype(jnp.float32)
        + hop.astype(jnp.float32)
    )
    grad_gate = mlp_total[:half, :block].T
    grad_up = mlp_total[half : 2 * half, :block].T
    down_total = mlp_total[2 * half :, :block]
    left, right = down_total[:, :q_cols], down_total[:, q_cols:]
    stay = jnp.where(core_id == 0, left, right)
    give = jnp.where(core_id == 0, right, left).astype(jnp.bfloat16)
    taken = swap_core(give).astype(jnp.float32)
    grad_down = jnp.where(
        core_id == 0, jnp.concatenate([stay, taken], 0), jnp.concatenate([taken, stay], 0)
    )

    kv_total = reduce_all(share_square(kv_mine))
    gain_total = after(jnp.concatenate([gain_one_grad, gain_two_grad], 1).T, *kv_mine)
    gain_total = gain_total + swap_core(gain_total)
    gain_total = gain_total + swap_dp(gain_total, 1)
    gain_total = gain_total + swap_dp(gain_total, 2)
    for mask in (2, 4):
        gain_total = gain_total + lax.ppermute(
            gain_total, "fsdp", [(j, j ^ mask) for j in range(8)]
        )
    gain_grad = lax.dynamic_slice_in_dim(gain_total, slot * q_cols, q_cols, 1)
    return (
        output,
        grad_tokens,
        grad_query,
        kv_total[:k_cols, :block].T,
        kv_total[k_cols:, :block].T,
        grad_out,
        grad_gate,
        grad_up,
        grad_down,
        gain_grad,
    )


def solution(mesh):
    in_specs = (
        P(None, ("dp", "fsdp"), None),
        P(None, ("dp", "fsdp"), None),
        P(None, ("dp", "fsdp")),
        P("dp", "fsdp"),
        P("dp", "fsdp"),
        P("dp", "fsdp"),
        P("dp", "fsdp"),
        P("dp", "fsdp"),
        P("dp", "fsdp"),
        P("dp", "fsdp"),
        P(None, "fsdp"),
    )
    out_specs = (
        P(None, ("dp", "fsdp"), None),
        P(None, ("dp", "fsdp"), None),
        P("dp", "fsdp"),
        P("dp", "fsdp"),
        P("dp", "fsdp"),
        P("dp", "fsdp"),
        P("dp", "fsdp"),
        P("dp", "fsdp"),
        P("dp", "fsdp"),
        P(None, "fsdp"),
    )
    square = mesh.shape["dp"] == 4 and mesh.shape["fsdp"] == 8
    return jax.shard_map(
        fast if square else local, mesh=mesh, in_specs=in_specs, out_specs=out_specs, check_vma=False)
```

```python
import functools

import jax
import jax.numpy as jnp
from jax import lax
from jax.experimental import pallas as pl
from jax.experimental.pallas import tpu as pltpu
from jax.sharding import PartitionSpec as P

MODEL_WIDTH = 960
QUERY_HEADS = 15
KEY_HEADS = 5
HEAD_WIDTH = 64


EPSILON = 1e-05
ROPE_BASE = 100000.0
SCORE_SCALE = 0.125


def rope_tables(position, head_size):
    half_size = head_size // 2
    frequency = ROPE_BASE ** (-(jnp.arange(half_size, dtype=jnp.float32) * 2.0) / head_size)
    angles = position.astype(jnp.float32)[:, None] * frequency[None, :]
    return (jnp.cos(angles)[:, None, :], jnp.sin(angles)[:, None, :])


def apply_rotation(values, cosine_table, sine_values):
    half_size = values.shape[-1] // 2
    front_half = values[..., :half_size]
    back_half = values[..., half_size:]
    return jnp.concatenate(
        [
            front_half * cosine_table - back_half * sine_values,
            back_half * cosine_table + front_half * sine_values,
        ],
        -1,
    )


def normalize(values, gain_row):
    inv_rms = lax.rsqrt(jnp.mean(values * values, -1, keepdims=True) + EPSILON)
    return (values * inv_rms * gain_row, inv_rms)


def norm_back(values, inv_rms, gain_row, incoming):
    weighted = incoming * gain_row
    return inv_rms * weighted - values * inv_rms * inv_rms * inv_rms * jnp.mean(
        weighted * values, -1, keepdims=True
    )


def build_mask(count_row, device, slot_capacity):
    group_width = count_row.shape[0]
    local_slot = jnp.arange(slot_capacity, dtype=jnp.int32)
    offsets = jnp.cumsum(count_row) - count_row
    is_mine = jnp.arange(group_width, dtype=jnp.int32) == device
    own_offset = jnp.sum(jnp.where(is_mine, offsets, 0))
    own_count = jnp.sum(jnp.where(is_mine, count_row, 0))
    query_pos = own_offset + local_slot
    query_valid = local_slot < own_count
    key_pos = (offsets[:, None] + local_slot[None, :]).reshape(-1)
    key_valid = (local_slot[None, :] < count_row[:, None]).reshape(-1)
    slot_ids = jnp.arange(group_width * slot_capacity, dtype=jnp.int32)
    own_slots = device * slot_capacity + local_slot
    allowed = query_valid[:, None] & key_valid[None, :] & (
        key_pos[None, :] <= query_pos[:, None]
    ) | (slot_ids[None, :] == own_slots[:, None])
    return (allowed, query_pos)


def kept_fetch(w_query, key_weight, value_weight, w_out, w_gate, w_up, w_down, gains):
    columns = (
        lax.all_gather(w_query, "fsdp", axis=1, tiled=True),
        lax.all_gather(key_weight, "fsdp", axis=1, tiled=True),
        lax.all_gather(value_weight, "fsdp", axis=1, tiled=True),
        lax.all_gather(w_out, "fsdp", axis=1, tiled=True),
        lax.all_gather(w_gate, "fsdp", axis=1, tiled=True),
        lax.all_gather(w_up, "fsdp", axis=1, tiled=True),
        lax.all_gather(w_down, "fsdp", axis=1, tiled=True),
        lax.all_gather(gains, "fsdp", axis=1, tiled=True),
    )
    matrices = (
        lax.all_gather(columns[0], "dp", axis=0, tiled=True),
        lax.all_gather(columns[1], "dp", axis=0, tiled=True),
        lax.all_gather(columns[2], "dp", axis=0, tiled=True),
        lax.all_gather(columns[3], "dp", axis=0, tiled=True),
        lax.all_gather(columns[4], "dp", axis=0, tiled=True),
        lax.all_gather(columns[5], "dp", axis=0, tiled=True),
        lax.all_gather(columns[6], "dp", axis=0, tiled=True),
    )
    return (matrices, columns[7].astype(jnp.float32))


def times_transpose(left, right):
    return jnp.einsum("rk,jk->rj", left, right, preferred_element_type=jnp.float32)


def rows_product(left, right):
    return jnp.einsum("rd,rk->dk", left, right, preferred_element_type=jnp.float32)


def local(
    tokens, cotangent, counts, w_query, key_weight, value_weight, w_out, w_gate, w_up, w_down, gains
):
    group_counts = lax.all_gather(counts, "fsdp", axis=1, tiled=True)
    device = lax.axis_index("fsdp")
    slot_capacity = tokens.shape[1]
    key_value_width = KEY_HEADS * HEAD_WIDTH
    device_share = QUERY_HEADS // KEY_HEADS
    kept_weights, kept_gain = kept_fetch(
        w_query, key_weight, value_weight, w_out, w_gate, w_up, w_down, gains
    )
    outputs = []
    grad_inputs = []
    saved = [[] for index_unused in range(11)]
    gain_one_total = jnp.zeros((MODEL_WIDTH,), jnp.float32)
    gain_two_total = jnp.zeros((MODEL_WIDTH,), jnp.float32)
    for micro_idx in range(tokens.shape[0]):
        matrices, gain_pair = (kept_weights, kept_gain)
        full_query, full_key, full_value, full_out, full_gate, full_up, full_down = matrices
        inputs = tokens[micro_idx].astype(jnp.float32)
        allowed, query_pos = build_mask(group_counts[micro_idx], device, slot_capacity)
        cosine_table, sine_values = rope_tables(query_pos, HEAD_WIDTH)
        first_normed, scale_one = normalize(inputs, gain_pair[0])
        normed_low = first_normed.astype(jnp.bfloat16)
        reduced_query = apply_rotation(
            jnp.dot(normed_low, full_query, preferred_element_type=jnp.float32).reshape(
                slot_capacity, QUERY_HEADS, HEAD_WIDTH
            ),
            cosine_table,
            sine_values,
        ).astype(jnp.bfloat16)
        key_low = (
            apply_rotation(
                jnp.dot(normed_low, full_key, preferred_element_type=jnp.float32).reshape(
                    slot_capacity, KEY_HEADS, HEAD_WIDTH
                ),
                cosine_table,
                sine_values,
            )
            .astype(jnp.bfloat16)
            .reshape(slot_capacity, key_value_width)
        )
        value_low = jnp.dot(normed_low, full_value, preferred_element_type=jnp.float32).astype(
            jnp.bfloat16
        )
        grouped_keys, grouped_values = (
            lax.all_gather(key_low, "fsdp", axis=0, tiled=True),
            lax.all_gather(value_low, "fsdp", axis=0, tiled=True),
        )
        heads_of_key = grouped_keys.reshape(-1, KEY_HEADS, HEAD_WIDTH)
        heads_of_value = grouped_values.reshape(-1, KEY_HEADS, HEAD_WIDTH)
        heads_of_query = reduced_query.reshape(slot_capacity, KEY_HEADS, device_share, HEAD_WIDTH)
        scores = (
            jnp.einsum(
                "qngd,knd->ngqk", heads_of_query, heads_of_key, preferred_element_type=jnp.float32
            )
            * SCORE_SCALE
        )
        masked = jnp.where(allowed, scores, -1e30)
        row_top = jnp.max(masked, -1, keepdims=True)
        exponent = jnp.where(allowed, jnp.exp(masked - row_top), 0.0)
        row_total = jnp.sum(exponent, -1, keepdims=True)
        prob_low = (exponent / row_total).astype(jnp.bfloat16)
        log_total = row_top + jnp.log(row_total)
        mixed_heads = jnp.einsum(
            "ngqk,knd->qngd", prob_low, heads_of_value, preferred_element_type=jnp.float32
        ).reshape(slot_capacity, MODEL_WIDTH)
        attended = mixed_heads.astype(jnp.bfloat16)
        hidden_state = inputs + jnp.dot(attended, full_out, preferred_element_type=jnp.float32)
        normed_two, scale_two = normalize(hidden_state, gain_pair[1])
        normed_two_low = normed_two.astype(jnp.bfloat16)
        gate_act = jnp.dot(normed_two_low, full_gate, preferred_element_type=jnp.float32)
        upward = jnp.dot(normed_two_low, full_up, preferred_element_type=jnp.float32)
        sigmoid_gate = jax.nn.sigmoid(gate_act)
        product = (gate_act * sigmoid_gate * upward).astype(jnp.bfloat16)
        outputs.append(
            (hidden_state + jnp.dot(product, full_down, preferred_element_type=jnp.float32)).astype(
                jnp.bfloat16
            )
        )
        matrices, gain_pair = (kept_weights, kept_gain)
        full_query, full_key, full_value, full_out, full_gate, full_up, full_down = matrices
        grad_low = cotangent[micro_idx]
        grad_product = times_transpose(grad_low, full_down)
        grad_gate = (
            grad_product * upward * sigmoid_gate * (1.0 + gate_act * (1.0 - sigmoid_gate))
        ).astype(jnp.bfloat16)
        grad_upward = (grad_product * gate_act * sigmoid_gate).astype(jnp.bfloat16)
        grad_normed_two = times_transpose(grad_gate, full_gate) + times_transpose(
            grad_upward, full_up
        )
        gain_two_total = gain_two_total + jnp.sum(grad_normed_two * hidden_state * scale_two, 0)
        grad_hidden = grad_low.astype(jnp.float32) + norm_back(
            hidden_state, scale_two, gain_pair[1], grad_normed_two
        )
        grad_branch = grad_hidden.astype(jnp.bfloat16)
        mixed_gradient = times_transpose(grad_branch, full_out).astype(jnp.bfloat16)
        head_gradient = mixed_gradient.reshape(slot_capacity, KEY_HEADS, device_share, HEAD_WIDTH)
        again_scores = (
            jnp.einsum(
                "qngd,knd->ngqk", heads_of_query, heads_of_key, preferred_element_type=jnp.float32
            )
            * SCORE_SCALE
        )
        probability = jnp.where(allowed, jnp.exp(again_scores - log_total), 0.0)
        grad_prob = jnp.einsum(
            "qngd,knd->ngqk", head_gradient, heads_of_value, preferred_element_type=jnp.float32
        )
        row_delta = jnp.sum(probability * grad_prob, -1, keepdims=True)
        grad_scores = (probability * (grad_prob - row_delta)).astype(jnp.bfloat16)
        grad_query_rot = (
            jnp.einsum(
                "ngqk,knd->qngd", grad_scores, heads_of_key, preferred_element_type=jnp.float32
            ).reshape(slot_capacity, QUERY_HEADS, HEAD_WIDTH)
            * SCORE_SCALE
        )
        key_part = (
            jnp.einsum(
                "ngqk,qngd->knd", grad_scores, heads_of_query, preferred_element_type=jnp.float32
            ).reshape(-1, key_value_width)
            * SCORE_SCALE
        )
        value_part = jnp.einsum(
            "ngqk,qngd->knd",
            probability.astype(jnp.bfloat16),
            head_gradient,
            preferred_element_type=jnp.float32,
        ).reshape(-1, key_value_width)
        key_gradient, value_grad = (
            lax.psum_scatter(
                key_part.astype(jnp.bfloat16), "fsdp", scatter_dimension=0, tiled=True
            ).astype(jnp.float32),
            lax.psum_scatter(
                value_part.astype(jnp.bfloat16), "fsdp", scatter_dimension=0, tiled=True
            ).astype(jnp.float32),
        )
        grad_query = (
            apply_rotation(grad_query_rot, cosine_table, -sine_values)
            .astype(jnp.bfloat16)
            .reshape(slot_capacity, MODEL_WIDTH)
        )
        grad_key = (
            apply_rotation(
                key_gradient.reshape(slot_capacity, KEY_HEADS, HEAD_WIDTH),
                cosine_table,
                -sine_values,
            )
            .astype(jnp.bfloat16)
            .reshape(slot_capacity, key_value_width)
        )
        grad_value = value_grad.astype(jnp.bfloat16)
        grad_normed_one = (
            times_transpose(grad_query, full_query)
            + times_transpose(grad_key, full_key)
            + times_transpose(grad_value, full_value)
        )
        gain_one_total = gain_one_total + jnp.sum(grad_normed_one * inputs * scale_one, 0)
        grad_inputs.append(
            grad_hidden + norm_back(inputs, scale_one, gain_pair[0], grad_normed_one)
        )
        kept_rows = (
            normed_low,
            grad_query,
            grad_key,
            grad_value,
            attended,
            grad_branch,
            normed_two_low,
            grad_gate,
            grad_upward,
            product,
            grad_low,
        )
        for slot_index in range(11):
            saved[slot_index].append(kept_rows[slot_index])
    joined = [jnp.concatenate(column_list, 0) for column_list in saved]
    gain_terms = jnp.stack([gain_one_total, gain_two_total], 0)
    slices = (
        lax.all_to_all(joined[1], "fsdp", split_axis=1, concat_axis=0, tiled=True),
        lax.all_to_all(joined[2], "fsdp", split_axis=1, concat_axis=0, tiled=True),
        lax.all_to_all(joined[3], "fsdp", split_axis=1, concat_axis=0, tiled=True),
        lax.all_to_all(joined[5], "fsdp", split_axis=1, concat_axis=0, tiled=True),
        lax.all_to_all(joined[7], "fsdp", split_axis=1, concat_axis=0, tiled=True),
        lax.all_to_all(joined[8], "fsdp", split_axis=1, concat_axis=0, tiled=True),
        lax.all_to_all(joined[10], "fsdp", split_axis=1, concat_axis=0, tiled=True),
    )
    pieces = (
        lax.all_gather(joined[0], "fsdp", axis=0, tiled=True),
        lax.all_gather(joined[4], "fsdp", axis=0, tiled=True),
        lax.all_gather(joined[6], "fsdp", axis=0, tiled=True),
        lax.all_gather(joined[9], "fsdp", axis=0, tiled=True),
    )
    picked = [member for member in slices]
    gain_part = lax.psum_scatter(gain_terms, "fsdp", scatter_dimension=1, tiled=True)
    summed_rows = (
        lax.psum_scatter(
            rows_product(pieces[0], picked[0]).astype(jnp.bfloat16),
            "dp",
            scatter_dimension=0,
            tiled=True,
        ).astype(jnp.float32),
        lax.psum_scatter(
            rows_product(pieces[0], picked[1]).astype(jnp.bfloat16),
            "dp",
            scatter_dimension=0,
            tiled=True,
        ).astype(jnp.float32),
        lax.psum_scatter(
            rows_product(pieces[0], picked[2]).astype(jnp.bfloat16),
            "dp",
            scatter_dimension=0,
            tiled=True,
        ).astype(jnp.float32),
        lax.psum_scatter(
            rows_product(pieces[1], picked[3]).astype(jnp.bfloat16),
            "dp",
            scatter_dimension=0,
            tiled=True,
        ).astype(jnp.float32),
        lax.psum_scatter(
            rows_product(pieces[2], picked[4]).astype(jnp.bfloat16),
            "dp",
            scatter_dimension=0,
            tiled=True,
        ).astype(jnp.float32),
        lax.psum_scatter(
            rows_product(pieces[2], picked[5]).astype(jnp.bfloat16),
            "dp",
            scatter_dimension=0,
            tiled=True,
        ).astype(jnp.float32),
        lax.psum_scatter(
            rows_product(pieces[3], picked[6]).astype(jnp.bfloat16),
            "dp",
            scatter_dimension=0,
            tiled=True,
        ).astype(jnp.float32),
    )
    gain_grad = lax.psum(gain_part, "dp")
    return (
        jnp.stack(outputs, 0),
        jnp.stack(grad_inputs, 0),
        summed_rows[0],
        summed_rows[1],
        summed_rows[2],
        summed_rows[3],
        summed_rows[4],
        summed_rows[5],
        summed_rows[6],
        gain_grad,
    )


def swap_core(value):
    return lax.ppermute(value, "fsdp", [(j, j ^ 1) for j in range(8)])


def swap_dp(value, mask):
    return lax.ppermute(value, "dp", [(j, j ^ mask) for j in range(4)])


def shift_z(value, step):
    return lax.ppermute(value, "fsdp", [(j, (j + 2 * step) % 8) for j in range(8)])


def shift_z_up(value, step):
    return lax.ppermute(value, "fsdp", [(j, j + 2 * step) for j in range(8) if j + 2 * step < 8])


def shift_z_down(value, step):
    return lax.ppermute(value, "fsdp", [(j, j - 2 * step) for j in range(8) if j - 2 * step >= 0])


def add_low(*terms):
    total = terms[0].astype(jnp.float32)
    for term in terms[1:]:
        total = total + term.astype(jnp.float32)
    return total.astype(jnp.bfloat16)


def product_nn(left, right):
    return lax.dot_general(
        left, right, (((1,), (0,)), ((), ())), preferred_element_type=jnp.float32
    )


def product_nt(left, right):
    return lax.dot_general(
        left, right, (((1,), (1,)), ((), ())), preferred_element_type=jnp.float32
    )


def product_tn(left, right):
    return lax.dot_general(
        left, right, (((0,), (0,)), ((), ())), preferred_element_type=jnp.float32
    )


VMEM = pl.BlockSpec(memory_space=pltpu.VMEM)
SMEM = pl.BlockSpec(memory_space=pltpu.SMEM)
HBM = pl.BlockSpec(memory_space=pltpu.HBM)


def run(body, name, ins, in_specs, outs, out_specs, scratch, flops, megabytes):
    moved = sum(v.size * v.dtype.itemsize for v in ins)
    moved += sum(v.size * v.dtype.itemsize for v in outs)
    return pl.pallas_call(
        body,
        out_shape=tuple(outs),
        in_specs=in_specs,
        out_specs=tuple(out_specs),
        scratch_shapes=scratch,
        compiler_params=pltpu.CompilerParams(vmem_limit_bytes=megabytes * 1024 * 1024),
        cost_estimate=pl.CostEstimate(flops=flops, bytes_accessed=moved, transcendentals=0),
        name=name,
    )(*ins)


def struct(shape, dtype=jnp.bfloat16):
    return jax.ShapeDtypeStruct(shape, dtype)


def column_index(ids_ref, core_rel, s):
    return 2 * lax.rem(ids_ref[1] - s + 4, 4) + (ids_ref[2] ^ core_rel)


def start_row(index, size):
    return pl.ds(pl.multiple_of(index * size, 8), size)


def after(value, *others):
    return lax.optimization_barrier((value,) + others)[0]


def pack_first_kernel(counts_ref, wq_ref, wk_ref, wv_ref, gains_ref, out_ref):
    block = wq_ref.shape[0]
    gains = gains_ref[...].astype(jnp.float32)
    row = lax.broadcasted_iota(jnp.int32, (8, block), 0)
    lane = lax.broadcasted_iota(jnp.int32, (8, block), 1)
    first = jnp.concatenate([gains[:1], gains[1:]], 1)
    used = jnp.where(
        lane == 0,
        counts_ref[0, 0].astype(jnp.float32),
        jnp.where(lane == 1, counts_ref[1, 0].astype(jnp.float32), 0.0),
    )
    extra = jnp.where(row == 0, first, jnp.where(row == 1, used, 0.0))
    full = jnp.concatenate(
        [
            wq_ref[...].astype(jnp.float32).T,
            extra,
            wk_ref[...].astype(jnp.float32),
            wv_ref[...].astype(jnp.float32),
        ],
        0,
    )
    out_ref[...] = jnp.zeros_like(out_ref)
    out_ref[:, :block] = full.astype(jnp.bfloat16)


def pack_mlp_kernel(ids_ref, wg_ref, wu_ref, wd_ref, other_ref, wo_ref, out_ref):
    half, block = wg_ref.shape
    core = ids_ref[2]
    out_ref[...] = jnp.zeros_like(out_ref)
    out_ref[:half, :block] = wg_ref[...]
    out_ref[half : 2 * half, :block] = wu_ref[...]
    down = wd_ref[...].astype(jnp.float32)
    own = jnp.where(core == 0, down[:, :half], down[:, half:])
    other = other_ref[:, :half].astype(jnp.float32)
    low = jnp.where(core == 0, own, other)
    high = jnp.where(core == 0, other, own)
    out_ref[2 * half : 3 * half, :block] = jnp.concatenate([low, high], 0).T.astype(jnp.bfloat16)
    out_ref[3 * half :, :block] = jnp.concatenate(
        [wo_ref[...].astype(jnp.float32).T, jnp.zeros((8, block), jnp.float32)], 0
    ).astype(jnp.bfloat16)


def turn_in_kernel(x_ref, dy_ref, xt_ref, dyt_ref):
    xt_ref[...] = x_ref[...].astype(jnp.float32).T.astype(jnp.bfloat16)
    dyt_ref[...] = jnp.zeros_like(dyt_ref)
    dyt_ref[:, : dy_ref.shape[0]] = dy_ref[...].astype(jnp.float32).T.astype(jnp.bfloat16)


def fill_relative(ids_ref, target_ref, *sources):
    block, lanes = sources[0].shape[1], target_ref.shape[1]
    wide = target_ref.shape[0] // 4
    for k in range(4):
        parts = [source[ids_ref[0] ^ k] for source in sources]
        target_ref[k * wide : k * wide + block, :] = (
            parts[0] if len(parts) == 1 else jnp.concatenate(parts, 1)
        )
        target_ref[k * wide + block : (k + 1) * wide, :] = jnp.zeros(
            (wide - block, lanes), target_ref.dtype
        )


def wide_rows(refs, s, low, high):
    along, by_x, by_y, far_a, far_b = refs
    far = far_a if s < 2 else far_b
    return jnp.concatenate(
        [along[s, low:high], by_x[s, low:high], by_y[s, low:high], far[s % 2, low:high]], 1
    )


def project_kernel(*refs):
    ids_ref, own, other = refs[0], refs[1:6], refs[6:11]
    n1_ref, cos_ref, sin_ref, q_ref, kv_ref, all_ref, proj_ref, turned_ref, rel_ref = refs[11:]
    width = n1_ref.shape[0] * n1_ref.shape[1]
    kv_width = KEY_HEADS * HEAD_WIDTH
    q_cols, k_cols = width // 8, kv_width // 8
    depth = own[0].shape[1]
    fill_relative(ids_ref, rel_ref, n1_ref)
    for core_rel, weights in ((0, own), (1, other)):
        for s in range(4):
            f = column_index(ids_ref, core_rel, s)
            all_ref[core_rel * 4 + s] = wide_rows(weights, s, 0, depth)
            total = product_nn(all_ref[core_rel * 4 + s], rel_ref[...])
            proj_ref[start_row(f, q_cols), :] = total[:q_cols]
            proj_ref[pl.ds(pl.multiple_of(width + f * k_cols, 8), k_cols), :] = total[
                q_cols + 8 : q_cols + 8 + k_cols
            ]
            proj_ref[pl.ds(pl.multiple_of(width + kv_width + f * k_cols, 8), k_cols), :] = total[
                q_cols + 8 + k_cols :
            ]
    cosine, sine = cos_ref[...], sin_ref[...]
    half = HEAD_WIDTH // 2

    def heads(head, carry):
        front = proj_ref[pl.ds(pl.multiple_of(head * HEAD_WIDTH, 8), half), :]
        back = proj_ref[pl.ds(pl.multiple_of(head * HEAD_WIDTH + half, 8), half), :]
        q_ref[head, :half, :] = (
            (front * cosine - back * sine).astype(jnp.bfloat16) * SCORE_SCALE
        ).astype(jnp.bfloat16)
        q_ref[head, half:, :] = (
            (back * cosine + front * sine).astype(jnp.bfloat16) * SCORE_SCALE
        ).astype(jnp.bfloat16)
        return carry

    lax.fori_loop(0, QUERY_HEADS, heads, 0)
    for head in range(KEY_HEADS):
        base = width + head * HEAD_WIDTH
        front = proj_ref[base : base + half, :]
        back = proj_ref[base + half : base + 2 * half, :]
        turned_ref[head * HEAD_WIDTH : head * HEAD_WIDTH + half, :] = front * cosine - back * sine
        turned_ref[head * HEAD_WIDTH + half : (head + 1) * HEAD_WIDTH, :] = (
            back * cosine + front * sine
        )
    turned_ref[kv_width:, :] = proj_ref[width + kv_width :, :]
    kv_ref[...] = turned_ref[...].T.astype(jnp.bfloat16)


def stage_heads(mb, cap, blocks, k_ref, v_ref):
    kv_width = KEY_HEADS * HEAD_WIDTH
    for block, source in enumerate(blocks):
        rows = source[mb * cap : (mb + 1) * cap, :]
        for n in range(KEY_HEADS):
            lanes = n * HEAD_WIDTH
            k_ref[n, block * cap : (block + 1) * cap, :] = rows[:, lanes : lanes + HEAD_WIDTH]
            lanes += kv_width
            v_ref[n, block * cap : (block + 1) * cap, :] = rows[:, lanes : lanes + HEAD_WIDTH]


def stage_bias(ids_ref, counts_ref, mb, cap, share, bias_ref):
    slot = ids_ref[3]
    own_count = counts_ref[mb * 8 + slot]
    key = lax.broadcasted_iota(jnp.int32, (cap, cap), 0)
    query = lax.broadcasted_iota(jnp.int32, (cap, cap), 1)
    query_used = query < own_count
    for core_rel in range(2):
        for s in range(4):
            block = core_rel * 4 + s
            f = column_index(ids_ref, core_rel, s)
            count = counts_ref[mb * 8 + f]
            reach = jnp.where(f < slot, cap, jnp.where(f == slot, 0, -2 * cap))
            self_off = jnp.where(f == slot, 0, 2 * cap)
            allowed = (query_used & (key < count) & (key <= query + reach)) | (
                key == query + self_off
            )
            tile = jnp.where(allowed, 0.0, -1e30)
            for g in range(share):
                bias_ref[block * cap : (block + 1) * cap, g * cap : (g + 1) * cap] = tile


def join_heads(ref, n, share, mb, cap):
    return jnp.concatenate(
        [ref[share * n + g, :, mb * cap : (mb + 1) * cap] for g in range(share)], 1
    )


def attend_kernel(mb, *refs):
    ids_ref, counts_ref, q_ref = refs[:3]
    blocks = refs[3:11]
    att_ref, lse_ref, k_ref, v_ref, bias_ref = refs[11:]
    cap = q_ref.shape[2] // 2
    share = QUERY_HEADS // KEY_HEADS
    stage_heads(mb, cap, blocks, k_ref, v_ref)
    stage_bias(ids_ref, counts_ref, mb, cap, share, bias_ref)

    def body(n, carry):
        scores = product_nn(k_ref[n], join_heads(q_ref, n, share, mb, cap)) + bias_ref[...]
        top = jnp.max(scores, 0, keepdims=True)
        exponent = jnp.exp(scores - top)
        total = jnp.sum(exponent, 0, keepdims=True)
        mixed = product_tn(v_ref[n], exponent.astype(jnp.bfloat16)) / total
        mixed = mixed.astype(jnp.bfloat16)
        for g in range(share):
            att_ref[share * n + g] = mixed[:, g * cap : (g + 1) * cap]
        lse_ref[n] = top + jnp.log(total)
        return carry

    lax.fori_loop(0, KEY_HEADS, body, 0)


def attend_back_kernel(mb, *refs):
    ids_ref, counts_ref, q_ref, do_ref, k_ref, v_ref, lse_ref, cos_ref, sin_ref = refs[:9]
    dq_ref = refs[9]
    targets = [ref.at[s] for ref in refs[10:12] for s in range(4)]
    bias_ref, dk_ref, dv_ref = refs[12:]
    cap = q_ref.shape[2] // 2
    share = QUERY_HEADS // KEY_HEADS
    half = HEAD_WIDTH // 2
    kv_width = KEY_HEADS * HEAD_WIDTH
    stage_bias(ids_ref, counts_ref, mb, cap, share, bias_ref)
    cosine = jnp.concatenate([cos_ref[:, mb * cap : (mb + 1) * cap]] * share, 1)
    sine = jnp.concatenate([sin_ref[:, mb * cap : (mb + 1) * cap]] * share, 1)

    def body(n, carry):
        query = join_heads(q_ref, n, share, mb, cap)
        grad = join_heads(do_ref, n, share, mb, cap)
        keys = k_ref[n]
        prob = jnp.exp(product_nn(keys, query) + bias_ref[...] - lse_ref[n])
        dprob = product_nn(v_ref[n], grad)
        delta = jnp.sum(prob * dprob, 0, keepdims=True)
        dscore = (prob * (dprob - delta)).astype(jnp.bfloat16)
        dq = product_tn(keys, dscore) * SCORE_SCALE
        front, back = dq[:half], dq[half:]
        turned = jnp.concatenate(
            [front * cosine + back * sine, back * cosine - front * sine], 0
        ).astype(jnp.bfloat16)
        for g in range(share):
            dq_ref[share * n + g] = turned[:, g * cap : (g + 1) * cap]
        dk_ref[n] = product_nt(dscore, query).astype(jnp.bfloat16)
        dv_ref[n] = product_nt(prob.astype(jnp.bfloat16), grad).astype(jnp.bfloat16)
        return carry

    lax.fori_loop(0, KEY_HEADS, body, 0)
    for block, target in enumerate(targets):
        for n in range(KEY_HEADS):
            lanes = n * HEAD_WIDTH
            target[:, lanes : lanes + HEAD_WIDTH] = dk_ref[n, block * cap : (block + 1) * cap, :]
            lanes += kv_width
            target[:, lanes : lanes + HEAD_WIDTH] = dv_ref[n, block * cap : (block + 1) * cap, :]


def collect_kernel(*refs):
    pieces, out_ref, sem = refs[:16], refs[16], refs[17]
    rows, wide = out_ref.shape[1], pieces[0].shape[1]
    copies = []
    for k in range(4):
        for s in range(4):
            copies.append(
                pltpu.make_async_copy(
                    pieces[k * 4 + s].at[pl.ds(pieces[0].shape[0] - rows, rows)],
                    out_ref.at[s, :, pl.ds(k * wide, wide)],
                    sem.at[k * 4 + s],
                )
            )
    for copy in copies:
        copy.start()
    for copy in copies:
        copy.wait()


def hidden_kernel(
    ids_ref, own_ref, other_ref, att_a_ref, att_b_ref, x_ref, gain_ref, h_ref, n2_ref, rel_ref
):
    q_cols, rows = h_ref.shape[0] // 8, h_ref.shape[1]
    fill_relative(ids_ref, rel_ref, att_a_ref, att_b_ref)
    for core_rel, w_ref in ((0, own_ref), (1, other_ref)):
        for s in range(4):
            f = column_index(ids_ref, core_rel, s)
            h_ref[start_row(f, q_cols), :] = product_nn(w_ref[s], rel_ref[...])[:q_cols]
    h = h_ref[...] + x_ref[...].astype(jnp.float32)
    h_ref[...] = h
    n2_ref[...] = jnp.zeros_like(n2_ref)
    n2_ref[:, :rows] = (h * mean_square(h) * gain_ref[...]).astype(jnp.bfloat16)


def turn_point_kernel(
    ids_ref,
    parts_ref,
    arrived_ref,
    h_ref,
    dy_ref,
    gain_ref,
    own_ref,
    other_ref,
    out_ref,
    dh_ref,
    do_ref,
    gain_grad_ref,
    pieces_ref,
    da_ref,
):
    width, rows = h_ref.shape
    q_cols = width // 8
    block = do_ref.shape[1]
    wide = own_ref.shape[2] // 4
    h = h_ref[...]
    out_ref[...] = (h + parts_ref[0] + arrived_ref[0, :, :rows].astype(jnp.float32)).astype(
        jnp.bfloat16
    )
    dn = parts_ref[1] + arrived_ref[1, :, :rows].astype(jnp.float32)
    rms = mean_square(h)
    gain_grad_ref[...] = jnp.sum(dn * h * rms, 1, keepdims=True)
    weighted = dn * gain_ref[...]
    dh = (
        dy_ref[:, :rows].astype(jnp.float32)
        + rms * weighted
        - h * (rms * rms * rms * jnp.mean(weighted * h, 0, keepdims=True))
    )
    dh_ref[...] = dh
    da_ref[...] = dh
    spread(ids_ref, da_ref, pieces_ref, q_cols)
    half = pieces_ref.shape[0] // 2
    mixed = product_tn(own_ref[...].reshape(half, 4 * wide), pieces_ref[:half, :])
    mixed += product_tn(other_ref[...].reshape(half, 4 * wide), pieces_ref[half:, :])
    mixed = mixed.astype(jnp.bfloat16)
    for k in range(4):
        do_ref[ids_ref[0] ^ k] = mixed[k * wide : k * wide + block]


def spread(ids_ref, source_ref, target_ref, cols):
    rows = source_ref.shape[1]
    for core_rel in range(2):
        for s in range(4):
            f = column_index(ids_ref, core_rel, s)
            low = (core_rel * 4 + s) * (cols + 8)
            target_ref[low : low + cols + 8, :] = jnp.concatenate(
                [source_ref[start_row(f, cols), :], jnp.zeros((8, rows), jnp.float32)], 0
            ).astype(jnp.bfloat16)


def targets_of(refs):
    return list(refs[:4]) + [refs[4].at[pl.ds(4 * k, 4)] for k in range(4)]


def out_grad_kernel(ids_ref, att_a_ref, att_b_ref, pieces_ref, *refs):
    grads, att_rel = targets_of(refs[:5]), refs[5]
    depth = pieces_ref.shape[0] // 8
    wide = att_rel.shape[0] // 4
    fill_relative(ids_ref, att_rel, att_a_ref, att_b_ref)
    for core_rel in range(2):
        for s in range(4):
            low = (core_rel * 4 + s) * depth
            got = product_nt(pieces_ref[low : low + depth, :], att_rel[...]).astype(jnp.bfloat16)
            for k in range(4):
                grads[core_rel * 4 + k][s] = got[:, k * wide : (k + 1) * wide]


def finish_q_kernel(*refs):
    ids_ref, all_ref, n1_ref, dq_a_ref, dq_b_ref = refs[:5]
    out_grads = targets_of(refs[5:10])
    dn_ref, grads = refs[10], targets_of(refs[11:16])
    n1_rel, d_ref, dq_ref = refs[16:]
    cap = dq_a_ref.shape[1]
    width = dq_a_ref.shape[0]
    q_cols = width // 8
    depth = q_cols + 8
    block = n1_ref.shape[1]
    wide = n1_rel.shape[0] // 4
    d_ref[:, :cap] = dq_a_ref[...].astype(jnp.float32)
    d_ref[:, cap:] = dq_b_ref[...].astype(jnp.float32)
    spread(ids_ref, d_ref, dq_ref, q_cols)
    fill_relative(ids_ref, n1_rel, n1_ref)
    weights = jnp.concatenate([all_ref[j, :depth, :] for j in range(8)], 0)
    dn = product_tn(weights, dq_ref[...])
    for k in range(4):
        dn_ref[ids_ref[0] ^ k] = dn[k * wide : k * wide + block]
    for core_rel in range(2):
        for s in range(4):
            low = (core_rel * 4 + s) * depth
            gq = product_nt(dq_ref[low : low + depth, :], n1_rel[...]).astype(jnp.bfloat16)
            for k in range(4):
                target = grads[core_rel * 4 + k]
                target[s, :depth, :] = gq[:, k * wide : (k + 1) * wide]
                target[s, depth:, :] = out_grads[core_rel * 4 + k][s]


def kv_grad_kernel(
    ids_ref, n1_ref, dkv_a_ref, dkv_b_ref, cos_ref, sin_ref, dkv_ref, *refs
):
    grads = targets_of(refs[:5])
    n1_rel, d_ref = refs[5:]
    cap = dkv_a_ref.shape[0]
    kv_width = KEY_HEADS * HEAD_WIDTH
    k_cols = kv_width // 8
    half = HEAD_WIDTH // 2
    wide = n1_rel.shape[0] // 4
    cosine, sine = cos_ref[...], sin_ref[...]
    d_ref[:, :cap] = dkv_a_ref[...].T
    d_ref[:, cap:] = dkv_b_ref[...].T
    for head in range(KEY_HEADS):
        base = head * HEAD_WIDTH
        front = d_ref[base : base + half, :]
        back = d_ref[base + half : base + 2 * half, :]
        d_ref[base : base + half, :] = front * cosine + back * sine
        d_ref[base + half : base + 2 * half, :] = back * cosine - front * sine
    for core_rel in range(2):
        for s in range(4):
            f = column_index(ids_ref, core_rel, s)
            low = (core_rel * 4 + s) * 2 * k_cols
            dkv_ref[low : low + 2 * k_cols, :] = jnp.concatenate(
                [
                    d_ref[start_row(f, k_cols), :],
                    d_ref[pl.ds(pl.multiple_of(kv_width + f * k_cols, 8), k_cols), :],
                ],
                0,
            ).astype(jnp.bfloat16)
    fill_relative(ids_ref, n1_rel, n1_ref)
    for core_rel in range(2):
        for s in range(4):
            low = (core_rel * 4 + s) * 2 * k_cols
            got = product_nt(dkv_ref[low : low + 2 * k_cols, :], n1_rel[...]).astype(jnp.bfloat16)
            for k in range(4):
                grads[core_rel * 4 + k][s] = got[:, k * wide : (k + 1) * wide]


def finish_kernel(*refs):
    ids_ref, all_ref, dkv_ref, dn_ref, dh_ref, x_ref, gain_ref = refs[:7]
    tokens_ref, gain_grad_ref = refs[7:]
    width = dh_ref.shape[0]
    block = dn_ref.shape[1]
    kv_rows = dkv_ref.shape[0] // 8
    low = all_ref.shape[1] - kv_rows
    wide = all_ref.shape[2] // 4
    weights = jnp.concatenate([all_ref[j, low:, :] for j in range(8)], 0)
    dn = product_tn(weights, dkv_ref[...])
    for k in range(4):
        i = ids_ref[0] ^ k
        tokens_ref[pl.ds(pl.multiple_of(i * block, 16), block), :] = (
            dn[k * wide : k * wide + block] + dn_ref[i]
        )
    x = x_ref[...].astype(jnp.float32)
    rms = mean_square(x)
    dn = tokens_ref[...]
    gain_grad_ref[...] = jnp.sum(dn * x * rms, 1, keepdims=True)
    weighted = dn * gain_ref[...]
    tokens_ref[...] = (
        dh_ref[...]
        + rms * weighted
        - x * (rms * rms * rms * jnp.mean(weighted * x, 0, keepdims=True))
    )


def mlp_kernel(*refs):
    ids_ref, n2_own, n2_other, dy_own, dy_other = refs[:5]
    pieces = refs[5:21]
    keep_ref, send_ref = refs[21:23]
    x_first, y_first = refs[35:37]
    grads = list(refs[23:27]) + [refs[27], x_first.at[1], refs[28], refs[29]]
    grads += [y_first.at[1], refs[30], refs[31], refs[32]]
    grads += [y_first.at[0], x_first.at[0], refs[33], refs[34]]
    wgu, wdn, gu_ref, prod_ref, dgu_ref, n2_rel, dy_rel, sem_in, sem_out = refs[37:]
    dp_id = ids_ref[0]
    z_id = ids_ref[1]
    block, rows = keep_ref.shape[1] // 4, keep_ref.shape[2]
    pair = 2 * rows
    wide = pieces[0].shape[1]
    half = prod_ref.shape[0] // 4

    def gate_up_part(ref, piece, k, s):
        return piece.at[pl.ds(0, 2 * half)], ref.at[
            pl.ds(s * 2 * half, 2 * half), pl.ds(k * wide, wide)
        ]

    def down_part(ref, piece, k, s):
        return piece.at[pl.ds(2 * half, half)], ref.at[
            pl.ds(k * half, half), pl.ds(s * wide, wide)
        ]

    loads, more_loads = [], []
    for s in range(4):
        for k in range(4):
            source, target = gate_up_part(wgu, pieces[k * 4 + s], k, s)
            loads.append(pltpu.make_async_copy(source, target, sem_in.at[0, k * 4 + s]))
            source, target = down_part(wdn, pieces[k * 4 + s], k, s)
            more_loads.append(pltpu.make_async_copy(source, target, sem_in.at[1, k * 4 + s]))
    for load in loads + more_loads:
        load.start()
    pad = jnp.zeros((wide - block, pair), jnp.bfloat16)
    for j in range(4):
        i = dp_id ^ j
        zz = lax.rem(z_id - j + 4, 4)
        n2_rel[j * wide : j * wide + block, :] = jnp.concatenate(
            [n2_own[i][:, :rows], n2_other[i][:, :rows]], 1
        )
        dy_rel[j * wide : j * wide + block, :] = jnp.concatenate(
            [dy_own[zz][:, :rows], dy_other[zz][:, :rows]], 1
        )
        n2_rel[j * wide + block : (j + 1) * wide, :] = pad
        dy_rel[j * wide + block : (j + 1) * wide, :] = pad

    def rows_of(index, size):
        return pl.ds(pl.multiple_of(index * size, 16), size)

    for s in range(4):
        for load in loads[4 * s : 4 * s + 4]:
            load.wait()
        k = lax.rem(z_id - s + 4, 4) ^ dp_id
        total = product_nn(wgu[s * 2 * half : (s + 1) * 2 * half, :], n2_rel[...])
        gu_ref[rows_of(k, 2 * half), :] = total
        gate = total[:half]
        prod_ref[rows_of(k, half), :] = (gate * jax.nn.sigmoid(gate) * total[half:]).astype(
            jnp.bfloat16
        )
    for load in more_loads:
        load.wait()
    for k in range(4):
        s = lax.rem(z_id - (dp_id ^ k) + 4, 4)
        dprod = product_nn(wdn[k * half : (k + 1) * half, :], dy_rel[...])
        gate = gu_ref[k * 2 * half : k * 2 * half + half, :]
        up = gu_ref[k * 2 * half + half : (k + 1) * 2 * half, :]
        sig = jax.nn.sigmoid(gate)
        dgu_ref[rows_of(s, 2 * half), :] = jnp.concatenate(
            [dprod * up * sig * (1.0 + gate * (1.0 - sig)), dprod * gate * sig], 0
        ).astype(jnp.bfloat16)
    for j in range(4):
        lanes = slice(j * wide, (j + 1) * wide)
        out = product_tn(wdn[:, lanes], prod_ref[...])[:block]
        zz = rows_of(lax.rem(z_id - j + 4, 4), block)
        keep_ref[0, zz, :] = out[:, :rows]
        send_ref[0, zz, :rows] = out[:, rows:].astype(jnp.bfloat16)
    for k in range(4):
        here = slice(k * half, (k + 1) * half)
        wdn[here, :] = product_nt(prod_ref[here, :], dy_rel[...]).astype(jnp.bfloat16)
    stores = []
    for k in range(4):
        for s in range(4):
            target, source = down_part(wdn, grads[k * 4 + s], k, s)
            stores.append(pltpu.make_async_copy(source, target, sem_out.at[1, k * 4 + s]))
    for store in stores:
        store.start()
    for j in range(4):
        lanes = slice(j * wide, (j + 1) * wide)
        dn = product_tn(wgu[:, lanes], dgu_ref[...])[:block]
        i = rows_of(dp_id ^ j, block)
        keep_ref[1, i, :] = dn[:, :rows]
        send_ref[1, i, :rows] = dn[:, rows:].astype(jnp.bfloat16)
    send_ref[:, :, rows:] = jnp.zeros((2, 4 * block, send_ref.shape[2] - rows), jnp.bfloat16)
    for s in range(4):
        here = slice(s * 2 * half, (s + 1) * 2 * half)
        wgu[here, :] = product_nt(dgu_ref[here, :], n2_rel[...]).astype(jnp.bfloat16)
        for k in range(4):
            target, source = gate_up_part(wgu, grads[k * 4 + s], k, s)
            store = pltpu.make_async_copy(source, target, sem_out.at[0, k * 4 + s])
            store.start()
            stores.append(store)
    for store in stores:
        store.wait()


def mean_square(values):
    return lax.rsqrt(jnp.mean(values * values, 0, keepdims=True) + EPSILON)


def fast(
    tokens, cotangent, counts, w_query, key_weight, value_weight, w_out, w_gate, w_up, w_down, gains
):
    dp_id = lax.axis_index("dp")
    slot = lax.axis_index("fsdp")
    z_id = slot // 2
    core_id = slot % 2
    ids = jnp.stack([dp_id, z_id, core_id, slot]).astype(jnp.int32)
    batches, cap, width = tokens.shape
    rows = batches * cap
    block = w_query.shape[0]
    wide = -(-block // 128) * 128
    q_cols, k_cols = w_query.shape[1], key_weight.shape[1]
    half = w_gate.shape[1]
    kv_width = KEY_HEADS * HEAD_WIDTH
    share = QUERY_HEADS // KEY_HEADS
    q_rows = q_cols + 8
    depth = q_rows + 2 * k_cols
    mlp_rows = 3 * half + q_rows
    padded = -(-rows // 128) * 128

    (first_piece,) = run(
        pack_first_kernel,
        "pack_first",
        (counts, w_query, key_weight.T, value_weight.T, gains),
        [SMEM] + [VMEM] * 4,
        [struct((depth, wide))],
        [VMEM],
        [],
        0,
        16,
    )
    chain = [first_piece] + [shift_z(first_piece, step) for step in (1, 2, 3)]
    down = w_down.T
    give = jnp.where(core_id == 0, down[:, half:], down[:, :half])
    other_down = swap_core(jnp.pad(give, ((0, 0), (0, -half % 128))))
    (mlp_piece,) = run(
        pack_mlp_kernel,
        "pack_mlp",
        (ids, w_gate.T, w_up.T, down, other_down, w_out),
        [SMEM] + [VMEM] * 5,
        [struct((mlp_rows, wide))],
        [VMEM],
        [],
        0,
        16,
    )
    x, dy = run(
        turn_in_kernel,
        "turn_in",
        (tokens.reshape(rows, width), cotangent.reshape(rows, width)),
        [VMEM] * 2,
        [struct((width, rows)), struct((width, padded))],
        [VMEM] * 2,
        [],
        0,
        16,
    )

    along = jnp.stack(chain, 0)
    extras = along[:, q_cols : q_cols + 2, :block]
    other_extras = swap_core(extras)
    from_x = swap_dp(along, 1)
    from_y = swap_dp(along, 2)
    first_own = [along, from_x, from_y, swap_dp(from_x[:2], 2), swap_dp(from_y[2:], 1)]
    first_other = [swap_core(piece) for piece in first_own]

    z_one = shift_z(after(mlp_piece, along), 1)
    z_two = shift_z(z_one, 1)
    z_three = shift_z(z_two, 1)
    mlp_next = after(mlp_piece, *first_own[3:])
    x_zero, y_zero = swap_dp(mlp_next, 1), swap_dp(mlp_next, 2)

    by_core = jnp.where(
        core_id == 0, jnp.stack([extras, other_extras], 1), jnp.stack([other_extras, extras], 1)
    )
    by_core = by_core[::-1]
    by_core = lax.dynamic_slice_in_dim(jnp.concatenate([by_core, by_core], 0), 3 - z_id, 4, 0)
    gain = by_core[:, :, 0, :].reshape(8, 2, q_cols).transpose(0, 2, 1).reshape(width, 2)
    gain = gain.astype(jnp.float32)
    gain_one, gain_two = gain[:, :1], gain[:, 1:]
    group_counts = by_core[:, :, 1, :batches].reshape(8, batches).astype(jnp.int32)
    flat_counts = group_counts.T.reshape(-1)
    before = jnp.sum(
        jnp.where(jnp.arange(8, dtype=jnp.int32)[:, None] < slot, group_counts, 0), 0
    )
    position = (before[:, None] + jnp.arange(cap, dtype=jnp.int32)[None, :]).reshape(-1)
    cosine, sine = rope_tables(position, HEAD_WIDTH)
    cosine, sine = cosine[:, 0, :].T, sine[:, 0, :].T
    x_wide = x.astype(jnp.float32)
    n1 = (x_wide * mean_square(x_wide) * gain_one).astype(jnp.bfloat16).reshape(4, block, rows)
    n1_next = after(n1, z_two, flat_counts, gain_one, gain_two)

    query, kv, first_all = run(
        project_kernel,
        "project",
        (ids, *first_own, *first_other, n1_next, cosine, sine),
        [SMEM] + [VMEM] * 13,
        (
            struct((QUERY_HEADS, HEAD_WIDTH, rows)),
            struct((rows, 2 * kv_width)),
            struct((8, depth, 4 * wide)),
        ),
        [VMEM] * 3,
        [
            pltpu.VMEM((width + 2 * kv_width, rows), jnp.float32),
            pltpu.VMEM((2 * kv_width, rows), jnp.float32),
            pltpu.VMEM((4 * wide, rows), jnp.bfloat16),
        ],
        2 * (width + 2 * kv_width) * width * rows,
        20,
    )
    kv_zero = after(kv, x_zero, y_zero)
    kv_one = shift_z_up(kv_zero, 1)
    x_one = swap_dp(after(z_one, kv_zero), 1)
    far_zero = swap_dp(after(x_zero, kv_zero), 2)
    wave = (kv_one, x_one, far_zero, z_three)
    kv_two = shift_z_up(after(*wave), 1)
    x_two = swap_dp(after(z_two, *wave), 1)
    y_one = swap_dp(after(z_one, *wave), 2)
    wave = (kv_two, x_two, y_one)
    kv_three = shift_z_up(after(*wave), 1)
    far_one = swap_dp(after(y_one, *wave), 1)
    y_two = swap_dp(after(z_two, *wave), 2)
    wave = (kv_three, far_one, y_two)
    x_three = swap_dp(after(z_three, *wave), 1)
    y_three = swap_dp(after(z_three, *wave), 2)
    kv_own = [kv, kv_one, kv_two, kv_three]
    kv_other = [swap_core(piece) for piece in (kv_zero, kv_one, kv_two, kv_three)]
    pair_flops = 2 * QUERY_HEADS * HEAD_WIDTH * rows * 8 * cap
    bias_scratch = pltpu.VMEM((8 * cap, share * cap), jnp.float32)
    def attend(mb, queries):
        return run(
            functools.partial(attend_kernel, mb),
            "attend",
            (ids, flat_counts, queries, *kv_own, *kv_other),
            [SMEM, SMEM] + [VMEM] * 9,
            (
                struct((QUERY_HEADS, HEAD_WIDTH, cap)),
                struct((KEY_HEADS, 1, share * cap), jnp.float32),
                struct((KEY_HEADS, 8 * cap, HEAD_WIDTH)),
                struct((KEY_HEADS, 8 * cap, HEAD_WIDTH)),
            ),
            [VMEM] * 4,
            [bias_scratch],
            4 * pair_flops,
            20,
        )

    att_a, lse_a, *heads_a = attend(0, after(query, far_one, y_two))
    wave = (att_a, x_three, y_three)
    far_two = swap_dp(after(x_two, *wave), 2)
    far_three = swap_dp(after(y_three, *wave), 1)
    dy_other = swap_core(after(dy, att_a))
    att_b, lse_b, *heads_b = attend(1, after(query, *wave))
    pieces = [mlp_piece, z_one, z_two, z_three]
    pieces += [x_zero, x_one, x_two, x_three]
    pieces += [y_zero, y_one, y_two, y_three]
    pieces += [far_zero, far_one, far_two, far_three]
    (out_own,) = run(
        collect_kernel,
        "collect",
        tuple(pieces[:15]) + (after(far_three, att_b),),
        [HBM] * 16,
        [struct((4, q_rows, 4 * wide))],
        [VMEM],
        [pltpu.SemaphoreType.DMA((16,))],
        0,
        8,
    )
    out_other = swap_core(out_own)
    att_a = att_a.reshape(4, block, cap)
    att_b = att_b.reshape(4, block, cap)
    lse = (lse_a, lse_b)
    blocks = (4, block, rows)
    wide_blocks = (4, block, padded)
    h, n2 = run(
        hidden_kernel,
        "hidden",
        (ids, out_own, out_other, att_a, att_b, after(x, dy_other), gain_two),
        [SMEM] + [VMEM] * 6,
        (struct((width, rows), jnp.float32), struct((width, padded))),
        [VMEM] * 2,
        [pltpu.VMEM((4 * wide, rows), jnp.bfloat16)],
        2 * width * width * rows,
        16,
    )
    n2_other = swap_core(n2)
    results = run(
        mlp_kernel,
        "mlp",
        (
            ids,
            n2.reshape(wide_blocks),
            n2_other.reshape(wide_blocks),
            dy.reshape(wide_blocks),
            dy_other.reshape(wide_blocks),
            *pieces,
        ),
        [SMEM] + [VMEM] * 4 + [HBM] * 16,
        [struct((2, width, rows), jnp.float32), struct((2, width, padded))]
        + [struct((3 * half, wide))] * 12
        + [struct((2, 3 * half, wide))] * 2,
        [VMEM] * 2 + [HBM] * 14,
        [
            pltpu.VMEM((8 * half, 4 * wide), jnp.bfloat16),
            pltpu.VMEM((4 * half, 4 * wide), jnp.bfloat16),
            pltpu.VMEM((8 * half, 2 * rows), jnp.float32),
            pltpu.VMEM((4 * half, 2 * rows), jnp.bfloat16),
            pltpu.VMEM((8 * half, 2 * rows), jnp.bfloat16),
            pltpu.VMEM((4 * wide, 2 * rows), jnp.bfloat16),
            pltpu.VMEM((4 * wide, 2 * rows), jnp.bfloat16),
            pltpu.SemaphoreType.DMA((2, 16)),
            pltpu.SemaphoreType.DMA((2, 16)),
        ],
        18 * 16 * half * block * 2 * rows,
        52,
    )
    keep, send = results[:2]
    home = results[2:6]
    to_x_zero, to_x_two, to_x_three, to_y_one, to_y_two, to_y_three = results[6:12]
    far_two, far_three, x_first, y_first = results[12:]
    arrived = swap_core(send)

    output, dh, mixed_gradient, gain_two_grad, da_pieces = run(
        turn_point_kernel,
        "turn_point",
        (ids, keep, arrived, h, dy, gain_two, out_own, out_other),
        [SMEM] + [VMEM] * 7,
        (
            struct((width, rows)),
            struct((width, rows), jnp.float32),
            struct(blocks),
            struct((width, 1), jnp.float32),
            struct((8 * q_rows, rows)),
        ),
        [VMEM] * 5,
        [pltpu.VMEM((width, rows), jnp.float32)],
        2 * width * width * rows,
        22,
    )
    output = output.T.reshape(batches, cap, width)
    def attend_back(mb, mixed):
        return run(
            functools.partial(attend_back_kernel, mb),
            "attend_back",
            (
                ids,
                flat_counts,
                query,
                mixed.reshape(QUERY_HEADS, HEAD_WIDTH, rows),
                *(heads_a, heads_b)[mb],
                lse[mb],
                cosine,
                sine,
            ),
            [SMEM, SMEM] + [VMEM] * 7,
            [struct((QUERY_HEADS, HEAD_WIDTH, cap))] + [struct((4, cap, 2 * kv_width))] * 2,
            [VMEM] * 3,
            [
                bias_scratch,
                pltpu.VMEM((KEY_HEADS, 8 * cap, HEAD_WIDTH), jnp.bfloat16),
                pltpu.VMEM((KEY_HEADS, 8 * cap, HEAD_WIDTH), jnp.bfloat16),
            ],
            10 * pair_flops,
            24,
        )

    def sum_cores(own, other):
        arrived = swap_core(other)
        return [add_low(own[s], arrived[s]) for s in range(4)]

    def sum_z(summed):
        total = summed[0].astype(jnp.float32)
        for s in (3, 2, 1):
            total = total + shift_z_down(summed[s], s).astype(jnp.float32)
        return total

    via_three = swap_dp(after(far_three, mixed_gradient), 1)
    via_two = swap_dp(after(far_two, mixed_gradient), 2)
    x_three = swap_dp(after(to_x_three, mixed_gradient), 1)
    y_two = swap_dp(after(to_y_two, mixed_gradient), 2)
    back_a = attend_back(0, mixed_gradient)
    wave = (back_a[0], via_three, via_two, x_three, y_two)
    x_two = swap_dp(add_low(to_x_two, after(via_two, *wave)), 1)
    y_three = swap_dp(add_low(to_y_three, after(via_three, *wave)), 2)
    out_grads = run(
        out_grad_kernel,
        "out_grad",
        (ids, att_a, att_b, after(da_pieces, *wave)),
        [SMEM] + [VMEM] * 3,
        [struct((4, q_rows, wide))] * 4 + [struct((16, q_rows, wide))],
        [VMEM] * 5,
        [pltpu.VMEM((4 * wide, rows), jnp.bfloat16)],
        2 * width * width * rows,
        14,
    )
    summed_a = sum_cores(*back_a[1:])
    wave = (x_two, y_three, out_grads[0])
    dkv_a = sum_z([after(piece, *wave) for piece in summed_a])
    x_first, y_first = swap_dp(after(x_first, *wave), 1), swap_dp(after(y_first, *wave), 2)
    via_one, x_one = x_first[0], x_first[1]
    via_zero, y_zero = y_first[0], y_first[1]
    back_b = attend_back(1, after(mixed_gradient, *summed_a, *wave))
    wave = (back_b[0], dkv_a, x_first, y_first)
    summed_b = sum_cores(back_b[1], after(back_b[2], *wave))
    parts_b = [shift_z_down(summed_b[s], s) for s in (1, 2, 3)]

    def sum_pair(parts):
        arrived = swap_core(parts[4])
        return [add_low(parts[k], arrived[4 * k : 4 * k + 4]) for k in range(4)]

    def share_square(mine):
        return [mine[0]] + [swap_dp(mine[k], k) for k in (1, 2, 3)]

    def reduce_all(summed):
        out = [add_low(*[piece[s] for piece in summed]) for s in range(4)]
        total = out[0].astype(jnp.float32)
        for s in (1, 2, 3):
            total = total + shift_z(out[s], -s).astype(jnp.float32)
        return total

    q_results = run(
        finish_q_kernel,
        "finish_q",
        (
            ids,
            first_all,
            after(n1, *wave),
            back_a[0].reshape(width, cap),
            back_b[0].reshape(width, cap),
            *out_grads,
        ),
        [SMEM] + [VMEM] * 9,
        [struct(blocks, jnp.float32)]
        + [struct((4, 2 * q_rows, wide))] * 4
        + [struct((16, 2 * q_rows, wide))],
        [VMEM] * 6,
        [
            pltpu.VMEM((4 * wide, rows), jnp.bfloat16),
            pltpu.VMEM((width, rows), jnp.float32),
            pltpu.VMEM((8 * q_rows, rows), jnp.bfloat16),
        ],
        4 * width * width * rows,
        22,
    )
    dn_q = q_results[0]
    dkv_b = summed_b[0].astype(jnp.float32)
    for part in parts_b:
        dkv_b = dkv_b + part.astype(jnp.float32)
    x_zero = swap_dp(add_low(to_x_zero, via_zero), 1)
    y_one = swap_dp(add_low(to_y_one, via_one), 2)
    hop = shift_z(add_low(after(home[3], dkv_b), x_three, y_three), -1)
    q_out_mine = sum_pair(q_results[1:])
    q_out_shared = share_square(q_out_mine)
    q_out_total = reduce_all(q_out_shared)
    grad_query = q_out_total[:q_cols, :block].T
    grad_out = q_out_total[q_rows : q_rows + q_cols, :block].T

    dkv_pieces, *kv_grads = run(
        kv_grad_kernel,
        "kv_grad",
        (ids, after(n1, x_zero, y_one, *q_out_mine), dkv_a, dkv_b, cosine, sine),
        [SMEM] + [VMEM] * 5,
        [struct((16 * k_cols, rows))]
        + [struct((4, 2 * k_cols, wide))] * 4
        + [struct((16, 2 * k_cols, wide))],
        [VMEM] * 6,
        [
            pltpu.VMEM((4 * wide, rows), jnp.bfloat16),
            pltpu.VMEM((2 * kv_width, rows), jnp.float32),
        ],
        4 * kv_width * width * rows,
        14,
    )
    grad_tokens, gain_one_grad = run(
        finish_kernel,
        "finish",
        (ids, first_all, dkv_pieces, dn_q, dh, after(x, *q_out_shared), gain_one),
        [SMEM] + [VMEM] * 6,
        [struct((width, rows), jnp.float32), struct((width, 1), jnp.float32)],
        [VMEM] * 2,
        [],
        4 * kv_width * width * rows,
        20,
    )
    grad_tokens = grad_tokens.T.reshape(batches, cap, width)
    kv_mine = sum_pair(kv_grads)
    hop = shift_z(add_low(home[2], x_two, y_two, after(hop, dkv_pieces)), -1)
    hop = shift_z(add_low(home[1], x_one, y_one, after(hop, *kv_mine)), -1)
    mlp_total = (
        home[0].astype(jnp.float32)
        + y_zero.astype(jnp.float32)
        + x_zero.astype(jnp.float32)
        + hop.astype(jnp.float32)
    )
    grad_gate = mlp_total[:half, :block].T
    grad_up = mlp_total[half : 2 * half, :block].T
    down_total = mlp_total[2 * half :, :block]
    left, right = down_total[:, :q_cols], down_total[:, q_cols:]
    stay = jnp.where(core_id == 0, left, right)
    give = jnp.where(core_id == 0, right, left).astype(jnp.bfloat16)
    taken = swap_core(give).astype(jnp.float32)
    grad_down = jnp.where(
        core_id == 0, jnp.concatenate([stay, taken], 0), jnp.concatenate([taken, stay], 0)
    )

    kv_total = reduce_all(share_square(kv_mine))
    gain_total = after(jnp.concatenate([gain_one_grad, gain_two_grad], 1).T, *kv_mine)
    gain_total = gain_total + swap_core(gain_total)
    gain_total = gain_total + swap_dp(gain_total, 1)
    gain_total = gain_total + swap_dp(gain_total, 2)
    for mask in (2, 4):
        gain_total = gain_total + lax.ppermute(
            gain_total, "fsdp", [(j, j ^ mask) for j in range(8)]
        )
    gain_grad = lax.dynamic_slice_in_dim(gain_total, slot * q_cols, q_cols, 1)
    return (
        output,
        grad_tokens,
        grad_query,
        kv_total[:k_cols, :block].T,
        kv_total[k_cols:, :block].T,
        grad_out,
        grad_gate,
        grad_up,
        grad_down,
        gain_grad,
    )


def solution(mesh):
    in_specs = (
        P(None, ("dp", "fsdp"), None),
        P(None, ("dp", "fsdp"), None),
        P(None, ("dp", "fsdp")),
        P("dp", "fsdp"),
        P("dp", "fsdp"),
        P("dp", "fsdp"),
        P("dp", "fsdp"),
        P("dp", "fsdp"),
        P("dp", "fsdp"),
        P("dp", "fsdp"),
        P(None, "fsdp"),
    )
    out_specs = (
        P(None, ("dp", "fsdp"), None),
        P(None, ("dp", "fsdp"), None),
        P("dp", "fsdp"),
        P("dp", "fsdp"),
        P("dp", "fsdp"),
        P("dp", "fsdp"),
        P("dp", "fsdp"),
        P("dp", "fsdp"),
        P("dp", "fsdp"),
        P(None, "fsdp"),
    )
    square = mesh.shape["dp"] == 4 and mesh.shape["fsdp"] == 8
    return jax.shard_map(
        fast if square else local, mesh=mesh, in_specs=in_specs, out_specs=out_specs, check_vma=False)
```

```python
import functools

import jax
import jax.numpy as jnp
from jax import lax
from jax.experimental import pallas as pl
from jax.experimental.pallas import tpu as pltpu
from jax.sharding import PartitionSpec as P

MODEL_WIDTH = 960
QUERY_HEADS = 15
KEY_HEADS = 5
HEAD_WIDTH = 64


EPSILON = 1e-05
ROPE_BASE = 100000.0
SCORE_SCALE = 0.125


def rope_tables(position, head_size):
    half_size = head_size // 2
    frequency = ROPE_BASE ** (-(jnp.arange(half_size, dtype=jnp.float32) * 2.0) / head_size)
    angles = position.astype(jnp.float32)[:, None] * frequency[None, :]
    return (jnp.cos(angles)[:, None, :], jnp.sin(angles)[:, None, :])


def apply_rotation(values, cosine_table, sine_values):
    half_size = values.shape[-1] // 2
    front_half = values[..., :half_size]
    back_half = values[..., half_size:]
    return jnp.concatenate(
        [
            front_half * cosine_table - back_half * sine_values,
            back_half * cosine_table + front_half * sine_values,
        ],
        -1,
    )


def normalize(values, gain_row):
    inv_rms = lax.rsqrt(jnp.mean(values * values, -1, keepdims=True) + EPSILON)
    return (values * inv_rms * gain_row, inv_rms)


def norm_back(values, inv_rms, gain_row, incoming):
    weighted = incoming * gain_row
    return inv_rms * weighted - values * inv_rms * inv_rms * inv_rms * jnp.mean(
        weighted * values, -1, keepdims=True
    )


def build_mask(count_row, device, slot_capacity):
    group_width = count_row.shape[0]
    local_slot = jnp.arange(slot_capacity, dtype=jnp.int32)
    offsets = jnp.cumsum(count_row) - count_row
    is_mine = jnp.arange(group_width, dtype=jnp.int32) == device
    own_offset = jnp.sum(jnp.where(is_mine, offsets, 0))
    own_count = jnp.sum(jnp.where(is_mine, count_row, 0))
    query_pos = own_offset + local_slot
    query_valid = local_slot < own_count
    key_pos = (offsets[:, None] + local_slot[None, :]).reshape(-1)
    key_valid = (local_slot[None, :] < count_row[:, None]).reshape(-1)
    slot_ids = jnp.arange(group_width * slot_capacity, dtype=jnp.int32)
    own_slots = device * slot_capacity + local_slot
    allowed = query_valid[:, None] & key_valid[None, :] & (
        key_pos[None, :] <= query_pos[:, None]
    ) | (slot_ids[None, :] == own_slots[:, None])
    return (allowed, query_pos)


def kept_fetch(w_query, key_weight, value_weight, w_out, w_gate, w_up, w_down, gains):
    columns = (
        lax.all_gather(w_query, "fsdp", axis=1, tiled=True),
        lax.all_gather(key_weight, "fsdp", axis=1, tiled=True),
        lax.all_gather(value_weight, "fsdp", axis=1, tiled=True),
        lax.all_gather(w_out, "fsdp", axis=1, tiled=True),
        lax.all_gather(w_gate, "fsdp", axis=1, tiled=True),
        lax.all_gather(w_up, "fsdp", axis=1, tiled=True),
        lax.all_gather(w_down, "fsdp", axis=1, tiled=True),
        lax.all_gather(gains, "fsdp", axis=1, tiled=True),
    )
    matrices = (
        lax.all_gather(columns[0], "dp", axis=0, tiled=True),
        lax.all_gather(columns[1], "dp", axis=0, tiled=True),
        lax.all_gather(columns[2], "dp", axis=0, tiled=True),
        lax.all_gather(columns[3], "dp", axis=0, tiled=True),
        lax.all_gather(columns[4], "dp", axis=0, tiled=True),
        lax.all_gather(columns[5], "dp", axis=0, tiled=True),
        lax.all_gather(columns[6], "dp", axis=0, tiled=True),
    )
    return (matrices, columns[7].astype(jnp.float32))


def times_transpose(left, right):
    return jnp.einsum("rk,jk->rj", left, right, preferred_element_type=jnp.float32)


def rows_product(left, right):
    return jnp.einsum("rd,rk->dk", left, right, preferred_element_type=jnp.float32)


def local(
    tokens, cotangent, counts, w_query, key_weight, value_weight, w_out, w_gate, w_up, w_down, gains
):
    group_counts = lax.all_gather(counts, "fsdp", axis=1, tiled=True)
    device = lax.axis_index("fsdp")
    slot_capacity = tokens.shape[1]
    key_value_width = KEY_HEADS * HEAD_WIDTH
    device_share = QUERY_HEADS // KEY_HEADS
    kept_weights, kept_gain = kept_fetch(
        w_query, key_weight, value_weight, w_out, w_gate, w_up, w_down, gains
    )
    outputs = []
    grad_inputs = []
    saved = [[] for index_unused in range(11)]
    gain_one_total = jnp.zeros((MODEL_WIDTH,), jnp.float32)
    gain_two_total = jnp.zeros((MODEL_WIDTH,), jnp.float32)
    for micro_idx in range(tokens.shape[0]):
        matrices, gain_pair = (kept_weights, kept_gain)
        full_query, full_key, full_value, full_out, full_gate, full_up, full_down = matrices
        inputs = tokens[micro_idx].astype(jnp.float32)
        allowed, query_pos = build_mask(group_counts[micro_idx], device, slot_capacity)
        cosine_table, sine_values = rope_tables(query_pos, HEAD_WIDTH)
        first_normed, scale_one = normalize(inputs, gain_pair[0])
        normed_low = first_normed.astype(jnp.bfloat16)
        reduced_query = apply_rotation(
            jnp.dot(normed_low, full_query, preferred_element_type=jnp.float32).reshape(
                slot_capacity, QUERY_HEADS, HEAD_WIDTH
            ),
            cosine_table,
            sine_values,
        ).astype(jnp.bfloat16)
        key_low = (
            apply_rotation(
                jnp.dot(normed_low, full_key, preferred_element_type=jnp.float32).reshape(
                    slot_capacity, KEY_HEADS, HEAD_WIDTH
                ),
                cosine_table,
                sine_values,
            )
            .astype(jnp.bfloat16)
            .reshape(slot_capacity, key_value_width)
        )
        value_low = jnp.dot(normed_low, full_value, preferred_element_type=jnp.float32).astype(
            jnp.bfloat16
        )
        grouped_keys, grouped_values = (
            lax.all_gather(key_low, "fsdp", axis=0, tiled=True),
            lax.all_gather(value_low, "fsdp", axis=0, tiled=True),
        )
        heads_of_key = grouped_keys.reshape(-1, KEY_HEADS, HEAD_WIDTH)
        heads_of_value = grouped_values.reshape(-1, KEY_HEADS, HEAD_WIDTH)
        heads_of_query = reduced_query.reshape(slot_capacity, KEY_HEADS, device_share, HEAD_WIDTH)
        scores = (
            jnp.einsum(
                "qngd,knd->ngqk", heads_of_query, heads_of_key, preferred_element_type=jnp.float32
            )
            * SCORE_SCALE
        )
        masked = jnp.where(allowed, scores, -1e30)
        row_top = jnp.max(masked, -1, keepdims=True)
        exponent = jnp.where(allowed, jnp.exp(masked - row_top), 0.0)
        row_total = jnp.sum(exponent, -1, keepdims=True)
        prob_low = (exponent / row_total).astype(jnp.bfloat16)
        log_total = row_top + jnp.log(row_total)
        mixed_heads = jnp.einsum(
            "ngqk,knd->qngd", prob_low, heads_of_value, preferred_element_type=jnp.float32
        ).reshape(slot_capacity, MODEL_WIDTH)
        attended = mixed_heads.astype(jnp.bfloat16)
        hidden_state = inputs + jnp.dot(attended, full_out, preferred_element_type=jnp.float32)
        normed_two, scale_two = normalize(hidden_state, gain_pair[1])
        normed_two_low = normed_two.astype(jnp.bfloat16)
        gate_act = jnp.dot(normed_two_low, full_gate, preferred_element_type=jnp.float32)
        upward = jnp.dot(normed_two_low, full_up, preferred_element_type=jnp.float32)
        sigmoid_gate = jax.nn.sigmoid(gate_act)
        product = (gate_act * sigmoid_gate * upward).astype(jnp.bfloat16)
        outputs.append(
            (hidden_state + jnp.dot(product, full_down, preferred_element_type=jnp.float32)).astype(
                jnp.bfloat16
            )
        )
        matrices, gain_pair = (kept_weights, kept_gain)
        full_query, full_key, full_value, full_out, full_gate, full_up, full_down = matrices
        grad_low = cotangent[micro_idx]
        grad_product = times_transpose(grad_low, full_down)
        grad_gate = (
            grad_product * upward * sigmoid_gate * (1.0 + gate_act * (1.0 - sigmoid_gate))
        ).astype(jnp.bfloat16)
        grad_upward = (grad_product * gate_act * sigmoid_gate).astype(jnp.bfloat16)
        grad_normed_two = times_transpose(grad_gate, full_gate) + times_transpose(
            grad_upward, full_up
        )
        gain_two_total = gain_two_total + jnp.sum(grad_normed_two * hidden_state * scale_two, 0)
        grad_hidden = grad_low.astype(jnp.float32) + norm_back(
            hidden_state, scale_two, gain_pair[1], grad_normed_two
        )
        grad_branch = grad_hidden.astype(jnp.bfloat16)
        mixed_gradient = times_transpose(grad_branch, full_out).astype(jnp.bfloat16)
        head_gradient = mixed_gradient.reshape(slot_capacity, KEY_HEADS, device_share, HEAD_WIDTH)
        again_scores = (
            jnp.einsum(
                "qngd,knd->ngqk", heads_of_query, heads_of_key, preferred_element_type=jnp.float32
            )
            * SCORE_SCALE
        )
        probability = jnp.where(allowed, jnp.exp(again_scores - log_total), 0.0)
        grad_prob = jnp.einsum(
            "qngd,knd->ngqk", head_gradient, heads_of_value, preferred_element_type=jnp.float32
        )
        row_delta = jnp.sum(probability * grad_prob, -1, keepdims=True)
        grad_scores = (probability * (grad_prob - row_delta)).astype(jnp.bfloat16)
        grad_query_rot = (
            jnp.einsum(
                "ngqk,knd->qngd", grad_scores, heads_of_key, preferred_element_type=jnp.float32
            ).reshape(slot_capacity, QUERY_HEADS, HEAD_WIDTH)
            * SCORE_SCALE
        )
        key_part = (
            jnp.einsum(
                "ngqk,qngd->knd", grad_scores, heads_of_query, preferred_element_type=jnp.float32
            ).reshape(-1, key_value_width)
            * SCORE_SCALE
        )
        value_part = jnp.einsum(
            "ngqk,qngd->knd",
            probability.astype(jnp.bfloat16),
            head_gradient,
            preferred_element_type=jnp.float32,
        ).reshape(-1, key_value_width)
        key_gradient, value_grad = (
            lax.psum_scatter(
                key_part.astype(jnp.bfloat16), "fsdp", scatter_dimension=0, tiled=True
            ).astype(jnp.float32),
            lax.psum_scatter(
                value_part.astype(jnp.bfloat16), "fsdp", scatter_dimension=0, tiled=True
            ).astype(jnp.float32),
        )
        grad_query = (
            apply_rotation(grad_query_rot, cosine_table, -sine_values)
            .astype(jnp.bfloat16)
            .reshape(slot_capacity, MODEL_WIDTH)
        )
        grad_key = (
            apply_rotation(
                key_gradient.reshape(slot_capacity, KEY_HEADS, HEAD_WIDTH),
                cosine_table,
                -sine_values,
            )
            .astype(jnp.bfloat16)
            .reshape(slot_capacity, key_value_width)
        )
        grad_value = value_grad.astype(jnp.bfloat16)
        grad_normed_one = (
            times_transpose(grad_query, full_query)
            + times_transpose(grad_key, full_key)
            + times_transpose(grad_value, full_value)
        )
        gain_one_total = gain_one_total + jnp.sum(grad_normed_one * inputs * scale_one, 0)
        grad_inputs.append(
            grad_hidden + norm_back(inputs, scale_one, gain_pair[0], grad_normed_one)
        )
        kept_rows = (
            normed_low,
            grad_query,
            grad_key,
            grad_value,
            attended,
            grad_branch,
            normed_two_low,
            grad_gate,
            grad_upward,
            product,
            grad_low,
        )
        for slot_index in range(11):
            saved[slot_index].append(kept_rows[slot_index])
    joined = [jnp.concatenate(column_list, 0) for column_list in saved]
    gain_terms = jnp.stack([gain_one_total, gain_two_total], 0)
    slices = (
        lax.all_to_all(joined[1], "fsdp", split_axis=1, concat_axis=0, tiled=True),
        lax.all_to_all(joined[2], "fsdp", split_axis=1, concat_axis=0, tiled=True),
        lax.all_to_all(joined[3], "fsdp", split_axis=1, concat_axis=0, tiled=True),
        lax.all_to_all(joined[5], "fsdp", split_axis=1, concat_axis=0, tiled=True),
        lax.all_to_all(joined[7], "fsdp", split_axis=1, concat_axis=0, tiled=True),
        lax.all_to_all(joined[8], "fsdp", split_axis=1, concat_axis=0, tiled=True),
        lax.all_to_all(joined[10], "fsdp", split_axis=1, concat_axis=0, tiled=True),
    )
    pieces = (
        lax.all_gather(joined[0], "fsdp", axis=0, tiled=True),
        lax.all_gather(joined[4], "fsdp", axis=0, tiled=True),
        lax.all_gather(joined[6], "fsdp", axis=0, tiled=True),
        lax.all_gather(joined[9], "fsdp", axis=0, tiled=True),
    )
    picked = [member for member in slices]
    gain_part = lax.psum_scatter(gain_terms, "fsdp", scatter_dimension=1, tiled=True)
    summed_rows = (
        lax.psum_scatter(
            rows_product(pieces[0], picked[0]).astype(jnp.bfloat16),
            "dp",
            scatter_dimension=0,
            tiled=True,
        ).astype(jnp.float32),
        lax.psum_scatter(
            rows_product(pieces[0], picked[1]).astype(jnp.bfloat16),
            "dp",
            scatter_dimension=0,
            tiled=True,
        ).astype(jnp.float32),
        lax.psum_scatter(
            rows_product(pieces[0], picked[2]).astype(jnp.bfloat16),
            "dp",
            scatter_dimension=0,
            tiled=True,
        ).astype(jnp.float32),
        lax.psum_scatter(
            rows_product(pieces[1], picked[3]).astype(jnp.bfloat16),
            "dp",
            scatter_dimension=0,
            tiled=True,
        ).astype(jnp.float32),
        lax.psum_scatter(
            rows_product(pieces[2], picked[4]).astype(jnp.bfloat16),
            "dp",
            scatter_dimension=0,
            tiled=True,
        ).astype(jnp.float32),
        lax.psum_scatter(
            rows_product(pieces[2], picked[5]).astype(jnp.bfloat16),
            "dp",
            scatter_dimension=0,
            tiled=True,
        ).astype(jnp.float32),
        lax.psum_scatter(
            rows_product(pieces[3], picked[6]).astype(jnp.bfloat16),
            "dp",
            scatter_dimension=0,
            tiled=True,
        ).astype(jnp.float32),
    )
    gain_grad = lax.psum(gain_part, "dp")
    return (
        jnp.stack(outputs, 0),
        jnp.stack(grad_inputs, 0),
        summed_rows[0],
        summed_rows[1],
        summed_rows[2],
        summed_rows[3],
        summed_rows[4],
        summed_rows[5],
        summed_rows[6],
        gain_grad,
    )


def swap_core(value):
    return lax.ppermute(value, "fsdp", [(j, j ^ 1) for j in range(8)])


def swap_dp(value, mask):
    return lax.ppermute(value, "dp", [(j, j ^ mask) for j in range(4)])


def shift_z(value, step):
    return lax.ppermute(value, "fsdp", [(j, (j + 2 * step) % 8) for j in range(8)])


def shift_z_up(value, step):
    return lax.ppermute(value, "fsdp", [(j, j + 2 * step) for j in range(8) if j + 2 * step < 8])


def shift_z_down(value, step):
    return lax.ppermute(value, "fsdp", [(j, j - 2 * step) for j in range(8) if j - 2 * step >= 0])


def add_low(*terms):
    total = terms[0].astype(jnp.float32)
    for term in terms[1:]:
        total = total + term.astype(jnp.float32)
    return total.astype(jnp.bfloat16)


def product_nn(left, right):
    return lax.dot_general(
        left, right, (((1,), (0,)), ((), ())), preferred_element_type=jnp.float32
    )


def product_nt(left, right):
    return lax.dot_general(
        left, right, (((1,), (1,)), ((), ())), preferred_element_type=jnp.float32
    )


def product_tn(left, right):
    return lax.dot_general(
        left, right, (((0,), (0,)), ((), ())), preferred_element_type=jnp.float32
    )


VMEM = pl.BlockSpec(memory_space=pltpu.VMEM)
SMEM = pl.BlockSpec(memory_space=pltpu.SMEM)
HBM = pl.BlockSpec(memory_space=pltpu.HBM)


def run(body, name, ins, in_specs, outs, out_specs, scratch, flops, megabytes):
    moved = sum(v.size * v.dtype.itemsize for v in ins)
    moved += sum(v.size * v.dtype.itemsize for v in outs)
    return pl.pallas_call(
        body,
        out_shape=tuple(outs),
        in_specs=in_specs,
        out_specs=tuple(out_specs),
        scratch_shapes=scratch,
        compiler_params=pltpu.CompilerParams(vmem_limit_bytes=megabytes * 1024 * 1024),
        cost_estimate=pl.CostEstimate(flops=flops, bytes_accessed=moved, transcendentals=0),
        name=name,
    )(*ins)


def struct(shape, dtype=jnp.bfloat16):
    return jax.ShapeDtypeStruct(shape, dtype)


def column_index(ids_ref, core_rel, s):
    return 2 * lax.rem(ids_ref[1] - s + 4, 4) + (ids_ref[2] ^ core_rel)


def start_row(index, size):
    return pl.ds(pl.multiple_of(index * size, 8), size)


def after(value, *others):
    return lax.optimization_barrier((value,) + others)[0]


def pack_first_kernel(counts_ref, wq_ref, wk_ref, wv_ref, gains_ref, out_ref):
    block = wq_ref.shape[0]
    gains = gains_ref[...].astype(jnp.float32)
    row = lax.broadcasted_iota(jnp.int32, (8, block), 0)
    lane = lax.broadcasted_iota(jnp.int32, (8, block), 1)
    first = jnp.concatenate([gains[:1], gains[1:]], 1)
    used = jnp.where(
        lane == 0,
        counts_ref[0, 0].astype(jnp.float32),
        jnp.where(lane == 1, counts_ref[1, 0].astype(jnp.float32), 0.0),
    )
    extra = jnp.where(row == 0, first, jnp.where(row == 1, used, 0.0))
    full = jnp.concatenate(
        [
            wq_ref[...].astype(jnp.float32).T,
            extra,
            wk_ref[...].astype(jnp.float32),
            wv_ref[...].astype(jnp.float32),
        ],
        0,
    )
    out_ref[...] = jnp.zeros_like(out_ref)
    out_ref[:, :block] = full.astype(jnp.bfloat16)


def pack_mlp_kernel(ids_ref, wg_ref, wu_ref, wd_ref, other_ref, wo_ref, out_ref):
    half, block = wg_ref.shape
    core = ids_ref[2]
    out_ref[...] = jnp.zeros_like(out_ref)
    out_ref[:half, :block] = wg_ref[...]
    out_ref[half : 2 * half, :block] = wu_ref[...]
    down = wd_ref[...].astype(jnp.float32)
    own = jnp.where(core == 0, down[:, :half], down[:, half:])
    other = other_ref[:, :half].astype(jnp.float32)
    low = jnp.where(core == 0, own, other)
    high = jnp.where(core == 0, other, own)
    out_ref[2 * half : 3 * half, :block] = jnp.concatenate([low, high], 0).T.astype(jnp.bfloat16)
    out_ref[3 * half :, :block] = jnp.concatenate(
        [wo_ref[...].astype(jnp.float32).T, jnp.zeros((8, block), jnp.float32)], 0
    ).astype(jnp.bfloat16)


def turn_in_kernel(x_ref, dy_ref, xt_ref, dyt_ref):
    xt_ref[...] = x_ref[...].astype(jnp.float32).T.astype(jnp.bfloat16)
    dyt_ref[...] = jnp.zeros_like(dyt_ref)
    dyt_ref[:, : dy_ref.shape[0]] = dy_ref[...].astype(jnp.float32).T.astype(jnp.bfloat16)


def fill_relative(ids_ref, target_ref, *sources):
    block, lanes = sources[0].shape[1], target_ref.shape[1]
    wide = target_ref.shape[0] // 4
    for k in range(4):
        parts = [source[ids_ref[0] ^ k] for source in sources]
        target_ref[k * wide : k * wide + block, :] = (
            parts[0] if len(parts) == 1 else jnp.concatenate(parts, 1)
        )
        target_ref[k * wide + block : (k + 1) * wide, :] = jnp.zeros(
            (wide - block, lanes), target_ref.dtype
        )


def wide_rows(refs, s, low, high):
    along, by_x, by_y, far_a, far_b = refs
    far = far_a if s < 2 else far_b
    return jnp.concatenate(
        [along[s, low:high], by_x[s, low:high], by_y[s, low:high], far[s % 2, low:high]], 1
    )


def project_kernel(*refs):
    ids_ref, own, other = refs[0], refs[1:6], refs[6:11]
    n1_ref, cos_ref, sin_ref, q_ref, kv_ref, all_ref, proj_ref, turned_ref, rel_ref = refs[11:]
    width = n1_ref.shape[0] * n1_ref.shape[1]
    kv_width = KEY_HEADS * HEAD_WIDTH
    q_cols, k_cols = width // 8, kv_width // 8
    depth = own[0].shape[1]
    fill_relative(ids_ref, rel_ref, n1_ref)
    for core_rel, weights in ((0, own), (1, other)):
        for s in range(4):
            f = column_index(ids_ref, core_rel, s)
            all_ref[core_rel * 4 + s] = wide_rows(weights, s, 0, depth)
            total = product_nn(all_ref[core_rel * 4 + s], rel_ref[...])
            proj_ref[start_row(f, q_cols), :] = total[:q_cols]
            proj_ref[pl.ds(pl.multiple_of(width + f * k_cols, 8), k_cols), :] = total[
                q_cols + 8 : q_cols + 8 + k_cols
            ]
            proj_ref[pl.ds(pl.multiple_of(width + kv_width + f * k_cols, 8), k_cols), :] = total[
                q_cols + 8 + k_cols :
            ]
    cosine, sine = cos_ref[...], sin_ref[...]
    half = HEAD_WIDTH // 2

    def heads(head, carry):
        front = proj_ref[pl.ds(pl.multiple_of(head * HEAD_WIDTH, 8), half), :]
        back = proj_ref[pl.ds(pl.multiple_of(head * HEAD_WIDTH + half, 8), half), :]
        q_ref[head, :half, :] = (
            (front * cosine - back * sine).astype(jnp.bfloat16) * SCORE_SCALE
        ).astype(jnp.bfloat16)
        q_ref[head, half:, :] = (
            (back * cosine + front * sine).astype(jnp.bfloat16) * SCORE_SCALE
        ).astype(jnp.bfloat16)
        return carry

    lax.fori_loop(0, QUERY_HEADS, heads, 0)
    for head in range(KEY_HEADS):
        base = width + head * HEAD_WIDTH
        front = proj_ref[base : base + half, :]
        back = proj_ref[base + half : base + 2 * half, :]
        turned_ref[head * HEAD_WIDTH : head * HEAD_WIDTH + half, :] = front * cosine - back * sine
        turned_ref[head * HEAD_WIDTH + half : (head + 1) * HEAD_WIDTH, :] = (
            back * cosine + front * sine
        )
    turned_ref[kv_width:, :] = proj_ref[width + kv_width :, :]
    kv_ref[...] = turned_ref[...].T.astype(jnp.bfloat16)


def stage_heads(mb, cap, blocks, k_ref, v_ref):
    kv_width = KEY_HEADS * HEAD_WIDTH
    for block, source in enumerate(blocks):
        rows = source[mb * cap : (mb + 1) * cap, :]
        for n in range(KEY_HEADS):
            lanes = n * HEAD_WIDTH
            k_ref[n, block * cap : (block + 1) * cap, :] = rows[:, lanes : lanes + HEAD_WIDTH]
            lanes += kv_width
            v_ref[n, block * cap : (block + 1) * cap, :] = rows[:, lanes : lanes + HEAD_WIDTH]


def stage_bias(ids_ref, counts_ref, mb, cap, share, bias_ref):
    slot = ids_ref[3]
    own_count = counts_ref[mb * 8 + slot]
    key = lax.broadcasted_iota(jnp.int32, (cap, cap), 0)
    query = lax.broadcasted_iota(jnp.int32, (cap, cap), 1)
    query_used = query < own_count
    for core_rel in range(2):
        for s in range(4):
            block = core_rel * 4 + s
            f = column_index(ids_ref, core_rel, s)
            count = counts_ref[mb * 8 + f]
            reach = jnp.where(f < slot, cap, jnp.where(f == slot, 0, -2 * cap))
            self_off = jnp.where(f == slot, 0, 2 * cap)
            allowed = (query_used & (key < count) & (key <= query + reach)) | (
                key == query + self_off
            )
            tile = jnp.where(allowed, 0.0, -1e30)
            for g in range(share):
                bias_ref[block * cap : (block + 1) * cap, g * cap : (g + 1) * cap] = tile


def join_heads(ref, n, share, mb, cap):
    return jnp.concatenate(
        [ref[share * n + g, :, mb * cap : (mb + 1) * cap] for g in range(share)], 1
    )


def attend_kernel(mb, *refs):
    ids_ref, counts_ref, q_ref = refs[:3]
    blocks = refs[3:11]
    att_ref, lse_ref, k_ref, v_ref, bias_ref = refs[11:]
    cap = q_ref.shape[2] // 2
    share = QUERY_HEADS // KEY_HEADS
    stage_heads(mb, cap, blocks, k_ref, v_ref)
    stage_bias(ids_ref, counts_ref, mb, cap, share, bias_ref)

    def body(n, carry):
        scores = product_nn(k_ref[n], join_heads(q_ref, n, share, mb, cap)) + bias_ref[...]
        top = jnp.max(scores, 0, keepdims=True)
        exponent = jnp.exp(scores - top)
        total = jnp.sum(exponent, 0, keepdims=True)
        mixed = product_tn(v_ref[n], exponent.astype(jnp.bfloat16)) / total
        mixed = mixed.astype(jnp.bfloat16)
        for g in range(share):
            att_ref[share * n + g] = mixed[:, g * cap : (g + 1) * cap]
        lse_ref[n] = top + jnp.log(total)
        return carry

    lax.fori_loop(0, KEY_HEADS, body, 0)


def attend_back_kernel(mb, *refs):
    ids_ref, counts_ref, q_ref, do_ref, k_ref, v_ref, lse_ref, cos_ref, sin_ref = refs[:9]
    dq_ref = refs[9]
    targets = [ref.at[s] for ref in refs[10:12] for s in range(4)]
    bias_ref, dk_ref, dv_ref = refs[12:]
    cap = q_ref.shape[2] // 2
    share = QUERY_HEADS // KEY_HEADS
    half = HEAD_WIDTH // 2
    kv_width = KEY_HEADS * HEAD_WIDTH
    stage_bias(ids_ref, counts_ref, mb, cap, share, bias_ref)
    cosine = jnp.concatenate([cos_ref[:, mb * cap : (mb + 1) * cap]] * share, 1)
    sine = jnp.concatenate([sin_ref[:, mb * cap : (mb + 1) * cap]] * share, 1)

    def body(n, carry):
        query = join_heads(q_ref, n, share, mb, cap)
        grad = join_heads(do_ref, n, share, mb, cap)
        keys = k_ref[n]
        prob = jnp.exp(product_nn(keys, query) + bias_ref[...] - lse_ref[n])
        dprob = product_nn(v_ref[n], grad)
        delta = jnp.sum(prob * dprob, 0, keepdims=True)
        dscore = (prob * (dprob - delta)).astype(jnp.bfloat16)
        dq = product_tn(keys, dscore) * SCORE_SCALE
        front, back = dq[:half], dq[half:]
        turned = jnp.concatenate(
            [front * cosine + back * sine, back * cosine - front * sine], 0
        ).astype(jnp.bfloat16)
        for g in range(share):
            dq_ref[share * n + g] = turned[:, g * cap : (g + 1) * cap]
        dk_ref[n] = product_nt(dscore, query).astype(jnp.bfloat16)
        dv_ref[n] = product_nt(prob.astype(jnp.bfloat16), grad).astype(jnp.bfloat16)
        return carry

    lax.fori_loop(0, KEY_HEADS, body, 0)
    for block, target in enumerate(targets):
        for n in range(KEY_HEADS):
            lanes = n * HEAD_WIDTH
            target[:, lanes : lanes + HEAD_WIDTH] = dk_ref[n, block * cap : (block + 1) * cap, :]
            lanes += kv_width
            target[:, lanes : lanes + HEAD_WIDTH] = dv_ref[n, block * cap : (block + 1) * cap, :]


def collect_kernel(*refs):
    pieces, out_ref, sem = refs[:16], refs[16], refs[17]
    rows, wide = out_ref.shape[1], pieces[0].shape[1]
    copies = []
    for k in range(4):
        for s in range(4):
            copies.append(
                pltpu.make_async_copy(
                    pieces[k * 4 + s].at[pl.ds(pieces[0].shape[0] - rows, rows)],
                    out_ref.at[s, :, pl.ds(k * wide, wide)],
                    sem.at[k * 4 + s],
                )
            )
    for copy in copies:
        copy.start()
    for copy in copies:
        copy.wait()


def hidden_kernel(
    ids_ref, own_ref, other_ref, att_a_ref, att_b_ref, x_ref, gain_ref, h_ref, n2_ref, rel_ref
):
    q_cols, rows = h_ref.shape[0] // 8, h_ref.shape[1]
    fill_relative(ids_ref, rel_ref, att_a_ref, att_b_ref)
    for core_rel, w_ref in ((0, own_ref), (1, other_ref)):
        for s in range(4):
            f = column_index(ids_ref, core_rel, s)
            h_ref[start_row(f, q_cols), :] = product_nn(w_ref[s], rel_ref[...])[:q_cols]
    h = h_ref[...] + x_ref[...].astype(jnp.float32)
    h_ref[...] = h
    n2_ref[...] = jnp.zeros_like(n2_ref)
    n2_ref[:, :rows] = (h * mean_square(h) * gain_ref[...]).astype(jnp.bfloat16)


def turn_point_kernel(
    ids_ref,
    parts_ref,
    arrived_ref,
    h_ref,
    dy_ref,
    gain_ref,
    own_ref,
    other_ref,
    out_ref,
    dh_ref,
    do_ref,
    gain_grad_ref,
    pieces_ref,
    da_ref,
):
    width, rows = h_ref.shape
    q_cols = width // 8
    block = do_ref.shape[1]
    wide = own_ref.shape[2] // 4
    h = h_ref[...]
    out_ref[...] = (h + parts_ref[0] + arrived_ref[0, :, :rows].astype(jnp.float32)).astype(
        jnp.bfloat16
    )
    dn = parts_ref[1] + arrived_ref[1, :, :rows].astype(jnp.float32)
    rms = mean_square(h)
    gain_grad_ref[...] = jnp.sum(dn * h * rms, 1, keepdims=True)
    weighted = dn * gain_ref[...]
    dh = (
        dy_ref[:, :rows].astype(jnp.float32)
        + rms * weighted
        - h * (rms * rms * rms * jnp.mean(weighted * h, 0, keepdims=True))
    )
    dh_ref[...] = dh
    da_ref[...] = dh
    spread(ids_ref, da_ref, pieces_ref, q_cols)
    half = pieces_ref.shape[0] // 2
    mixed = product_tn(own_ref[...].reshape(half, 4 * wide), pieces_ref[:half, :])
    mixed += product_tn(other_ref[...].reshape(half, 4 * wide), pieces_ref[half:, :])
    mixed = mixed.astype(jnp.bfloat16)
    for k in range(4):
        do_ref[ids_ref[0] ^ k] = mixed[k * wide : k * wide + block]


def spread(ids_ref, source_ref, target_ref, cols):
    rows = source_ref.shape[1]
    for core_rel in range(2):
        for s in range(4):
            f = column_index(ids_ref, core_rel, s)
            low = (core_rel * 4 + s) * (cols + 8)
            target_ref[low : low + cols + 8, :] = jnp.concatenate(
                [source_ref[start_row(f, cols), :], jnp.zeros((8, rows), jnp.float32)], 0
            ).astype(jnp.bfloat16)


def targets_of(refs):
    return list(refs[:4]) + [refs[4].at[pl.ds(4 * k, 4)] for k in range(4)]


def out_grad_kernel(ids_ref, att_a_ref, att_b_ref, pieces_ref, *refs):
    grads, att_rel = targets_of(refs[:5]), refs[5]
    depth = pieces_ref.shape[0] // 8
    wide = att_rel.shape[0] // 4
    fill_relative(ids_ref, att_rel, att_a_ref, att_b_ref)
    for core_rel in range(2):
        for s in range(4):
            low = (core_rel * 4 + s) * depth
            got = product_nt(pieces_ref[low : low + depth, :], att_rel[...]).astype(jnp.bfloat16)
            for k in range(4):
                grads[core_rel * 4 + k][s] = got[:, k * wide : (k + 1) * wide]


def finish_q_kernel(*refs):
    ids_ref, all_ref, n1_ref, dq_a_ref, dq_b_ref = refs[:5]
    out_grads = targets_of(refs[5:10])
    dn_ref, grads = refs[10], targets_of(refs[11:16])
    n1_rel, d_ref, dq_ref = refs[16:]
    cap = dq_a_ref.shape[1]
    width = dq_a_ref.shape[0]
    q_cols = width // 8
    depth = q_cols + 8
    block = n1_ref.shape[1]
    wide = n1_rel.shape[0] // 4
    d_ref[:, :cap] = dq_a_ref[...].astype(jnp.float32)
    d_ref[:, cap:] = dq_b_ref[...].astype(jnp.float32)
    spread(ids_ref, d_ref, dq_ref, q_cols)
    fill_relative(ids_ref, n1_rel, n1_ref)
    weights = jnp.concatenate([all_ref[j, :depth, :] for j in range(8)], 0)
    dn = product_tn(weights, dq_ref[...])
    for k in range(4):
        dn_ref[ids_ref[0] ^ k] = dn[k * wide : k * wide + block]
    for core_rel in range(2):
        for s in range(4):
            low = (core_rel * 4 + s) * depth
            gq = product_nt(dq_ref[low : low + depth, :], n1_rel[...]).astype(jnp.bfloat16)
            for k in range(4):
                target = grads[core_rel * 4 + k]
                target[s, :depth, :] = gq[:, k * wide : (k + 1) * wide]
                target[s, depth:, :] = out_grads[core_rel * 4 + k][s]


def kv_grad_kernel(
    ids_ref, n1_ref, dkv_a_ref, dkv_b_ref, cos_ref, sin_ref, dkv_ref, *refs
):
    grads = targets_of(refs[:5])
    n1_rel, d_ref = refs[5:]
    cap = dkv_a_ref.shape[0]
    kv_width = KEY_HEADS * HEAD_WIDTH
    k_cols = kv_width // 8
    half = HEAD_WIDTH // 2
    wide = n1_rel.shape[0] // 4
    cosine, sine = cos_ref[...], sin_ref[...]
    d_ref[:, :cap] = dkv_a_ref[...].T
    d_ref[:, cap:] = dkv_b_ref[...].T
    for head in range(KEY_HEADS):
        base = head * HEAD_WIDTH
        front = d_ref[base : base + half, :]
        back = d_ref[base + half : base + 2 * half, :]
        d_ref[base : base + half, :] = front * cosine + back * sine
        d_ref[base + half : base + 2 * half, :] = back * cosine - front * sine
    for core_rel in range(2):
        for s in range(4):
            f = column_index(ids_ref, core_rel, s)
            low = (core_rel * 4 + s) * 2 * k_cols
            dkv_ref[low : low + 2 * k_cols, :] = jnp.concatenate(
                [
                    d_ref[start_row(f, k_cols), :],
                    d_ref[pl.ds(pl.multiple_of(kv_width + f * k_cols, 8), k_cols), :],
                ],
                0,
            ).astype(jnp.bfloat16)
    fill_relative(ids_ref, n1_rel, n1_ref)
    for core_rel in range(2):
        for s in range(4):
            low = (core_rel * 4 + s) * 2 * k_cols
            got = product_nt(dkv_ref[low : low + 2 * k_cols, :], n1_rel[...]).astype(jnp.bfloat16)
            for k in range(4):
                grads[core_rel * 4 + k][s] = got[:, k * wide : (k + 1) * wide]


def finish_kernel(*refs):
    ids_ref, all_ref, dkv_ref, dn_ref, dh_ref, x_ref, gain_ref = refs[:7]
    tokens_ref, gain_grad_ref = refs[7:]
    width = dh_ref.shape[0]
    block = dn_ref.shape[1]
    kv_rows = dkv_ref.shape[0] // 8
    low = all_ref.shape[1] - kv_rows
    wide = all_ref.shape[2] // 4
    weights = jnp.concatenate([all_ref[j, low:, :] for j in range(8)], 0)
    dn = product_tn(weights, dkv_ref[...])
    for k in range(4):
        i = ids_ref[0] ^ k
        tokens_ref[pl.ds(pl.multiple_of(i * block, 16), block), :] = (
            dn[k * wide : k * wide + block] + dn_ref[i]
        )
    x = x_ref[...].astype(jnp.float32)
    rms = mean_square(x)
    dn = tokens_ref[...]
    gain_grad_ref[...] = jnp.sum(dn * x * rms, 1, keepdims=True)
    weighted = dn * gain_ref[...]
    tokens_ref[...] = (
        dh_ref[...]
        + rms * weighted
        - x * (rms * rms * rms * jnp.mean(weighted * x, 0, keepdims=True))
    )


def mlp_kernel(*refs):
    ids_ref, n2_own, n2_other, dy_own, dy_other = refs[:5]
    pieces = refs[5:21]
    keep_ref, send_ref = refs[21:23]
    grads = refs[23:39]
    wgu, wdn, gu_ref, prod_ref, dgu_ref, n2_rel, dy_rel, sem_in, sem_out = refs[39:]
    dp_id = ids_ref[0]
    z_id = ids_ref[1]
    block, rows = keep_ref.shape[1] // 4, keep_ref.shape[2]
    pair = 2 * rows
    wide = pieces[0].shape[1]
    half = prod_ref.shape[0] // 4

    def gate_up_part(ref, piece, k, s):
        return piece.at[pl.ds(0, 2 * half)], ref.at[
            pl.ds(s * 2 * half, 2 * half), pl.ds(k * wide, wide)
        ]

    def down_part(ref, piece, k, s):
        return piece.at[pl.ds(2 * half, half)], ref.at[
            pl.ds(k * half, half), pl.ds(s * wide, wide)
        ]

    loads, more_loads = [], []
    for s in range(4):
        for k in range(4):
            source, target = gate_up_part(wgu, pieces[k * 4 + s], k, s)
            loads.append(pltpu.make_async_copy(source, target, sem_in.at[0, k * 4 + s]))
            source, target = down_part(wdn, pieces[k * 4 + s], k, s)
            more_loads.append(pltpu.make_async_copy(source, target, sem_in.at[1, k * 4 + s]))
    for load in loads + more_loads:
        load.start()
    pad = jnp.zeros((wide - block, pair), jnp.bfloat16)
    for j in range(4):
        i = dp_id ^ j
        zz = lax.rem(z_id - j + 4, 4)
        n2_rel[j * wide : j * wide + block, :] = jnp.concatenate(
            [n2_own[i][:, :rows], n2_other[i][:, :rows]], 1
        )
        dy_rel[j * wide : j * wide + block, :] = jnp.concatenate(
            [dy_own[zz][:, :rows], dy_other[zz][:, :rows]], 1
        )
        n2_rel[j * wide + block : (j + 1) * wide, :] = pad
        dy_rel[j * wide + block : (j + 1) * wide, :] = pad

    def rows_of(index, size):
        return pl.ds(pl.multiple_of(index * size, 16), size)

    for s in range(4):
        for load in loads[4 * s : 4 * s + 4]:
            load.wait()
        k = lax.rem(z_id - s + 4, 4) ^ dp_id
        total = product_nn(wgu[s * 2 * half : (s + 1) * 2 * half, :], n2_rel[...])
        gu_ref[rows_of(k, 2 * half), :] = total
        gate = total[:half]
        prod_ref[rows_of(k, half), :] = (gate * jax.nn.sigmoid(gate) * total[half:]).astype(
            jnp.bfloat16
        )
    for load in more_loads:
        load.wait()
    for k in range(4):
        s = lax.rem(z_id - (dp_id ^ k) + 4, 4)
        dprod = product_nn(wdn[k * half : (k + 1) * half, :], dy_rel[...])
        gate = gu_ref[k * 2 * half : k * 2 * half + half, :]
        up = gu_ref[k * 2 * half + half : (k + 1) * 2 * half, :]
        sig = jax.nn.sigmoid(gate)
        dgu_ref[rows_of(s, 2 * half), :] = jnp.concatenate(
            [dprod * up * sig * (1.0 + gate * (1.0 - sig)), dprod * gate * sig], 0
        ).astype(jnp.bfloat16)
    for j in range(4):
        lanes = slice(j * wide, (j + 1) * wide)
        out = product_tn(wdn[:, lanes], prod_ref[...])[:block]
        zz = rows_of(lax.rem(z_id - j + 4, 4), block)
        keep_ref[0, zz, :] = out[:, :rows]
        send_ref[0, zz, :rows] = out[:, rows:].astype(jnp.bfloat16)
    for k in range(4):
        here = slice(k * half, (k + 1) * half)
        wdn[here, :] = product_nt(prod_ref[here, :], dy_rel[...]).astype(jnp.bfloat16)
    stores = []
    for k in range(4):
        for s in range(4):
            target, source = down_part(wdn, grads[k * 4 + s], k, s)
            stores.append(pltpu.make_async_copy(source, target, sem_out.at[1, k * 4 + s]))
    for store in stores:
        store.start()
    for j in range(4):
        lanes = slice(j * wide, (j + 1) * wide)
        dn = product_tn(wgu[:, lanes], dgu_ref[...])[:block]
        i = rows_of(dp_id ^ j, block)
        keep_ref[1, i, :] = dn[:, :rows]
        send_ref[1, i, :rows] = dn[:, rows:].astype(jnp.bfloat16)
    send_ref[:, :, rows:] = jnp.zeros((2, 4 * block, send_ref.shape[2] - rows), jnp.bfloat16)
    for s in range(4):
        here = slice(s * 2 * half, (s + 1) * 2 * half)
        wgu[here, :] = product_nt(dgu_ref[here, :], n2_rel[...]).astype(jnp.bfloat16)
        for k in range(4):
            target, source = gate_up_part(wgu, grads[k * 4 + s], k, s)
            store = pltpu.make_async_copy(source, target, sem_out.at[0, k * 4 + s])
            store.start()
            stores.append(store)
    for store in stores:
        store.wait()


def mean_square(values):
    return lax.rsqrt(jnp.mean(values * values, 0, keepdims=True) + EPSILON)


def fast(
    tokens, cotangent, counts, w_query, key_weight, value_weight, w_out, w_gate, w_up, w_down, gains
):
    dp_id = lax.axis_index("dp")
    slot = lax.axis_index("fsdp")
    z_id = slot // 2
    core_id = slot % 2
    ids = jnp.stack([dp_id, z_id, core_id, slot]).astype(jnp.int32)
    batches, cap, width = tokens.shape
    rows = batches * cap
    block = w_query.shape[0]
    wide = -(-block // 128) * 128
    q_cols, k_cols = w_query.shape[1], key_weight.shape[1]
    half = w_gate.shape[1]
    kv_width = KEY_HEADS * HEAD_WIDTH
    share = QUERY_HEADS // KEY_HEADS
    q_rows = q_cols + 8
    depth = q_rows + 2 * k_cols
    mlp_rows = 3 * half + q_rows
    padded = -(-rows // 128) * 128

    (first_piece,) = run(
        pack_first_kernel,
        "pack_first",
        (counts, w_query, key_weight.T, value_weight.T, gains),
        [SMEM] + [VMEM] * 4,
        [struct((depth, wide))],
        [VMEM],
        [],
        0,
        16,
    )
    chain = [first_piece] + [shift_z(first_piece, step) for step in (1, 2, 3)]
    down = w_down.T
    give = jnp.where(core_id == 0, down[:, half:], down[:, :half])
    other_down = swap_core(jnp.pad(give, ((0, 0), (0, -half % 128))))
    (mlp_piece,) = run(
        pack_mlp_kernel,
        "pack_mlp",
        (ids, w_gate.T, w_up.T, down, other_down, w_out),
        [SMEM] + [VMEM] * 5,
        [struct((mlp_rows, wide))],
        [VMEM],
        [],
        0,
        16,
    )
    x, dy = run(
        turn_in_kernel,
        "turn_in",
        (tokens.reshape(rows, width), cotangent.reshape(rows, width)),
        [VMEM] * 2,
        [struct((width, rows)), struct((width, padded))],
        [VMEM] * 2,
        [],
        0,
        16,
    )

    along = jnp.stack(chain, 0)
    extras = along[:, q_cols : q_cols + 2, :block]
    other_extras = swap_core(extras)
    from_x = swap_dp(along, 1)
    from_y = swap_dp(along, 2)
    first_own = [along, from_x, from_y, swap_dp(from_x[:2], 2), swap_dp(from_y[2:], 1)]
    first_other = [swap_core(piece) for piece in first_own]

    z_one = shift_z(after(mlp_piece, along), 1)
    z_two = shift_z(z_one, 1)
    z_three = shift_z(z_two, 1)
    mlp_next = after(mlp_piece, *first_own[3:])
    x_zero, y_zero = swap_dp(mlp_next, 1), swap_dp(mlp_next, 2)

    by_core = jnp.where(
        core_id == 0, jnp.stack([extras, other_extras], 1), jnp.stack([other_extras, extras], 1)
    )
    by_core = by_core[::-1]
    by_core = lax.dynamic_slice_in_dim(jnp.concatenate([by_core, by_core], 0), 3 - z_id, 4, 0)
    gain = by_core[:, :, 0, :].reshape(8, 2, q_cols).transpose(0, 2, 1).reshape(width, 2)
    gain = gain.astype(jnp.float32)
    gain_one, gain_two = gain[:, :1], gain[:, 1:]
    group_counts = by_core[:, :, 1, :batches].reshape(8, batches).astype(jnp.int32)
    flat_counts = group_counts.T.reshape(-1)
    before = jnp.sum(
        jnp.where(jnp.arange(8, dtype=jnp.int32)[:, None] < slot, group_counts, 0), 0
    )
    position = (before[:, None] + jnp.arange(cap, dtype=jnp.int32)[None, :]).reshape(-1)
    cosine, sine = rope_tables(position, HEAD_WIDTH)
    cosine, sine = cosine[:, 0, :].T, sine[:, 0, :].T
    x_wide = x.astype(jnp.float32)
    n1 = (x_wide * mean_square(x_wide) * gain_one).astype(jnp.bfloat16).reshape(4, block, rows)
    n1_next = after(n1, z_two, flat_counts, gain_one, gain_two)

    query, kv, first_all = run(
        project_kernel,
        "project",
        (ids, *first_own, *first_other, n1_next, cosine, sine),
        [SMEM] + [VMEM] * 13,
        (
            struct((QUERY_HEADS, HEAD_WIDTH, rows)),
            struct((rows, 2 * kv_width)),
            struct((8, depth, 4 * wide)),
        ),
        [VMEM] * 3,
        [
            pltpu.VMEM((width + 2 * kv_width, rows), jnp.float32),
            pltpu.VMEM((2 * kv_width, rows), jnp.float32),
            pltpu.VMEM((4 * wide, rows), jnp.bfloat16),
        ],
        2 * (width + 2 * kv_width) * width * rows,
        20,
    )
    kv_zero = after(kv, x_zero, y_zero)
    kv_one = shift_z_up(kv_zero, 1)
    x_one = swap_dp(after(z_one, kv_zero), 1)
    far_zero = swap_dp(after(x_zero, kv_zero), 2)
    wave = (kv_one, x_one, far_zero, z_three)
    kv_two = shift_z_up(after(*wave), 1)
    x_two = swap_dp(after(z_two, *wave), 1)
    y_one = swap_dp(after(z_one, *wave), 2)
    wave = (kv_two, x_two, y_one)
    kv_three = shift_z_up(after(*wave), 1)
    far_one = swap_dp(after(y_one, *wave), 1)
    y_two = swap_dp(after(z_two, *wave), 2)
    wave = (kv_three, far_one, y_two)
    x_three = swap_dp(after(z_three, *wave), 1)
    y_three = swap_dp(after(z_three, *wave), 2)
    kv_own = [kv, kv_one, kv_two, kv_three]
    kv_other = [swap_core(piece) for piece in (kv_zero, kv_one, kv_two, kv_three)]
    pair_flops = 2 * QUERY_HEADS * HEAD_WIDTH * rows * 8 * cap
    bias_scratch = pltpu.VMEM((8 * cap, share * cap), jnp.float32)
    def attend(mb, queries):
        return run(
            functools.partial(attend_kernel, mb),
            "attend",
            (ids, flat_counts, queries, *kv_own, *kv_other),
            [SMEM, SMEM] + [VMEM] * 9,
            (
                struct((QUERY_HEADS, HEAD_WIDTH, cap)),
                struct((KEY_HEADS, 1, share * cap), jnp.float32),
                struct((KEY_HEADS, 8 * cap, HEAD_WIDTH)),
                struct((KEY_HEADS, 8 * cap, HEAD_WIDTH)),
            ),
            [VMEM] * 4,
            [bias_scratch],
            4 * pair_flops,
            20,
        )

    att_a, lse_a, *heads_a = attend(0, after(query, far_one, y_two))
    wave = (att_a, x_three, y_three)
    far_two = swap_dp(after(x_two, *wave), 2)
    far_three = swap_dp(after(y_three, *wave), 1)
    dy_other = swap_core(after(dy, att_a))
    att_b, lse_b, *heads_b = attend(1, after(query, *wave))
    pieces = [mlp_piece, z_one, z_two, z_three]
    pieces += [x_zero, x_one, x_two, x_three]
    pieces += [y_zero, y_one, y_two, y_three]
    pieces += [far_zero, far_one, far_two, far_three]
    (out_own,) = run(
        collect_kernel,
        "collect",
        tuple(pieces[:15]) + (after(far_three, att_b),),
        [HBM] * 16,
        [struct((4, q_rows, 4 * wide))],
        [VMEM],
        [pltpu.SemaphoreType.DMA((16,))],
        0,
        8,
    )
    out_other = swap_core(out_own)
    att_a = att_a.reshape(4, block, cap)
    att_b = att_b.reshape(4, block, cap)
    lse = (lse_a, lse_b)
    blocks = (4, block, rows)
    wide_blocks = (4, block, padded)
    h, n2 = run(
        hidden_kernel,
        "hidden",
        (ids, out_own, out_other, att_a, att_b, after(x, dy_other), gain_two),
        [SMEM] + [VMEM] * 6,
        (struct((width, rows), jnp.float32), struct((width, padded))),
        [VMEM] * 2,
        [pltpu.VMEM((4 * wide, rows), jnp.bfloat16)],
        2 * width * width * rows,
        16,
    )
    n2_other = swap_core(n2)
    results = run(
        mlp_kernel,
        "mlp",
        (
            ids,
            n2.reshape(wide_blocks),
            n2_other.reshape(wide_blocks),
            dy.reshape(wide_blocks),
            dy_other.reshape(wide_blocks),
            *pieces,
        ),
        [SMEM] + [VMEM] * 4 + [HBM] * 16,
        [struct((2, width, rows), jnp.float32), struct((2, width, padded))]
        + [struct((3 * half, wide))] * 16,
        [VMEM] * 2 + [HBM] * 16,
        [
            pltpu.VMEM((8 * half, 4 * wide), jnp.bfloat16),
            pltpu.VMEM((4 * half, 4 * wide), jnp.bfloat16),
            pltpu.VMEM((8 * half, 2 * rows), jnp.float32),
            pltpu.VMEM((4 * half, 2 * rows), jnp.bfloat16),
            pltpu.VMEM((8 * half, 2 * rows), jnp.bfloat16),
            pltpu.VMEM((4 * wide, 2 * rows), jnp.bfloat16),
            pltpu.VMEM((4 * wide, 2 * rows), jnp.bfloat16),
            pltpu.SemaphoreType.DMA((2, 16)),
            pltpu.SemaphoreType.DMA((2, 16)),
        ],
        18 * 16 * half * block * 2 * rows,
        56,
    )
    keep, send = results[:2]
    home, to_x, to_y, far = results[2:6], results[6:10], results[10:14], results[14:18]
    arrived = swap_core(send)
    via_three, via_two = swap_dp(far[3], 1), swap_dp(far[2], 2)

    output, dh, mixed_gradient, gain_two_grad, da_pieces = run(
        turn_point_kernel,
        "turn_point",
        (ids, keep, arrived, h, dy, gain_two, out_own, out_other),
        [SMEM] + [VMEM] * 7,
        (
            struct((width, rows)),
            struct((width, rows), jnp.float32),
            struct(blocks),
            struct((width, 1), jnp.float32),
            struct((8 * q_rows, rows)),
        ),
        [VMEM] * 5,
        [pltpu.VMEM((width, rows), jnp.float32)],
        2 * width * width * rows,
        22,
    )
    output = output.T.reshape(batches, cap, width)
    def attend_back(mb, mixed):
        return run(
            functools.partial(attend_back_kernel, mb),
            "attend_back",
            (
                ids,
                flat_counts,
                query,
                mixed.reshape(QUERY_HEADS, HEAD_WIDTH, rows),
                *(heads_a, heads_b)[mb],
                lse[mb],
                cosine,
                sine,
            ),
            [SMEM, SMEM] + [VMEM] * 7,
            [struct((QUERY_HEADS, HEAD_WIDTH, cap))] + [struct((4, cap, 2 * kv_width))] * 2,
            [VMEM] * 3,
            [
                bias_scratch,
                pltpu.VMEM((KEY_HEADS, 8 * cap, HEAD_WIDTH), jnp.bfloat16),
                pltpu.VMEM((KEY_HEADS, 8 * cap, HEAD_WIDTH), jnp.bfloat16),
            ],
            10 * pair_flops,
            24,
        )

    def sum_cores(own, other):
        arrived = swap_core(other)
        return [add_low(own[s], arrived[s]) for s in range(4)]

    def sum_z(summed):
        total = summed[0].astype(jnp.float32)
        for s in (3, 2, 1):
            total = total + shift_z_down(summed[s], s).astype(jnp.float32)
        return total

    wave = (via_three, via_two, mixed_gradient)
    x_three, y_two = swap_dp(after(to_x[3], *wave), 1), swap_dp(after(to_y[2], *wave), 2)
    x_two = swap_dp(add_low(to_x[2], after(via_two, *wave)), 1)
    y_three = swap_dp(add_low(to_y[3], after(via_three, *wave)), 2)
    back_a = attend_back(0, after(mixed_gradient, *wave))
    wave = (back_a[0], x_three, y_two, x_two, y_three)
    via_one, via_zero = swap_dp(after(far[1], *wave), 1), swap_dp(after(far[0], *wave), 2)
    hop = shift_z(add_low(after(home[3], back_a[0]), x_three, y_three), -1)
    out_grads = run(
        out_grad_kernel,
        "out_grad",
        (ids, att_a, att_b, after(da_pieces, *wave)),
        [SMEM] + [VMEM] * 3,
        [struct((4, q_rows, wide))] * 4 + [struct((16, q_rows, wide))],
        [VMEM] * 5,
        [pltpu.VMEM((4 * wide, rows), jnp.bfloat16)],
        2 * width * width * rows,
        14,
    )
    summed_a = sum_cores(*back_a[1:])
    wave = (via_one, via_zero, hop, out_grads[0])
    dkv_a = sum_z([after(piece, *wave) for piece in summed_a])
    x_one, y_zero = swap_dp(after(to_x[1], *wave), 1), swap_dp(after(to_y[0], *wave), 2)
    back_b = attend_back(1, after(mixed_gradient, *summed_a, *wave))
    wave = (back_b[0], dkv_a, x_one, y_zero)
    x_zero = swap_dp(add_low(to_x[0], after(via_zero, *wave)), 1)
    y_one = swap_dp(add_low(to_y[1], after(via_one, *wave)), 2)
    summed_b = sum_cores(back_b[1], after(back_b[2], dkv_a, x_one, y_zero))
    parts_b = [shift_z_down(summed_b[s], s) for s in (1, 2, 3)]

    def sum_pair(parts):
        arrived = swap_core(parts[4])
        return [add_low(parts[k], arrived[4 * k : 4 * k + 4]) for k in range(4)]

    def share_square(mine):
        return [mine[0]] + [swap_dp(mine[k], k) for k in (1, 2, 3)]

    def reduce_all(summed):
        out = [add_low(*[piece[s] for piece in summed]) for s in range(4)]
        total = out[0].astype(jnp.float32)
        for s in (1, 2, 3):
            total = total + shift_z(out[s], -s).astype(jnp.float32)
        return total

    q_results = run(
        finish_q_kernel,
        "finish_q",
        (
            ids,
            first_all,
            after(n1, *wave, *summed_b),
            back_a[0].reshape(width, cap),
            back_b[0].reshape(width, cap),
            *out_grads,
        ),
        [SMEM] + [VMEM] * 9,
        [struct(blocks, jnp.float32)]
        + [struct((4, 2 * q_rows, wide))] * 4
        + [struct((16, 2 * q_rows, wide))],
        [VMEM] * 6,
        [
            pltpu.VMEM((4 * wide, rows), jnp.bfloat16),
            pltpu.VMEM((width, rows), jnp.float32),
            pltpu.VMEM((8 * q_rows, rows), jnp.bfloat16),
        ],
        4 * width * width * rows,
        22,
    )
    dn_q = q_results[0]
    dkv_b = after(summed_b[0], dn_q).astype(jnp.float32)
    for part in parts_b:
        dkv_b = dkv_b + part.astype(jnp.float32)
    hop = shift_z(add_low(home[2], x_two, y_two, after(hop, dkv_b)), -1)
    q_out_mine = sum_pair(q_results[1:])
    q_out_shared = share_square(q_out_mine)
    q_out_total = reduce_all(q_out_shared)
    grad_query = q_out_total[:q_cols, :block].T
    grad_out = q_out_total[q_rows : q_rows + q_cols, :block].T

    dkv_pieces, *kv_grads = run(
        kv_grad_kernel,
        "kv_grad",
        (ids, after(n1, x_zero, y_one, *q_out_mine), dkv_a, dkv_b, cosine, sine),
        [SMEM] + [VMEM] * 5,
        [struct((16 * k_cols, rows))]
        + [struct((4, 2 * k_cols, wide))] * 4
        + [struct((16, 2 * k_cols, wide))],
        [VMEM] * 6,
        [
            pltpu.VMEM((4 * wide, rows), jnp.bfloat16),
            pltpu.VMEM((2 * kv_width, rows), jnp.float32),
        ],
        4 * kv_width * width * rows,
        14,
    )
    grad_tokens, gain_one_grad = run(
        finish_kernel,
        "finish",
        (ids, first_all, dkv_pieces, dn_q, dh, after(x, *q_out_shared), gain_one),
        [SMEM] + [VMEM] * 6,
        [struct((width, rows), jnp.float32), struct((width, 1), jnp.float32)],
        [VMEM] * 2,
        [],
        4 * kv_width * width * rows,
        20,
    )
    grad_tokens = grad_tokens.T.reshape(batches, cap, width)
    kv_mine = sum_pair(kv_grads)
    hop = shift_z(add_low(home[1], x_one, y_one, after(hop, gain_one_grad)), -1)
    mlp_total = (
        home[0].astype(jnp.float32)
        + y_zero.astype(jnp.float32)
        + x_zero.astype(jnp.float32)
        + hop.astype(jnp.float32)
    )
    grad_gate = mlp_total[:half, :block].T
    grad_up = mlp_total[half : 2 * half, :block].T
    down_total = mlp_total[2 * half :, :block]
    left, right = down_total[:, :q_cols], down_total[:, q_cols:]
    stay = jnp.where(core_id == 0, left, right)
    give = jnp.where(core_id == 0, right, left).astype(jnp.bfloat16)
    taken = swap_core(give).astype(jnp.float32)
    grad_down = jnp.where(
        core_id == 0, jnp.concatenate([stay, taken], 0), jnp.concatenate([taken, stay], 0)
    )

    kv_total = reduce_all(share_square(kv_mine))
    gain_total = after(jnp.concatenate([gain_one_grad, gain_two_grad], 1).T, *kv_mine)
    gain_total = gain_total + swap_core(gain_total)
    gain_total = gain_total + swap_dp(gain_total, 1)
    gain_total = gain_total + swap_dp(gain_total, 2)
    for mask in (2, 4):
        gain_total = gain_total + lax.ppermute(
            gain_total, "fsdp", [(j, j ^ mask) for j in range(8)]
        )
    gain_grad = lax.dynamic_slice_in_dim(gain_total, slot * q_cols, q_cols, 1)
    return (
        output,
        grad_tokens,
        grad_query,
        kv_total[:k_cols, :block].T,
        kv_total[k_cols:, :block].T,
        grad_out,
        grad_gate,
        grad_up,
        grad_down,
        gain_grad,
    )


def solution(mesh):
    in_specs = (
        P(None, ("dp", "fsdp"), None),
        P(None, ("dp", "fsdp"), None),
        P(None, ("dp", "fsdp")),
        P("dp", "fsdp"),
        P("dp", "fsdp"),
        P("dp", "fsdp"),
        P("dp", "fsdp"),
        P("dp", "fsdp"),
        P("dp", "fsdp"),
        P("dp", "fsdp"),
        P(None, "fsdp"),
    )
    out_specs = (
        P(None, ("dp", "fsdp"), None),
        P(None, ("dp", "fsdp"), None),
        P("dp", "fsdp"),
        P("dp", "fsdp"),
        P("dp", "fsdp"),
        P("dp", "fsdp"),
        P("dp", "fsdp"),
        P("dp", "fsdp"),
        P("dp", "fsdp"),
        P(None, "fsdp"),
    )
    square = mesh.shape["dp"] == 4 and mesh.shape["fsdp"] == 8
    return jax.shard_map(
        fast if square else local, mesh=mesh, in_specs=in_specs, out_specs=out_specs, check_vma=False)
```
